32 devices in a mesh: dp: 2 (over x), seq: 16 (over z, y, core).
Axes of the slice: x: 2, y: 2, z: 4, core: 2. Of those that a mesh axis runs over, the one named last changes fastest.
Arguments:
- tokens: bfloat16 [2, 2048, 768], P('dp', 'seq'), may hold values from -6 to 6
- cotangent: bfloat16 [2, 2048, 768], P('dp', 'seq'), may hold values from -6 to 6
- mix_gain: float32 [2, 768], replicated, may hold values from 0.5 to 1.5
- in_proj: bfloat16 [2, 768, 2304], replicated, may hold values from -0.21875 to 0.21875
- short_taps: float32 [2, 3, 2304], replicated, may hold values from -3 to 3
- filter_first: float32 [2, 33, 64], replicated, may hold values from -1 to 1
- filter_middle: float32 [2, 64, 64], replicated, may hold values from -0.75 to 0.75
- filter_last: float32 [2, 64, 768], replicated, may hold values from -1 to 1
- filter_skip: float32 [2, 768], replicated, may hold values from -4 to 4
- decay_rates: float32 [2, 768], replicated, may hold values from 0.00024414062 to 0.03
- out_proj: bfloat16 [2, 768, 768], replicated, may hold values from -0.21875 to 0.21875
- mlp_gain: float32 [2, 768], replicated, may hold values from 0.5 to 1.5
- up_proj: bfloat16 [2, 768, 3072], replicated, may hold values from -0.21875 to 0.21875
- down_proj: bfloat16 [2, 3072, 768], replicated, may hold values from -0.109375 to 0.109375
Outputs:
- outputs: float32 [2, 2048, 768], P('dp', 'seq')
- grad_tokens: float32 [2, 2048, 768], P('dp', 'seq')
- grad_mix_gain: float32 [2, 768], replicated
- grad_in_proj: float32 [2, 768, 2304], P(None, 'seq', 'dp')
- grad_short_taps: float32 [2, 3, 2304], replicated
- grad_filter_first: float32 [2, 33, 64], replicated
- grad_filter_middle: float32 [2, 64, 64], replicated
- grad_filter_last: float32 [2, 64, 768], P(None, None, 'seq')
- grad_filter_skip: float32 [2, 768], P(None, 'seq')
- grad_out_proj: float32 [2, 768, 768], P(None, 'seq', 'dp')
- grad_mlp_gain: float32 [2, 768], replicated
- grad_up_proj: float32 [2, 768, 3072], P(None, 'seq', 'dp')
- grad_down_proj: float32 [2, 3072, 768], P(None, 'seq', 'dp')
The draws below stay inside these ranges and needn't reach their ends.
All inputs are finite; a program needn't handle non-finite values.
Results may differ from the reference program's by a relative error of at most 0.023.
Values may be sent and summed in bfloat16 or wider, within the bound.
No kernel may reach another device: no remote copies, remote signals or barrier semaphores. Data moves between devices by JAX's collectives and lax.ppermute only.
A program may use at most 320 MiB of HBM per device.

```python
import math
import jax
import jax.numpy as jnp
from jax import lax

D = 768
FF = 3072
FILT = 64
FEATS = 33
LAYERS = 2
LEN = 2048
N_DP = 2


def level_of(key, extent, pieces, smallest, largest):
    def one(axis_at, parts):
        draws = jax.random.uniform(jax.random.fold_in(jax.random.fold_in(key, 6), axis_at), (parts,), jnp.float32, smallest / len(pieces), largest / len(pieces))
        return jnp.repeat(jnp.exp(draws), extent[axis_at] // parts).reshape((-1,) + (1,) * (len(extent) - axis_at - 1))

    factor_of = one(*pieces[0])
    for cut in pieces[1:]:
        factor_of = factor_of * one(*cut)
    return factor_of


def normal_values(stream_key, shape, scale, limit, cuts=(), held_as=jnp.bfloat16):
    array = jax.random.normal(stream_key, shape, jnp.float32) * scale
    if len(cuts) > 0:
        array = level_of(stream_key, shape, cuts, -0.22, 0.18) * array
    return jnp.clip(array, min=-limit, max=limit).astype(held_as)


def setup_inputs(seed: int = 0) -> dict:
    streams_of = jax.random.split(jax.random.key(seed), 15)
    tokens = normal_values(streams_of[0], (N_DP, LEN, D), 1.0, 6.0, ((0, 2), (1, 16)))
    cotangent = normal_values(streams_of[1], (N_DP, LEN, D), 1.0, 6.0, ((0, 2), (1, 16)))
    mix_gain = jnp.clip(1.0 + 0.1 * jax.random.normal(streams_of[2], (LAYERS, D), jnp.float32), 0.5, 1.5)
    in_proj = normal_values(streams_of[3], (LAYERS, D, 3 * D), D ** -0.5, 0.21875)
    short_taps = normal_values(streams_of[4], (LAYERS, 3, 3 * D), 0.6, 3.0, (), jnp.float32)
    filter_first = normal_values(streams_of[5], (LAYERS, FEATS, FILT), FEATS ** -0.5, 1.0, (), jnp.float32)
    filter_middle = normal_values(streams_of[6], (LAYERS, FILT, FILT), FILT ** -0.5, 0.75, (), jnp.float32)
    filter_last = normal_values(streams_of[7], (LAYERS, FILT, D), (FILT // 2) ** -0.5, 1.0, (), jnp.float32)
    filter_skip = normal_values(streams_of[8], (LAYERS, D), 1.0, 4.0, (), jnp.float32)
    decay_rates = jnp.clip(jnp.exp(jax.random.uniform(streams_of[9], (LAYERS, D), jnp.float32, math.log(0.00024414062), math.log(0.03))), 0.00024414062, 0.03)
    out_proj = normal_values(streams_of[10], (LAYERS, D, D), D ** -0.5, 0.21875)
    mlp_gain = jnp.clip(1.0 + 0.1 * jax.random.normal(streams_of[11], (LAYERS, D), jnp.float32), 0.5, 1.5)
    up_proj = normal_values(streams_of[12], (LAYERS, D, FF), D ** -0.5, 0.21875)
    down_proj = normal_values(streams_of[13], (LAYERS, FF, D), FF ** -0.5, 0.109375)
    return dict(tokens=tokens, cotangent=cotangent, mix_gain=mix_gain, in_proj=in_proj, short_taps=short_taps, filter_first=filter_first, filter_middle=filter_middle, filter_last=filter_last, filter_skip=filter_skip, decay_rates=decay_rates, out_proj=out_proj, mlp_gain=mlp_gain, up_proj=up_proj, down_proj=down_proj)


HIGHEST = lax.Precision.HIGHEST
EPSILON = 1e-05

@jax.custom_vjp
def low(v):
    return lax.optimization_barrier(v.astype(jnp.bfloat16)).astype(jnp.float32)

@jax.custom_vjp
def low_back(v):
    return v

def low_keep(v):
    return (low(v), None)

def low_pass(kept, grad):
    return (grad,)

def back_keep(v):
    return (v, None)

def back_low(kept, grad):
    return (low(grad),)
low.defvjp(low_keep, low_pass)
low_back.defvjp(back_keep, back_low)

def layer_norm(state, gain):
    centred = state - lax.optimization_barrier(jnp.mean(state, axis=-1, keepdims=True))
    variance = lax.optimization_barrier(jnp.mean(centred * centred, axis=-1, keepdims=True))
    return centred * lax.rsqrt(variance + EPSILON) * gain

def features_table():
    count = (FEATS - 1) // 2
    steps = jnp.arange(LEN, dtype=jnp.int32)[:, None]
    frequency = jnp.arange(1, count + 1, dtype=jnp.int32)[None, :]
    angle = (steps * frequency % LEN).astype(jnp.float32) * (2.0 * math.pi / LEN)
    ramp = steps.astype(jnp.float32) / LEN
    return jnp.concatenate([ramp, jnp.cos(angle), jnp.sin(angle)], axis=1)

def long_filter(first, middle, last, rates):
    act_one = jnp.sin(jnp.dot(features_table(), first, precision=HIGHEST))
    act_two = jnp.sin(jnp.dot(act_one, middle, precision=HIGHEST))
    raw = jnp.dot(act_two, last, precision=HIGHEST)
    steps = jnp.arange(LEN, dtype=jnp.int32).astype(jnp.float32)[:, None]
    return raw * (jnp.exp(-rates[None, :] * steps) * jnp.sqrt(rates[None, :] + 1.0 / LEN))

def causal_conv(signal, response):
    size = 2 * LEN
    spectrum = jnp.fft.rfft(signal, n=size, axis=0) * jnp.fft.rfft(response, n=size, axis=0)
    return jnp.fft.irfft(spectrum, n=size, axis=0)[:LEN]

def short_conv(projected, taps):
    one = jnp.pad(projected, ((1, 0), (0, 0)))[:LEN]
    two = jnp.pad(projected, ((2, 0), (0, 0)))[:LEN]
    return taps[0] * projected + taps[1] * one + taps[2] * two

def layer(state, mix_gain, in_proj, short_taps, first, middle, last, skip, rates, out_proj, mlp_gain, up_proj, down_proj):
    normed = low(layer_norm(state, mix_gain))
    projected = low_back(low(jnp.dot(normed, in_proj, precision=HIGHEST)))
    shorted = short_conv(projected, short_taps)
    branch_zero = shorted[:, :D]
    branch_one = shorted[:, D:2 * D]
    branch_value = shorted[:, 2 * D:]
    gated = low_back(low(branch_value * branch_one))
    response = long_filter(first, middle, last, rates)
    conv = low_back(low(causal_conv(gated, response) + skip * gated))
    mixed = low_back(low(conv * branch_zero))
    middle_state = state + low_back(jnp.dot(mixed, out_proj, precision=HIGHEST))
    normed_mlp = low(layer_norm(middle_state, mlp_gain))
    hidden = low_back(jnp.dot(normed_mlp, up_proj, precision=HIGHEST))
    active = low(jax.nn.gelu(hidden))
    return middle_state + low_back(jnp.dot(active, down_proj, precision=HIGHEST))

def forward(tokens, weights, rates):
    results = []
    for group in range(N_DP):
        state = tokens[group]
        for level in range(LAYERS):
            picked = [item[level] for item in weights]
            state = layer(state, picked[0], picked[1], picked[2], picked[3], picked[4], picked[5], picked[6], rates[level], picked[7], picked[8], picked[9], picked[10])
        results.append(state)
    return jnp.stack(results)

def reference(tokens, cotangent, mix_gain, in_proj, short_taps, filter_first, filter_middle, filter_last, filter_skip, decay_rates, out_proj, mlp_gain, up_proj, down_proj):
    weights = tuple((item.astype(jnp.float32) for item in (mix_gain, in_proj, short_taps, filter_first, filter_middle, filter_last, filter_skip, out_proj, mlp_gain, up_proj, down_proj)))
    rates = decay_rates.astype(jnp.float32)

    def run(start, *params):
        return forward(start, params, rates)
    outputs, pull = jax.vjp(run, tokens.astype(jnp.float32), *weights)
    grads = pull(cotangent.astype(jnp.float32))
    return (outputs, grads[0], grads[1], grads[2], grads[3], grads[4], grads[5], grads[6], grads[7], grads[8], grads[9], grads[10], grads[11])
```

```python
import functools
import math

import jax
import jax.numpy as jnp
import ml_dtypes
import numpy as np
from jax import lax
from jax.experimental import pallas as pl
from jax.experimental.pallas import tpu as pltpu
from jax.sharding import PartitionSpec as P

FEATS = 33
FFT_COLS = 512


HIGHEST = lax.Precision.HIGHEST
EPSILON = 1e-05


def from_behind(block, axis, distance):
    devices = range(lax.axis_size(axis))
    route = [(i - distance, i) for i in devices if i - distance in devices]
    return lax.ppermute(block, axis, route)


def high_einsum(form, left, right):
    return jnp.einsum(form, left, right, precision=HIGHEST)


def low_einsum(form, left, right):
    return jnp.einsum(form, left, right, preferred_element_type=jnp.float32)


def to_low(value):
    return lax.optimization_barrier(value.astype(jnp.bfloat16))


def angle_table(rows, columns, modulus):
    product = lax.broadcasted_iota(jnp.int32, (rows, columns), 0) * lax.broadcasted_iota(
        jnp.int32, (rows, columns), 1
    )
    angle = (product % modulus).astype(jnp.float32) * (2.0 * math.pi / modulus)
    return (jnp.cos(angle), jnp.sin(angle))


def transform_tables(length, columns):
    total = 2 * length
    rows = total // columns
    cos_rows, sin_rows = angle_table(rows, rows, rows)
    cos_columns, sin_columns = angle_table(columns, columns, columns)
    cos_turn, sin_turn = angle_table(rows, columns, total)
    return (cos_rows, sin_rows, cos_columns, sin_columns, cos_turn, sin_turn)


def forward_transform(signal, tables):
    cos_rows, sin_rows, cos_columns, sin_columns, cos_turn, sin_turn = tables
    channels, length = signal.shape
    rows, columns = cos_turn.shape
    padded = jnp.pad(signal, ((0, 0), (0, length))).reshape(channels, rows, columns)
    first_real = high_einsum("kq,cqp->ckp", cos_rows, padded)
    first_imag = -high_einsum("kq,cqp->ckp", sin_rows, padded)
    turned_real = first_real * cos_turn + first_imag * sin_turn
    turned_imag = first_imag * cos_turn - first_real * sin_turn
    spec_real = high_einsum("ckp,pj->ckj", turned_real, cos_columns) + high_einsum(
        "ckp,pj->ckj", turned_imag, sin_columns
    )
    spec_imag = high_einsum("ckp,pj->ckj", turned_imag, cos_columns) - high_einsum(
        "ckp,pj->ckj", turned_real, sin_columns
    )
    return (spec_real, spec_imag)


def inverse_transform(spec_real, spec_imag, tables):
    cos_rows, sin_rows, cos_columns, sin_columns, cos_turn, sin_turn = tables
    rows, columns = cos_turn.shape
    back_real = high_einsum("ckp,pj->ckj", spec_real, cos_columns) - high_einsum(
        "ckp,pj->ckj", spec_imag, sin_columns
    )
    back_imag = high_einsum("ckp,pj->ckj", spec_imag, cos_columns) + high_einsum(
        "ckp,pj->ckj", spec_real, sin_columns
    )
    turned_real = back_real * cos_turn - back_imag * sin_turn
    turned_imag = back_imag * cos_turn + back_real * sin_turn
    signal = high_einsum("qk,ckp->cqp", cos_rows, turned_real) - high_einsum(
        "qk,ckp->cqp", sin_rows, turned_imag
    )
    total = rows * columns
    return signal.reshape(signal.shape[0], total)[:, : total // 2] / total


def position_features(length):
    count = (FEATS - 1) // 2
    steps = lax.broadcasted_iota(jnp.int32, (count, length), 1)
    frequency = lax.broadcasted_iota(jnp.int32, (count, length), 0) + 1
    angle = (steps * frequency % length).astype(jnp.float32) * (2.0 * math.pi / length)
    ramp = lax.broadcasted_iota(jnp.int32, (1, length), 1).astype(jnp.float32) / length
    return jnp.concatenate([ramp, jnp.cos(angle), jnp.sin(angle)], axis=0)


def filter_forward(features, first, middle, last_columns, rate_columns, length):
    pre_one = high_einsum("fk,ft->kt", first, features)
    act_one = jnp.sin(pre_one)
    pre_two = high_einsum("kj,kt->jt", middle, act_one)
    act_two = jnp.sin(pre_two)
    raw = high_einsum("kc,kt->ct", last_columns, act_two)
    steps = lax.broadcasted_iota(jnp.int32, (1, length), 1).astype(jnp.float32)
    window = jnp.exp(-rate_columns[:, None] * steps) * jnp.sqrt(
        rate_columns[:, None] + 1.0 / length
    )
    return (raw * window, (pre_one, act_one, pre_two, act_two, window))


def filter_backward(d_response, features, middle, last_columns, kept):
    pre_one, act_one, pre_two, act_two, window = kept
    d_raw = d_response * window
    g_last = high_einsum("kt,ct->kc", act_two, d_raw)
    d_two = high_einsum("kc,ct->kt", last_columns, d_raw) * jnp.cos(pre_two)
    g_middle = high_einsum("kt,jt->kj", act_one, d_two)
    d_one = high_einsum("kj,jt->kt", middle, d_two) * jnp.cos(pre_one)
    g_first = high_einsum("ft,kt->fk", features, d_one)
    return (g_first, g_middle, g_last)


def normalize(state):
    centred = state - jnp.mean(state, axis=1, keepdims=True)
    scale = lax.rsqrt(jnp.mean(centred * centred, axis=1, keepdims=True) + EPSILON)
    return (centred * scale, scale)


def normalize_back(d_out, normed, scale, gain):
    d_normed = d_out * gain
    g_gain = jnp.sum(d_out * normed, axis=0)
    d_state = scale * (
        d_normed
        - jnp.mean(d_normed, axis=1, keepdims=True)
        - normed * jnp.mean(d_normed * normed, axis=1, keepdims=True)
    )
    return (d_state, g_gain)


def short_forward(extended, taps):
    length = extended.shape[-1] - 2
    return (
        taps[0] * extended[..., 2:]
        + taps[1] * extended[..., 1 : length + 1]
        + taps[2] * extended[..., :length]
    )


def short_backward(d_extended, taps):
    length = d_extended.shape[-1] - 2
    return (
        taps[0] * d_extended[..., :length]
        + taps[1] * d_extended[..., 1 : length + 1]
        + taps[2] * d_extended[..., 2:]
    )


def tap_grads(d_shorted, extended):
    length = d_shorted.shape[-1]
    return jnp.stack(
        [
            jnp.sum(d_shorted * extended[..., 2 - lag : 2 - lag + length], axis=-1)
            for lag in range(3)
        ]
    )


def long_forward(gated, filter_real, filter_imag, skip_columns, tables):
    signal = gated.astype(jnp.float32)
    sig_real, sig_imag = forward_transform(signal, tables)
    result = inverse_transform(
        sig_real * filter_real - sig_imag * filter_imag,
        sig_real * filter_imag + sig_imag * filter_real,
        tables,
    )
    return (result + skip_columns[:, None] * signal, (sig_real, sig_imag))


def long_backward(d_conv, gated, filter_real, filter_imag, skip_columns, signal_spec, tables):
    d_signal = d_conv.astype(jnp.float32)
    d_real, d_imag = forward_transform(d_signal, tables)
    sig_real, sig_imag = signal_spec
    d_gated = (
        inverse_transform(
            d_real * filter_real + d_imag * filter_imag,
            d_imag * filter_real - d_real * filter_imag,
            tables,
        )
        + skip_columns[:, None] * d_signal
    )
    d_response = inverse_transform(
        d_real * sig_real + d_imag * sig_imag, d_imag * sig_real - d_real * sig_imag, tables
    )
    g_skip = jnp.sum(d_signal * gated.astype(jnp.float32), axis=1)
    return (d_gated, d_response, g_skip)


def unit(k,n):
    k%=n
    if (4*k)%n==0:
        q=(4*k)//n
        return [(1.0,0.0),(0.0,-1.0),(-1.0,0.0),(0.0,1.0)][q]
    a=-2.0*math.pi*k/n
    return (math.cos(a),math.sin(a))
def times(z,w):
    re,im=z; c,s=w
    if s==0.0: return (re,im) if c==1.0 else (-re,-im)
    if c==0.0: return (-im,re) if s==1.0 else (im,-re)
    return (re*c-im*s, re*s+im*c)
def plus(a,b): return (a[0]+b[0],a[1]+b[1])
def minus(a,b): return (a[0]-b[0],a[1]-b[1])
def complex_dft(zs,sign):
    n=len(zs)
    if n==1: return zs
    ev=complex_dft(zs[0::2],sign); od=complex_dft(zs[1::2],sign)
    lo,hi=[],[]
    for k in range(n//2):
        v=times(od[k],unit(sign*k,n))
        lo.append(plus(ev[k],v)); hi.append(minus(ev[k],v))
    return lo+hi
def odd_bins(xs):
    n=len(xs); h=n//2; N=2*n
    zs=[times((xs[j],-xs[j+h]),unit(j,N)) for j in range(h)]
    bins={}
    for q,z in enumerate(complex_dft(zs,1)):
        k=4*q+1
        if k<=n: bins[k]=z
        else: bins[N-k]=(z[0],-z[1])
    return bins
def real_bins(xs):
    n=len(xs)
    if n==1: return {0:(xs[0],None)}
    if n==2: return {0:(xs[0]+xs[1],None),1:(xs[0]-xs[1],None)}
    h=n//2
    bins={2*k:z for k,z in real_bins([xs[j]+xs[j+h] for j in range(h)]).items()}
    bins.update(odd_bins([xs[j]-xs[j+h] for j in range(h)]))
    return bins
def padded_bins(xs):
    bins={2*k:z for k,z in real_bins(xs).items()}
    bins.update(odd_bins(xs))
    return bins
def odd_back(bins,n):
    h=n//2; N=2*n
    zs=[]
    for q in range(h):
        k=4*q+1
        if k<=n: zs.append(bins[k])
        else:
            re,im=bins[N-k]; zs.append((re,-im))
    vs=[times(z,unit(-j,N)) for j,z in enumerate(complex_dft(zs,-1))]
    return [v[0] for v in vs]+[-v[1] for v in vs]
def real_back(bins,n):
    if n==1: return [bins[0][0]]
    if n==2: return [bins[0][0]+bins[1][0],bins[0][0]-bins[1][0]]
    h=n//2
    ev=real_back({k//2:z for k,z in bins.items() if k%2==0},h)
    od=odd_back(bins,h)
    return [ev[j]+od[j] for j in range(h)]+[ev[j]-od[j] for j in range(h)]
def padded_back(bins,n):
    ev=real_back({k//2:z for k,z in bins.items() if k%2==0},n)
    od=odd_back(bins,n)
    return [a+b for a,b in zip(ev,od)]


def turn_table(shards, rows):
    total = 2 * shards * rows
    early = np.arange(rows)[None, :, None]
    late = np.arange(rows)[None, None, :]
    bins = np.arange(shards + 1)[:, None, None]
    angle = (early * (bins + 2 * shards * late) % total) * (2.0 * np.pi / total)
    cos, sin = np.cos(angle), np.sin(angle)
    top = np.concatenate([cos, -sin], axis=2)
    bottom = np.concatenate([sin, cos], axis=2)
    return jnp.asarray(np.concatenate([top, bottom], axis=1).astype(ml_dtypes.bfloat16))


def position_table(length):
    count = (FEATS - 1) // 2
    steps = np.arange(length)[None, :]
    angle = (steps * np.arange(1, count + 1)[:, None] % length) * (2.0 * np.pi / length)
    table = np.concatenate([steps / length, np.cos(angle), np.sin(angle)], axis=0)
    return jnp.asarray(table.astype(np.float32))


def chunks_of(channels):
    step = 16 if channels % 16 == 0 else channels
    return [slice(at, at + step) for at in range(0, channels, step)]


def load_bins(blocks, bins_ref, chunk):
    lanes = blocks[0].shape[-1]
    for k, (re, im) in padded_bins(blocks).items():
        im = jnp.zeros_like(re) if im is None else im
        bins_ref[k, chunk, :lanes] = re.astype(jnp.bfloat16)
        bins_ref[k, chunk, lanes:] = im.astype(jnp.bfloat16)


def fold_bins(back_ref, chunk, count, lanes):
    bins = {
        k: (back_ref[k, chunk, :lanes], back_ref[k, chunk, lanes:]) for k in range(count + 1)
    }
    return padded_back(bins, count)


def bin_scale(k, shards, rows):
    total = 2 * shards * rows
    return (1.0 if k in (0, shards) else 2.0) / total


def bin_product(left, right, conjugate):
    lanes = left.shape[1] // 2
    a, b = left[:, :lanes], left[:, lanes:]
    c, d = right[:, :lanes], right[:, lanes:]
    if conjugate:
        return jnp.concatenate([a * c + b * d, b * c - a * d], axis=1)
    return jnp.concatenate([a * c - b * d, a * d + b * c], axis=1)


def turn(left, table):
    return jnp.dot(left, table, preferred_element_type=jnp.float32)


def turn_back(left, table):
    return lax.dot_general(
        left.astype(jnp.bfloat16),
        table,
        (((1,), (1,)), ((), ())),
        preferred_element_type=jnp.float32,
    )


def sin_cos(angle):
    steps = jnp.floor(angle * (2.0 / math.pi) + 0.5)
    rest = angle - steps * 1.5703125
    rest = rest - steps * 4.837512969970703e-4
    rest = rest - steps * 7.549789954891882e-8
    square = rest * rest
    sin = rest + rest * square * (
        -1.6666654611e-1 + square * (8.3321608736e-3 + square * -1.9515295891e-4)
    )
    cos = (
        1.0
        - 0.5 * square
        + square
        * square
        * (4.166664568298827e-2 + square * (-1.388731625493765e-3 + square * 2.443315711809948e-5))
    )
    quarter = steps.astype(jnp.int32)
    odd = (quarter & 1) == 1
    sin_out = jnp.where(odd, cos, sin)
    cos_out = jnp.where(odd, sin, cos)
    sin_out = jnp.where((quarter & 2) == 2, -sin_out, sin_out)
    cos_out = jnp.where(((quarter + 1) & 2) == 2, -cos_out, cos_out)
    return sin_out, cos_out


def across(left, right, left_side, right_side):
    return lax.dot_general(
        left,
        right,
        (((left_side,), (right_side,)), ((), ())),
        precision=HIGHEST,
        preferred_element_type=jnp.float32,
    )


def filter_network_kernel(
    feature_ref,
    first_ref,
    middle_ref,
    last_ref,
    rate_ref,
    table_ref,
    spec_ref,
    one_ref,
    slope_one_ref,
    two_ref,
    slope_two_ref,
    window_ref,
    raw_ref,
    bins_ref,
):
    shards, channels, rows = window_ref.shape
    one, slope_one = sin_cos(across(first_ref[...], feature_ref[...], 0, 0))
    one_ref[...] = one
    slope_one_ref[...] = slope_one
    two, slope_two = sin_cos(across(middle_ref[...], one, 0, 0))
    two_ref[...] = two
    slope_two_ref[...] = slope_two
    raw_ref[...] = across(last_ref[...], two, 0, 0)
    rate = rate_ref[...]
    size = jnp.sqrt(rate + 1.0 / (shards * rows))
    step = lax.broadcasted_iota(jnp.int32, (channels, rows), 1)
    for j in range(shards):
        window = jnp.exp(-rate * (step + j * rows).astype(jnp.float32)) * size
        window_ref[j] = window
        at = slice(j * rows, (j + 1) * rows)
        raw_ref[:, at] = raw_ref[:, at] * window
    for chunk in chunks_of(channels):
        load_bins(
            [raw_ref[chunk, j * rows : (j + 1) * rows] for j in range(shards)], bins_ref, chunk
        )
    for k in range(shards + 1):
        spec_ref[k] = turn(bins_ref[k], table_ref[k]) * bin_scale(k, shards, rows)


def filter_network(features, first, middle, last, rates, table):
    hidden, channels = last.shape
    length = features.shape[1]
    bins, span, _ = table.shape
    rows = span // 2
    shards = length // rows
    wide = jax.ShapeDtypeStruct((hidden, length), jnp.float32)
    return pl.pallas_call(
        filter_network_kernel,
        out_shape=[
            jax.ShapeDtypeStruct((bins, channels, span), jnp.float32),
            wide,
            wide,
            wide,
            wide,
            jax.ShapeDtypeStruct((shards, channels, rows), jnp.float32),
        ],
        scratch_shapes=[
            pltpu.VMEM((channels, length), jnp.float32),
            pltpu.VMEM((bins, channels, span), jnp.bfloat16),
        ],
        compiler_params=pltpu.CompilerParams(vmem_limit_bytes=40 << 20),
        name="filter_network",
    )(features, first, middle, last, rates, table)


def conv_forward_kernel(
    gated_ref, filter_ref, skip_ref, table_ref, conv_ref, spec_ref, bins_ref, back_ref
):
    shards, channels, rows = gated_ref.shape
    for chunk in chunks_of(channels):
        load_bins(
            [gated_ref[j, chunk].astype(jnp.float32) for j in range(shards)], bins_ref, chunk
        )
    for k in range(shards + 1):
        spec = turn(bins_ref[k], table_ref[k])
        spec_ref[k] = spec.astype(jnp.bfloat16)
        back_ref[k] = turn_back(bin_product(spec, filter_ref[k], False), table_ref[k])
    for chunk in chunks_of(channels):
        skip = skip_ref[chunk]
        for j, block in enumerate(fold_bins(back_ref, chunk, shards, rows)):
            conv = block + skip * gated_ref[j, chunk].astype(jnp.float32)
            conv_ref[j, chunk] = conv.astype(jnp.bfloat16)


def conv_backward_kernel(
    gated_ref, filter_ref, skip_ref, table_ref, conv_ref, spec_ref, bins_ref, back_ref
):
    shards, channels, rows = gated_ref.shape
    for chunk in chunks_of(channels):
        load_bins(
            [gated_ref[j, chunk].astype(jnp.float32) for j in range(shards)], bins_ref, chunk
        )
    for k in range(shards + 1):
        spec = turn(bins_ref[k], table_ref[k])
        spec_ref[k] = spec.astype(jnp.bfloat16)
        back_ref[k] = turn_back(bin_product(spec, filter_ref[k], True), table_ref[k])
    for chunk in chunks_of(channels):
        skip = skip_ref[chunk]
        for j, block in enumerate(fold_bins(back_ref, chunk, shards, rows)):
            conv = block + skip * gated_ref[j, chunk].astype(jnp.float32)
            conv_ref[j, chunk] = conv.astype(jnp.bfloat16)


def conv_call(kernel, name, gated, filter_spec, skip, table):
    bins, channels, span = filter_spec.shape
    return pl.pallas_call(
        kernel,
        out_shape=[
            jax.ShapeDtypeStruct(gated.shape, jnp.bfloat16),
            jax.ShapeDtypeStruct((bins, channels, span), jnp.bfloat16),
        ],
        scratch_shapes=[
            pltpu.VMEM((bins, channels, span), jnp.bfloat16),
            pltpu.VMEM((bins, channels, span), jnp.float32),
        ],
        compiler_params=pltpu.CompilerParams(vmem_limit_bytes=40 << 20),
        name=name,
    )(gated, filter_spec, skip, table)


def conv_forward(gated, filter_spec, skip, table):
    return conv_call(conv_forward_kernel, "conv_forward", gated, filter_spec, skip, table)


def conv_backward(d_conv, filter_spec, skip, table):
    return conv_call(conv_backward_kernel, "conv_backward", d_conv, filter_spec, skip, table)


def filter_back_kernel(
    d_spec_ref,
    spec_ref,
    d_conv_ref,
    gated_ref,
    feature_ref,
    middle_ref,
    last_ref,
    one_ref,
    slope_one_ref,
    two_ref,
    slope_two_ref,
    window_ref,
    table_ref,
    g_first_ref,
    g_middle_ref,
    g_last_ref,
    g_skip_ref,
    back_ref,
    raw_ref,
):
    shards, channels, rows = d_conv_ref.shape
    for k in range(shards + 1):
        spec = bin_product(
            d_spec_ref[k].astype(jnp.float32), spec_ref[k].astype(jnp.float32), True
        )
        back_ref[k] = turn_back(spec * bin_scale(k, shards, rows), table_ref[k])
    for chunk in chunks_of(channels):
        total = None
        for j, block in enumerate(fold_bins(back_ref, chunk, shards, rows)):
            raw_ref[chunk, j * rows : (j + 1) * rows] = block * window_ref[j, chunk]
            term = d_conv_ref[j, chunk].astype(jnp.float32) * gated_ref[j, chunk].astype(
                jnp.float32
            )
            total = term if total is None else total + term
        g_skip_ref[chunk] = jnp.sum(total, axis=1, keepdims=True)
    d_raw = raw_ref[...]
    g_last_ref[...] = across(two_ref[...], d_raw, 1, 1)
    d_two = across(last_ref[...], d_raw, 1, 0) * slope_two_ref[...]
    g_middle_ref[...] = across(one_ref[...], d_two, 1, 1)
    d_one = across(middle_ref[...], d_two, 1, 0) * slope_one_ref[...]
    g_first_ref[...] = across(feature_ref[...], d_one, 1, 1)


def filter_network_back(
    d_spec, spec, d_conv, gated, features, middle, last, kept, table
):
    _, one, slope_one, two, slope_two, window = kept
    bins, channels, span = spec.shape
    hidden, length = one.shape
    feats = features.shape[0]
    return pl.pallas_call(
        filter_back_kernel,
        out_shape=[
            jax.ShapeDtypeStruct((feats, hidden), jnp.float32),
            jax.ShapeDtypeStruct((hidden, hidden), jnp.float32),
            jax.ShapeDtypeStruct((hidden, channels), jnp.float32),
            jax.ShapeDtypeStruct((channels, 1), jnp.float32),
        ],
        scratch_shapes=[
            pltpu.VMEM((bins, channels, span), jnp.float32),
            pltpu.VMEM((channels, length), jnp.float32),
        ],
        compiler_params=pltpu.CompilerParams(vmem_limit_bytes=40 << 20),
        name="filter_network_back",
    )(
        d_spec,
        spec,
        d_conv,
        gated,
        features,
        middle,
        last,
        one,
        slope_one,
        two,
        slope_two,
        window,
        table,
    )


def layer_forward(state, weights, setting):
    (
        mix_gain,
        in_proj,
        short_taps,
        first,
        middle,
        last,
        skip,
        rates,
        out_proj,
        mlp_gain,
        up_proj,
        down_proj,
    ) = weights
    features, tables, offset = setting
    rows, width = state.shape
    length = features.shape[1]
    channels = width // (length // rows)
    normed_mix, scale_mix = normalize(state)
    u_mix = to_low(normed_mix * mix_gain)
    projected = to_low(low_einsum("td,dc->ct", u_mix, in_proj)).reshape(3, width, rows)
    last_columns = lax.dynamic_slice_in_dim(last, offset, channels, 1)
    skip_columns = lax.dynamic_slice_in_dim(skip, offset, channels, 0)
    rate_columns = lax.dynamic_slice_in_dim(rates, offset, channels, 0)
    filter_kept = filter_network(
        features, first, middle, last_columns, rate_columns[:, None], tables
    )
    filter_spec = filter_kept[0]
    taps = short_taps.reshape(3, 3, width)
    edge = from_behind(projected[:, :, rows - 2 :], "seq", 1)
    extended = jnp.concatenate([edge, projected], axis=2).astype(jnp.float32)
    tap_use = taps[:, :, :, None]
    shorted = short_forward(extended, tap_use)
    gated_rows = to_low(shorted[2] * shorted[1])
    shards = length // rows
    gated = lax.all_to_all(
        gated_rows.reshape(shards, channels, rows), "seq", split_axis=0, concat_axis=0, tiled=True
    )
    conv_low, signal_spec = conv_forward(gated, filter_spec, skip_columns[:, None], tables)
    conv_here = lax.all_to_all(
        conv_low, "seq", split_axis=0, concat_axis=0, tiled=True
    ).reshape(width, rows)
    mixed = to_low(conv_here.astype(jnp.float32) * shorted[0])
    middle_state = state + low_einsum("ct,ce->te", mixed, out_proj)
    normed_mlp, scale_mlp = normalize(middle_state)
    u_mlp = to_low(normed_mlp * mlp_gain)
    hidden = low_einsum("td,df->tf", u_mlp, up_proj)
    active = to_low(jax.nn.gelu(hidden))
    result = middle_state + low_einsum("tf,fe->te", active, down_proj)
    kept = (
        normed_mix,
        scale_mix,
        u_mix,
        extended,
        shorted,
        gated,
        conv_here,
        mixed,
        filter_kept,
        filter_spec,
        signal_spec,
        normed_mlp,
        scale_mlp,
        u_mlp,
        hidden,
        active,
        last_columns,
        skip_columns,
        tap_use,
    )
    return (result, kept)


def layer_backward(upstream, kept, weights, setting):
    (
        mix_gain,
        in_proj,
        short_taps,
        first,
        middle,
        last,
        skip,
        rates,
        out_proj,
        mlp_gain,
        up_proj,
        down_proj,
    ) = weights
    features, tables, offset = setting
    (
        normed_mix,
        scale_mix,
        u_mix,
        extended,
        shorted,
        gated,
        conv_here,
        mixed,
        filter_kept,
        filter_spec,
        signal_spec,
        normed_mlp,
        scale_mlp,
        u_mlp,
        hidden,
        active,
        last_columns,
        skip_columns,
        tap_use,
    ) = kept
    rows, width = upstream.shape
    d_down = to_low(upstream)
    g_down = low_einsum("tf,te->fe", active, d_down)
    d_active = low_einsum("te,fe->tf", d_down, down_proj)
    d_hidden = to_low(jax.vjp(jax.nn.gelu, hidden)[1](d_active)[0])
    g_up = low_einsum("td,tf->df", u_mlp, d_hidden)
    d_u_mlp = low_einsum("tf,df->td", d_hidden, up_proj)
    d_middle, g_mlp_gain = normalize_back(d_u_mlp, normed_mlp, scale_mlp, mlp_gain)
    d_middle = d_middle + upstream
    d_branch = to_low(d_middle)
    g_out = low_einsum("ct,te->ce", mixed, d_branch)
    d_mixed = to_low(low_einsum("te,ce->ct", d_branch, out_proj))
    d_mixed_wide = d_mixed.astype(jnp.float32)
    d_conv_rows = to_low(d_mixed_wide * shorted[0])
    d_zero = d_mixed_wide * conv_here.astype(jnp.float32)
    shards, channels, _ = gated.shape
    d_conv = lax.all_to_all(
        d_conv_rows.reshape(gated.shape), "seq", split_axis=0, concat_axis=0, tiled=True
    )
    d_gated, d_spec = conv_backward(d_conv, filter_spec, skip_columns[:, None], tables)
    d_gated_rows = lax.all_to_all(
        d_gated, "seq", split_axis=0, concat_axis=0, tiled=True
    ).reshape(width, rows).astype(jnp.float32)
    d_shorted = jnp.stack([d_zero, d_gated_rows * shorted[2], d_gated_rows * shorted[1]])
    after = from_behind(d_shorted[:, :, :2], "seq", -1)
    d_extended = jnp.concatenate([d_shorted, after], axis=2)
    d_projected = to_low(short_backward(d_extended, tap_use))
    g_taps = tap_grads(d_shorted, extended)
    g_first, g_middle, g_last, g_skip = filter_network_back(
        d_spec, signal_spec, d_conv, gated, features, middle, last_columns, filter_kept, tables
    )
    g_skip = g_skip[:, 0]
    d_flat = d_projected.reshape(3 * width, rows)
    g_in = low_einsum("td,ct->dc", u_mix, d_flat)
    d_u_mix = low_einsum("ct,dc->td", d_flat, in_proj)
    d_state, g_mix_gain = normalize_back(d_u_mix, normed_mix, scale_mix, mix_gain)
    d_state = d_state + d_middle
    large = (g_in, g_out, g_up, g_down)
    small = (g_mix_gain, g_taps.reshape(3, 3 * width), g_first, g_middle, g_mlp_gain)
    column_part = (g_last, g_skip)
    return (d_state, large, small, column_part)


def body(
    tokens,
    cotangent,
    mix_gain,
    in_proj,
    short_taps,
    filter_first,
    filter_middle,
    filter_last,
    filter_skip,
    decay_rates,
    out_proj,
    mlp_gain,
    up_proj,
    down_proj,
):
    rows = tokens.shape[1]
    width = tokens.shape[2]
    layer_count = mix_gain.shape[0]
    shards = lax.axis_size("seq")
    length = rows * shards
    offset = lax.axis_index("seq") * (width // shards)
    setting = (position_table(length), turn_table(shards, rows), offset)
    stacks = (
        mix_gain,
        in_proj,
        short_taps,
        filter_first,
        filter_middle,
        filter_last,
        filter_skip,
        decay_rates,
        out_proj,
        mlp_gain,
        up_proj,
        down_proj,
    )
    state = tokens[0].astype(jnp.float32)
    kept_all = []
    for level in range(layer_count):
        weights = tuple((item[level] for item in stacks))
        state, kept = layer_forward(state, weights, setting)
        kept_all.append(kept)
    upstream = cotangent[0].astype(jnp.float32)
    large_all = [None] * layer_count
    small_all = [None] * layer_count
    column_all = [None] * layer_count
    for level in reversed(range(layer_count)):
        weights = tuple((item[level] for item in stacks))
        upstream, large, small, column_part = layer_backward(
            upstream, kept_all[level], weights, setting
        )
        large_all[level] = large
        small_all[level] = small
        column_all[level] = column_part
    stacked_large = [
        jnp.stack([large_all[level][member] for level in range(layer_count)]) for member in range(4)
    ]
    row_in, row_out, row_up, row_down = (
        lax.psum_scatter(stacked_large[0], "seq", scatter_dimension=1, tiled=True),
        lax.psum_scatter(stacked_large[1], "seq", scatter_dimension=1, tiled=True),
        lax.psum_scatter(stacked_large[2], "seq", scatter_dimension=1, tiled=True),
        lax.psum_scatter(stacked_large[3], "seq", scatter_dimension=1, tiled=True),
    )
    g_in, g_out, g_up, g_down = (
        lax.psum_scatter(row_in.astype(jnp.bfloat16), "dp", scatter_dimension=2, tiled=True).astype(
            jnp.float32
        ),
        lax.psum_scatter(
            row_out.astype(jnp.bfloat16), "dp", scatter_dimension=2, tiled=True
        ).astype(jnp.float32),
        lax.psum_scatter(row_up.astype(jnp.bfloat16), "dp", scatter_dimension=2, tiled=True).astype(
            jnp.float32
        ),
        lax.psum_scatter(
            row_down.astype(jnp.bfloat16), "dp", scatter_dimension=2, tiled=True
        ).astype(jnp.float32),
    )
    stacked_small = [
        jnp.stack([small_all[level][member] for level in range(layer_count)]) for member in range(5)
    ]
    g_mix_gain, g_taps, g_first, g_middle, g_mlp_gain = lax.psum(
        (stacked_small[0], stacked_small[1], stacked_small[2], stacked_small[3], stacked_small[4]),
        ("dp", "seq"),
    )
    stacked_last = jnp.stack([column_all[level][0] for level in range(layer_count)])
    stacked_skip = jnp.stack([column_all[level][1] for level in range(layer_count)])
    g_last, g_skip = lax.psum((stacked_last, stacked_skip), "dp")
    return (
        state[None],
        upstream[None],
        g_mix_gain,
        g_in,
        g_taps,
        g_first,
        g_middle,
        g_last,
        g_skip,
        g_out,
        g_mlp_gain,
        g_up,
        g_down,
    )


def solution(mesh):
    in_specs = (
        P("dp", "seq", None),
        P("dp", "seq", None),
        P(),
        P(),
        P(),
        P(),
        P(),
        P(),
        P(),
        P(),
        P(),
        P(),
        P(),
        P(),
    )
    out_specs = (
        P("dp", "seq", None),
        P("dp", "seq", None),
        P(),
        P(None, "seq", "dp"),
        P(),
        P(),
        P(),
        P(None, None, "seq"),
        P(None, "seq"),
        P(None, "seq", "dp"),
        P(),
        P(None, "seq", "dp"),
        P(None, "seq", "dp"),
    )
    return jax.shard_map(body, mesh=mesh, in_specs=in_specs, out_specs=out_specs, check_vma=False)
```

```python
import functools
import math

import jax
import jax.numpy as jnp
import ml_dtypes
import numpy as np
from jax import lax
from jax.experimental import pallas as pl
from jax.experimental.pallas import tpu as pltpu
from jax.sharding import PartitionSpec as P

FEATS = 33
FFT_COLS = 512


HIGHEST = lax.Precision.HIGHEST
EPSILON = 1e-05


def from_behind(block, axis, distance):
    devices = range(lax.axis_size(axis))
    route = [(i - distance, i) for i in devices if i - distance in devices]
    return lax.ppermute(block, axis, route)


def high_einsum(form, left, right):
    return jnp.einsum(form, left, right, precision=HIGHEST)


def low_einsum(form, left, right):
    return jnp.einsum(form, left, right, preferred_element_type=jnp.float32)


def to_low(value):
    return lax.optimization_barrier(value.astype(jnp.bfloat16))


def angle_table(rows, columns, modulus):
    product = lax.broadcasted_iota(jnp.int32, (rows, columns), 0) * lax.broadcasted_iota(
        jnp.int32, (rows, columns), 1
    )
    angle = (product % modulus).astype(jnp.float32) * (2.0 * math.pi / modulus)
    return (jnp.cos(angle), jnp.sin(angle))


def transform_tables(length, columns):
    total = 2 * length
    rows = total // columns
    cos_rows, sin_rows = angle_table(rows, rows, rows)
    cos_columns, sin_columns = angle_table(columns, columns, columns)
    cos_turn, sin_turn = angle_table(rows, columns, total)
    return (cos_rows, sin_rows, cos_columns, sin_columns, cos_turn, sin_turn)


def forward_transform(signal, tables):
    cos_rows, sin_rows, cos_columns, sin_columns, cos_turn, sin_turn = tables
    channels, length = signal.shape
    rows, columns = cos_turn.shape
    padded = jnp.pad(signal, ((0, 0), (0, length))).reshape(channels, rows, columns)
    first_real = high_einsum("kq,cqp->ckp", cos_rows, padded)
    first_imag = -high_einsum("kq,cqp->ckp", sin_rows, padded)
    turned_real = first_real * cos_turn + first_imag * sin_turn
    turned_imag = first_imag * cos_turn - first_real * sin_turn
    spec_real = high_einsum("ckp,pj->ckj", turned_real, cos_columns) + high_einsum(
        "ckp,pj->ckj", turned_imag, sin_columns
    )
    spec_imag = high_einsum("ckp,pj->ckj", turned_imag, cos_columns) - high_einsum(
        "ckp,pj->ckj", turned_real, sin_columns
    )
    return (spec_real, spec_imag)


def inverse_transform(spec_real, spec_imag, tables):
    cos_rows, sin_rows, cos_columns, sin_columns, cos_turn, sin_turn = tables
    rows, columns = cos_turn.shape
    back_real = high_einsum("ckp,pj->ckj", spec_real, cos_columns) - high_einsum(
        "ckp,pj->ckj", spec_imag, sin_columns
    )
    back_imag = high_einsum("ckp,pj->ckj", spec_imag, cos_columns) + high_einsum(
        "ckp,pj->ckj", spec_real, sin_columns
    )
    turned_real = back_real * cos_turn - back_imag * sin_turn
    turned_imag = back_imag * cos_turn + back_real * sin_turn
    signal = high_einsum("qk,ckp->cqp", cos_rows, turned_real) - high_einsum(
        "qk,ckp->cqp", sin_rows, turned_imag
    )
    total = rows * columns
    return signal.reshape(signal.shape[0], total)[:, : total // 2] / total


def position_features(length):
    count = (FEATS - 1) // 2
    steps = lax.broadcasted_iota(jnp.int32, (count, length), 1)
    frequency = lax.broadcasted_iota(jnp.int32, (count, length), 0) + 1
    angle = (steps * frequency % length).astype(jnp.float32) * (2.0 * math.pi / length)
    ramp = lax.broadcasted_iota(jnp.int32, (1, length), 1).astype(jnp.float32) / length
    return jnp.concatenate([ramp, jnp.cos(angle), jnp.sin(angle)], axis=0)


def filter_forward(features, first, middle, last_columns, rate_columns, length):
    pre_one = high_einsum("fk,ft->kt", first, features)
    act_one = jnp.sin(pre_one)
    pre_two = high_einsum("kj,kt->jt", middle, act_one)
    act_two = jnp.sin(pre_two)
    raw = high_einsum("kc,kt->ct", last_columns, act_two)
    steps = lax.broadcasted_iota(jnp.int32, (1, length), 1).astype(jnp.float32)
    window = jnp.exp(-rate_columns[:, None] * steps) * jnp.sqrt(
        rate_columns[:, None] + 1.0 / length
    )
    return (raw * window, (pre_one, act_one, pre_two, act_two, window))


def filter_backward(d_response, features, middle, last_columns, kept):
    pre_one, act_one, pre_two, act_two, window = kept
    d_raw = d_response * window
    g_last = high_einsum("kt,ct->kc", act_two, d_raw)
    d_two = high_einsum("kc,ct->kt", last_columns, d_raw) * jnp.cos(pre_two)
    g_middle = high_einsum("kt,jt->kj", act_one, d_two)
    d_one = high_einsum("kj,jt->kt", middle, d_two) * jnp.cos(pre_one)
    g_first = high_einsum("ft,kt->fk", features, d_one)
    return (g_first, g_middle, g_last)


def normalize(state):
    centred = state - jnp.mean(state, axis=1, keepdims=True)
    scale = lax.rsqrt(jnp.mean(centred * centred, axis=1, keepdims=True) + EPSILON)
    return (centred * scale, scale)


def normalize_back(d_out, normed, scale, gain):
    d_normed = d_out * gain
    g_gain = jnp.sum(d_out * normed, axis=0)
    d_state = scale * (
        d_normed
        - jnp.mean(d_normed, axis=1, keepdims=True)
        - normed * jnp.mean(d_normed * normed, axis=1, keepdims=True)
    )
    return (d_state, g_gain)


def short_forward(extended, taps):
    length = extended.shape[-1] - 2
    return (
        taps[0] * extended[..., 2:]
        + taps[1] * extended[..., 1 : length + 1]
        + taps[2] * extended[..., :length]
    )


def short_backward(d_extended, taps):
    length = d_extended.shape[-1] - 2
    return (
        taps[0] * d_extended[..., :length]
        + taps[1] * d_extended[..., 1 : length + 1]
        + taps[2] * d_extended[..., 2:]
    )


def tap_grads(d_shorted, extended):
    length = d_shorted.shape[-1]
    return jnp.stack(
        [
            jnp.sum(d_shorted * extended[..., 2 - lag : 2 - lag + length], axis=-1)
            for lag in range(3)
        ]
    )


def long_forward(gated, filter_real, filter_imag, skip_columns, tables):
    signal = gated.astype(jnp.float32)
    sig_real, sig_imag = forward_transform(signal, tables)
    result = inverse_transform(
        sig_real * filter_real - sig_imag * filter_imag,
        sig_real * filter_imag + sig_imag * filter_real,
        tables,
    )
    return (result + skip_columns[:, None] * signal, (sig_real, sig_imag))


def long_backward(d_conv, gated, filter_real, filter_imag, skip_columns, signal_spec, tables):
    d_signal = d_conv.astype(jnp.float32)
    d_real, d_imag = forward_transform(d_signal, tables)
    sig_real, sig_imag = signal_spec
    d_gated = (
        inverse_transform(
            d_real * filter_real + d_imag * filter_imag,
            d_imag * filter_real - d_real * filter_imag,
            tables,
        )
        + skip_columns[:, None] * d_signal
    )
    d_response = inverse_transform(
        d_real * sig_real + d_imag * sig_imag, d_imag * sig_real - d_real * sig_imag, tables
    )
    g_skip = jnp.sum(d_signal * gated.astype(jnp.float32), axis=1)
    return (d_gated, d_response, g_skip)


def unit(k,n):
    k%=n
    if (4*k)%n==0:
        q=(4*k)//n
        return [(1.0,0.0),(0.0,-1.0),(-1.0,0.0),(0.0,1.0)][q]
    a=-2.0*math.pi*k/n
    return (math.cos(a),math.sin(a))
def times(z,w):
    re,im=z; c,s=w
    if s==0.0: return (re,im) if c==1.0 else (-re,-im)
    if c==0.0: return (-im,re) if s==1.0 else (im,-re)
    return (re*c-im*s, re*s+im*c)
def plus(a,b): return (a[0]+b[0],a[1]+b[1])
def minus(a,b): return (a[0]-b[0],a[1]-b[1])
def complex_dft(zs,sign):
    n=len(zs)
    if n==1: return zs
    ev=complex_dft(zs[0::2],sign); od=complex_dft(zs[1::2],sign)
    lo,hi=[],[]
    for k in range(n//2):
        v=times(od[k],unit(sign*k,n))
        lo.append(plus(ev[k],v)); hi.append(minus(ev[k],v))
    return lo+hi
def odd_bins(xs):
    n=len(xs); h=n//2; N=2*n
    zs=[times((xs[j],-xs[j+h]),unit(j,N)) for j in range(h)]
    bins={}
    for q,z in enumerate(complex_dft(zs,1)):
        k=4*q+1
        if k<=n: bins[k]=z
        else: bins[N-k]=(z[0],-z[1])
    return bins
def real_bins(xs):
    n=len(xs)
    if n==1: return {0:(xs[0],None)}
    if n==2: return {0:(xs[0]+xs[1],None),1:(xs[0]-xs[1],None)}
    h=n//2
    bins={2*k:z for k,z in real_bins([xs[j]+xs[j+h] for j in range(h)]).items()}
    bins.update(odd_bins([xs[j]-xs[j+h] for j in range(h)]))
    return bins
def padded_bins(xs):
    bins={2*k:z for k,z in real_bins(xs).items()}
    bins.update(odd_bins(xs))
    return bins
def odd_back(bins,n):
    h=n//2; N=2*n
    zs=[]
    for q in range(h):
        k=4*q+1
        if k<=n: zs.append(bins[k])
        else:
            re,im=bins[N-k]; zs.append((re,-im))
    vs=[times(z,unit(-j,N)) for j,z in enumerate(complex_dft(zs,-1))]
    return [v[0] for v in vs]+[-v[1] for v in vs]
def real_back(bins,n):
    if n==1: return [bins[0][0]]
    if n==2: return [bins[0][0]+bins[1][0],bins[0][0]-bins[1][0]]
    h=n//2
    ev=real_back({k//2:z for k,z in bins.items() if k%2==0},h)
    od=odd_back(bins,h)
    return [ev[j]+od[j] for j in range(h)]+[ev[j]-od[j] for j in range(h)]
def padded_back(bins,n):
    ev=real_back({k//2:z for k,z in bins.items() if k%2==0},n)
    od=odd_back(bins,n)
    return [a+b for a,b in zip(ev,od)]


def turn_table(shards, rows):
    total = 2 * shards * rows
    early = np.arange(rows)[None, :, None]
    late = np.arange(rows)[None, None, :]
    bins = np.arange(shards + 1)[:, None, None]
    angle = (early * (bins + 2 * shards * late) % total) * (2.0 * np.pi / total)
    cos, sin = np.cos(angle), np.sin(angle)
    top = np.concatenate([cos, -sin], axis=2)
    bottom = np.concatenate([sin, cos], axis=2)
    return jnp.asarray(np.concatenate([top, bottom], axis=1).astype(ml_dtypes.bfloat16))


def position_table(length):
    count = (FEATS - 1) // 2
    steps = np.arange(length)[None, :]
    angle = (steps * np.arange(1, count + 1)[:, None] % length) * (2.0 * np.pi / length)
    table = np.concatenate([steps / length, np.cos(angle), np.sin(angle)], axis=0)
    return jnp.asarray(table.astype(np.float32))


def chunks_of(channels):
    step = 16 if channels % 16 == 0 else channels
    return [slice(at, at + step) for at in range(0, channels, step)]


def load_bins(blocks, bins_ref, chunk):
    lanes = blocks[0].shape[-1]
    for k, (re, im) in padded_bins(blocks).items():
        im = jnp.zeros_like(re) if im is None else im
        bins_ref[k, chunk, :lanes] = re.astype(jnp.bfloat16)
        bins_ref[k, chunk, lanes:] = im.astype(jnp.bfloat16)


def fold_bins(back_ref, chunk, count, lanes):
    bins = {
        k: (back_ref[k, chunk, :lanes], back_ref[k, chunk, lanes:]) for k in range(count + 1)
    }
    return padded_back(bins, count)


def bin_scale(k, shards, rows):
    total = 2 * shards * rows
    return (1.0 if k in (0, shards) else 2.0) / total


def bin_product(left, right, conjugate):
    lanes = left.shape[1] // 2
    a, b = left[:, :lanes], left[:, lanes:]
    c, d = right[:, :lanes], right[:, lanes:]
    if conjugate:
        return jnp.concatenate([a * c + b * d, b * c - a * d], axis=1)
    return jnp.concatenate([a * c - b * d, a * d + b * c], axis=1)


def turn(left, table):
    return jnp.dot(left, table, preferred_element_type=jnp.float32)


def turn_back(left, table):
    return lax.dot_general(
        left.astype(jnp.bfloat16),
        table,
        (((1,), (1,)), ((), ())),
        preferred_element_type=jnp.float32,
    )


def sin_cos(angle):
    steps = jnp.floor(angle * (2.0 / math.pi) + 0.5)
    rest = angle - steps * 1.5703125
    rest = rest - steps * 4.837512969970703e-4
    rest = rest - steps * 7.549789954891882e-8
    square = rest * rest
    sin = rest + rest * square * (
        -1.6666654611e-1 + square * (8.3321608736e-3 + square * -1.9515295891e-4)
    )
    cos = (
        1.0
        - 0.5 * square
        + square
        * square
        * (4.166664568298827e-2 + square * (-1.388731625493765e-3 + square * 2.443315711809948e-5))
    )
    quarter = steps.astype(jnp.int32)
    odd = (quarter & 1) == 1
    sin_out = jnp.where(odd, cos, sin)
    cos_out = jnp.where(odd, sin, cos)
    sin_out = jnp.where((quarter & 2) == 2, -sin_out, sin_out)
    cos_out = jnp.where(((quarter + 1) & 2) == 2, -cos_out, cos_out)
    return sin_out, cos_out


def across(left, right, left_side, right_side):
    return lax.dot_general(
        left,
        right,
        (((left_side,), (right_side,)), ((), ())),
        precision=HIGHEST,
        preferred_element_type=jnp.float32,
    )


def filter_network_kernel(
    feature_ref,
    first_ref,
    middle_ref,
    last_ref,
    rate_ref,
    table_ref,
    spec_ref,
    one_ref,
    slope_one_ref,
    two_ref,
    slope_two_ref,
    window_ref,
    raw_ref,
    bins_ref,
):
    shards, channels, rows = window_ref.shape
    one, slope_one = sin_cos(across(first_ref[...], feature_ref[...], 0, 0))
    one_ref[...] = one
    slope_one_ref[...] = slope_one
    two, slope_two = sin_cos(across(middle_ref[...], one, 0, 0))
    two_ref[...] = two
    slope_two_ref[...] = slope_two
    raw_ref[...] = across(last_ref[...], two, 0, 0)
    rate = rate_ref[...]
    size = jnp.sqrt(rate + 1.0 / (shards * rows))
    step = lax.broadcasted_iota(jnp.int32, (channels, rows), 1)
    for j in range(shards):
        window = jnp.exp(-rate * (step + j * rows).astype(jnp.float32)) * size
        window_ref[j] = window
        at = slice(j * rows, (j + 1) * rows)
        raw_ref[:, at] = raw_ref[:, at] * window
    for chunk in chunks_of(channels):
        load_bins(
            [raw_ref[chunk, j * rows : (j + 1) * rows] for j in range(shards)], bins_ref, chunk
        )
    for k in range(shards + 1):
        spec_ref[k] = turn(bins_ref[k], table_ref[k]) * bin_scale(k, shards, rows)


def filter_network(features, first, middle, last, rates, table):
    hidden, channels = last.shape
    length = features.shape[1]
    bins, span, _ = table.shape
    rows = span // 2
    shards = length // rows
    wide = jax.ShapeDtypeStruct((hidden, length), jnp.float32)
    return pl.pallas_call(
        filter_network_kernel,
        out_shape=[
            jax.ShapeDtypeStruct((bins, channels, span), jnp.float32),
            wide,
            wide,
            wide,
            wide,
            jax.ShapeDtypeStruct((shards, channels, rows), jnp.float32),
        ],
        scratch_shapes=[
            pltpu.VMEM((channels, length), jnp.float32),
            pltpu.VMEM((bins, channels, span), jnp.bfloat16),
        ],
        compiler_params=pltpu.CompilerParams(vmem_limit_bytes=40 << 20),
        name="filter_network",
    )(features, first, middle, last, rates, table)


def conv_forward_kernel(
    gated_ref, filter_ref, skip_ref, table_ref, conv_ref, spec_ref, bins_ref, back_ref
):
    shards, channels, rows = gated_ref.shape
    for chunk in chunks_of(channels):
        load_bins(
            [gated_ref[j, chunk].astype(jnp.float32) for j in range(shards)], bins_ref, chunk
        )
    for k in range(shards + 1):
        spec = turn(bins_ref[k], table_ref[k])
        spec_ref[k] = spec.astype(jnp.bfloat16)
        back_ref[k] = turn_back(bin_product(spec, filter_ref[k], False), table_ref[k])
    for chunk in chunks_of(channels):
        skip = skip_ref[chunk]
        for j, block in enumerate(fold_bins(back_ref, chunk, shards, rows)):
            conv = block + skip * gated_ref[j, chunk].astype(jnp.float32)
            conv_ref[j, chunk] = conv.astype(jnp.bfloat16)


def conv_backward_kernel(
    gated_ref, filter_ref, skip_ref, table_ref, conv_ref, spec_ref, bins_ref, back_ref
):
    shards, channels, rows = gated_ref.shape
    for chunk in chunks_of(channels):
        load_bins(
            [gated_ref[j, chunk].astype(jnp.float32) for j in range(shards)], bins_ref, chunk
        )
    for k in range(shards + 1):
        spec = turn(bins_ref[k], table_ref[k])
        spec_ref[k] = spec.astype(jnp.bfloat16)
        back_ref[k] = turn_back(bin_product(spec, filter_ref[k], True), table_ref[k])
    for chunk in chunks_of(channels):
        skip = skip_ref[chunk]
        for j, block in enumerate(fold_bins(back_ref, chunk, shards, rows)):
            conv = block + skip * gated_ref[j, chunk].astype(jnp.float32)
            conv_ref[j, chunk] = conv.astype(jnp.bfloat16)


def conv_call(kernel, name, gated, filter_spec, skip, table):
    bins, channels, span = filter_spec.shape
    return pl.pallas_call(
        kernel,
        out_shape=[
            jax.ShapeDtypeStruct(gated.shape, jnp.bfloat16),
            jax.ShapeDtypeStruct((bins, channels, span), jnp.bfloat16),
        ],
        scratch_shapes=[
            pltpu.VMEM((bins, channels, span), jnp.bfloat16),
            pltpu.VMEM((bins, channels, span), jnp.float32),
        ],
        compiler_params=pltpu.CompilerParams(vmem_limit_bytes=40 << 20),
        name=name,
    )(gated, filter_spec, skip, table)


def conv_forward(gated, filter_spec, skip, table):
    return conv_call(conv_forward_kernel, "conv_forward", gated, filter_spec, skip, table)


def conv_backward(d_conv, filter_spec, skip, table):
    return conv_call(conv_backward_kernel, "conv_backward", d_conv, filter_spec, skip, table)


def filter_back_kernel(
    d_spec_ref,
    spec_ref,
    d_conv_ref,
    gated_ref,
    feature_ref,
    middle_ref,
    last_ref,
    one_ref,
    slope_one_ref,
    two_ref,
    slope_two_ref,
    window_ref,
    table_ref,
    g_first_ref,
    g_middle_ref,
    g_last_ref,
    g_skip_ref,
    back_ref,
    raw_ref,
):
    shards, channels, rows = d_conv_ref.shape
    for k in range(shards + 1):
        spec = bin_product(
            d_spec_ref[k].astype(jnp.float32), spec_ref[k].astype(jnp.float32), True
        )
        back_ref[k] = turn_back(spec * bin_scale(k, shards, rows), table_ref[k])
    for chunk in chunks_of(channels):
        total = None
        for j, block in enumerate(fold_bins(back_ref, chunk, shards, rows)):
            raw_ref[chunk, j * rows : (j + 1) * rows] = block * window_ref[j, chunk]
            term = d_conv_ref[j, chunk].astype(jnp.float32) * gated_ref[j, chunk].astype(
                jnp.float32
            )
            total = term if total is None else total + term
        g_skip_ref[chunk] = jnp.sum(total, axis=1, keepdims=True)
    d_raw = raw_ref[...]
    g_last_ref[...] = across(two_ref[...], d_raw, 1, 1)
    d_two = across(last_ref[...], d_raw, 1, 0) * slope_two_ref[...]
    g_middle_ref[...] = across(one_ref[...], d_two, 1, 1)
    d_one = across(middle_ref[...], d_two, 1, 0) * slope_one_ref[...]
    g_first_ref[...] = across(feature_ref[...], d_one, 1, 1)


def filter_network_back(
    d_spec, spec, d_conv, gated, features, middle, last, kept, table
):
    _, one, slope_one, two, slope_two, window = kept
    bins, channels, span = spec.shape
    hidden, length = one.shape
    feats = features.shape[0]
    return pl.pallas_call(
        filter_back_kernel,
        out_shape=[
            jax.ShapeDtypeStruct((feats, hidden), jnp.float32),
            jax.ShapeDtypeStruct((hidden, hidden), jnp.float32),
            jax.ShapeDtypeStruct((hidden, channels), jnp.float32),
            jax.ShapeDtypeStruct((channels, 1), jnp.float32),
        ],
        scratch_shapes=[
            pltpu.VMEM((bins, channels, span), jnp.float32),
            pltpu.VMEM((channels, length), jnp.float32),
        ],
        compiler_params=pltpu.CompilerParams(vmem_limit_bytes=40 << 20),
        name="filter_network_back",
    )(
        d_spec,
        spec,
        d_conv,
        gated,
        features,
        middle,
        last,
        one,
        slope_one,
        two,
        slope_two,
        window,
        table,
    )


def layer_forward(state, weights, setting):
    (
        mix_gain,
        in_proj,
        short_taps,
        first,
        middle,
        last,
        skip,
        rates,
        out_proj,
        mlp_gain,
        up_proj,
        down_proj,
    ) = weights
    features, tables, offset = setting
    rows, width = state.shape
    length = features.shape[1]
    channels = width // (length // rows)
    normed_mix, scale_mix = normalize(state)
    u_mix = to_low(normed_mix * mix_gain)
    projected = to_low(low_einsum("td,dc->ct", u_mix, in_proj)).reshape(3, width, rows)
    last_columns = lax.dynamic_slice_in_dim(last, offset, channels, 1)
    skip_columns = lax.dynamic_slice_in_dim(skip, offset, channels, 0)
    rate_columns = lax.dynamic_slice_in_dim(rates, offset, channels, 0)
    filter_kept = filter_network(
        features, first, middle, last_columns, rate_columns[:, None], tables
    )
    filter_spec = filter_kept[0]
    taps = short_taps.reshape(3, 3, width)
    edge = from_behind(projected[:, :, rows - 2 :], "seq", 1)
    extended = jnp.concatenate([edge, projected], axis=2).astype(jnp.float32)
    tap_use = taps[:, :, :, None]
    shorted = short_forward(extended, tap_use)
    gated_rows = to_low(shorted[2] * shorted[1])
    shards = length // rows
    gated = lax.all_to_all(
        gated_rows.reshape(shards, channels, rows), "seq", split_axis=0, concat_axis=0, tiled=True
    )
    conv_low, signal_spec = conv_forward(gated, filter_spec, skip_columns[:, None], tables)
    conv_here = lax.all_to_all(
        conv_low, "seq", split_axis=0, concat_axis=0, tiled=True
    ).reshape(width, rows)
    mixed = to_low(conv_here.astype(jnp.float32) * shorted[0])
    middle_state = state + low_einsum("ct,ce->te", mixed, out_proj)
    normed_mlp, scale_mlp = normalize(middle_state)
    u_mlp = to_low(normed_mlp * mlp_gain)
    hidden = low_einsum("td,df->tf", u_mlp, up_proj)
    active = to_low(jax.nn.gelu(hidden))
    result = middle_state + low_einsum("tf,fe->te", active, down_proj)
    kept = (
        normed_mix,
        scale_mix,
        u_mix,
        extended,
        shorted,
        gated,
        conv_here,
        mixed,
        filter_kept,
        filter_spec,
        signal_spec,
        normed_mlp,
        scale_mlp,
        u_mlp,
        hidden,
        active,
        last_columns,
        skip_columns,
        tap_use,
    )
    return (result, kept)


def layer_backward(upstream, kept, weights, setting):
    (
        mix_gain,
        in_proj,
        short_taps,
        first,
        middle,
        last,
        skip,
        rates,
        out_proj,
        mlp_gain,
        up_proj,
        down_proj,
    ) = weights
    features, tables, offset = setting
    (
        normed_mix,
        scale_mix,
        u_mix,
        extended,
        shorted,
        gated,
        conv_here,
        mixed,
        filter_kept,
        filter_spec,
        signal_spec,
        normed_mlp,
        scale_mlp,
        u_mlp,
        hidden,
        active,
        last_columns,
        skip_columns,
        tap_use,
    ) = kept
    rows, width = upstream.shape
    d_down = to_low(upstream)
    g_down = low_einsum("tf,te->fe", active, d_down)
    d_active = low_einsum("te,fe->tf", d_down, down_proj)
    d_hidden = to_low(jax.vjp(jax.nn.gelu, hidden)[1](d_active)[0])
    g_up = low_einsum("td,tf->df", u_mlp, d_hidden)
    d_u_mlp = low_einsum("tf,df->td", d_hidden, up_proj)
    d_middle, g_mlp_gain = normalize_back(d_u_mlp, normed_mlp, scale_mlp, mlp_gain)
    d_middle = d_middle + upstream
    d_branch = to_low(d_middle)
    g_out = low_einsum("ct,te->ce", mixed, d_branch)
    d_mixed = to_low(low_einsum("te,ce->ct", d_branch, out_proj))
    d_mixed_wide = d_mixed.astype(jnp.float32)
    d_conv_rows = to_low(d_mixed_wide * shorted[0])
    d_zero = d_mixed_wide * conv_here.astype(jnp.float32)
    shards, channels, _ = gated.shape
    d_conv = lax.all_to_all(
        d_conv_rows.reshape(gated.shape), "seq", split_axis=0, concat_axis=0, tiled=True
    )
    d_gated, d_spec = conv_backward(d_conv, filter_spec, skip_columns[:, None], tables)
    d_gated_rows = lax.all_to_all(
        d_gated, "seq", split_axis=0, concat_axis=0, tiled=True
    ).reshape(width, rows).astype(jnp.float32)
    d_shorted = jnp.stack([d_zero, d_gated_rows * shorted[2], d_gated_rows * shorted[1]])
    after = from_behind(d_shorted[:, :, :2], "seq", -1)
    d_extended = jnp.concatenate([d_shorted, after], axis=2)
    d_projected = to_low(short_backward(d_extended, tap_use))
    g_taps = tap_grads(d_shorted, extended)
    g_first, g_middle, g_last, g_skip = filter_network_back(
        d_spec, signal_spec, d_conv, gated, features, middle, last_columns, filter_kept, tables
    )
    g_skip = g_skip[:, 0]
    d_flat = d_projected.reshape(3 * width, rows)
    g_in = low_einsum("td,ct->dc", u_mix, d_flat)
    d_u_mix = low_einsum("ct,dc->td", d_flat, in_proj)
    d_state, g_mix_gain = normalize_back(d_u_mix, normed_mix, scale_mix, mix_gain)
    d_state = d_state + d_middle
    large = (g_in, g_out, g_up, g_down)
    small = (g_mix_gain, g_taps.reshape(3, 3 * width), g_first, g_middle, g_mlp_gain)
    column_part = (g_last, g_skip)
    return (d_state, large, small, column_part)


def body(
    tokens,
    cotangent,
    mix_gain,
    in_proj,
    short_taps,
    filter_first,
    filter_middle,
    filter_last,
    filter_skip,
    decay_rates,
    out_proj,
    mlp_gain,
    up_proj,
    down_proj,
):
    rows = tokens.shape[1]
    width = tokens.shape[2]
    layer_count = mix_gain.shape[0]
    shards = lax.axis_size("seq")
    length = rows * shards
    offset = lax.axis_index("seq") * (width // shards)
    setting = (position_table(length), turn_table(shards, rows), offset)
    stacks = (
        mix_gain,
        in_proj,
        short_taps,
        filter_first,
        filter_middle,
        filter_last,
        filter_skip,
        decay_rates,
        out_proj,
        mlp_gain,
        up_proj,
        down_proj,
    )
    state = tokens[0].astype(jnp.float32)
    kept_all = []
    for level in range(layer_count):
        weights = tuple((item[level] for item in stacks))
        state, kept = layer_forward(state, weights, setting)
        kept_all.append(kept)
    upstream = cotangent[0].astype(jnp.float32)
    large_all = [None] * layer_count
    small_all = [None] * layer_count
    column_all = [None] * layer_count
    for level in reversed(range(layer_count)):
        weights = tuple((item[level] for item in stacks))
        upstream, large, small, column_part = layer_backward(
            upstream, kept_all[level], weights, setting
        )
        large_all[level] = large
        small_all[level] = small
        column_all[level] = column_part
    stacked_large = [
        jnp.stack([large_all[level][member] for level in range(layer_count)]) for member in range(4)
    ]
    row_in, row_out, row_up, row_down = (
        lax.psum_scatter(stacked_large[0], "seq", scatter_dimension=1, tiled=True),
        lax.psum_scatter(stacked_large[1], "seq", scatter_dimension=1, tiled=True),
        lax.psum_scatter(stacked_large[2], "seq", scatter_dimension=1, tiled=True),
        lax.psum_scatter(stacked_large[3], "seq", scatter_dimension=1, tiled=True),
    )
    g_in, g_out, g_up, g_down = (
        lax.psum_scatter(row_in.astype(jnp.bfloat16), "dp", scatter_dimension=2, tiled=True).astype(
            jnp.float32
        ),
        lax.psum_scatter(
            row_out.astype(jnp.bfloat16), "dp", scatter_dimension=2, tiled=True
        ).astype(jnp.float32),
        lax.psum_scatter(row_up.astype(jnp.bfloat16), "dp", scatter_dimension=2, tiled=True).astype(
            jnp.float32
        ),
        lax.psum_scatter(
            row_down.astype(jnp.bfloat16), "dp", scatter_dimension=2, tiled=True
        ).astype(jnp.float32),
    )
    stacked_small = [
        jnp.stack([small_all[level][member] for level in range(layer_count)]) for member in range(5)
    ]
    g_mix_gain, g_taps, g_first, g_middle, g_mlp_gain = lax.psum(
        (stacked_small[0], stacked_small[1], stacked_small[2], stacked_small[3], stacked_small[4]),
        ("dp", "seq"),
    )
    stacked_last = jnp.stack([column_all[level][0] for level in range(layer_count)])
    stacked_skip = jnp.stack([column_all[level][1] for level in range(layer_count)])
    g_last, g_skip = lax.psum((stacked_last, stacked_skip), "dp")
    return (
        state[None],
        upstream[None],
        g_mix_gain,
        g_in,
        g_taps,
        g_first,
        g_middle,
        g_last,
        g_skip,
        g_out,
        g_mlp_gain,
        g_up,
        g_down,
    )


SEQ_BITS = 4
VMEM_BYTES = 63 << 20


class Board:
    def __init__(self, place, held, inputs, outputs):
        self.place = place
        self.held, self.arriving, self.outputs, self.leaving = held, {}, outputs, []
        for key, (source, target, sem) in inputs.items():
            copy = pltpu.make_async_copy(source, target, sem)
            copy.start()
            self.arriving[key] = copy
            held[key] = target
        for key, (source, _, _) in outputs.items():
            held[key] = source

    def __getattr__(self, key):
        held = self.__dict__["held"]
        if key not in held:
            raise AttributeError(key)
        if key in self.arriving:
            self.arriving.pop(key).wait()
        return held[key]

    def flush(self, *keys):
        for key in keys:
            copy = pltpu.make_async_copy(*self.outputs.pop(key))
            copy.start()
            self.leaving.append(copy)

    def finish(self):
        self.flush(*list(self.outputs))
        for copy in [*self.arriving.values(), *self.leaving]:
            copy.wait()


class Renamed:
    def __init__(self, board, **names):
        self.__dict__.update(board=board, names=names)

    def __getattr__(self, key):
        return getattr(self.__dict__["board"], self.__dict__["names"].get(key, key))


def local_call(name, body, place, inputs, outputs, scratch, remote=(), after=(), time_us=2, cuts=()):
    cuts = dict(cuts)
    near = [key for key in inputs if key not in remote]
    far = [key for key in inputs if key in remote]
    arrays = [inputs[key] for key in near] + [inputs[key] for key in far] + list(after)

    def shape_of(key):
        shape = list(inputs[key].shape)
        if key in cuts:
            shape[1] = cuts[key][1]
        return tuple(shape)

    def cut(key, ref):
        return ref.at[:, pl.ds(*cuts[key])] if key in cuts else ref

    def kernel(*refs):
        refs = list(refs)
        place_ref = refs.pop(0)
        given = [refs.pop(0) for _ in arrays]
        made = [refs.pop(0) for _ in outputs]
        here = [refs.pop(0) for _ in near]
        staged = [refs.pop(0) for _ in outputs]
        spare = [refs.pop(0) for _ in scratch]
        sems_in, sems_out = refs
        board = Board(
            place_ref,
            {**dict(zip(far, given[len(near) :])), **dict(zip(scratch, spare))},
            {
                key: (cut(key, given[at]), here[at], sems_in.at[at])
                for at, key in enumerate(near)
            },
            {key: (staged[at], made[at], sems_out.at[at]) for at, key in enumerate(outputs)},
        )
        body(board)
        board.finish()

    made = pl.pallas_call(
        kernel,
        in_specs=[pl.BlockSpec(memory_space=pltpu.SMEM)]
        + [pl.BlockSpec(memory_space=pltpu.HBM)] * len(arrays),
        out_specs=[pl.BlockSpec(memory_space=pltpu.HBM)] * len(outputs),
        out_shape=[jax.ShapeDtypeStruct(*item) for item in outputs.values()],
        scratch_shapes=[pltpu.VMEM(shape_of(key), inputs[key].dtype) for key in near]
        + [pltpu.VMEM(*item) for item in outputs.values()]
        + list(scratch.values())
        + [
            pltpu.SemaphoreType.DMA((max(len(near), 1),)),
            pltpu.SemaphoreType.DMA((len(outputs),)),
        ],
        compiler_params=pltpu.CompilerParams(vmem_limit_bytes=VMEM_BYTES),
        cost_estimate=pl.CostEstimate(
            flops=0, bytes_accessed=int(time_us * 3.0e6), transcendentals=0
        ),
        name=name,
    )(place, *arrays)
    return dict(zip(outputs, made, strict=True))


class Weights:
    def __init__(self, slots, sems):
        self.slots, self.sems, self.copies = slots, sems, []

    def fetch(self, source):
        at = len(self.copies)
        copy = pltpu.make_async_copy(source, self.slots.at[at], self.sems.at[at])
        copy.start()
        self.copies.append(copy)
        return at

    def fetch_columns(self, source, width):
        count = source.shape[1] // width
        return [self.fetch(source.at[:, pl.ds(j * width, width)]) for j in range(count)]

    def wait(self, at):
        if self.copies[at] is not None:
            self.copies[at].wait()
            self.copies[at] = None
        return self.slots[at]


def dot(left, right):
    return jnp.dot(left, right, preferred_element_type=jnp.float32)


def dot_rows(left, right):
    return lax.dot_general(
        left, right, (((1,), (1,)), ((), ())), preferred_element_type=jnp.float32
    )


def flip(block):
    return block.T


def wide(value):
    return value.astype(jnp.float32)


def narrow(value):
    return value.astype(jnp.bfloat16)


def shifted_down(block, edge):
    row = lax.broadcasted_iota(jnp.int32, block.shape, 0)
    one = jnp.where(row == 0, edge[1:2], pltpu.roll(block, 1, 0))
    two = jnp.where(row == 0, edge[0:1], jnp.where(row == 1, edge[1:2], pltpu.roll(block, 2, 0)))
    return one, two


def shifted_up(block, edge):
    rows = block.shape[0]
    row = lax.broadcasted_iota(jnp.int32, block.shape, 0)
    one = jnp.where(row == rows - 1, edge[0:1], pltpu.roll(block, rows - 1, 0))
    two = jnp.where(
        row == rows - 1,
        edge[1:2],
        jnp.where(row == rows - 2, edge[0:1], pltpu.roll(block, rows - 2, 0)),
    )
    return one, two


def short_branch(r, level, branch):
    width = r.projected.shape[1] // 3
    at = slice(branch * width, (branch + 1) * width)
    block = wide(r.projected[:, at])
    one, two = shifted_down(block, r.edge[2 * branch : 2 * branch + 2])
    taps = r.short_taps[level, :, at]
    return taps[0:1] * block + taps[1:2] * one + taps[2:3] * two


def norm_rows(state):
    centred = state - jnp.mean(state, axis=1, keepdims=True)
    scale = lax.rsqrt(jnp.mean(centred * centred, axis=1, keepdims=True) + EPSILON)
    return centred * scale, scale


def norm_rows_back(d_out, normed, scale, gain):
    q = d_out * gain
    return scale * (
        q
        - jnp.mean(q, axis=1, keepdims=True)
        - normed * jnp.mean(q * normed, axis=1, keepdims=True)
    )


def gelu_parts(x):
    inner = x * (0.7978845608028654 + 0.035677408136300125 * (x * x))
    return jnp.tanh(inner)


def gelu_value(x):
    return 0.5 * x * (1.0 + gelu_parts(x))


def gelu_slope(x):
    tanh = gelu_parts(x)
    inner = 0.7978845608028654 + 0.10703222440890037 * (x * x)
    return 0.5 * (1.0 + tanh) + 0.5 * x * (1.0 - tanh * tanh) * inner


def store_rows(target, start, first_block, block_rows, flipped):
    for j in range(flipped.shape[0] // block_rows):
        owner = first_block + j
        z, y, core = owner >> 2, (owner >> 1) & 1, owner & 1
        at = start + z * block_rows
        target[core, y, at : at + block_rows] = flipped[j * block_rows : (j + 1) * block_rows]


def store_line(target, line, vector):
    lanes = target.shape[1]
    pieces = vector.shape[1] // lanes
    for j in range(pieces):
        target[line * pieces + j : line * pieces + j + 1] = vector[:, j * lanes : (j + 1) * lanes]


def mix_forward(r, level, state, weights, squares, gain):
    normed, _ = norm_rows(state)
    u = narrow(normed * gain)
    width = u.shape[1]
    store_rows(r.next_rows, 0, 0, width >> SEQ_BITS, flip(u))
    for j, square in enumerate(squares):
        block = narrow(dot(u, weights.wait(square)))
        r.next_projected[:, j * width : (j + 1) * width] = block
        r.next_tail[2 * j : 2 * j + 2] = wide(block)[-2:]
    r.next_tail[6:] = jnp.zeros_like(r.next_tail[6:])
    r.flush("next_projected", "next_tail")


def enter_kernel(r):
    weights = Weights(r.slots, r.sems)
    squares = weights.fetch_columns(r.in_proj.at[0], r.tokens.shape[1])
    mix_forward(r, 0, wide(r.tokens[...]), weights, squares, r.mix_gain[0:1])


def short_kernel(level):
    def body(r):
        gated = narrow(short_branch(r, level, 2) * short_branch(r, level, 1))
        r.gated[...] = flip(gated).reshape(r.gated.shape)

    return body


def after_conv(r, level, weights, squares):
    out_square, up_squares, down_squares = squares
    rows, width = r.state.shape
    owned = width >> SEQ_BITS
    conv = flip(r.conv[...].reshape(width, rows))
    r.conv_rows[...] = conv
    r.flush("conv_rows")
    mixed = narrow(wide(conv) * short_branch(r, level, 0))
    store_rows(r.all_rows, 5 * 4 * owned, 0, owned, flip(mixed))
    middle = wide(r.state[...]) + dot(mixed, weights.wait(out_square))
    r.middle[...] = middle
    r.flush("middle")
    normed, _ = norm_rows(middle)
    u = narrow(normed * r.mlp_gain[level : level + 1])
    store_rows(r.all_rows, 4 * 4 * owned, 0, owned, flip(u))
    total = middle
    for j, (up, down) in enumerate(zip(up_squares, down_squares, strict=True)):
        hidden = dot(u, weights.wait(up))
        r.hidden[:, j * width : (j + 1) * width] = hidden
        active = narrow(gelu_value(hidden))
        store_rows(r.all_rows, 0, 4 * j, 4 * owned, flip(active))
        total = total + dot(active, weights.wait(down))
    for core in range(2):
        for y in range(2):
            r.all_rows[core, y, 6 * 4 * owned :] = r.rows[core, y]
    core = r.place[1]
    r.rows_keep[...] = r.all_rows[core]
    r.rows_send[...] = r.all_rows[1 - core]
    return total


def before_conv_back(r, level, upstream, weights, squares):
    out_square, up_squares, down_squares = squares
    rows, width = upstream.shape
    half = width // 2
    wide_half = 2 * width
    d_down = narrow(upstream)
    middle = r.middle[...]
    normed, scale = norm_rows(middle)
    d_u = jnp.zeros_like(middle)
    for j, (up, down) in enumerate(zip(up_squares, down_squares, strict=True)):
        d_active = dot_rows(d_down, weights.wait(down))
        hidden = r.hidden[:, j * width : (j + 1) * width]
        d_hidden = narrow(d_active * gelu_slope(hidden))
        side, at = divmod(j * width, wide_half)
        r.all_columns[side, :, at : at + width] = d_hidden
        d_u = d_u + dot_rows(d_hidden, weights.wait(up))
    r.g_mlp_gain[...] = jnp.broadcast_to(
        jnp.sum(d_u * normed, axis=0, keepdims=True), r.g_mlp_gain.shape
    )
    d_middle = upstream + norm_rows_back(d_u, normed, scale, r.mlp_gain[level : level + 1])
    r.d_middle[...] = d_middle
    r.flush("d_middle", "g_mlp_gain")
    d_branch = narrow(d_middle)
    for side in range(2):
        r.all_columns[side, :, wide_half : wide_half + half] = d_down[
            :, side * half : (side + 1) * half
        ]
        r.all_columns[side, :, wide_half + half :] = d_branch[:, side * half : (side + 1) * half]
    d_mixed = wide(narrow(dot_rows(d_branch, weights.wait(out_square))))
    r.d_x0[...] = d_mixed * wide(r.conv_rows[...])
    d_conv = narrow(d_mixed * short_branch(r, level, 0))
    r.d_conv[...] = flip(d_conv).reshape(r.d_conv.shape)
    r.flush("d_conv", "d_x0")
    side = r.place[0]
    r.columns_keep[...] = r.all_columns[side]
    r.columns_send[...] = r.all_columns[1 - side]


def mlp_fetch(r, level, weights):
    width = r.out_proj.shape[2]
    out_square = weights.fetch(r.out_proj.at[level])
    ups = range(r.up_proj.shape[2] // width)
    up_squares, down_squares = [], []
    for j in ups:
        at = pl.ds(j * width, width)
        up_squares.append(weights.fetch(r.up_proj.at[level, :, at]))
        down_squares.append(weights.fetch(r.down_proj.at[level, at]))
    return out_square, up_squares, down_squares


def mlp_fetch_back(r, level, weights):
    width = r.out_proj.shape[2]
    up_squares, down_squares = [], []
    for j in range(r.up_proj.shape[2] // width):
        at = pl.ds(j * width, width)
        down_squares.append(weights.fetch(r.down_proj.at[level, at]))
        up_squares.append(weights.fetch(r.up_proj.at[level, :, at]))
    out_square = weights.fetch(r.out_proj.at[level])
    return out_square, up_squares, down_squares


def middle_kernel(level):
    def body(r):
        weights = Weights(r.slots, r.sems)
        squares = mlp_fetch(r, level, weights)
        mix_squares = weights.fetch_columns(r.in_proj.at[level + 1], r.state.shape[1])
        state = after_conv(r, level, weights, squares)
        r.next_state[...] = state
        mix_forward(
            r, level + 1, state, weights, mix_squares, r.mix_gain[level + 1 : level + 2]
        )

    return body


def turn_kernel(level):
    def body(r):
        weights = Weights(r.slots, r.sems)
        squares = mlp_fetch(r, level, weights)
        r.next_state[...] = after_conv(r, level, weights, squares)
        before_conv_back(r, level, wide(r.cotangent[...]), weights, squares)

    return body


def short_back_kernel(level):
    def body(r):
        rows, width = r.d_x0.shape
        d_gated = wide(flip(r.d_gated[...].reshape(width, rows)))
        d_one = d_gated * short_branch(r, level, 2)
        d_value = d_gated * short_branch(r, level, 1)
        r.d_short[:, :width] = d_one
        r.d_short[:, width:] = d_value
        r.head[0:2] = r.d_x0[0:2]
        r.head[2:4] = d_one[0:2]
        r.head[4:6] = d_value[0:2]
        r.head[6:] = jnp.zeros_like(r.head[6:])

    return body


def after_short_back(r, level, weights, squares):
    rows, width = r.d_x0.shape
    half = 3 * width // 2
    d_u = jnp.zeros_like(r.d_x0[...])
    for branch, square in enumerate(squares):
        at = slice(branch * width, (branch + 1) * width)
        d_block = r.d_x0[...] if branch == 0 else r.d_short[:, at.start - width : at.stop - width]
        taps = r.short_taps[level, :, at]
        one, two = shifted_up(d_block, r.after[2 * branch : 2 * branch + 2])
        d_projected = narrow(taps[0:1] * d_block + taps[1:2] * one + taps[2:3] * two)
        for piece in range(2):
            spot = branch * 2 + piece
            side, lane = divmod(spot * (width // 2), half)
            r.in_columns[side, :, lane : lane + width // 2] = d_projected[
                :, piece * (width // 2) : (piece + 1) * (width // 2)
            ]
        d_u = d_u + dot_rows(d_projected, weights.wait(square))
        block = wide(r.projected[:, at])
        back_one, back_two = shifted_down(block, r.edge[2 * branch : 2 * branch + 2])
        for lag, item in enumerate((block, back_one, back_two)):
            store_line(r.small, 3 * lag + branch, jnp.sum(d_block * item, axis=0, keepdims=True))
    side = r.place[0]
    r.in_keep[...] = r.in_columns[side]
    r.in_send[...] = r.in_columns[1 - side]
    r.flush("in_keep", "in_send")
    normed, scale = norm_rows(wide(r.state[...]))
    store_line(r.small, 9, jnp.sum(d_u * normed, axis=0, keepdims=True))
    store_line(r.small, 10, r.g_mlp_gain_in[0:1])
    return r.d_middle_in[...] + norm_rows_back(
        d_u, normed, scale, r.mix_gain[level : level + 1]
    )


def between_kernel(level):
    def body(r):
        weights = Weights(r.slots, r.sems)
        mix_squares = weights.fetch_columns(r.in_proj.at[level], r.d_x0_in.shape[1])
        squares = mlp_fetch_back(r, level - 1, weights)
        upper = Renamed(r, d_x0="d_x0_in", projected="upper_projected", edge="upper_edge")
        upstream = after_short_back(upper, level, weights, mix_squares)
        before_conv_back(r, level - 1, upstream, weights, squares)

    return body


def leave_kernel(r):
    weights = Weights(r.slots, r.sems)
    squares = weights.fetch_columns(r.in_proj.at[0], r.d_x0.shape[1])
    r.upstream[...] = after_short_back(r, 0, weights, squares)


def filter_kernel(level):
    def body(r):
        shards, channels, rows = r.window.shape
        width = r.filter_last.shape[2]
        pick = (
            lax.broadcasted_iota(jnp.int32, (channels, width), 1)
            == lax.broadcasted_iota(jnp.int32, (channels, width), 0) + r.place[5]
        ).astype(jnp.float32)
        one, slope_one = sin_cos(across(r.filter_first[level], r.features[...], 0, 0))
        r.one[...] = one
        r.slope_one[...] = slope_one
        r.flush("one", "slope_one")
        two, slope_two = sin_cos(across(r.filter_middle[level], one, 0, 0))
        r.two[...] = two
        r.slope_two[...] = slope_two
        r.flush("two", "slope_two")
        last = across(pick, r.filter_last[level], 1, 1)
        r.last[...] = last
        r.raw[...] = across(last, two, 1, 0)
        rate = jnp.sum(pick * r.decay_rates[level : level + 1], axis=1, keepdims=True)
        skip = jnp.sum(pick * r.filter_skip[level : level + 1], axis=1, keepdims=True)
        r.skip[...] = jnp.broadcast_to(skip, r.skip.shape)
        size = jnp.sqrt(rate + 1.0 / (shards * rows))
        step = lax.broadcasted_iota(jnp.int32, (channels, rows), 1)
        for j in range(shards):
            window = jnp.exp(-rate * (step + j * rows).astype(jnp.float32)) * size
            r.window[j] = window
            at = slice(j * rows, (j + 1) * rows)
            r.raw[:, at] = r.raw[:, at] * window
        for chunk in chunks_of(channels):
            load_bins(
                [r.raw[chunk, j * rows : (j + 1) * rows] for j in range(shards)], r.bins, chunk
            )
        for k in range(shards + 1):
            r.filter_spec[k] = dot(r.bins[k], r.table[k]) * bin_scale(k, shards, rows)

    return body


def conv_kernel(conjugate):
    def body(r):
        shards, channels, rows = r.signal.shape
        for chunk in chunks_of(channels):
            load_bins([wide(r.signal[j, chunk]) for j in range(shards)], r.bins, chunk)
        for k in range(shards + 1):
            spec = dot(r.bins[k], r.table[k])
            r.spec[k] = narrow(spec)
            product = bin_product(spec, r.filter_spec[k], conjugate)
            r.back[k] = dot_rows(narrow(product), r.table[k])
        r.flush("spec")
        for chunk in chunks_of(channels):
            skip = r.skip[chunk]
            for j, block in enumerate(fold_bins(r.back, chunk, shards, rows)):
                r.result[j, chunk] = narrow(block + skip * wide(r.signal[j, chunk]))

    return body


def filter_grads_kernel(level):
    def body(r):
        shards, channels, rows = r.d_conv.shape
        hidden = r.one.shape[0]
        feats = r.features.shape[0]
        for k in range(shards + 1):
            spec = bin_product(wide(r.d_spec[k]), wide(r.spec[k]), True)
            r.back[k] = dot_rows(narrow(spec * bin_scale(k, shards, rows)), r.table[k])
        r.packed[...] = jnp.zeros_like(r.packed)
        for chunk in chunks_of(channels):
            total = None
            for j, block in enumerate(fold_bins(r.back, chunk, shards, rows)):
                r.raw[chunk, j * rows : (j + 1) * rows] = block * r.window[j, chunk]
                term = wide(r.d_conv[j, chunk]) * wide(r.gated[j, chunk])
                total = term if total is None else total + term
            r.packed[hidden + chunk.start : hidden + chunk.stop, hidden : hidden + 1] = jnp.sum(
                total, axis=1, keepdims=True
            )
        d_raw = r.raw[...]
        r.packed[hidden:, :channels] = across(r.two[...], d_raw, 1, 1)
        d_two = across(r.last[...], d_raw, 0, 0) * r.slope_two[...]
        r.packed[:hidden, hidden:] = across(r.one[...], d_two, 1, 1)
        d_one = across(r.filter_middle[level], d_two, 1, 0) * r.slope_one[...]
        r.packed[:feats, :hidden] = across(r.features[...], d_one, 1, 1)

    return body


SOURCES = ("keep", "x", "core", "core_x")


def grad_kernel(parts, split):
    def body(r):
        y_own, low, high = r.place[2], r.place[3], r.place[4]
        tile = r.blocks.shape[3]
        for y in range(2):
            start = 0
            for layer, row, count, column, columns in parts:
                at, lanes = slice(row, row + count), slice(column, column + columns)
                left = jnp.concatenate(
                    [getattr(r, f"rows_{layer}_{key}")[y, at] for key in SOURCES], axis=1
                )
                right = jnp.concatenate(
                    [getattr(r, f"columns_{layer}_{key}")[:, lanes] for key in SOURCES], axis=0
                )
                block = narrow(dot(left, right))
                owned = count // 4
                for z in range(4):
                    for piece in range(columns // tile):
                        spot = start + piece * owned
                        r.blocks[y, z, spot : spot + owned] = block[
                            z * owned : (z + 1) * owned, piece * tile : (piece + 1) * tile
                        ]
                start += owned * (columns // tile)
        for one in range(2):
            for two in range(2):
                z = (low ^ (1 - one)) + 2 * (high ^ (1 - two))
                r.p_send[one, two] = r.blocks[1 - y_own, z, :split]
                r.p_keep[one, two] = r.blocks[y_own, z, :split]
                z, y = 2 * (high ^ (1 - one)), y_own ^ (1 - two)
                r.q_send[one, two] = r.blocks[y, z + 1 - low, split:]
                r.q_keep[one, two] = r.blocks[y, z + low, split:]

    return body


def crossed(block, bit):
    count = lax.axis_size("seq")
    return lax.ppermute(block, "seq", [(i, i ^ bit) for i in range(count)])


def other_sequence(block):
    return lax.ppermute(block, "dp", [(0, 1), (1, 0)])


def share_rows(keep, send):
    core = crossed(send, 1)
    return {
        "rows_keep": keep,
        "rows_x": other_sequence(keep),
        "rows_core": core,
        "rows_core_x": other_sequence(core),
    }


def share_columns(keep, send):
    x = other_sequence(send)
    return {
        "columns_keep": keep,
        "columns_x": x,
        "columns_core": crossed(keep, 1),
        "columns_core_x": crossed(x, 1),
    }


def parts_tall(parts, tile):
    return sum(count // 4 * (width // tile) for _, _, count, _, width in parts)


def partial_grads(name, place, shared, parts, split, tile, cuts, time_us, after=()):
    tall = parts_tall(parts, tile)
    low = jnp.bfloat16
    first, second = ((2, 2, split, tile), low), ((2, 2, tall - split, tile), low)
    return local_call(
        name,
        grad_kernel(parts, split),
        place,
        shared,
        {"p_send": first, "q_send": second, "p_keep": first, "q_keep": second},
        {"blocks": pltpu.VMEM((2, 4, tall, tile), low)},
        time_us=time_us,
        cuts=cuts,
        after=after,
    )


def reduce_route(keep, send, bits):
    one = crossed(send, bits[0])
    two = crossed(narrow(wide(keep[0]) + wide(one[0])), bits[1])
    total = wide(keep[1]) + wide(one[1]) + wide(two)
    mine, three = total[1], crossed(narrow(total[0]), bits[2])
    return {"one": one, "two": two, "mine": mine, "three": three}


def sum_bits(block, bits):
    for bit in bits:
        block = block + crossed(block, bit)
    return block


def collect_kernel(groups, owned):
    def body(r):
        for group, places in groups:
            total = jnp.concatenate(
                [
                    getattr(r, f"{group}_{route}_mine")[...]
                    + wide(getattr(r, f"{group}_{route}_three")[...])
                    for route in "pq"
                ],
                axis=0,
            )
            tile = total.shape[1]
            start = 0
            for output, level, count, pieces in places:
                target = getattr(r, output)
                for j in range(pieces):
                    target[level, :, j * tile : (j + 1) * tile] = total[start : start + count]
                    start += count
        lines = r.g_mix_gain.shape[1] // 128
        for level in range(r.g_mix_gain.shape[0]):
            small = getattr(r, f"small_{level}")
            for j in range(lines):
                at = slice(j * 128, (j + 1) * 128)
                r.g_mix_gain[level : level + 1, at] = small[9 * lines + j : 9 * lines + j + 1]
                r.g_mlp_gain[level : level + 1, at] = small[10 * lines + j : 10 * lines + j + 1]
            for lag in range(3):
                for j in range(3 * lines):
                    line = 3 * lag * lines + j
                    r.g_taps[level, lag : lag + 1, j * 128 : (j + 1) * 128] = small[line : line + 1]
            hidden = r.g_middle.shape[1]
            start = 16 * lines
            r.g_first[level] = small[start : start + r.g_first.shape[1], :hidden]
            r.g_middle[level] = small[start : start + hidden, hidden:]
            last = getattr(r, f"last_{level}")[...]
            r.g_last[level] = last[:, :owned]
            r.g_skip[level : level + 1] = flip(last)[hidden : hidden + 1, :owned]

    return body


def fast_body(
    tokens,
    cotangent,
    mix_gain,
    in_proj,
    short_taps,
    filter_first,
    filter_middle,
    filter_last,
    filter_skip,
    decay_rates,
    out_proj,
    mlp_gain,
    up_proj,
    down_proj,
):
    tokens, cotangent = tokens[0], cotangent[0]
    rows, width = tokens.shape
    hidden = up_proj.shape[2]
    shards = lax.axis_size("seq")
    length = rows * shards
    owned = channels = width // shards
    inner, feats = filter_first.shape[2], filter_first.shape[1]
    seq = lax.axis_index("seq")
    place = jnp.stack(
        [
            lax.axis_index("dp"),
            seq & 1,
            (seq >> 1) & 1,
            (seq >> 2) & 1,
            (seq >> 3) & 1,
            seq * channels,
        ]
    ).astype(jnp.int32)
    features, table = position_table(length), turn_table(shards, rows)
    low, full = jnp.bfloat16, jnp.float32
    rows_tall = 28 * owned
    ups = hidden // width
    tile = width // 2
    bins, span = shards + 1, 2 * rows

    def slots(count):
        return {
            "slots": pltpu.VMEM((count, width, width), low),
            "sems": pltpu.SemaphoreType.DMA((count,)),
        }

    def exchange(block):
        return lax.all_to_all(block, "seq", split_axis=0, concat_axis=0, tiled=True)

    line = ((rows, width), full)
    edges = ((8, width), full)
    by_shard = ((shards, channels, rows), low)
    spectrum = ((bins, channels, span), low)
    mix_outputs = {
        "next_projected": ((rows, 3 * width), low),
        "next_tail": edges,
        "next_rows": ((2, 2, 4 * owned, rows), low),
    }
    mlp_outputs = {
        "next_state": line,
        "middle": line,
        "hidden": ((rows, hidden), full),
        "conv_rows": ((rows, width), low),
        "rows_keep": ((2, rows_tall, rows), low),
        "rows_send": ((2, rows_tall, rows), low),
    }
    back_outputs = {
        "d_conv": by_shard,
        "d_x0": line,
        "d_middle": line,
        "g_mlp_gain": edges,
        "columns_keep": ((rows, hidden // 2 + width), low),
        "columns_send": ((rows, hidden // 2 + width), low),
    }
    in_outputs = {
        "small": ((16 * width // 128, 128), full),
        "in_keep": ((rows, 3 * width // 2), low),
        "in_send": ((rows, 3 * width // 2), low),
    }
    rows_scratch = {"all_rows": pltpu.VMEM((2, 2, rows_tall, rows), low)}
    columns_scratch = {"all_columns": pltpu.VMEM((2, rows, hidden // 2 + width), low)}
    in_scratch = {"in_columns": pltpu.VMEM((2, rows, 3 * width // 2), low)}
    bins_scratch = pltpu.VMEM((bins, channels, span), low)
    back_scratch = pltpu.VMEM((bins, channels, span), full)
    raw_scratch = pltpu.VMEM((channels, length), full)
    mlp_weights = {"out_proj": out_proj, "up_proj": up_proj, "down_proj": down_proj}
    remote = ("in_proj", "out_proj", "up_proj", "down_proj")

    def filter_of(level):
        wave = ((inner, length), full)
        return local_call(
            "filter",
            filter_kernel(level),
            place,
            {
                "features": features,
                "filter_first": filter_first,
                "filter_middle": filter_middle,
                "filter_last": filter_last,
                "decay_rates": decay_rates,
                "filter_skip": filter_skip,
                "table": table,
            },
            {
                "filter_spec": ((bins, channels, span), full),
                "skip": ((channels, rows), full),
                "last": ((channels, inner), full),
                "one": wave,
                "slope_one": wave,
                "two": wave,
                "slope_two": wave,
                "window": ((shards, channels, rows), full),
            },
            {"raw": raw_scratch, "bins": bins_scratch},
            time_us=5,
        )

    def conv_of(signal, filters, conjugate, after=()):
        made = local_call(
            "conv_back" if conjugate else "conv",
            conv_kernel(conjugate),
            place,
            {
                "signal": signal,
                "table": table,
                "filter_spec": filters["filter_spec"],
                "skip": filters["skip"],
            },
            {"spec": spectrum, "result": by_shard},
            {"bins": bins_scratch, "back": back_scratch},
            after=after,
            time_us=3,
        )
        return made["result"], made["spec"]

    def filter_back_of(level, filters, d_spec, spec, d_conv, gated):
        return local_call(
            "filter_back",
            filter_grads_kernel(level),
            place,
            {
                "d_spec": d_spec,
                "spec": spec,
                "table": table,
                "d_conv": d_conv,
                "gated": gated,
                "window": filters["window"],
                "two": filters["two"],
                "last": filters["last"],
                "slope_two": filters["slope_two"],
                "one": filters["one"],
                "filter_middle": filter_middle,
                "slope_one": filters["slope_one"],
                "features": features,
            },
            {"packed": ((2 * inner, 128), full)},
            {"back": back_scratch, "raw": raw_scratch},
            time_us=5,
        )["packed"]

    def near_of(made):
        return {
            "projected": made["next_projected"],
            "edge": from_behind(made["next_tail"], "seq", 1),
            "short_taps": short_taps,
        }

    def gated_of(level, near):
        return exchange(
            local_call("short", short_kernel(level), place, near, {"gated": by_shard}, {})["gated"]
        )

    def share_rows(made):
        core = crossed(made["rows_send"], 1)
        return {
            "keep": made["rows_keep"],
            "x": other_sequence(made["rows_keep"]),
            "core": core,
            "core_x": other_sequence(core),
        }

    def share_columns(keep, send):
        x = other_sequence(send)
        return {"keep": keep, "x": x, "core": crossed(keep, 1), "core_x": crossed(x, 1)}

    def named(prefix, parts):
        return {f"{prefix}_{key}": value for key, value in parts.items()}

    entered = local_call(
        "enter",
        enter_kernel,
        place,
        {"tokens": tokens, "mix_gain": mix_gain, "in_proj": in_proj},
        mix_outputs,
        slots(3),
        remote,
        time_us=4,
    )
    near_0 = near_of(entered)
    gated_0 = gated_of(0, near_0)
    filters = [filter_of(0), filter_of(1)]
    conv, spec_0 = conv_of(gated_0, filters[0], False)
    lower = local_call(
        "middle",
        middle_kernel(0),
        place,
        {
            "conv": exchange(conv),
            **near_0,
            "state": tokens,
            "mlp_gain": mlp_gain,
            "rows": entered["next_rows"],
            "mix_gain": mix_gain,
            "in_proj": in_proj,
            **mlp_weights,
        },
        {**mlp_outputs, **mix_outputs},
        {**slots(1 + 2 * ups + 3), **rows_scratch},
        remote,
        time_us=8,
    )
    rows_0 = share_rows(lower)
    near_1 = near_of(lower)
    gated_1 = gated_of(1, near_1)
    conv, spec_1 = conv_of(gated_1, filters[1], False, after=[rows_0["core"]])
    upper = local_call(
        "turn",
        turn_kernel(1),
        place,
        {
            "conv": exchange(conv),
            **near_1,
            "state": lower["next_state"],
            "mlp_gain": mlp_gain,
            "rows": lower["next_rows"],
            "cotangent": cotangent,
            **mlp_weights,
        },
        {**mlp_outputs, **back_outputs},
        {**slots(1 + 2 * ups), **rows_scratch, **columns_scratch},
        remote,
        after=[rows_0["x"], rows_0["core_x"]],
        time_us=10,
    )
    rows_1 = share_rows(upper)
    columns_1 = share_columns(upper["columns_keep"], upper["columns_send"])

    d_conv_1 = exchange(upper["d_conv"])
    d_gated, d_spec = conv_of(
        d_conv_1, filters[1], True, after=[rows_1["core"], columns_1["core"]]
    )
    packed_1 = filter_back_of(1, filters[1], d_spec, spec_1, d_conv_1, gated_1)
    short_back = local_call(
        "short_back",
        short_back_kernel(1),
        place,
        {**near_1, "d_gated": exchange(d_gated), "d_x0": upper["d_x0"]},
        {"head": edges, "d_short": ((rows, 2 * width), full)},
        {},
        after=[rows_1["x"], packed_1],
    )
    between = local_call(
        "between",
        between_kernel(1),
        place,
        {
            "d_short": short_back["d_short"],
            "after": from_behind(short_back["head"], "seq", -1),
            "d_x0_in": upper["d_x0"],
            "upper_projected": near_1["projected"],
            "upper_edge": near_1["edge"],
            "short_taps": short_taps,
            "state": lower["next_state"],
            "d_middle_in": upper["d_middle"],
            "g_mlp_gain_in": upper["g_mlp_gain"],
            "mix_gain": mix_gain,
            "in_proj": in_proj,
            "projected": near_0["projected"],
            "edge": near_0["edge"],
            "middle": lower["middle"],
            "hidden": lower["hidden"],
            "conv_rows": lower["conv_rows"],
            "mlp_gain": mlp_gain,
            **mlp_weights,
        },
        {**in_outputs, **back_outputs},
        {**slots(1 + 2 * ups + 3), **columns_scratch, **in_scratch},
        remote,
        after=[columns_1["x"], columns_1["core_x"]],
        time_us=12,
    )
    columns_in_1 = share_columns(between["in_keep"], between["in_send"])
    columns_0 = share_columns(between["columns_keep"], between["columns_send"])

    def mlp_parts(layer):
        return (
            (layer, 0, 16 * owned, hidden // 2, tile),
            (layer, 16 * owned, 4 * owned, 0, hidden // 2),
            (layer, 20 * owned, 4 * owned, hidden // 2 + tile, tile),
        )

    def cuts_of(prefix, start, count):
        return {f"{prefix}_{key}": (start, count) for key in SOURCES}

    mlp_1 = partial_grads(
        "grad_mlp",
        place,
        {**named("rows_1", rows_1), **named("columns_1", columns_1)},
        mlp_parts(1),
        224,
        tile,
        cuts_of("rows_1", 0, 24 * owned),
        6,
        after=[between["d_conv"]],
    )
    routes = {}
    routes["mlp_p"] = reduce_route(mlp_1["p_keep"], mlp_1["p_send"], (2, 4, 8))
    routes["mlp_q"] = reduce_route(mlp_1["q_keep"], mlp_1["q_send"], (4, 8, 2))

    d_conv_0 = exchange(between["d_conv"])
    d_gated, d_spec = conv_of(d_conv_0, filters[0], True, after=[mlp_1["p_send"]])
    packed_0 = filter_back_of(0, filters[0], d_spec, spec_0, d_conv_0, gated_0)
    mid = partial_grads(
        "grad_mid",
        place,
        {
            **named("rows_0", rows_0),
            **named("columns_0", columns_0),
            **named("rows_1", rows_1),
            **named("columns_1", columns_in_1),
        },
        (*mlp_parts(0), (1, 0, 4 * owned, 0, 3 * tile)),
        288,
        tile,
        {**cuts_of("rows_0", 0, 24 * owned), **cuts_of("rows_1", 24 * owned, 4 * owned)},
        7,
        after=[d_gated],
    )
    routes["mid_p"] = reduce_route(mid["p_keep"], mid["p_send"], (2, 4, 8))
    routes["mid_q"] = reduce_route(mid["q_keep"], mid["q_send"], (4, 8, 2))
    short_back = local_call(
        "short_back",
        short_back_kernel(0),
        place,
        {**near_0, "d_gated": exchange(d_gated), "d_x0": between["d_x0"]},
        {"head": edges, "d_short": ((rows, 2 * width), full)},
        {},
        after=[mid["p_send"], packed_0],
    )
    leave = local_call(
        "leave",
        leave_kernel,
        place,
        {
            "d_short": short_back["d_short"],
            "after": from_behind(short_back["head"], "seq", -1),
            **near_0,
            "d_x0": between["d_x0"],
            "state": tokens,
            "d_middle_in": between["d_middle"],
            "g_mlp_gain_in": between["g_mlp_gain"],
            "mix_gain": mix_gain,
            "in_proj": in_proj,
        },
        {**in_outputs, "upstream": line},
        {**slots(3), **in_scratch},
        remote,
        after=[routes["mlp_p"]["one"], routes["mlp_q"]["one"]],
        time_us=5,
    )
    columns_in_0 = share_columns(leave["in_keep"], leave["in_send"])
    last = partial_grads(
        "grad_in",
        place,
        {**named("rows_0", rows_0), **named("columns_0", columns_in_0)},
        ((0, 0, 4 * owned, 0, 3 * tile),),
        80,
        tile,
        cuts_of("rows_0", 24 * owned, 4 * owned),
        2,
    )
    routes["in_p"] = reduce_route(last["p_keep"], last["p_send"], (2, 4, 8))
    routes["in_q"] = reduce_route(last["q_keep"], last["q_send"], (4, 8, 2))

    joined = jnp.concatenate([leave["small"], packed_0, between["small"], packed_1], axis=0)
    joined = joined + other_sequence(joined)
    each = joined.shape[0] // 2
    sums = {"last_0": joined[each - inner : each], "last_1": joined[2 * each - inner :]}
    kept = each - inner
    joined = jnp.concatenate([joined[:kept], joined[each : each + kept]], axis=0)
    joined = sum_bits(joined, (1, 2, 4, 8))
    sums.update(small_0=joined[:kept], small_1=joined[kept:])

    groups = (
        ("mlp", (("g_down", 1, 4 * owned, 1), ("g_up", 1, owned, 4), ("g_out", 1, owned, 1))),
        (
            "mid",
            (
                ("g_down", 0, 4 * owned, 1),
                ("g_up", 0, owned, 4),
                ("g_out", 0, owned, 1),
                ("g_in", 1, owned, 3),
            ),
        ),
        ("in", (("g_in", 0, owned, 3),)),
    )
    given = {
        f"{group}_{key}": routes[group][key] for group in routes for key in ("mine", "three")
    }
    made = local_call(
        "collect",
        collect_kernel(groups, owned),
        place,
        {**given, **sums},
        {
            "g_mix_gain": ((2, width), full),
            "g_in": ((2, owned, 3 * tile), full),
            "g_taps": ((2, 3, 3 * width), full),
            "g_first": ((2, feats, inner), full),
            "g_middle": ((2, inner, inner), full),
            "g_last": ((2, inner, owned), full),
            "g_skip": ((2, owned), full),
            "g_out": ((2, owned, tile), full),
            "g_mlp_gain": ((2, width), full),
            "g_up": ((2, owned, hidden // 2), full),
            "g_down": ((2, 4 * owned, tile), full),
        },
        {},
        time_us=3,
    )
    return (upper["next_state"][None], leave["upstream"][None], *made.values())


def is_fast(mesh):
    return dict(mesh.shape) == {"dp": 2, "seq": 1 << SEQ_BITS}


def solution(mesh):
    in_specs = (
        P("dp", "seq", None),
        P("dp", "seq", None),
        P(),
        P(),
        P(),
        P(),
        P(),
        P(),
        P(),
        P(),
        P(),
        P(),
        P(),
        P(),
    )
    out_specs = (
        P("dp", "seq", None),
        P("dp", "seq", None),
        P(),
        P(None, "seq", "dp"),
        P(),
        P(),
        P(),
        P(None, None, "seq"),
        P(None, "seq"),
        P(None, "seq", "dp"),
        P(),
        P(None, "seq", "dp"),
        P(None, "seq", "dp"),
    )
    chosen = fast_body if is_fast(mesh) else body
    return jax.shard_map(chosen, mesh=mesh, in_specs=in_specs, out_specs=out_specs, check_vma=False)
```

```python
import functools
import math

import jax
import jax.numpy as jnp
import ml_dtypes
import numpy as np
from jax import lax
from jax.experimental import pallas as pl
from jax.experimental.pallas import tpu as pltpu
from jax.sharding import PartitionSpec as P

FEATS = 33
FFT_COLS = 512


HIGHEST = lax.Precision.HIGHEST
EPSILON = 1e-05


def from_behind(block, axis, distance):
    devices = range(lax.axis_size(axis))
    route = [(i - distance, i) for i in devices if i - distance in devices]
    return lax.ppermute(block, axis, route)


def high_einsum(form, left, right):
    return jnp.einsum(form, left, right, precision=HIGHEST)


def low_einsum(form, left, right):
    return jnp.einsum(form, left, right, preferred_element_type=jnp.float32)


def to_low(value):
    return lax.optimization_barrier(value.astype(jnp.bfloat16))


def angle_table(rows, columns, modulus):
    product = lax.broadcasted_iota(jnp.int32, (rows, columns), 0) * lax.broadcasted_iota(
        jnp.int32, (rows, columns), 1
    )
    angle = (product % modulus).astype(jnp.float32) * (2.0 * math.pi / modulus)
    return (jnp.cos(angle), jnp.sin(angle))


def transform_tables(length, columns):
    total = 2 * length
    rows = total // columns
    cos_rows, sin_rows = angle_table(rows, rows, rows)
    cos_columns, sin_columns = angle_table(columns, columns, columns)
    cos_turn, sin_turn = angle_table(rows, columns, total)
    return (cos_rows, sin_rows, cos_columns, sin_columns, cos_turn, sin_turn)


def forward_transform(signal, tables):
    cos_rows, sin_rows, cos_columns, sin_columns, cos_turn, sin_turn = tables
    channels, length = signal.shape
    rows, columns = cos_turn.shape
    padded = jnp.pad(signal, ((0, 0), (0, length))).reshape(channels, rows, columns)
    first_real = high_einsum("kq,cqp->ckp", cos_rows, padded)
    first_imag = -high_einsum("kq,cqp->ckp", sin_rows, padded)
    turned_real = first_real * cos_turn + first_imag * sin_turn
    turned_imag = first_imag * cos_turn - first_real * sin_turn
    spec_real = high_einsum("ckp,pj->ckj", turned_real, cos_columns) + high_einsum(
        "ckp,pj->ckj", turned_imag, sin_columns
    )
    spec_imag = high_einsum("ckp,pj->ckj", turned_imag, cos_columns) - high_einsum(
        "ckp,pj->ckj", turned_real, sin_columns
    )
    return (spec_real, spec_imag)


def inverse_transform(spec_real, spec_imag, tables):
    cos_rows, sin_rows, cos_columns, sin_columns, cos_turn, sin_turn = tables
    rows, columns = cos_turn.shape
    back_real = high_einsum("ckp,pj->ckj", spec_real, cos_columns) - high_einsum(
        "ckp,pj->ckj", spec_imag, sin_columns
    )
    back_imag = high_einsum("ckp,pj->ckj", spec_imag, cos_columns) + high_einsum(
        "ckp,pj->ckj", spec_real, sin_columns
    )
    turned_real = back_real * cos_turn - back_imag * sin_turn
    turned_imag = back_imag * cos_turn + back_real * sin_turn
    signal = high_einsum("qk,ckp->cqp", cos_rows, turned_real) - high_einsum(
        "qk,ckp->cqp", sin_rows, turned_imag
    )
    total = rows * columns
    return signal.reshape(signal.shape[0], total)[:, : total // 2] / total


def position_features(length):
    count = (FEATS - 1) // 2
    steps = lax.broadcasted_iota(jnp.int32, (count, length), 1)
    frequency = lax.broadcasted_iota(jnp.int32, (count, length), 0) + 1
    angle = (steps * frequency % length).astype(jnp.float32) * (2.0 * math.pi / length)
    ramp = lax.broadcasted_iota(jnp.int32, (1, length), 1).astype(jnp.float32) / length
    return jnp.concatenate([ramp, jnp.cos(angle), jnp.sin(angle)], axis=0)


def filter_forward(features, first, middle, last_columns, rate_columns, length):
    pre_one = high_einsum("fk,ft->kt", first, features)
    act_one = jnp.sin(pre_one)
    pre_two = high_einsum("kj,kt->jt", middle, act_one)
    act_two = jnp.sin(pre_two)
    raw = high_einsum("kc,kt->ct", last_columns, act_two)
    steps = lax.broadcasted_iota(jnp.int32, (1, length), 1).astype(jnp.float32)
    window = jnp.exp(-rate_columns[:, None] * steps) * jnp.sqrt(
        rate_columns[:, None] + 1.0 / length
    )
    return (raw * window, (pre_one, act_one, pre_two, act_two, window))


def filter_backward(d_response, features, middle, last_columns, kept):
    pre_one, act_one, pre_two, act_two, window = kept
    d_raw = d_response * window
    g_last = high_einsum("kt,ct->kc", act_two, d_raw)
    d_two = high_einsum("kc,ct->kt", last_columns, d_raw) * jnp.cos(pre_two)
    g_middle = high_einsum("kt,jt->kj", act_one, d_two)
    d_one = high_einsum("kj,jt->kt", middle, d_two) * jnp.cos(pre_one)
    g_first = high_einsum("ft,kt->fk", features, d_one)
    return (g_first, g_middle, g_last)


def normalize(state):
    centred = state - jnp.mean(state, axis=1, keepdims=True)
    scale = lax.rsqrt(jnp.mean(centred * centred, axis=1, keepdims=True) + EPSILON)
    return (centred * scale, scale)


def normalize_back(d_out, normed, scale, gain):
    d_normed = d_out * gain
    g_gain = jnp.sum(d_out * normed, axis=0)
    d_state = scale * (
        d_normed
        - jnp.mean(d_normed, axis=1, keepdims=True)
        - normed * jnp.mean(d_normed * normed, axis=1, keepdims=True)
    )
    return (d_state, g_gain)


def short_forward(extended, taps):
    length = extended.shape[-1] - 2
    return (
        taps[0] * extended[..., 2:]
        + taps[1] * extended[..., 1 : length + 1]
        + taps[2] * extended[..., :length]
    )


def short_backward(d_extended, taps):
    length = d_extended.shape[-1] - 2
    return (
        taps[0] * d_extended[..., :length]
        + taps[1] * d_extended[..., 1 : length + 1]
        + taps[2] * d_extended[..., 2:]
    )


def tap_grads(d_shorted, extended):
    length = d_shorted.shape[-1]
    return jnp.stack(
        [
            jnp.sum(d_shorted * extended[..., 2 - lag : 2 - lag + length], axis=-1)
            for lag in range(3)
        ]
    )


def long_forward(gated, filter_real, filter_imag, skip_columns, tables):
    signal = gated.astype(jnp.float32)
    sig_real, sig_imag = forward_transform(signal, tables)
    result = inverse_transform(
        sig_real * filter_real - sig_imag * filter_imag,
        sig_real * filter_imag + sig_imag * filter_real,
        tables,
    )
    return (result + skip_columns[:, None] * signal, (sig_real, sig_imag))


def long_backward(d_conv, gated, filter_real, filter_imag, skip_columns, signal_spec, tables):
    d_signal = d_conv.astype(jnp.float32)
    d_real, d_imag = forward_transform(d_signal, tables)
    sig_real, sig_imag = signal_spec
    d_gated = (
        inverse_transform(
            d_real * filter_real + d_imag * filter_imag,
            d_imag * filter_real - d_real * filter_imag,
            tables,
        )
        + skip_columns[:, None] * d_signal
    )
    d_response = inverse_transform(
        d_real * sig_real + d_imag * sig_imag, d_imag * sig_real - d_real * sig_imag, tables
    )
    g_skip = jnp.sum(d_signal * gated.astype(jnp.float32), axis=1)
    return (d_gated, d_response, g_skip)


def unit(k,n):
    k%=n
    if (4*k)%n==0:
        q=(4*k)//n
        return [(1.0,0.0),(0.0,-1.0),(-1.0,0.0),(0.0,1.0)][q]
    a=-2.0*math.pi*k/n
    return (math.cos(a),math.sin(a))
def times(z,w):
    re,im=z; c,s=w
    if s==0.0: return (re,im) if c==1.0 else (-re,-im)
    if c==0.0: return (-im,re) if s==1.0 else (im,-re)
    return (re*c-im*s, re*s+im*c)
def plus(a,b): return (a[0]+b[0],a[1]+b[1])
def minus(a,b): return (a[0]-b[0],a[1]-b[1])
def complex_dft(zs,sign):
    n=len(zs)
    if n==1: return zs
    ev=complex_dft(zs[0::2],sign); od=complex_dft(zs[1::2],sign)
    lo,hi=[],[]
    for k in range(n//2):
        v=times(od[k],unit(sign*k,n))
        lo.append(plus(ev[k],v)); hi.append(minus(ev[k],v))
    return lo+hi
def odd_bins(xs):
    n=len(xs); h=n//2; N=2*n
    zs=[times((xs[j],-xs[j+h]),unit(j,N)) for j in range(h)]
    bins={}
    for q,z in enumerate(complex_dft(zs,1)):
        k=4*q+1
        if k<=n: bins[k]=z
        else: bins[N-k]=(z[0],-z[1])
    return bins
def real_bins(xs):
    n=len(xs)
    if n==1: return {0:(xs[0],None)}
    if n==2: return {0:(xs[0]+xs[1],None),1:(xs[0]-xs[1],None)}
    h=n//2
    bins={2*k:z for k,z in real_bins([xs[j]+xs[j+h] for j in range(h)]).items()}
    bins.update(odd_bins([xs[j]-xs[j+h] for j in range(h)]))
    return bins
def padded_bins(xs):
    bins={2*k:z for k,z in real_bins(xs).items()}
    bins.update(odd_bins(xs))
    return bins
def odd_back(bins,n):
    h=n//2; N=2*n
    zs=[]
    for q in range(h):
        k=4*q+1
        if k<=n: zs.append(bins[k])
        else:
            re,im=bins[N-k]; zs.append((re,-im))
    vs=[times(z,unit(-j,N)) for j,z in enumerate(complex_dft(zs,-1))]
    return [v[0] for v in vs]+[-v[1] for v in vs]
def real_back(bins,n):
    if n==1: return [bins[0][0]]
    if n==2: return [bins[0][0]+bins[1][0],bins[0][0]-bins[1][0]]
    h=n//2
    ev=real_back({k//2:z for k,z in bins.items() if k%2==0},h)
    od=odd_back(bins,h)
    return [ev[j]+od[j] for j in range(h)]+[ev[j]-od[j] for j in range(h)]
def padded_back(bins,n):
    ev=real_back({k//2:z for k,z in bins.items() if k%2==0},n)
    od=odd_back(bins,n)
    return [a+b for a,b in zip(ev,od)]


def turn_table(shards, rows):
    total = 2 * shards * rows
    early = np.arange(rows)[None, :, None]
    late = np.arange(rows)[None, None, :]
    bins = np.arange(shards + 1)[:, None, None]
    angle = (early * (bins + 2 * shards * late) % total) * (2.0 * np.pi / total)
    cos, sin = np.cos(angle), np.sin(angle)
    top = np.concatenate([cos, -sin], axis=2)
    bottom = np.concatenate([sin, cos], axis=2)
    return jnp.asarray(np.concatenate([top, bottom], axis=1).astype(ml_dtypes.bfloat16))


def position_table(length):
    count = (FEATS - 1) // 2
    steps = np.arange(length)[None, :]
    angle = (steps * np.arange(1, count + 1)[:, None] % length) * (2.0 * np.pi / length)
    table = np.concatenate([steps / length, np.cos(angle), np.sin(angle)], axis=0)
    return jnp.asarray(table.astype(np.float32))


def chunks_of(channels):
    step = 16 if channels % 16 == 0 else channels
    return [slice(at, at + step) for at in range(0, channels, step)]


def load_bins(blocks, bins_ref, chunk):
    lanes = blocks[0].shape[-1]
    for k, (re, im) in padded_bins(blocks).items():
        im = jnp.zeros_like(re) if im is None else im
        bins_ref[k, chunk, :lanes] = re.astype(jnp.bfloat16)
        bins_ref[k, chunk, lanes:] = im.astype(jnp.bfloat16)


def fold_bins(back_ref, chunk, count, lanes):
    bins = {
        k: (back_ref[k, chunk, :lanes], back_ref[k, chunk, lanes:]) for k in range(count + 1)
    }
    return padded_back(bins, count)


def bin_scale(k, shards, rows):
    total = 2 * shards * rows
    return (1.0 if k in (0, shards) else 2.0) / total


def bin_product(left, right, conjugate):
    lanes = left.shape[1] // 2
    a, b = left[:, :lanes], left[:, lanes:]
    c, d = right[:, :lanes], right[:, lanes:]
    if conjugate:
        return jnp.concatenate([a * c + b * d, b * c - a * d], axis=1)
    return jnp.concatenate([a * c - b * d, a * d + b * c], axis=1)


def turn(left, table):
    return jnp.dot(left, table, preferred_element_type=jnp.float32)


def turn_back(left, table):
    return lax.dot_general(
        left.astype(jnp.bfloat16),
        table,
        (((1,), (1,)), ((), ())),
        preferred_element_type=jnp.float32,
    )


def sin_cos(angle):
    steps = jnp.floor(angle * (2.0 / math.pi) + 0.5)
    rest = angle - steps * 1.5703125
    rest = rest - steps * 4.837512969970703e-4
    rest = rest - steps * 7.549789954891882e-8
    square = rest * rest
    sin = rest + rest * square * (
        -1.6666654611e-1 + square * (8.3321608736e-3 + square * -1.9515295891e-4)
    )
    cos = (
        1.0
        - 0.5 * square
        + square
        * square
        * (4.166664568298827e-2 + square * (-1.388731625493765e-3 + square * 2.443315711809948e-5))
    )
    quarter = steps.astype(jnp.int32)
    odd = (quarter & 1) == 1
    sin_out = jnp.where(odd, cos, sin)
    cos_out = jnp.where(odd, sin, cos)
    sin_out = jnp.where((quarter & 2) == 2, -sin_out, sin_out)
    cos_out = jnp.where(((quarter + 1) & 2) == 2, -cos_out, cos_out)
    return sin_out, cos_out


def across(left, right, left_side, right_side):
    return lax.dot_general(
        left,
        right,
        (((left_side,), (right_side,)), ((), ())),
        precision=HIGHEST,
        preferred_element_type=jnp.float32,
    )


def filter_network_kernel(
    feature_ref,
    first_ref,
    middle_ref,
    last_ref,
    rate_ref,
    table_ref,
    spec_ref,
    one_ref,
    slope_one_ref,
    two_ref,
    slope_two_ref,
    window_ref,
    raw_ref,
    bins_ref,
):
    shards, channels, rows = window_ref.shape
    one, slope_one = sin_cos(across(first_ref[...], feature_ref[...], 0, 0))
    one_ref[...] = one
    slope_one_ref[...] = slope_one
    two, slope_two = sin_cos(across(middle_ref[...], one, 0, 0))
    two_ref[...] = two
    slope_two_ref[...] = slope_two
    raw_ref[...] = across(last_ref[...], two, 0, 0)
    rate = rate_ref[...]
    size = jnp.sqrt(rate + 1.0 / (shards * rows))
    step = lax.broadcasted_iota(jnp.int32, (channels, rows), 1)
    for j in range(shards):
        window = jnp.exp(-rate * (step + j * rows).astype(jnp.float32)) * size
        window_ref[j] = window
        at = slice(j * rows, (j + 1) * rows)
        raw_ref[:, at] = raw_ref[:, at] * window
    for chunk in chunks_of(channels):
        load_bins(
            [raw_ref[chunk, j * rows : (j + 1) * rows] for j in range(shards)], bins_ref, chunk
        )
    for k in range(shards + 1):
        spec_ref[k] = turn(bins_ref[k], table_ref[k]) * bin_scale(k, shards, rows)


def filter_network(features, first, middle, last, rates, table):
    hidden, channels = last.shape
    length = features.shape[1]
    bins, span, _ = table.shape
    rows = span // 2
    shards = length // rows
    wide = jax.ShapeDtypeStruct((hidden, length), jnp.float32)
    return pl.pallas_call(
        filter_network_kernel,
        out_shape=[
            jax.ShapeDtypeStruct((bins, channels, span), jnp.float32),
            wide,
            wide,
            wide,
            wide,
            jax.ShapeDtypeStruct((shards, channels, rows), jnp.float32),
        ],
        scratch_shapes=[
            pltpu.VMEM((channels, length), jnp.float32),
            pltpu.VMEM((bins, channels, span), jnp.bfloat16),
        ],
        compiler_params=pltpu.CompilerParams(vmem_limit_bytes=40 << 20),
        name="filter_network",
    )(features, first, middle, last, rates, table)


def conv_forward_kernel(
    gated_ref, filter_ref, skip_ref, table_ref, conv_ref, spec_ref, bins_ref, back_ref
):
    shards, channels, rows = gated_ref.shape
    for chunk in chunks_of(channels):
        load_bins(
            [gated_ref[j, chunk].astype(jnp.float32) for j in range(shards)], bins_ref, chunk
        )
    for k in range(shards + 1):
        spec = turn(bins_ref[k], table_ref[k])
        spec_ref[k] = spec.astype(jnp.bfloat16)
        back_ref[k] = turn_back(bin_product(spec, filter_ref[k], False), table_ref[k])
    for chunk in chunks_of(channels):
        skip = skip_ref[chunk]
        for j, block in enumerate(fold_bins(back_ref, chunk, shards, rows)):
            conv = block + skip * gated_ref[j, chunk].astype(jnp.float32)
            conv_ref[j, chunk] = conv.astype(jnp.bfloat16)


def conv_backward_kernel(
    gated_ref, filter_ref, skip_ref, table_ref, conv_ref, spec_ref, bins_ref, back_ref
):
    shards, channels, rows = gated_ref.shape
    for chunk in chunks_of(channels):
        load_bins(
            [gated_ref[j, chunk].astype(jnp.float32) for j in range(shards)], bins_ref, chunk
        )
    for k in range(shards + 1):
        spec = turn(bins_ref[k], table_ref[k])
        spec_ref[k] = spec.astype(jnp.bfloat16)
        back_ref[k] = turn_back(bin_product(spec, filter_ref[k], True), table_ref[k])
    for chunk in chunks_of(channels):
        skip = skip_ref[chunk]
        for j, block in enumerate(fold_bins(back_ref, chunk, shards, rows)):
            conv = block + skip * gated_ref[j, chunk].astype(jnp.float32)
            conv_ref[j, chunk] = conv.astype(jnp.bfloat16)


def conv_call(kernel, name, gated, filter_spec, skip, table):
    bins, channels, span = filter_spec.shape
    return pl.pallas_call(
        kernel,
        out_shape=[
            jax.ShapeDtypeStruct(gated.shape, jnp.bfloat16),
            jax.ShapeDtypeStruct((bins, channels, span), jnp.bfloat16),
        ],
        scratch_shapes=[
            pltpu.VMEM((bins, channels, span), jnp.bfloat16),
            pltpu.VMEM((bins, channels, span), jnp.float32),
        ],
        compiler_params=pltpu.CompilerParams(vmem_limit_bytes=40 << 20),
        name=name,
    )(gated, filter_spec, skip, table)


def conv_forward(gated, filter_spec, skip, table):
    return conv_call(conv_forward_kernel, "conv_forward", gated, filter_spec, skip, table)


def conv_backward(d_conv, filter_spec, skip, table):
    return conv_call(conv_backward_kernel, "conv_backward", d_conv, filter_spec, skip, table)


def filter_back_kernel(
    d_spec_ref,
    spec_ref,
    d_conv_ref,
    gated_ref,
    feature_ref,
    middle_ref,
    last_ref,
    one_ref,
    slope_one_ref,
    two_ref,
    slope_two_ref,
    window_ref,
    table_ref,
    g_first_ref,
    g_middle_ref,
    g_last_ref,
    g_skip_ref,
    back_ref,
    raw_ref,
):
    shards, channels, rows = d_conv_ref.shape
    for k in range(shards + 1):
        spec = bin_product(
            d_spec_ref[k].astype(jnp.float32), spec_ref[k].astype(jnp.float32), True
        )
        back_ref[k] = turn_back(spec * bin_scale(k, shards, rows), table_ref[k])
    for chunk in chunks_of(channels):
        total = None
        for j, block in enumerate(fold_bins(back_ref, chunk, shards, rows)):
            raw_ref[chunk, j * rows : (j + 1) * rows] = block * window_ref[j, chunk]
            term = d_conv_ref[j, chunk].astype(jnp.float32) * gated_ref[j, chunk].astype(
                jnp.float32
            )
            total = term if total is None else total + term
        g_skip_ref[chunk] = jnp.sum(total, axis=1, keepdims=True)
    d_raw = raw_ref[...]
    g_last_ref[...] = across(two_ref[...], d_raw, 1, 1)
    d_two = across(last_ref[...], d_raw, 1, 0) * slope_two_ref[...]
    g_middle_ref[...] = across(one_ref[...], d_two, 1, 1)
    d_one = across(middle_ref[...], d_two, 1, 0) * slope_one_ref[...]
    g_first_ref[...] = across(feature_ref[...], d_one, 1, 1)


def filter_network_back(
    d_spec, spec, d_conv, gated, features, middle, last, kept, table
):
    _, one, slope_one, two, slope_two, window = kept
    bins, channels, span = spec.shape
    hidden, length = one.shape
    feats = features.shape[0]
    return pl.pallas_call(
        filter_back_kernel,
        out_shape=[
            jax.ShapeDtypeStruct((feats, hidden), jnp.float32),
            jax.ShapeDtypeStruct((hidden, hidden), jnp.float32),
            jax.ShapeDtypeStruct((hidden, channels), jnp.float32),
            jax.ShapeDtypeStruct((channels, 1), jnp.float32),
        ],
        scratch_shapes=[
            pltpu.VMEM((bins, channels, span), jnp.float32),
            pltpu.VMEM((channels, length), jnp.float32),
        ],
        compiler_params=pltpu.CompilerParams(vmem_limit_bytes=40 << 20),
        name="filter_network_back",
    )(
        d_spec,
        spec,
        d_conv,
        gated,
        features,
        middle,
        last,
        one,
        slope_one,
        two,
        slope_two,
        window,
        table,
    )


def layer_forward(state, weights, setting):
    (
        mix_gain,
        in_proj,
        short_taps,
        first,
        middle,
        last,
        skip,
        rates,
        out_proj,
        mlp_gain,
        up_proj,
        down_proj,
    ) = weights
    features, tables, offset = setting
    rows, width = state.shape
    length = features.shape[1]
    channels = width // (length // rows)
    normed_mix, scale_mix = normalize(state)
    u_mix = to_low(normed_mix * mix_gain)
    projected = to_low(low_einsum("td,dc->ct", u_mix, in_proj)).reshape(3, width, rows)
    last_columns = lax.dynamic_slice_in_dim(last, offset, channels, 1)
    skip_columns = lax.dynamic_slice_in_dim(skip, offset, channels, 0)
    rate_columns = lax.dynamic_slice_in_dim(rates, offset, channels, 0)
    filter_kept = filter_network(
        features, first, middle, last_columns, rate_columns[:, None], tables
    )
    filter_spec = filter_kept[0]
    taps = short_taps.reshape(3, 3, width)
    edge = from_behind(projected[:, :, rows - 2 :], "seq", 1)
    extended = jnp.concatenate([edge, projected], axis=2).astype(jnp.float32)
    tap_use = taps[:, :, :, None]
    shorted = short_forward(extended, tap_use)
    gated_rows = to_low(shorted[2] * shorted[1])
    shards = length // rows
    gated = lax.all_to_all(
        gated_rows.reshape(shards, channels, rows), "seq", split_axis=0, concat_axis=0, tiled=True
    )
    conv_low, signal_spec = conv_forward(gated, filter_spec, skip_columns[:, None], tables)
    conv_here = lax.all_to_all(
        conv_low, "seq", split_axis=0, concat_axis=0, tiled=True
    ).reshape(width, rows)
    mixed = to_low(conv_here.astype(jnp.float32) * shorted[0])
    middle_state = state + low_einsum("ct,ce->te", mixed, out_proj)
    normed_mlp, scale_mlp = normalize(middle_state)
    u_mlp = to_low(normed_mlp * mlp_gain)
    hidden = low_einsum("td,df->tf", u_mlp, up_proj)
    active = to_low(jax.nn.gelu(hidden))
    result = middle_state + low_einsum("tf,fe->te", active, down_proj)
    kept = (
        normed_mix,
        scale_mix,
        u_mix,
        extended,
        shorted,
        gated,
        conv_here,
        mixed,
        filter_kept,
        filter_spec,
        signal_spec,
        normed_mlp,
        scale_mlp,
        u_mlp,
        hidden,
        active,
        last_columns,
        skip_columns,
        tap_use,
    )
    return (result, kept)


def layer_backward(upstream, kept, weights, setting):
    (
        mix_gain,
        in_proj,
        short_taps,
        first,
        middle,
        last,
        skip,
        rates,
        out_proj,
        mlp_gain,
        up_proj,
        down_proj,
    ) = weights
    features, tables, offset = setting
    (
        normed_mix,
        scale_mix,
        u_mix,
        extended,
        shorted,
        gated,
        conv_here,
        mixed,
        filter_kept,
        filter_spec,
        signal_spec,
        normed_mlp,
        scale_mlp,
        u_mlp,
        hidden,
        active,
        last_columns,
        skip_columns,
        tap_use,
    ) = kept
    rows, width = upstream.shape
    d_down = to_low(upstream)
    g_down = low_einsum("tf,te->fe", active, d_down)
    d_active = low_einsum("te,fe->tf", d_down, down_proj)
    d_hidden = to_low(jax.vjp(jax.nn.gelu, hidden)[1](d_active)[0])
    g_up = low_einsum("td,tf->df", u_mlp, d_hidden)
    d_u_mlp = low_einsum("tf,df->td", d_hidden, up_proj)
    d_middle, g_mlp_gain = normalize_back(d_u_mlp, normed_mlp, scale_mlp, mlp_gain)
    d_middle = d_middle + upstream
    d_branch = to_low(d_middle)
    g_out = low_einsum("ct,te->ce", mixed, d_branch)
    d_mixed = to_low(low_einsum("te,ce->ct", d_branch, out_proj))
    d_mixed_wide = d_mixed.astype(jnp.float32)
    d_conv_rows = to_low(d_mixed_wide * shorted[0])
    d_zero = d_mixed_wide * conv_here.astype(jnp.float32)
    shards, channels, _ = gated.shape
    d_conv = lax.all_to_all(
        d_conv_rows.reshape(gated.shape), "seq", split_axis=0, concat_axis=0, tiled=True
    )
    d_gated, d_spec = conv_backward(d_conv, filter_spec, skip_columns[:, None], tables)
    d_gated_rows = lax.all_to_all(
        d_gated, "seq", split_axis=0, concat_axis=0, tiled=True
    ).reshape(width, rows).astype(jnp.float32)
    d_shorted = jnp.stack([d_zero, d_gated_rows * shorted[2], d_gated_rows * shorted[1]])
    after = from_behind(d_shorted[:, :, :2], "seq", -1)
    d_extended = jnp.concatenate([d_shorted, after], axis=2)
    d_projected = to_low(short_backward(d_extended, tap_use))
    g_taps = tap_grads(d_shorted, extended)
    g_first, g_middle, g_last, g_skip = filter_network_back(
        d_spec, signal_spec, d_conv, gated, features, middle, last_columns, filter_kept, tables
    )
    g_skip = g_skip[:, 0]
    d_flat = d_projected.reshape(3 * width, rows)
    g_in = low_einsum("td,ct->dc", u_mix, d_flat)
    d_u_mix = low_einsum("ct,dc->td", d_flat, in_proj)
    d_state, g_mix_gain = normalize_back(d_u_mix, normed_mix, scale_mix, mix_gain)
    d_state = d_state + d_middle
    large = (g_in, g_out, g_up, g_down)
    small = (g_mix_gain, g_taps.reshape(3, 3 * width), g_first, g_middle, g_mlp_gain)
    column_part = (g_last, g_skip)
    return (d_state, large, small, column_part)


def body(
    tokens,
    cotangent,
    mix_gain,
    in_proj,
    short_taps,
    filter_first,
    filter_middle,
    filter_last,
    filter_skip,
    decay_rates,
    out_proj,
    mlp_gain,
    up_proj,
    down_proj,
):
    rows = tokens.shape[1]
    width = tokens.shape[2]
    layer_count = mix_gain.shape[0]
    shards = lax.axis_size("seq")
    length = rows * shards
    offset = lax.axis_index("seq") * (width // shards)
    setting = (position_table(length), turn_table(shards, rows), offset)
    stacks = (
        mix_gain,
        in_proj,
        short_taps,
        filter_first,
        filter_middle,
        filter_last,
        filter_skip,
        decay_rates,
        out_proj,
        mlp_gain,
        up_proj,
        down_proj,
    )
    state = tokens[0].astype(jnp.float32)
    kept_all = []
    for level in range(layer_count):
        weights = tuple((item[level] for item in stacks))
        state, kept = layer_forward(state, weights, setting)
        kept_all.append(kept)
    upstream = cotangent[0].astype(jnp.float32)
    large_all = [None] * layer_count
    small_all = [None] * layer_count
    column_all = [None] * layer_count
    for level in reversed(range(layer_count)):
        weights = tuple((item[level] for item in stacks))
        upstream, large, small, column_part = layer_backward(
            upstream, kept_all[level], weights, setting
        )
        large_all[level] = large
        small_all[level] = small
        column_all[level] = column_part
    stacked_large = [
        jnp.stack([large_all[level][member] for level in range(layer_count)]) for member in range(4)
    ]
    row_in, row_out, row_up, row_down = (
        lax.psum_scatter(stacked_large[0], "seq", scatter_dimension=1, tiled=True),
        lax.psum_scatter(stacked_large[1], "seq", scatter_dimension=1, tiled=True),
        lax.psum_scatter(stacked_large[2], "seq", scatter_dimension=1, tiled=True),
        lax.psum_scatter(stacked_large[3], "seq", scatter_dimension=1, tiled=True),
    )
    g_in, g_out, g_up, g_down = (
        lax.psum_scatter(row_in.astype(jnp.bfloat16), "dp", scatter_dimension=2, tiled=True).astype(
            jnp.float32
        ),
        lax.psum_scatter(
            row_out.astype(jnp.bfloat16), "dp", scatter_dimension=2, tiled=True
        ).astype(jnp.float32),
        lax.psum_scatter(row_up.astype(jnp.bfloat16), "dp", scatter_dimension=2, tiled=True).astype(
            jnp.float32
        ),
        lax.psum_scatter(
            row_down.astype(jnp.bfloat16), "dp", scatter_dimension=2, tiled=True
        ).astype(jnp.float32),
    )
    stacked_small = [
        jnp.stack([small_all[level][member] for level in range(layer_count)]) for member in range(5)
    ]
    g_mix_gain, g_taps, g_first, g_middle, g_mlp_gain = lax.psum(
        (stacked_small[0], stacked_small[1], stacked_small[2], stacked_small[3], stacked_small[4]),
        ("dp", "seq"),
    )
    stacked_last = jnp.stack([column_all[level][0] for level in range(layer_count)])
    stacked_skip = jnp.stack([column_all[level][1] for level in range(layer_count)])
    g_last, g_skip = lax.psum((stacked_last, stacked_skip), "dp")
    return (
        state[None],
        upstream[None],
        g_mix_gain,
        g_in,
        g_taps,
        g_first,
        g_middle,
        g_last,
        g_skip,
        g_out,
        g_mlp_gain,
        g_up,
        g_down,
    )


SEQ_BITS = 4
VMEM_BYTES = 62 << 20
COST = 3000
LOW, FULL = jnp.bfloat16, jnp.float32


class Board:
    def __init__(self, place, held, inputs, outputs):
        self.place = place
        self.held, self.arriving, self.outputs, self.leaving = held, {}, outputs, []
        for key, (source, target, sem) in inputs.items():
            copy = pltpu.make_async_copy(source, target, sem)
            copy.start()
            self.arriving[key] = copy
            held[key] = target
        for key, (source, _, _) in outputs.items():
            held[key] = source

    def __getattr__(self, key):
        return self[key]

    def __getitem__(self, key):
        if key in self.arriving:
            self.arriving.pop(key).wait()
        return self.held[key]

    def flush(self, *refs):
        for key in [key for key, item in self.outputs.items() if any(item[0] is ref for ref in refs)]:
            copy = pltpu.make_async_copy(*self.outputs.pop(key))
            copy.start()
            self.leaving.append(copy)

    def finish(self):
        self.flush(*[item[0] for item in self.outputs.values()])
        for copy in [*self.arriving.values(), *self.leaving]:
            copy.wait()


class Made:
    def __init__(self, items):
        self.__dict__.update(kept=dict(items))

    def __getattr__(self, key):
        return self.kept[key]

    def __getitem__(self, key):
        return self.kept[key]


class Renamed:
    def __init__(self, board, **names):
        self.__dict__.update(board=board, names=names)

    def __getattr__(self, key):
        return getattr(self.__dict__["board"], self.__dict__["names"].get(key, key))


def local_call(
    name,
    body,
    place,
    near,
    outputs,
    scratch=None,
    far=None,
    direct=None,
    cuts=None,
    after=(),
):
    scratch, far, direct, cuts = scratch or {}, far or {}, direct or {}, cuts or {}
    arrays = [*near.values(), *far.values(), *after]
    made_shapes = {**outputs, **direct}

    def shape_of(key):
        shape = list(near[key].shape)
        if key in cuts:
            shape[1] = cuts[key][1]
        return tuple(shape)

    def cut(key, ref):
        return ref.at[:, pl.ds(*cuts[key])] if key in cuts else ref

    def kernel(*refs):
        refs = list(refs)
        place_ref = refs.pop(0)
        given = [refs.pop(0) for _ in arrays]
        made = [refs.pop(0) for _ in made_shapes]
        here = [refs.pop(0) for _ in near]
        staged = [refs.pop(0) for _ in outputs]
        spare = [refs.pop(0) for _ in scratch]
        sems_in, sems_out = refs
        held = dict(zip(far, given[len(near) :]))
        held.update(zip(scratch, spare))
        held.update(zip(direct, made[len(outputs) :]))
        board = Board(
            place_ref,
            held,
            {key: (cut(key, given[at]), here[at], sems_in.at[at]) for at, key in enumerate(near)},
            {key: (staged[at], made[at], sems_out.at[at]) for at, key in enumerate(outputs)},
        )
        body(board)
        board.finish()

    made = pl.pallas_call(
        kernel,
        in_specs=[pl.BlockSpec(memory_space=pltpu.SMEM)]
        + [pl.BlockSpec(memory_space=pltpu.HBM)] * len(arrays),
        out_specs=[pl.BlockSpec(memory_space=pltpu.HBM)] * len(made_shapes),
        out_shape=[jax.ShapeDtypeStruct(*item) for item in made_shapes.values()],
        scratch_shapes=[pltpu.VMEM(shape_of(key), near[key].dtype) for key in near]
        + [pltpu.VMEM(*item) for item in outputs.values()]
        + list(scratch.values())
        + [
            pltpu.SemaphoreType.DMA((max(len(near), 1),)),
            pltpu.SemaphoreType.DMA((max(len(outputs), 1),)),
        ],
        compiler_params=pltpu.CompilerParams(vmem_limit_bytes=VMEM_BYTES),
        cost_estimate=pl.CostEstimate(flops=0, bytes_accessed=COST, transcendentals=0),
        name=name,
    )(place, *arrays)
    return Made(zip(made_shapes, made, strict=True))


class Weights:
    def __init__(self, slots, sems):
        self.slots, self.sems, self.copies = slots, sems, []

    def fetch(self, source):
        at = len(self.copies)
        copy = pltpu.make_async_copy(source, self.slots.at[at], self.sems.at[at])
        copy.start()
        self.copies.append(copy)
        return at

    def fetch_columns(self, source, width):
        count = source.shape[1] // width
        return [self.fetch(source.at[:, pl.ds(j * width, width)]) for j in range(count)]

    def fetch_rows(self, source, width):
        count = source.shape[0] // width
        return [self.fetch(source.at[pl.ds(j * width, width)]) for j in range(count)]

    def wait(self, at):
        if self.copies[at] is not None:
            self.copies[at].wait()
            self.copies[at] = None
        return self.slots[at]


def dot(left, right):
    return jnp.dot(left, right, preferred_element_type=jnp.float32)


def dot_rows(left, right):
    return lax.dot_general(
        left, right, (((1,), (1,)), ((), ())), preferred_element_type=jnp.float32
    )


def low_across(left, right, left_side, right_side):
    return lax.dot_general(
        narrow(left),
        narrow(right),
        (((left_side,), (right_side,)), ((), ())),
        preferred_element_type=jnp.float32,
    )


def flip(block):
    return block.T


def wide(value):
    return value.astype(jnp.float32)


def narrow(value):
    return value.astype(jnp.bfloat16)


def rotate(block, shift):
    return pltpu.roll(block, shift % block.shape[1], 1)


def shifted_down(block, edge):
    row = lax.broadcasted_iota(jnp.int32, block.shape, 0)
    one = jnp.where(row == 0, edge[1:2], pltpu.roll(block, 1, 0))
    two = jnp.where(row == 0, edge[0:1], jnp.where(row == 1, edge[1:2], pltpu.roll(block, 2, 0)))
    return one, two


def shifted_up(block, edge):
    rows = block.shape[0]
    row = lax.broadcasted_iota(jnp.int32, block.shape, 0)
    one = jnp.where(row == rows - 1, edge[0:1], pltpu.roll(block, rows - 1, 0))
    two = jnp.where(
        row == rows - 1,
        edge[1:2],
        jnp.where(row == rows - 2, edge[0:1], pltpu.roll(block, rows - 2, 0)),
    )
    return one, two


def branch_columns(r, branch):
    width = r.projected.shape[1] // 3
    return slice(branch * width, (branch + 1) * width)


def taps_of(r, level, branch):
    width = r.short_taps.shape[2] // 3
    at = slice(branch * width, (branch + 1) * width)
    return [r.short_taps[lag, level : level + 1, at] for lag in range(3)]


def lagged(r, branch):
    block = wide(r.projected[:, branch_columns(r, branch)])
    return (block, *shifted_down(block, r.edge[2 * branch : 2 * branch + 2]))


def tapped(taps, items):
    return taps[0] * items[0] + taps[1] * items[1] + taps[2] * items[2]


def short_branch(r, level, branch):
    return tapped(taps_of(r, level, branch), lagged(r, branch))


def short_ahead(r, level, branch):
    here = wide(r.projected[-16:, branch_columns(r, branch)])[-2:]
    ahead = r.ahead[2 * branch : 2 * branch + 2]
    taps = taps_of(r, level, branch)
    first = tapped(taps, (ahead[0:1], here[1:2], here[0:1]))
    return first, tapped(taps, (ahead[1:2], ahead[0:1], here[1:2]))


def norm_rows(state):
    centred = state - jnp.mean(state, axis=1, keepdims=True)
    scale = lax.rsqrt(jnp.mean(centred * centred, axis=1, keepdims=True) + EPSILON)
    return centred * scale, scale


def norm_rows_back(d_out, normed, scale, gain):
    q = d_out * gain
    return scale * (
        q
        - jnp.mean(q, axis=1, keepdims=True)
        - normed * jnp.mean(q * normed, axis=1, keepdims=True)
    )


def gelu_and_slope(x):
    square = x * x
    tanh = jnp.tanh(x * (0.7978845608028654 + 0.035677408136300125 * square))
    half = 0.5 + 0.5 * tanh
    inner = 0.7978845608028654 + 0.10703222440890037 * square
    return x * half, half + 0.5 * x * (1.0 - tanh * tanh) * inner


def store_rows(target, start, first_block, block_rows, flipped):
    for j in range(flipped.shape[0] // block_rows):
        owner = first_block + j
        z, y, core = owner >> 2, (owner >> 1) & 1, owner & 1
        at = start + z * block_rows
        target[core, y, at : at + block_rows] = flipped[j * block_rows : (j + 1) * block_rows]


def store_line(target, line, vector):
    lanes = target.shape[1]
    pieces = vector.shape[1] // lanes
    for j in range(pieces):
        target[line * pieces + j : line * pieces + j + 1] = vector[:, j * lanes : (j + 1) * lanes]


def store_blocks(target, flipped, ends):
    owned = flipped.shape[0] >> SEQ_BITS
    lanes = target.shape[2]
    lane = lax.broadcasted_iota(jnp.int32, (ends.shape[0], lanes), 1)
    for j in range(1 << SEQ_BITS):
        target[j, :owned] = flipped[j * owned : (j + 1) * owned]
        beside = rotate(ends, -j * owned)[:, :lanes]
        target[j, owned:] = narrow(jnp.where(lane < owned, beside, 0.0))


def mix_forward(r, level, state, weights, squares, gain):
    normed, _ = norm_rows(state)
    u = narrow(normed * gain)
    rows, width = u.shape
    owned = width >> SEQ_BITS
    nothing = jnp.zeros((2, width), jnp.float32)
    r.ends[...] = jnp.zeros_like(r.ends)
    gate = None
    for branch in (1, 2, 0):
        block = narrow(dot(u, weights.wait(squares[branch])))
        r.next_projected[:, branch * width : (branch + 1) * width] = block
        block = wide(block)
        at = slice(2 * branch, 2 * branch + 2)
        r.next_head[at], r.next_tail[at] = block[:2], block[-2:]
        if branch > 0:
            spot = 4 * branch - 4
            r.ends[spot : spot + 2], r.ends[spot + 2 : spot + 4] = block[:2], block[-2:]
            items = (block, *shifted_down(block, nothing))
            part = tapped(taps_of(r, level, branch), items)
            gate = part if gate is None else gate * part
        if branch == 2:
            store_blocks(r.next_gated, flip(narrow(gate)), r.ends[...])
            r.flush(r.next_gated)
    r.next_head[6:] = jnp.zeros_like(r.next_head[6:])
    r.next_tail[6:] = jnp.zeros_like(r.next_tail[6:])
    r.flush(r.next_projected, r.next_head, r.next_tail)
    store_rows(r.next_rows, 0, 0, owned, flip(u))


def enter_kernel(r):
    weights = Weights(r.slots, r.sems)
    squares = weights.fetch_columns(r.in_proj.at[0], r.tokens.shape[1])
    mix_forward(r, 0, wide(r.tokens[...]), weights, squares, r.mix_gain[0:1])


def after_conv(r, level, weights, squares, pieces):
    out_square, ups, downs = squares
    rows, width = r.state.shape
    owned = width >> SEQ_BITS
    conv = flip(r.conv[...].reshape(width, rows))
    r.conv_rows[...] = conv
    r.flush(r.conv_rows)
    mixed = narrow(wide(conv) * short_branch(r, level, 0))
    middle = wide(r.state[...]) + dot(mixed, weights.wait(out_square))
    r.middle[...] = middle
    r.flush(r.middle)
    normed, _ = norm_rows(middle)
    u = narrow(normed * r.mlp_gain[level : level + 1])
    hidden = dot(u, weights.wait(ups[0]))
    total = middle
    for j, down in enumerate(downs):
        following = weights.wait(ups[j + 1]) if j + 1 < len(ups) else None
        down = weights.wait(down)
        coming = None if following is None else dot(u, following)
        active, slope = gelu_and_slope(hidden)
        r.slope[:, j * width : (j + 1) * width] = slope
        active = narrow(active)
        total = total + dot(active, down)
        store_rows(r.all_rows, 0, 4 * j, 4 * owned, flip(active))
        hidden = coming
    store_rows(r.all_rows, 4 * 4 * owned, 0, owned, flip(u))
    store_rows(r.all_rows, 5 * 4 * owned, 0, owned, flip(mixed))
    for core in range(2):
        for y in range(2):
            r.all_rows[core, y, 6 * 4 * owned :] = r.rows[core, y]
    core = r.place[1]
    for keep, send, start, count in pieces:
        r[send][...] = r.all_rows[1 - core, :, start : start + count]
        r[keep][...] = r.all_rows[core, :, start : start + count]
    return total


def before_conv_back(r, level, upstream, weights, squares):
    out_square, ups, downs = squares
    rows, width = upstream.shape
    half, wide_half = width // 2, 2 * width
    d_down = narrow(upstream)
    middle = r.middle[...]
    normed, scale = norm_rows(middle)
    d_u = jnp.zeros_like(middle)
    d_active = dot_rows(d_down, weights.wait(downs[0]))
    for j, up in enumerate(ups):
        following = weights.wait(downs[j + 1]) if j + 1 < len(downs) else None
        up = weights.wait(up)
        coming = None if following is None else dot_rows(d_down, following)
        d_hidden = narrow(d_active * r.slope[:, j * width : (j + 1) * width])
        side, at = divmod(j * width, wide_half)
        r.all_columns[side, :, at : at + width] = d_hidden
        d_u = d_u + dot_rows(d_hidden, up)
        d_active = coming
    r.g_mlp_gain[...] = jnp.broadcast_to(
        jnp.sum(d_u * normed, axis=0, keepdims=True), r.g_mlp_gain.shape
    )
    d_middle = upstream + norm_rows_back(d_u, normed, scale, r.mlp_gain[level : level + 1])
    d_branch = narrow(d_middle)
    d_mixed = wide(narrow(dot_rows(d_branch, weights.wait(out_square))))
    d_conv = narrow(d_mixed * short_branch(r, level, 0))
    d_x0 = d_mixed * wide(r.conv_rows[...])
    r.ends[...] = jnp.zeros_like(r.ends)
    r.ends[:2] = d_x0[:2]
    store_blocks(r.d_conv, flip(d_conv), r.ends[...])
    r.flush(r.d_conv)
    r.d_x0[...] = d_x0
    r.d_middle[...] = d_middle
    for side in range(2):
        at = slice(side * half, (side + 1) * half)
        r.all_columns[side, :, wide_half : wide_half + half] = d_branch[:, at]
        r.all_columns[side, :, wide_half + half : wide_half + width] = d_down[:, at]
    side = r.place[0]
    r.columns_send[...] = r.all_columns[1 - side]
    r.columns_keep[...] = r.all_columns[side]


def mlp_fetch(r, level, weights):
    width = r.out_proj.shape[2]
    out_square = weights.fetch(r.out_proj.at[level])
    ups, downs = [], []
    for j in range(r.up_proj.shape[2] // width):
        at = pl.ds(j * width, width)
        ups.append(weights.fetch(r.up_proj.at[level, :, at]))
        downs.append(weights.fetch(r.down_proj.at[level, at]))
    return out_square, ups, downs


def mlp_fetch_back(r, level, weights):
    width = r.out_proj.shape[2]
    ups, downs = [], []
    for j in range(r.up_proj.shape[2] // width):
        at = pl.ds(j * width, width)
        downs.append(weights.fetch(r.down_proj.at[level, at]))
        ups.append(weights.fetch(r.up_proj.at[level, :, at]))
    return weights.fetch(r.out_proj.at[level]), ups, downs


def middle_kernel(level, pieces):
    def body(r):
        weights = Weights(r.slots, r.sems)
        squares = mlp_fetch(r, level, weights)
        mix_squares = weights.fetch_columns(r.in_proj.at[level + 1], r.state.shape[1])
        state = after_conv(r, level, weights, squares, pieces)
        r.next_state[...] = state
        gain = r.mix_gain[level + 1 : level + 2]
        mix_forward(r, level + 1, state, weights, mix_squares, gain)

    return body


def turn_kernel(level, pieces):
    def body(r):
        weights = Weights(r.slots, r.sems)
        squares = mlp_fetch(r, level, weights)
        r.next_state[...] = after_conv(r, level, weights, squares, pieces)
        before_conv_back(r, level, wide(r.cotangent[...]), weights, squares)

    return body


def after_short_back(r, level, weights, squares):
    rows, width = r.d_x0.shape
    owned = width >> SEQ_BITS
    half, wide_half = width // 2, 3 * width // 2
    d_gated = wide(flip(r.d_gated[:, :owned].reshape(width, rows)))
    ahead = jnp.zeros((16, width), jnp.float32)
    for j in range(1 << SEQ_BITS):
        piece = wide(r.d_gated[j, owned:])
        filled = jnp.concatenate([piece, jnp.zeros((16, width - rows), jnp.float32)], axis=1)
        ahead = ahead + rotate(filled, j * owned)
    d_u = jnp.zeros_like(d_gated)
    shorted = {}
    for branch in (1, 2, 0):
        taps = taps_of(r, level, branch)
        items = lagged(r, branch)
        if branch == 0:
            d_block, d_ahead = r.d_x0[...], ahead[8:10]
        else:
            other = 3 - branch
            d_block = d_gated * short_branch(r, level, other)
            first, second = short_ahead(r, level, other)
            d_ahead = (ahead[0:1] * first, ahead[1:2] * second)
            d_ahead = jnp.concatenate(d_ahead, axis=0)
        d_projected = narrow(tapped(taps, (d_block, *shifted_up(d_block, d_ahead))))
        for piece in range(2):
            side, lane = divmod((branch * 2 + piece) * half, wide_half)
            lane += r.all_columns.shape[2] - wide_half
            r.all_columns[side, :, lane : lane + half] = d_projected[
                :, piece * half : (piece + 1) * half
            ]
        d_u = d_u + dot_rows(d_projected, weights.wait(squares[branch]))
        for lag, item in enumerate(items):
            store_line(r.small, 3 * lag + branch, jnp.sum(d_block * item, axis=0, keepdims=True))
    return d_u


def input_gradient(r, level, d_u):
    normed, scale = norm_rows(wide(r.state[...]))
    store_line(r.small, 9, jnp.sum(d_u * normed, axis=0, keepdims=True))
    store_line(r.small, 10, r.g_mlp_gain_in[0:1])
    lines = 11 * (r.state.shape[1] // r.small.shape[1])
    r.small[lines:] = jnp.zeros_like(r.small[lines:])
    return r.d_middle_in[...] + norm_rows_back(
        d_u, normed, scale, r.mix_gain[level : level + 1]
    )


def between_kernel(level):
    def body(r):
        weights = Weights(r.slots, r.sems)
        mix_squares = weights.fetch_columns(r.in_proj.at[level], r.d_x0_in.shape[1])
        squares = mlp_fetch_back(r, level - 1, weights)
        upper = Renamed(
            r, d_x0="d_x0_in", projected="upper_projected", edge="upper_edge", ahead="upper_ahead"
        )
        d_u = after_short_back(upper, level, weights, mix_squares)
        upstream = input_gradient(upper, level, d_u)
        before_conv_back(r, level - 1, upstream, weights, squares)

    return body


def leave_kernel(r):
    weights = Weights(r.slots, r.sems)
    squares = weights.fetch_columns(r.in_proj.at[0], r.d_x0.shape[1])
    d_u = after_short_back(r, 0, weights, squares)
    side = r.place[0]
    r.in_send[...] = r.all_columns[1 - side]
    r.in_keep[...] = r.all_columns[side]
    r.flush(r.in_send, r.in_keep)
    r.upstream[...] = input_gradient(r, 0, d_u)


def filter_kernel(level):
    def body(r):
        shards, channels, rows = r.window.shape
        width = r.filter_last.shape[2]
        pick = (
            lax.broadcasted_iota(jnp.int32, (channels, width), 1)
            == lax.broadcasted_iota(jnp.int32, (channels, width), 0) + r.place[5]
        ).astype(jnp.float32)
        one, slope_one = sin_cos(across(r.filter_first[:, level], r.features[...], 0, 0))
        r.one[...] = one
        r.slope_one[...] = slope_one
        r.flush(r.one, r.slope_one)
        two, slope_two = sin_cos(across(r.filter_middle[level], one, 0, 0))
        r.two[...] = two
        r.slope_two[...] = slope_two
        r.flush(r.two, r.slope_two)
        last = across(pick, r.filter_last[level], 1, 1)
        r.last[...] = last
        r.raw[...] = across(last, two, 1, 0)

        def own(row):
            return jnp.sum(pick * row, axis=1, keepdims=True)

        rate = own(r.decay_rates[level : level + 1])
        lane = lax.broadcasted_iota(jnp.int32, r.near.shape, 1)
        near = jnp.broadcast_to(own(r.filter_skip[level : level + 1]), r.near.shape)
        for branch in (1, 2):
            for lag, row in enumerate(taps_of(r, level, branch)):
                near = jnp.where(lane == 3 * branch - 2 + lag, own(row), near)
        r.near[...] = near
        size = jnp.sqrt(rate + 1.0 / (shards * rows))
        step = lax.broadcasted_iota(jnp.int32, (channels, rows), 1)
        for j in range(shards):
            window = jnp.exp(-rate * (step + j * rows).astype(jnp.float32)) * size
            r.window[j] = window
            at = slice(j * rows, (j + 1) * rows)
            r.raw[:, at] = r.raw[:, at] * window
        r.flush(r.window)
        for chunk in chunks_of(channels):
            load_bins(
                [r.raw[chunk, j * rows : (j + 1) * rows] for j in range(shards)], r.bins, chunk
            )
        for k in range(shards + 1):
            r.filter_spec[k] = dot(r.bins[k], r.table[k]) * bin_scale(k, shards, rows)

    return body


def transformed(r, conjugate):
    shards, channels, rows = r.fixed.shape
    for chunk in chunks_of(channels):
        load_bins([r.fixed[j, chunk] for j in range(shards)], r.bins, chunk)
    for k in range(shards + 1):
        spec = dot(r.bins[k], r.table[k])
        r.spec[k] = narrow(spec)
        product = bin_product(spec, r.filter_spec[k], conjugate)
        r.back[k] = dot_rows(narrow(product), r.table[k])
    r.flush(r.spec)
    for chunk in chunks_of(channels):
        skip = r.near[chunk, 0:1]
        blocks = fold_bins(r.back, chunk, shards, rows)
        yield chunk, [block + skip * r.fixed[j, chunk] for j, block in enumerate(blocks)]


def conv_kernel(r):
    shards, channels, rows = r.fixed.shape
    ends = jnp.concatenate([wide(r.signal[j, channels:])[:8] for j in range(shards)], axis=0)
    ends = flip(ends)[:channels]
    lane = lax.broadcasted_iota(jnp.int32, ends.shape, 1)

    def first_two(block, taps):
        before_two = jnp.where(lane >= 8, rotate(block, 6), 0.0)
        before_one = jnp.where(lane >= 8, rotate(block, 5), 0.0)
        first = tapped(taps, (block, before_one, before_two))
        return first, tapped(taps, (rotate(block, -1), block, before_one))

    near = r.near[...]
    one = first_two(ends, [near[:, at : at + 1] for at in (1, 2, 3)])
    value = first_two(rotate(ends, -4), [near[:, at : at + 1] for at in (4, 5, 6)])
    first, second = (wide(narrow(a * b)) for a, b in zip(one, value, strict=True))
    both = jnp.where(lane % 8 == 0, first, rotate(second, 1))
    for j in range(shards):
        fixed = jnp.where(lane < 2, rotate(both, -8 * j), wide(r.signal[j, :channels]))
        r.fixed[j] = fixed
        r.gated[j] = narrow(fixed)
    r.flush(r.gated)
    for chunk, blocks in transformed(r, False):
        for j, block in enumerate(blocks):
            r.result[j, chunk] = narrow(block)


def conv_back_kernel(r):
    shards, channels, rows = r.fixed.shape
    for j in range(shards):
        r.fixed[j] = wide(r.signal[j, :channels])
    r.ends[...] = jnp.zeros_like(r.ends)
    for chunk, blocks in transformed(r, True):
        lane = lax.broadcasted_iota(jnp.int32, blocks[0].shape, 1)
        ends = jnp.zeros_like(blocks[0])
        for j, block in enumerate(blocks):
            block = narrow(block)
            r.result[j, chunk] = block
            inside = (lane >= 8 * j) & (lane < 8 * j + 2)
            ends = jnp.where(inside, rotate(wide(block), 8 * j), ends)
        r.ends[chunk] = ends
    ends = flip(r.ends[...])
    for j in range(shards - 1):
        beside = wide(r.signal[j + 1, channels:])[:8]
        ahead = jnp.concatenate([ends[8 * j + 8 : 8 * j + 16], beside], axis=0)
        r.result[j, channels:] = narrow(ahead)
    r.result[shards - 1, channels:] = jnp.zeros((16, rows), LOW)
    r.flush(r.result)
    if 0 in r.held:
        r[1][...] = r[0][...]


def filter_grads_kernel(level):
    def body(r):
        shards, channels, rows = r.gated.shape
        hidden = r.one.shape[0]
        feats = r.features.shape[0]
        for k in range(shards + 1):
            spec = bin_product(wide(r.d_spec[k]), wide(r.spec[k]), True)
            r.back[k] = dot_rows(narrow(spec * bin_scale(k, shards, rows)), r.table[k])
        r.packed[...] = jnp.zeros_like(r.packed)
        for chunk in chunks_of(channels):
            total = None
            for j, block in enumerate(fold_bins(r.back, chunk, shards, rows)):
                r.raw[chunk, j * rows : (j + 1) * rows] = block * r.window[j, chunk]
                term = wide(r.d_conv[j, chunk]) * wide(r.gated[j, chunk])
                total = term if total is None else total + term
            r.packed[hidden + chunk.start : hidden + chunk.stop, hidden : hidden + 1] = jnp.sum(
                total, axis=1, keepdims=True
            )
        d_raw = r.raw[...]
        r.packed[hidden:, :channels] = low_across(r.two[...], d_raw, 1, 1)
        d_two = low_across(r.last[...], d_raw, 0, 0) * r.slope_two[...]
        r.packed[:hidden, hidden:] = low_across(r.one[...], d_two, 1, 1)
        d_one = low_across(r.filter_middle[level], d_two, 1, 0) * r.slope_one[...]
        r.packed[:feats, :hidden] = low_across(r.features[...], d_one, 1, 1)

    return body


def grad_kernel(parts, split):
    def body(r):
        y_own, low, high = r.place[2], r.place[3], r.place[4]
        tile = r.blocks.shape[3]
        for y in range(2):
            start = 0
            for rows_of, columns_of, row, count, column, columns in parts:
                at, lanes = slice(row, row + count), slice(column, column + columns)
                left = jnp.concatenate([r[0, rows_of, i][y, at] for i in range(4)], axis=1)
                right = jnp.concatenate([r[1, columns_of, i][:, lanes] for i in range(4)], axis=0)
                block = narrow(dot(left, right))
                owned = count // 4
                for z in range(4):
                    for piece in range(columns // tile):
                        spot = start + piece * owned
                        r.blocks[y, z, spot : spot + owned] = block[
                            z * owned : (z + 1) * owned, piece * tile : (piece + 1) * tile
                        ]
                start += owned * (columns // tile)
        for one in range(2):
            for two in range(2):
                z = (low ^ (1 - one)) + 2 * (high ^ (1 - two))
                r.p_send[one, two] = r.blocks[1 - y_own, z, :split]
                z, y = 2 * (high ^ (1 - two)), y_own ^ (1 - one)
                r.q_send[one, two] = r.blocks[y, z + 1 - low, split:]
        r.flush(r.p_send, r.q_send)
        for one in range(2):
            for two in range(2):
                z = (low ^ (1 - one)) + 2 * (high ^ (1 - two))
                r.p_keep[one, two] = r.blocks[y_own, z, :split]
                z, y = 2 * (high ^ (1 - two)), y_own ^ (1 - one)
                r.q_keep[one, two] = r.blocks[y, z + low, split:]

    return body


def crossed(block, bit):
    count = lax.axis_size("seq")
    return lax.ppermute(block, "seq", [(i, i ^ bit) for i in range(count)])


def other_sequence(block):
    return lax.ppermute(block, "dp", [(0, 1), (1, 0)])


def share_rows(keep, send):
    core = crossed(send, 1)
    return keep, other_sequence(keep), core, other_sequence(core)


def share_columns(keep, send):
    x = other_sequence(send)
    return keep, x, crossed(keep, 1), crossed(x, 1)


def partial_grads(name, place, rows, columns, parts, split, tile, cuts, after=()):
    tall = sum(count // 4 * (width // tile) for _, _, _, count, _, width in parts)
    near = {(0, key, i): item for key, items in rows.items() for i, item in enumerate(items)}
    near.update({(1, key, i): item for key, items in columns.items() for i, item in enumerate(items)})
    first, second = ((2, 2, split, tile), LOW), ((2, 2, tall - split, tile), LOW)
    return local_call(
        name,
        grad_kernel(parts, split),
        place,
        near,
        dict(p_send=first, q_send=second, p_keep=first, q_keep=second),
        dict(blocks=pltpu.VMEM((2, 4, tall, tile), LOW)),
        cuts={(0, key, i): cut for key, cut in cuts.items() for i in range(4)},
        after=after,
    )


def first_sum_kernel(r):
    for keep, one, following, mine in (
        (r.p_keep, r.p_one, r.p_next, r.p_mine),
        (r.q_keep, r.q_one, r.q_next, r.q_mine),
    ):
        following[...] = narrow(wide(keep[0]) + wide(one[0]))
        r.flush(following)
        mine[...] = wide(keep[1]) + wide(one[1])


def second_sum_kernel(r):
    split = r.p_two.shape[1]
    for mine, two, at in (
        (r.p_mine, r.p_two, slice(0, split)),
        (r.q_mine, r.q_two, slice(split, r.following.shape[0])),
    ):
        r.following[at] = narrow(mine[0] + wide(two[0]))
    r.flush(r.following)
    for mine, two, at in (
        (r.p_mine, r.p_two, slice(0, split)),
        (r.q_mine, r.q_two, slice(split, r.following.shape[0])),
    ):
        r.last[at] = mine[1] + wide(two[1])


class Reduction:
    def __init__(self, place, made):
        self.place, self.made = place, made
        self.p_one, self.q_one = crossed(made.p_send, 2), crossed(made.q_send, 4)
        self.p_shape, self.q_shape = made.p_send.shape[1:], made.q_send.shape[1:]

    def first(self, after=()):
        keep = dict(p_keep=self.made.p_keep, q_keep=self.made.q_keep)
        made = local_call(
            "first_sum",
            first_sum_kernel,
            self.place,
            dict(p_one=self.p_one, q_one=self.q_one, **keep),
            dict(
                p_next=(self.p_shape, LOW),
                q_next=(self.q_shape, LOW),
                p_mine=(self.p_shape, FULL),
                q_mine=(self.q_shape, FULL),
            ),
            after=after,
        )
        self.first_made = made
        self.p_two, self.q_two = crossed(made.p_next, 4), crossed(made.q_next, 2)
        return made.p_next

    def second(self, after=()):
        mine = dict(p_mine=self.first_made.p_mine, q_mine=self.first_made.q_mine)
        shape = (self.p_shape[1] + self.q_shape[1], self.p_shape[2])
        made = local_call(
            "second_sum",
            second_sum_kernel,
            self.place,
            dict(p_two=self.p_two, q_two=self.q_two, **mine),
            dict(following=(shape, LOW), last=(shape, FULL)),
            after=after,
        )
        self.three = crossed(made.following, 8)
        self.result = (made.last, self.three)
        return made.following


def collect_kernel(groups, owned):
    def body(r):
        for at, places in enumerate(groups):
            total = r[at, 0][...] + wide(r[at, 1][...])
            tile = total.shape[1]
            start = 0
            for output, level, count, pieces in places:
                for j in range(pieces):
                    r[output][level, :, j * tile : (j + 1) * tile] = total[start : start + count]
                    start += count
        width = r.g_mix_gain.shape[1]
        lines = width // 128
        hidden = r.g_middle.shape[1]
        for level, (small, last) in enumerate(((r.small_0, r.last_0), (r.small_1, r.last_1))):
            for j in range(lines):
                at = slice(j * 128, (j + 1) * 128)
                r.g_mix_gain[level : level + 1, at] = small[9 * lines + j : 9 * lines + j + 1]
                r.g_mlp_gain[level : level + 1, at] = small[10 * lines + j : 10 * lines + j + 1]
            for lag in range(3):
                for j in range(3 * lines):
                    line = 3 * lag * lines + j
                    r.g_taps[lag, level : level + 1, j * 128 : (j + 1) * 128] = small[
                        line : line + 1
                    ]
            start = 16 * lines
            r.g_first[:, level] = small[start : start + r.g_first.shape[0], :hidden]
            r.g_middle[level] = small[start : start + hidden, hidden:]
            r.g_last[level] = last[:, :owned]
            r.g_skip[level : level + 1] = flip(last[...])[hidden : hidden + 1, :owned]

    return body


def fast_body(
    tokens,
    cotangent,
    mix_gain,
    in_proj,
    short_taps,
    filter_first,
    filter_middle,
    filter_last,
    filter_skip,
    decay_rates,
    out_proj,
    mlp_gain,
    up_proj,
    down_proj,
):
    tokens, cotangent = tokens[0], cotangent[0]
    rows, width = tokens.shape
    hidden = up_proj.shape[2]
    shards = lax.axis_size("seq")
    length = rows * shards
    owned = channels = width // shards
    inner, feats = filter_first.shape[2], filter_first.shape[1]
    seq = lax.axis_index("seq")
    place = jnp.stack(
        [lax.axis_index("dp"), seq & 1, (seq >> 1) & 1, (seq >> 2) & 1, (seq >> 3) & 1, seq * channels]
    ).astype(jnp.int32)
    features, table = position_table(length), turn_table(shards, rows)
    short_taps = short_taps.transpose(1, 0, 2)
    filter_first = filter_first.transpose(1, 0, 2)
    ups, tile, half = hidden // width, width // 2, hidden // 2
    bins, span = shards + 1, 2 * rows
    down_rows, rest_rows = 16 * owned, 12 * owned
    tall, mlp_rows = down_rows + rest_rows, 24 * owned

    def slots(count):
        return dict(
            slots=pltpu.VMEM((count, width, width), LOW), sems=pltpu.SemaphoreType.DMA((count,))
        )

    def exchange(block):
        return lax.all_to_all(block, "seq", split_axis=0, concat_axis=0, tiled=True)

    line, edges = ((rows, width), FULL), ((8, width), FULL)
    by_shard = ((shards, channels, rows), LOW)
    with_ends = ((shards, channels + 16, rows), LOW)
    spectrum = ((bins, channels, span), LOW)
    mix_outputs = dict(
        next_gated=with_ends,
        next_projected=((rows, 3 * width), LOW),
        next_tail=edges,
        next_head=edges,
        next_rows=((2, 2, 4 * owned, rows), LOW),
    )
    mlp_outputs = dict(
        next_state=line,
        middle=line,
        slope=((rows, hidden), FULL),
        conv_rows=((rows, width), LOW),
    )
    rows_scratch = dict(all_rows=pltpu.VMEM((2, 2, tall, rows), LOW))

    def columns_outputs(count):
        return dict(columns_keep=((rows, count), LOW), columns_send=((rows, count), LOW))

    def columns_scratch(count):
        return dict(all_columns=pltpu.VMEM((2, rows, count), LOW), ends=ends_scratch)

    back_outputs = dict(
        d_conv=with_ends, d_x0=line, d_middle=line, g_mlp_gain=edges
    )
    small_output = ((16 * width // 128, 128), FULL)
    in_half = ((rows, 3 * tile), LOW)
    in_columns = ((2, *in_half[0]), LOW)
    bins_scratch = pltpu.VMEM((bins, channels, span), LOW)
    back_scratch = pltpu.VMEM((bins, channels, span), FULL)
    fixed_scratch = pltpu.VMEM((shards, channels, rows), FULL)
    ends_scratch = pltpu.VMEM((16, width), FULL)
    raw_scratch = pltpu.VMEM((channels, length), FULL)
    mlp_weights = dict(out_proj=out_proj, up_proj=up_proj, down_proj=down_proj)
    all_weights = dict(in_proj=in_proj, **mlp_weights)

    def filter_of(level):
        wave = ((inner, length), FULL)
        return local_call(
            "filter",
            filter_kernel(level),
            place,
            dict(
                features=features,
                filter_first=filter_first,
                filter_middle=filter_middle,
                filter_last=filter_last,
                decay_rates=decay_rates,
                filter_skip=filter_skip,
                short_taps=short_taps,
                table=table,
            ),
            dict(
                filter_spec=((bins, channels, span), FULL),
                near=((channels, rows), FULL),
                last=((channels, inner), FULL),
                one=wave,
                slope_one=wave,
                two=wave,
                slope_two=wave,
                window=((shards, channels, rows), FULL),
            ),
            dict(raw=raw_scratch, bins=bins_scratch),
        )

    def conv_inputs(signal, filters):
        return dict(
            signal=signal, near=filters.near, table=table, filter_spec=filters.filter_spec
        )

    conv_scratch = dict(bins=bins_scratch, back=back_scratch, fixed=fixed_scratch)

    def conv_of(signal, filters, after=()):
        return local_call(
            "conv",
            conv_kernel,
            place,
            conv_inputs(signal, filters),
            dict(spec=spectrum, gated=by_shard, result=by_shard),
            conv_scratch,
            after=after,
        )

    def conv_back_of(signal, filters, after=(), passing=None):
        near, made = conv_inputs(signal, filters), dict(spec=spectrum, result=with_ends)
        if passing is not None:
            near[0], made[1] = passing, (passing.shape, passing.dtype)
        return local_call(
            "conv_back",
            conv_back_kernel,
            place,
            near,
            made,
            dict(ends=pltpu.VMEM((rows, rows), FULL), **conv_scratch),
            after=after,
        )

    def filter_grads_of(level, filters, back, conv, d_conv, after=()):
        return local_call(
            "filter_grads",
            filter_grads_kernel(level),
            place,
            dict(
                d_spec=back.spec,
                spec=conv.spec,
                table=table,
                d_conv=d_conv,
                gated=conv.gated,
                window=filters.window,
                two=filters.two,
                last=filters.last,
                slope_two=filters.slope_two,
                one=filters.one,
                filter_middle=filter_middle,
                slope_one=filters.slope_one,
                features=features,
            ),
            dict(packed=((2 * inner, 128), FULL)),
            dict(back=back_scratch, raw=raw_scratch),
            after=after,
        )["packed"]

    def near_of(made):
        return dict(
            projected=made.next_projected,
            edge=from_behind(made.next_tail, "seq", 1),
            ahead=from_behind(made.next_head, "seq", -1),
        )

    def row_shape(count):
        return ((2, count, rows), LOW)

    entered = local_call(
        "enter",
        enter_kernel,
        place,
        dict(tokens=tokens, mix_gain=mix_gain, short_taps=short_taps),
        mix_outputs,
        dict(ends=ends_scratch, **slots(3)),
        far=dict(in_proj=in_proj),
    )
    filters_0 = filter_of(0)
    near_0 = near_of(entered)
    conv_0 = conv_of(exchange(entered.next_gated), filters_0)
    filters_1 = filter_of(1)
    lower = local_call(
        "middle",
        middle_kernel(0, ((0, 1, 0, mlp_rows), (2, 3, mlp_rows, tall - mlp_rows))),
        place,
        dict(
            conv=exchange(conv_0.result),
            projected=near_0["projected"],
            edge=near_0["edge"],
            short_taps=short_taps,
            state=tokens,
            mlp_gain=mlp_gain,
            mix_gain=mix_gain,
            rows=entered.next_rows,
        ),
        {
            **mlp_outputs,
            **mix_outputs,
            0: row_shape(mlp_rows),
            1: row_shape(mlp_rows),
            2: row_shape(tall - mlp_rows),
            3: row_shape(tall - mlp_rows),
        },
        dict(ends=ends_scratch, **rows_scratch, **slots(1 + 2 * ups + 3)),
        far=all_weights,
        after=[filters_1.near],
    )
    near_1 = near_of(lower)
    rows_0 = share_rows(lower[0], lower[1])
    conv_1 = conv_of(exchange(lower.next_gated), filters_1, after=[rows_0[2]])
    in_rows_0 = share_rows(lower[2], lower[3])
    upper = turn = local_call(
        "turn",
        turn_kernel(1, ((0, 1, 0, tall),)),
        place,
        dict(
            conv=exchange(conv_1.result),
            projected=near_1["projected"],
            edge=near_1["edge"],
            short_taps=short_taps,
            state=lower.next_state,
            mlp_gain=mlp_gain,
            rows=lower.next_rows,
            cotangent=cotangent,
        ),
        {
            **mlp_outputs,
            **back_outputs,
            **columns_outputs(half + width),
            0: row_shape(tall),
            1: row_shape(tall),
        },
        {**columns_scratch(half + width), **rows_scratch, **slots(1 + 2 * ups)},
        far=mlp_weights,
        after=[rows_0[1], rows_0[3]],
    )
    rows_1 = share_rows(upper[0], upper[1])

    columns_1 = share_columns(turn.columns_keep, turn.columns_send)
    d_conv_1 = exchange(turn.d_conv)
    back_1 = conv_back_of(d_conv_1, filters_1, after=[rows_1[1], rows_1[2], columns_1[2]])
    packed_1 = filter_grads_of(1, filters_1, back_1, conv_1, d_conv_1)
    mlp_parts = (
        (0, 0, 0, 16 * owned, half + tile, tile),
        (0, 0, 16 * owned, 4 * owned, 0, half),
        (0, 0, 20 * owned, 4 * owned, half, tile),
    )
    between = local_call(
        "between",
        between_kernel(1),
        place,
        dict(
            d_gated=exchange(back_1.result),
            short_taps=short_taps,
            upper_projected=near_1["projected"],
            upper_edge=near_1["edge"],
            upper_ahead=near_1["ahead"],
            d_x0_in=turn.d_x0,
            state=lower.next_state,
            d_middle_in=turn.d_middle,
            g_mlp_gain_in=turn.g_mlp_gain,
            mix_gain=mix_gain,
            projected=near_0["projected"],
            edge=near_0["edge"],
            middle=lower.middle,
            slope=lower.slope,
            conv_rows=lower.conv_rows,
            mlp_gain=mlp_gain,
        ),
        dict(
            small=small_output, **back_outputs, **columns_outputs(half + width + 3 * tile)
        ),
        {**columns_scratch(half + width + 3 * tile), **slots(1 + 2 * ups + 3)},
        far=all_weights,
        after=[packed_1, rows_1[3]],
    )

    keep, send = between.columns_keep, between.columns_send
    columns_0 = (keep, other_sequence(send), crossed(keep, 1))
    d_conv_0 = exchange(between.d_conv)
    mlp_sum = Reduction(
        place,
        partial_grads(
            "grad_mlp",
            place,
            {0: rows_1},
            {0: columns_1},
            mlp_parts,
            224,
            tile,
            {0: (0, 24 * owned)},
            after=[between.d_conv],
        ),
    )
    back_0 = conv_back_of(
        d_conv_0, filters_0, after=[mlp_sum.made.p_send], passing=columns_0[1]
    )
    columns_0 = (*columns_0, crossed(back_0[1], 1))
    packed_0 = filter_grads_of(0, filters_0, back_0, conv_0, d_conv_0)
    mark = mlp_sum.first(after=[packed_0])
    d_gated_0 = exchange(back_0.result)
    mid_sum = Reduction(
        place,
        partial_grads(
            "grad_mid",
            place,
            {0: rows_0, 1: rows_1},
            {0: columns_0},
            (*mlp_parts, (1, 0, 0, 4 * owned, half + width, 3 * tile)),
            288,
            tile,
            {1: (24 * owned, 4 * owned)},
            after=[d_gated_0, mark],
        ),
    )
    leave = local_call(
        "leave",
        leave_kernel,
        place,
        dict(
            d_gated=d_gated_0,
            short_taps=short_taps,
            **near_0,
            d_x0=between.d_x0,
            state=tokens,
            d_middle_in=between.d_middle,
            g_mlp_gain_in=between.g_mlp_gain,
            mix_gain=mix_gain,
        ),
        dict(in_send=in_half, in_keep=in_half, small=small_output, upstream=line),
        dict(all_columns=pltpu.VMEM(*in_columns), **slots(3)),
        far=dict(in_proj=in_proj),
        after=[mid_sum.made.p_send, mlp_sum.p_two, mlp_sum.q_two],
    )
    columns_in_0 = share_columns(leave.in_keep, leave.in_send)
    in_sum = Reduction(
        place,
        partial_grads(
            "grad_in",
            place,
            {0: in_rows_0},
            {0: columns_in_0},
            ((0, 0, 0, 4 * owned, 0, 3 * tile),),
            80,
            tile,
            {},
            after=[mid_sum.p_one, mid_sum.q_one],
        ),
    )
    small = jnp.concatenate([leave.small, packed_0, between.small, packed_1], axis=0)
    small = small + other_sequence(small)
    each = small.shape[0] // 2
    kept = each - inner
    sums = dict(last_0=small[kept:each], last_1=small[each + kept :])
    small = jnp.concatenate([small[:kept], small[each : each + kept]], axis=0)
    small = small + crossed(small, 1)
    mark = mid_sum.first(after=[in_sum.made.p_send])
    mark = mlp_sum.second(after=[mark])
    small = small + crossed(small, 2)
    mark = in_sum.first(after=[mark])
    mark = mid_sum.second(after=[mark, small])
    small = small + crossed(small, 4)
    in_sum.second(after=[mark, small])
    small = small + crossed(small, 8)
    sums.update(small_0=small[:kept], small_1=small[kept:])
    routes = [item.result for item in (mlp_sum, mid_sum, in_sum)]

    made = dict(
        g_mix_gain=((2, width), FULL),
        g_in=((2, owned, 3 * tile), FULL),
        g_taps=((3, 2, 3 * width), FULL),
        g_first=((feats, 2, inner), FULL),
        g_middle=((2, inner, inner), FULL),
        g_last=((2, inner, owned), FULL),
        g_skip=((2, owned), FULL),
        g_out=((2, owned, tile), FULL),
        g_mlp_gain=((2, width), FULL),
        g_up=((2, owned, half), FULL),
        g_down=((2, 4 * owned, tile), FULL),
    )
    in_key, out_key, up_key, down_key = (list(made)[at] for at in (1, 7, 9, 10))
    groups = (
        ((down_key, 1, 4 * owned, 1), (up_key, 1, owned, 4), (out_key, 1, owned, 1)),
        (
            (down_key, 0, 4 * owned, 1),
            (up_key, 0, owned, 4),
            (out_key, 0, owned, 1),
            (in_key, 1, owned, 3),
        ),
        ((in_key, 0, owned, 3),),
    )
    sums.update({(at, i): item for at, route in enumerate(routes) for i, item in enumerate(route)})
    turned = [list(made)[at] for at in (2, 3)]
    made = local_call("collect", collect_kernel(groups, owned), place, sums, made).kept
    for key in turned:
        made[key] = made[key].transpose(1, 0, 2)
    return (upper.next_state[None], leave.upstream[None], *made.values())


def is_fast(mesh):
    return dict(mesh.shape) == dict(dp=2, seq=1 << SEQ_BITS)


def solution(mesh):
    in_specs = (
        P("dp", "seq", None),
        P("dp", "seq", None),
        P(),
        P(),
        P(),
        P(),
        P(),
        P(),
        P(),
        P(),
        P(),
        P(),
        P(),
        P(),
    )
    out_specs = (
        P("dp", "seq", None),
        P("dp", "seq", None),
        P(),
        P(None, "seq", "dp"),
        P(),
        P(),
        P(),
        P(None, None, "seq"),
        P(None, "seq"),
        P(None, "seq", "dp"),
        P(),
        P(None, "seq", "dp"),
        P(None, "seq", "dp"),
    )
    chosen = fast_body if is_fast(mesh) else body
    return jax.shard_map(chosen, mesh=mesh, in_specs=in_specs, out_specs=out_specs, check_vma=False)
```

```python
import functools
import math

import jax
import jax.numpy as jnp
import ml_dtypes
import numpy as np
from jax import lax
from jax.experimental import pallas as pl
from jax.experimental.pallas import tpu as pltpu
from jax.sharding import PartitionSpec as P

FEATS = 33
FFT_COLS = 512


HIGHEST = lax.Precision.HIGHEST
EPSILON = 1e-05


def from_behind(block, axis, distance):
    devices = range(lax.axis_size(axis))
    route = [(i - distance, i) for i in devices if i - distance in devices]
    return lax.ppermute(block, axis, route)


def high_einsum(form, left, right):
    return jnp.einsum(form, left, right, precision=HIGHEST)


def low_einsum(form, left, right):
    return jnp.einsum(form, left, right, preferred_element_type=jnp.float32)


def to_low(value):
    return lax.optimization_barrier(value.astype(jnp.bfloat16))


def angle_table(rows, columns, modulus):
    product = lax.broadcasted_iota(jnp.int32, (rows, columns), 0) * lax.broadcasted_iota(
        jnp.int32, (rows, columns), 1
    )
    angle = (product % modulus).astype(jnp.float32) * (2.0 * math.pi / modulus)
    return (jnp.cos(angle), jnp.sin(angle))


def transform_tables(length, columns):
    total = 2 * length
    rows = total // columns
    cos_rows, sin_rows = angle_table(rows, rows, rows)
    cos_columns, sin_columns = angle_table(columns, columns, columns)
    cos_turn, sin_turn = angle_table(rows, columns, total)
    return (cos_rows, sin_rows, cos_columns, sin_columns, cos_turn, sin_turn)


def forward_transform(signal, tables):
    cos_rows, sin_rows, cos_columns, sin_columns, cos_turn, sin_turn = tables
    channels, length = signal.shape
    rows, columns = cos_turn.shape
    padded = jnp.pad(signal, ((0, 0), (0, length))).reshape(channels, rows, columns)
    first_real = high_einsum("kq,cqp->ckp", cos_rows, padded)
    first_imag = -high_einsum("kq,cqp->ckp", sin_rows, padded)
    turned_real = first_real * cos_turn + first_imag * sin_turn
    turned_imag = first_imag * cos_turn - first_real * sin_turn
    spec_real = high_einsum("ckp,pj->ckj", turned_real, cos_columns) + high_einsum(
        "ckp,pj->ckj", turned_imag, sin_columns
    )
    spec_imag = high_einsum("ckp,pj->ckj", turned_imag, cos_columns) - high_einsum(
        "ckp,pj->ckj", turned_real, sin_columns
    )
    return (spec_real, spec_imag)


def inverse_transform(spec_real, spec_imag, tables):
    cos_rows, sin_rows, cos_columns, sin_columns, cos_turn, sin_turn = tables
    rows, columns = cos_turn.shape
    back_real = high_einsum("ckp,pj->ckj", spec_real, cos_columns) - high_einsum(
        "ckp,pj->ckj", spec_imag, sin_columns
    )
    back_imag = high_einsum("ckp,pj->ckj", spec_imag, cos_columns) + high_einsum(
        "ckp,pj->ckj", spec_real, sin_columns
    )
    turned_real = back_real * cos_turn - back_imag * sin_turn
    turned_imag = back_imag * cos_turn + back_real * sin_turn
    signal = high_einsum("qk,ckp->cqp", cos_rows, turned_real) - high_einsum(
        "qk,ckp->cqp", sin_rows, turned_imag
    )
    total = rows * columns
    return signal.reshape(signal.shape[0], total)[:, : total // 2] / total


def position_features(length):
    count = (FEATS - 1) // 2
    steps = lax.broadcasted_iota(jnp.int32, (count, length), 1)
    frequency = lax.broadcasted_iota(jnp.int32, (count, length), 0) + 1
    angle = (steps * frequency % length).astype(jnp.float32) * (2.0 * math.pi / length)
    ramp = lax.broadcasted_iota(jnp.int32, (1, length), 1).astype(jnp.float32) / length
    return jnp.concatenate([ramp, jnp.cos(angle), jnp.sin(angle)], axis=0)


def filter_forward(features, first, middle, last_columns, rate_columns, length):
    pre_one = high_einsum("fk,ft->kt", first, features)
    act_one = jnp.sin(pre_one)
    pre_two = high_einsum("kj,kt->jt", middle, act_one)
    act_two = jnp.sin(pre_two)
    raw = high_einsum("kc,kt->ct", last_columns, act_two)
    steps = lax.broadcasted_iota(jnp.int32, (1, length), 1).astype(jnp.float32)
    window = jnp.exp(-rate_columns[:, None] * steps) * jnp.sqrt(
        rate_columns[:, None] + 1.0 / length
    )
    return (raw * window, (pre_one, act_one, pre_two, act_two, window))


def filter_backward(d_response, features, middle, last_columns, kept):
    pre_one, act_one, pre_two, act_two, window = kept
    d_raw = d_response * window
    g_last = high_einsum("kt,ct->kc", act_two, d_raw)
    d_two = high_einsum("kc,ct->kt", last_columns, d_raw) * jnp.cos(pre_two)
    g_middle = high_einsum("kt,jt->kj", act_one, d_two)
    d_one = high_einsum("kj,jt->kt", middle, d_two) * jnp.cos(pre_one)
    g_first = high_einsum("ft,kt->fk", features, d_one)
    return (g_first, g_middle, g_last)


def normalize(state):
    centred = state - jnp.mean(state, axis=1, keepdims=True)
    scale = lax.rsqrt(jnp.mean(centred * centred, axis=1, keepdims=True) + EPSILON)
    return (centred * scale, scale)


def normalize_back(d_out, normed, scale, gain):
    d_normed = d_out * gain
    g_gain = jnp.sum(d_out * normed, axis=0)
    d_state = scale * (
        d_normed
        - jnp.mean(d_normed, axis=1, keepdims=True)
        - normed * jnp.mean(d_normed * normed, axis=1, keepdims=True)
    )
    return (d_state, g_gain)


def short_forward(extended, taps):
    length = extended.shape[-1] - 2
    return (
        taps[0] * extended[..., 2:]
        + taps[1] * extended[..., 1 : length + 1]
        + taps[2] * extended[..., :length]
    )


def short_backward(d_extended, taps):
    length = d_extended.shape[-1] - 2
    return (
        taps[0] * d_extended[..., :length]
        + taps[1] * d_extended[..., 1 : length + 1]
        + taps[2] * d_extended[..., 2:]
    )


def tap_grads(d_shorted, extended):
    length = d_shorted.shape[-1]
    return jnp.stack(
        [
            jnp.sum(d_shorted * extended[..., 2 - lag : 2 - lag + length], axis=-1)
            for lag in range(3)
        ]
    )


def long_forward(gated, filter_real, filter_imag, skip_columns, tables):
    signal = gated.astype(jnp.float32)
    sig_real, sig_imag = forward_transform(signal, tables)
    result = inverse_transform(
        sig_real * filter_real - sig_imag * filter_imag,
        sig_real * filter_imag + sig_imag * filter_real,
        tables,
    )
    return (result + skip_columns[:, None] * signal, (sig_real, sig_imag))


def long_backward(d_conv, gated, filter_real, filter_imag, skip_columns, signal_spec, tables):
    d_signal = d_conv.astype(jnp.float32)
    d_real, d_imag = forward_transform(d_signal, tables)
    sig_real, sig_imag = signal_spec
    d_gated = (
        inverse_transform(
            d_real * filter_real + d_imag * filter_imag,
            d_imag * filter_real - d_real * filter_imag,
            tables,
        )
        + skip_columns[:, None] * d_signal
    )
    d_response = inverse_transform(
        d_real * sig_real + d_imag * sig_imag, d_imag * sig_real - d_real * sig_imag, tables
    )
    g_skip = jnp.sum(d_signal * gated.astype(jnp.float32), axis=1)
    return (d_gated, d_response, g_skip)


def unit(k,n):
    k%=n
    if (4*k)%n==0:
        q=(4*k)//n
        return [(1.0,0.0),(0.0,-1.0),(-1.0,0.0),(0.0,1.0)][q]
    a=-2.0*math.pi*k/n
    return (math.cos(a),math.sin(a))
def times(z,w):
    re,im=z; c,s=w
    if s==0.0: return (re,im) if c==1.0 else (-re,-im)
    if c==0.0: return (-im,re) if s==1.0 else (im,-re)
    return (re*c-im*s, re*s+im*c)
def plus(a,b): return (a[0]+b[0],a[1]+b[1])
def minus(a,b): return (a[0]-b[0],a[1]-b[1])
def complex_dft(zs,sign):
    n=len(zs)
    if n==1: return zs
    ev=complex_dft(zs[0::2],sign); od=complex_dft(zs[1::2],sign)
    lo,hi=[],[]
    for k in range(n//2):
        v=times(od[k],unit(sign*k,n))
        lo.append(plus(ev[k],v)); hi.append(minus(ev[k],v))
    return lo+hi
def odd_bins(xs):
    n=len(xs); h=n//2; N=2*n
    zs=[times((xs[j],-xs[j+h]),unit(j,N)) for j in range(h)]
    bins={}
    for q,z in enumerate(complex_dft(zs,1)):
        k=4*q+1
        if k<=n: bins[k]=z
        else: bins[N-k]=(z[0],-z[1])
    return bins
def real_bins(xs):
    n=len(xs)
    if n==1: return {0:(xs[0],None)}
    if n==2: return {0:(xs[0]+xs[1],None),1:(xs[0]-xs[1],None)}
    h=n//2
    bins={2*k:z for k,z in real_bins([xs[j]+xs[j+h] for j in range(h)]).items()}
    bins.update(odd_bins([xs[j]-xs[j+h] for j in range(h)]))
    return bins
def padded_bins(xs):
    bins={2*k:z for k,z in real_bins(xs).items()}
    bins.update(odd_bins(xs))
    return bins
def odd_back(bins,n):
    h=n//2; N=2*n
    zs=[]
    for q in range(h):
        k=4*q+1
        if k<=n: zs.append(bins[k])
        else:
            re,im=bins[N-k]; zs.append((re,-im))
    vs=[times(z,unit(-j,N)) for j,z in enumerate(complex_dft(zs,-1))]
    return [v[0] for v in vs]+[-v[1] for v in vs]
def real_back(bins,n):
    if n==1: return [bins[0][0]]
    if n==2: return [bins[0][0]+bins[1][0],bins[0][0]-bins[1][0]]
    h=n//2
    ev=real_back({k//2:z for k,z in bins.items() if k%2==0},h)
    od=odd_back(bins,h)
    return [ev[j]+od[j] for j in range(h)]+[ev[j]-od[j] for j in range(h)]
def padded_back(bins,n):
    ev=real_back({k//2:z for k,z in bins.items() if k%2==0},n)
    od=odd_back(bins,n)
    return [a+b for a,b in zip(ev,od)]


def turn_table(shards, rows):
    total = 2 * shards * rows
    early = np.arange(rows)[None, :, None]
    late = np.arange(rows)[None, None, :]
    bins = np.arange(shards + 1)[:, None, None]
    angle = (early * (bins + 2 * shards * late) % total) * (2.0 * np.pi / total)
    cos, sin = np.cos(angle), np.sin(angle)
    top = np.concatenate([cos, -sin], axis=2)
    bottom = np.concatenate([sin, cos], axis=2)
    return jnp.asarray(np.concatenate([top, bottom], axis=1).astype(ml_dtypes.bfloat16))


def position_table(length):
    count = (FEATS - 1) // 2
    steps = np.arange(length)[None, :]
    angle = (steps * np.arange(1, count + 1)[:, None] % length) * (2.0 * np.pi / length)
    table = np.concatenate([steps / length, np.cos(angle), np.sin(angle)], axis=0)
    return jnp.asarray(table.astype(np.float32))


def chunks_of(channels):
    step = 16 if channels % 16 == 0 else channels
    return [slice(at, at + step) for at in range(0, channels, step)]


def load_bins(blocks, bins_ref, chunk):
    lanes = blocks[0].shape[-1]
    for k, (re, im) in padded_bins(blocks).items():
        im = jnp.zeros_like(re) if im is None else im
        bins_ref[k, chunk, :lanes] = re.astype(jnp.bfloat16)
        bins_ref[k, chunk, lanes:] = im.astype(jnp.bfloat16)


def fold_bins(back_ref, chunk, count, lanes):
    bins = {
        k: (back_ref[k, chunk, :lanes], back_ref[k, chunk, lanes:]) for k in range(count + 1)
    }
    return padded_back(bins, count)


def bin_scale(k, shards, rows):
    total = 2 * shards * rows
    return (1.0 if k in (0, shards) else 2.0) / total


def bin_product(left, right, conjugate):
    lanes = left.shape[1] // 2
    a, b = left[:, :lanes], left[:, lanes:]
    c, d = right[:, :lanes], right[:, lanes:]
    if conjugate:
        return jnp.concatenate([a * c + b * d, b * c - a * d], axis=1)
    return jnp.concatenate([a * c - b * d, a * d + b * c], axis=1)


def turn(left, table):
    return jnp.dot(left, table, preferred_element_type=jnp.float32)


def turn_back(left, table):
    return lax.dot_general(
        left.astype(jnp.bfloat16),
        table,
        (((1,), (1,)), ((), ())),
        preferred_element_type=jnp.float32,
    )


def sin_cos(angle):
    steps = jnp.floor(angle * (2.0 / math.pi) + 0.5)
    rest = angle - steps * 1.5703125
    rest = rest - steps * 4.837512969970703e-4
    rest = rest - steps * 7.549789954891882e-8
    square = rest * rest
    sin = rest + rest * square * (
        -1.6666654611e-1 + square * (8.3321608736e-3 + square * -1.9515295891e-4)
    )
    cos = (
        1.0
        - 0.5 * square
        + square
        * square
        * (4.166664568298827e-2 + square * (-1.388731625493765e-3 + square * 2.443315711809948e-5))
    )
    quarter = steps.astype(jnp.int32)
    odd = (quarter & 1) == 1
    sin_out = jnp.where(odd, cos, sin)
    cos_out = jnp.where(odd, sin, cos)
    sin_out = jnp.where((quarter & 2) == 2, -sin_out, sin_out)
    cos_out = jnp.where(((quarter + 1) & 2) == 2, -cos_out, cos_out)
    return sin_out, cos_out


def across(left, right, left_side, right_side):
    return lax.dot_general(
        left,
        right,
        (((left_side,), (right_side,)), ((), ())),
        precision=HIGHEST,
        preferred_element_type=jnp.float32,
    )


def filter_network_kernel(
    feature_ref,
    first_ref,
    middle_ref,
    last_ref,
    rate_ref,
    table_ref,
    spec_ref,
    one_ref,
    slope_one_ref,
    two_ref,
    slope_two_ref,
    window_ref,
    raw_ref,
    bins_ref,
):
    shards, channels, rows = window_ref.shape
    one, slope_one = sin_cos(across(first_ref[...], feature_ref[...], 0, 0))
    one_ref[...] = one
    slope_one_ref[...] = slope_one
    two, slope_two = sin_cos(across(middle_ref[...], one, 0, 0))
    two_ref[...] = two
    slope_two_ref[...] = slope_two
    raw_ref[...] = across(last_ref[...], two, 0, 0)
    rate = rate_ref[...]
    size = jnp.sqrt(rate + 1.0 / (shards * rows))
    step = lax.broadcasted_iota(jnp.int32, (channels, rows), 1)
    for j in range(shards):
        window = jnp.exp(-rate * (step + j * rows).astype(jnp.float32)) * size
        window_ref[j] = window
        at = slice(j * rows, (j + 1) * rows)
        raw_ref[:, at] = raw_ref[:, at] * window
    for chunk in chunks_of(channels):
        load_bins(
            [raw_ref[chunk, j * rows : (j + 1) * rows] for j in range(shards)], bins_ref, chunk
        )
    for k in range(shards + 1):
        spec_ref[k] = turn(bins_ref[k], table_ref[k]) * bin_scale(k, shards, rows)


def filter_network(features, first, middle, last, rates, table):
    hidden, channels = last.shape
    length = features.shape[1]
    bins, span, _ = table.shape
    rows = span // 2
    shards = length // rows
    wide = jax.ShapeDtypeStruct((hidden, length), jnp.float32)
    return pl.pallas_call(
        filter_network_kernel,
        out_shape=[
            jax.ShapeDtypeStruct((bins, channels, span), jnp.float32),
            wide,
            wide,
            wide,
            wide,
            jax.ShapeDtypeStruct((shards, channels, rows), jnp.float32),
        ],
        scratch_shapes=[
            pltpu.VMEM((channels, length), jnp.float32),
            pltpu.VMEM((bins, channels, span), jnp.bfloat16),
        ],
        compiler_params=pltpu.CompilerParams(vmem_limit_bytes=40 << 20),
        name="filter_network",
    )(features, first, middle, last, rates, table)


def conv_forward_kernel(
    gated_ref, filter_ref, skip_ref, table_ref, conv_ref, spec_ref, bins_ref, back_ref
):
    shards, channels, rows = gated_ref.shape
    for chunk in chunks_of(channels):
        load_bins(
            [gated_ref[j, chunk].astype(jnp.float32) for j in range(shards)], bins_ref, chunk
        )
    for k in range(shards + 1):
        spec = turn(bins_ref[k], table_ref[k])
        spec_ref[k] = spec.astype(jnp.bfloat16)
        back_ref[k] = turn_back(bin_product(spec, filter_ref[k], False), table_ref[k])
    for chunk in chunks_of(channels):
        skip = skip_ref[chunk]
        for j, block in enumerate(fold_bins(back_ref, chunk, shards, rows)):
            conv = block + skip * gated_ref[j, chunk].astype(jnp.float32)
            conv_ref[j, chunk] = conv.astype(jnp.bfloat16)


def conv_backward_kernel(
    gated_ref, filter_ref, skip_ref, table_ref, conv_ref, spec_ref, bins_ref, back_ref
):
    shards, channels, rows = gated_ref.shape
    for chunk in chunks_of(channels):
        load_bins(
            [gated_ref[j, chunk].astype(jnp.float32) for j in range(shards)], bins_ref, chunk
        )
    for k in range(shards + 1):
        spec = turn(bins_ref[k], table_ref[k])
        spec_ref[k] = spec.astype(jnp.bfloat16)
        back_ref[k] = turn_back(bin_product(spec, filter_ref[k], True), table_ref[k])
    for chunk in chunks_of(channels):
        skip = skip_ref[chunk]
        for j, block in enumerate(fold_bins(back_ref, chunk, shards, rows)):
            conv = block + skip * gated_ref[j, chunk].astype(jnp.float32)
            conv_ref[j, chunk] = conv.astype(jnp.bfloat16)


def conv_call(kernel, name, gated, filter_spec, skip, table):
    bins, channels, span = filter_spec.shape
    return pl.pallas_call(
        kernel,
        out_shape=[
            jax.ShapeDtypeStruct(gated.shape, jnp.bfloat16),
            jax.ShapeDtypeStruct((bins, channels, span), jnp.bfloat16),
        ],
        scratch_shapes=[
            pltpu.VMEM((bins, channels, span), jnp.bfloat16),
            pltpu.VMEM((bins, channels, span), jnp.float32),
        ],
        compiler_params=pltpu.CompilerParams(vmem_limit_bytes=40 << 20),
        name=name,
    )(gated, filter_spec, skip, table)


def conv_forward(gated, filter_spec, skip, table):
    return conv_call(conv_forward_kernel, "conv_forward", gated, filter_spec, skip, table)


def conv_backward(d_conv, filter_spec, skip, table):
    return conv_call(conv_backward_kernel, "conv_backward", d_conv, filter_spec, skip, table)


def filter_back_kernel(
    d_spec_ref,
    spec_ref,
    d_conv_ref,
    gated_ref,
    feature_ref,
    middle_ref,
    last_ref,
    one_ref,
    slope_one_ref,
    two_ref,
    slope_two_ref,
    window_ref,
    table_ref,
    g_first_ref,
    g_middle_ref,
    g_last_ref,
    g_skip_ref,
    back_ref,
    raw_ref,
):
    shards, channels, rows = d_conv_ref.shape
    for k in range(shards + 1):
        spec = bin_product(
            d_spec_ref[k].astype(jnp.float32), spec_ref[k].astype(jnp.float32), True
        )
        back_ref[k] = turn_back(spec * bin_scale(k, shards, rows), table_ref[k])
    for chunk in chunks_of(channels):
        total = None
        for j, block in enumerate(fold_bins(back_ref, chunk, shards, rows)):
            raw_ref[chunk, j * rows : (j + 1) * rows] = block * window_ref[j, chunk]
            term = d_conv_ref[j, chunk].astype(jnp.float32) * gated_ref[j, chunk].astype(
                jnp.float32
            )
            total = term if total is None else total + term
        g_skip_ref[chunk] = jnp.sum(total, axis=1, keepdims=True)
    d_raw = raw_ref[...]
    g_last_ref[...] = across(two_ref[...], d_raw, 1, 1)
    d_two = across(last_ref[...], d_raw, 1, 0) * slope_two_ref[...]
    g_middle_ref[...] = across(one_ref[...], d_two, 1, 1)
    d_one = across(middle_ref[...], d_two, 1, 0) * slope_one_ref[...]
    g_first_ref[...] = across(feature_ref[...], d_one, 1, 1)


def filter_network_back(
    d_spec, spec, d_conv, gated, features, middle, last, kept, table
):
    _, one, slope_one, two, slope_two, window = kept
    bins, channels, span = spec.shape
    hidden, length = one.shape
    feats = features.shape[0]
    return pl.pallas_call(
        filter_back_kernel,
        out_shape=[
            jax.ShapeDtypeStruct((feats, hidden), jnp.float32),
            jax.ShapeDtypeStruct((hidden, hidden), jnp.float32),
            jax.ShapeDtypeStruct((hidden, channels), jnp.float32),
            jax.ShapeDtypeStruct((channels, 1), jnp.float32),
        ],
        scratch_shapes=[
            pltpu.VMEM((bins, channels, span), jnp.float32),
            pltpu.VMEM((channels, length), jnp.float32),
        ],
        compiler_params=pltpu.CompilerParams(vmem_limit_bytes=40 << 20),
        name="filter_network_back",
    )(
        d_spec,
        spec,
        d_conv,
        gated,
        features,
        middle,
        last,
        one,
        slope_one,
        two,
        slope_two,
        window,
        table,
    )


def layer_forward(state, weights, setting):
    (
        mix_gain,
        in_proj,
        short_taps,
        first,
        middle,
        last,
        skip,
        rates,
        out_proj,
        mlp_gain,
        up_proj,
        down_proj,
    ) = weights
    features, tables, offset = setting
    rows, width = state.shape
    length = features.shape[1]
    channels = width // (length // rows)
    normed_mix, scale_mix = normalize(state)
    u_mix = to_low(normed_mix * mix_gain)
    projected = to_low(low_einsum("td,dc->ct", u_mix, in_proj)).reshape(3, width, rows)
    last_columns = lax.dynamic_slice_in_dim(last, offset, channels, 1)
    skip_columns = lax.dynamic_slice_in_dim(skip, offset, channels, 0)
    rate_columns = lax.dynamic_slice_in_dim(rates, offset, channels, 0)
    filter_kept = filter_network(
        features, first, middle, last_columns, rate_columns[:, None], tables
    )
    filter_spec = filter_kept[0]
    taps = short_taps.reshape(3, 3, width)
    edge = from_behind(projected[:, :, rows - 2 :], "seq", 1)
    extended = jnp.concatenate([edge, projected], axis=2).astype(jnp.float32)
    tap_use = taps[:, :, :, None]
    shorted = short_forward(extended, tap_use)
    gated_rows = to_low(shorted[2] * shorted[1])
    shards = length // rows
    gated = lax.all_to_all(
        gated_rows.reshape(shards, channels, rows), "seq", split_axis=0, concat_axis=0, tiled=True
    )
    conv_low, signal_spec = conv_forward(gated, filter_spec, skip_columns[:, None], tables)
    conv_here = lax.all_to_all(
        conv_low, "seq", split_axis=0, concat_axis=0, tiled=True
    ).reshape(width, rows)
    mixed = to_low(conv_here.astype(jnp.float32) * shorted[0])
    middle_state = state + low_einsum("ct,ce->te", mixed, out_proj)
    normed_mlp, scale_mlp = normalize(middle_state)
    u_mlp = to_low(normed_mlp * mlp_gain)
    hidden = low_einsum("td,df->tf", u_mlp, up_proj)
    active = to_low(jax.nn.gelu(hidden))
    result = middle_state + low_einsum("tf,fe->te", active, down_proj)
    kept = (
        normed_mix,
        scale_mix,
        u_mix,
        extended,
        shorted,
        gated,
        conv_here,
        mixed,
        filter_kept,
        filter_spec,
        signal_spec,
        normed_mlp,
        scale_mlp,
        u_mlp,
        hidden,
        active,
        last_columns,
        skip_columns,
        tap_use,
    )
    return (result, kept)


def layer_backward(upstream, kept, weights, setting):
    (
        mix_gain,
        in_proj,
        short_taps,
        first,
        middle,
        last,
        skip,
        rates,
        out_proj,
        mlp_gain,
        up_proj,
        down_proj,
    ) = weights
    features, tables, offset = setting
    (
        normed_mix,
        scale_mix,
        u_mix,
        extended,
        shorted,
        gated,
        conv_here,
        mixed,
        filter_kept,
        filter_spec,
        signal_spec,
        normed_mlp,
        scale_mlp,
        u_mlp,
        hidden,
        active,
        last_columns,
        skip_columns,
        tap_use,
    ) = kept
    rows, width = upstream.shape
    d_down = to_low(upstream)
    g_down = low_einsum("tf,te->fe", active, d_down)
    d_active = low_einsum("te,fe->tf", d_down, down_proj)
    d_hidden = to_low(jax.vjp(jax.nn.gelu, hidden)[1](d_active)[0])
    g_up = low_einsum("td,tf->df", u_mlp, d_hidden)
    d_u_mlp = low_einsum("tf,df->td", d_hidden, up_proj)
    d_middle, g_mlp_gain = normalize_back(d_u_mlp, normed_mlp, scale_mlp, mlp_gain)
    d_middle = d_middle + upstream
    d_branch = to_low(d_middle)
    g_out = low_einsum("ct,te->ce", mixed, d_branch)
    d_mixed = to_low(low_einsum("te,ce->ct", d_branch, out_proj))
    d_mixed_wide = d_mixed.astype(jnp.float32)
    d_conv_rows = to_low(d_mixed_wide * shorted[0])
    d_zero = d_mixed_wide * conv_here.astype(jnp.float32)
    shards, channels, _ = gated.shape
    d_conv = lax.all_to_all(
        d_conv_rows.reshape(gated.shape), "seq", split_axis=0, concat_axis=0, tiled=True
    )
    d_gated, d_spec = conv_backward(d_conv, filter_spec, skip_columns[:, None], tables)
    d_gated_rows = lax.all_to_all(
        d_gated, "seq", split_axis=0, concat_axis=0, tiled=True
    ).reshape(width, rows).astype(jnp.float32)
    d_shorted = jnp.stack([d_zero, d_gated_rows * shorted[2], d_gated_rows * shorted[1]])
    after = from_behind(d_shorted[:, :, :2], "seq", -1)
    d_extended = jnp.concatenate([d_shorted, after], axis=2)
    d_projected = to_low(short_backward(d_extended, tap_use))
    g_taps = tap_grads(d_shorted, extended)
    g_first, g_middle, g_last, g_skip = filter_network_back(
        d_spec, signal_spec, d_conv, gated, features, middle, last_columns, filter_kept, tables
    )
    g_skip = g_skip[:, 0]
    d_flat = d_projected.reshape(3 * width, rows)
    g_in = low_einsum("td,ct->dc", u_mix, d_flat)
    d_u_mix = low_einsum("ct,dc->td", d_flat, in_proj)
    d_state, g_mix_gain = normalize_back(d_u_mix, normed_mix, scale_mix, mix_gain)
    d_state = d_state + d_middle
    large = (g_in, g_out, g_up, g_down)
    small = (g_mix_gain, g_taps.reshape(3, 3 * width), g_first, g_middle, g_mlp_gain)
    column_part = (g_last, g_skip)
    return (d_state, large, small, column_part)


def body(
    tokens,
    cotangent,
    mix_gain,
    in_proj,
    short_taps,
    filter_first,
    filter_middle,
    filter_last,
    filter_skip,
    decay_rates,
    out_proj,
    mlp_gain,
    up_proj,
    down_proj,
):
    rows = tokens.shape[1]
    width = tokens.shape[2]
    layer_count = mix_gain.shape[0]
    shards = lax.axis_size("seq")
    length = rows * shards
    offset = lax.axis_index("seq") * (width // shards)
    setting = (position_table(length), turn_table(shards, rows), offset)
    stacks = (
        mix_gain,
        in_proj,
        short_taps,
        filter_first,
        filter_middle,
        filter_last,
        filter_skip,
        decay_rates,
        out_proj,
        mlp_gain,
        up_proj,
        down_proj,
    )
    state = tokens[0].astype(jnp.float32)
    kept_all = []
    for level in range(layer_count):
        weights = tuple((item[level] for item in stacks))
        state, kept = layer_forward(state, weights, setting)
        kept_all.append(kept)
    upstream = cotangent[0].astype(jnp.float32)
    large_all = [None] * layer_count
    small_all = [None] * layer_count
    column_all = [None] * layer_count
    for level in reversed(range(layer_count)):
        weights = tuple((item[level] for item in stacks))
        upstream, large, small, column_part = layer_backward(
            upstream, kept_all[level], weights, setting
        )
        large_all[level] = large
        small_all[level] = small
        column_all[level] = column_part
    stacked_large = [
        jnp.stack([large_all[level][member] for level in range(layer_count)]) for member in range(4)
    ]
    row_in, row_out, row_up, row_down = (
        lax.psum_scatter(stacked_large[0], "seq", scatter_dimension=1, tiled=True),
        lax.psum_scatter(stacked_large[1], "seq", scatter_dimension=1, tiled=True),
        lax.psum_scatter(stacked_large[2], "seq", scatter_dimension=1, tiled=True),
        lax.psum_scatter(stacked_large[3], "seq", scatter_dimension=1, tiled=True),
    )
    g_in, g_out, g_up, g_down = (
        lax.psum_scatter(row_in.astype(jnp.bfloat16), "dp", scatter_dimension=2, tiled=True).astype(
            jnp.float32
        ),
        lax.psum_scatter(
            row_out.astype(jnp.bfloat16), "dp", scatter_dimension=2, tiled=True
        ).astype(jnp.float32),
        lax.psum_scatter(row_up.astype(jnp.bfloat16), "dp", scatter_dimension=2, tiled=True).astype(
            jnp.float32
        ),
        lax.psum_scatter(
            row_down.astype(jnp.bfloat16), "dp", scatter_dimension=2, tiled=True
        ).astype(jnp.float32),
    )
    stacked_small = [
        jnp.stack([small_all[level][member] for level in range(layer_count)]) for member in range(5)
    ]
    g_mix_gain, g_taps, g_first, g_middle, g_mlp_gain = lax.psum(
        (stacked_small[0], stacked_small[1], stacked_small[2], stacked_small[3], stacked_small[4]),
        ("dp", "seq"),
    )
    stacked_last = jnp.stack([column_all[level][0] for level in range(layer_count)])
    stacked_skip = jnp.stack([column_all[level][1] for level in range(layer_count)])
    g_last, g_skip = lax.psum((stacked_last, stacked_skip), "dp")
    return (
        state[None],
        upstream[None],
        g_mix_gain,
        g_in,
        g_taps,
        g_first,
        g_middle,
        g_last,
        g_skip,
        g_out,
        g_mlp_gain,
        g_up,
        g_down,
    )


SEQ_BITS = 4
VMEM_BYTES = 64 << 20
COST = 3000
LOW, FULL = jnp.bfloat16, jnp.float32


class Board:
    def __init__(self, place, held, inputs, outputs, later):
        self.place = place
        self.held, self.arriving, self.outputs, self.leaving = held, {}, outputs, []
        self.later = {}
        for key, (source, target, sem) in inputs.items():
            copy = pltpu.make_async_copy(source, target, sem)
            if key in later:
                self.later[key] = copy
            else:
                copy.start()
                self.arriving[key] = copy
            held[key] = target
        for key, (source, _, _) in outputs.items():
            held[key] = source

    def begin(self):
        for key, copy in self.later.items():
            copy.start()
            self.arriving[key] = copy
        self.later = {}

    def __getattr__(self, key):
        return self[key]

    def __getitem__(self, key):
        if key in self.later:
            self.begin()
        if key in self.arriving:
            self.arriving.pop(key).wait()
        return self.held[key]

    def flush(self, *refs):
        for key in [key for key, item in self.outputs.items() if any(item[0] is ref for ref in refs)]:
            copy = pltpu.make_async_copy(*self.outputs.pop(key))
            copy.start()
            self.leaving.append(copy)

    def finish(self):
        self.begin()
        self.flush(*[item[0] for item in self.outputs.values()])
        for copy in [*self.arriving.values(), *self.leaving]:
            copy.wait()


class Made:
    def __init__(self, items):
        self.__dict__.update(kept=dict(items))

    def __getattr__(self, key):
        return self.kept[key]

    def __getitem__(self, key):
        return self.kept[key]


class Renamed:
    def __init__(self, board, **names):
        self.__dict__.update(board=board, names=names)

    def __getattr__(self, key):
        return getattr(self.__dict__["board"], self.__dict__["names"].get(key, key))


def local_call(
    name,
    body,
    place,
    near,
    outputs,
    scratch=None,
    far=None,
    cuts=None,
    after=(),
    later=None,
):
    scratch, far, cuts, later = scratch or {}, far or {}, cuts or {}, later or {}
    near = {**near, **later}
    arrays = [*near.values(), *far.values(), *after]

    def shape_of(key):
        shape = list(near[key].shape)
        if key in cuts:
            shape[1] = cuts[key][1]
        return tuple(shape)

    def cut(key, ref):
        return ref.at[:, pl.ds(*cuts[key])] if key in cuts else ref

    def kernel(*refs):
        refs = list(refs)
        place_ref = refs.pop(0)
        given = [refs.pop(0) for _ in arrays]
        made = [refs.pop(0) for _ in outputs]
        here = [refs.pop(0) for _ in near]
        staged = [refs.pop(0) for _ in outputs]
        spare = [refs.pop(0) for _ in scratch]
        sems_in, sems_out = refs
        held = dict(zip(far, given[len(near) :]))
        held.update(zip(scratch, spare))
        board = Board(
            place_ref,
            held,
            {key: (cut(key, given[at]), here[at], sems_in.at[at]) for at, key in enumerate(near)},
            {key: (staged[at], made[at], sems_out.at[at]) for at, key in enumerate(outputs)},
            later,
        )
        body(board)
        board.finish()

    made = pl.pallas_call(
        kernel,
        in_specs=[pl.BlockSpec(memory_space=pltpu.SMEM)]
        + [pl.BlockSpec(memory_space=pltpu.HBM)] * len(arrays),
        out_specs=[pl.BlockSpec(memory_space=pltpu.HBM)] * len(outputs),
        out_shape=[jax.ShapeDtypeStruct(*item) for item in outputs.values()],
        scratch_shapes=[pltpu.VMEM(shape_of(key), near[key].dtype) for key in near]
        + [pltpu.VMEM(*item) for item in outputs.values()]
        + list(scratch.values())
        + [
            pltpu.SemaphoreType.DMA((max(len(near), 1),)),
            pltpu.SemaphoreType.DMA((max(len(outputs), 1),)),
        ],
        compiler_params=pltpu.CompilerParams(vmem_limit_bytes=VMEM_BYTES),
        cost_estimate=pl.CostEstimate(flops=0, bytes_accessed=COST, transcendentals=0),
        name=name,
    )(place, *arrays)
    return Made(zip(outputs, made, strict=True))


class Weights:
    def __init__(self, slots, sems):
        self.slots, self.sems, self.copies = slots, sems, []

    def fetch(self, source):
        at = len(self.copies)
        copy = pltpu.make_async_copy(source, self.slots.at[at], self.sems.at[at])
        copy.start()
        self.copies.append(copy)
        return at

    def fetch_columns(self, source, width):
        count = source.shape[1] // width
        return [self.fetch(source.at[:, pl.ds(j * width, width)]) for j in range(count)]

    def fetch_rows(self, source, width):
        count = source.shape[0] // width
        return [self.fetch(source.at[pl.ds(j * width, width)]) for j in range(count)]

    def wait(self, at):
        if self.copies[at] is not None:
            self.copies[at].wait()
            self.copies[at] = None
        return self.slots[at]


def dot(left, right):
    return jnp.dot(left, right, preferred_element_type=jnp.float32)


def dot_rows(left, right):
    return lax.dot_general(
        left, right, (((1,), (1,)), ((), ())), preferred_element_type=jnp.float32
    )


def low_across(left, right, left_side, right_side):
    return lax.dot_general(
        narrow(left),
        narrow(right),
        (((left_side,), (right_side,)), ((), ())),
        preferred_element_type=jnp.float32,
    )


def flip(block):
    return block.T


def wide(value):
    return value.astype(jnp.float32)


def narrow(value):
    return value.astype(jnp.bfloat16)


def rotate(block, shift):
    return pltpu.roll(block, shift % block.shape[1], 1)


def shifted_down(block, edge):
    row = lax.broadcasted_iota(jnp.int32, block.shape, 0)
    one = jnp.where(row == 0, edge[1:2], pltpu.roll(block, 1, 0))
    two = jnp.where(row == 0, edge[0:1], jnp.where(row == 1, edge[1:2], pltpu.roll(block, 2, 0)))
    return one, two


def shifted_up(block, edge):
    rows = block.shape[0]
    row = lax.broadcasted_iota(jnp.int32, block.shape, 0)
    one = jnp.where(row == rows - 1, edge[0:1], pltpu.roll(block, rows - 1, 0))
    two = jnp.where(
        row == rows - 1,
        edge[1:2],
        jnp.where(row == rows - 2, edge[0:1], pltpu.roll(block, rows - 2, 0)),
    )
    return one, two


def branch_columns(r, branch):
    width = r.projected.shape[1] // 3
    return slice(branch * width, (branch + 1) * width)


def taps_of(r, level, branch):
    width = r.short_taps.shape[2] // 3
    at = slice(branch * width, (branch + 1) * width)
    return [r.short_taps[lag, level : level + 1, at] for lag in range(3)]


def lagged(r, branch):
    block = wide(r.projected[:, branch_columns(r, branch)])
    return (block, *shifted_down(block, r.edge[2 * branch : 2 * branch + 2]))


def tapped(taps, items):
    return taps[0] * items[0] + taps[1] * items[1] + taps[2] * items[2]


def short_branch(r, level, branch):
    return tapped(taps_of(r, level, branch), lagged(r, branch))


def short_ahead(r, level, branch):
    here = wide(r.projected[-16:, branch_columns(r, branch)])[-2:]
    ahead = r.ahead[2 * branch : 2 * branch + 2]
    taps = taps_of(r, level, branch)
    first = tapped(taps, (ahead[0:1], here[1:2], here[0:1]))
    return first, tapped(taps, (ahead[1:2], ahead[0:1], here[1:2]))


def norm_rows(state):
    centred = state - jnp.mean(state, axis=1, keepdims=True)
    scale = lax.rsqrt(jnp.mean(centred * centred, axis=1, keepdims=True) + EPSILON)
    return centred * scale, scale


def norm_rows_back(d_out, normed, scale, gain):
    q = d_out * gain
    return scale * (
        q
        - jnp.mean(q, axis=1, keepdims=True)
        - normed * jnp.mean(q * normed, axis=1, keepdims=True)
    )


def gelu_and_slope(x):
    square = x * x
    tanh = jnp.tanh(x * (0.7978845608028654 + 0.035677408136300125 * square))
    half = 0.5 + 0.5 * tanh
    inner = 0.7978845608028654 + 0.10703222440890037 * square
    return x * half, half + 0.5 * x * (1.0 - tanh * tanh) * inner


def store_rows(target, start, first_block, block_rows, flipped):
    for j in range(flipped.shape[0] // block_rows):
        owner = first_block + j
        z, y, core = owner >> 2, (owner >> 1) & 1, owner & 1
        at = start + z * block_rows
        target[core, y, at : at + block_rows] = flipped[j * block_rows : (j + 1) * block_rows]


def store_line(target, line, vector):
    lanes = target.shape[1]
    pieces = vector.shape[1] // lanes
    for j in range(pieces):
        target[line * pieces + j : line * pieces + j + 1] = vector[:, j * lanes : (j + 1) * lanes]


def store_blocks(target, flipped, ends):
    owned = flipped.shape[0] >> SEQ_BITS
    lanes = target.shape[2]
    lane = lax.broadcasted_iota(jnp.int32, (ends.shape[0], lanes), 1)
    for j in range(1 << SEQ_BITS):
        target[j, :owned] = flipped[j * owned : (j + 1) * owned]
        beside = rotate(ends, -j * owned)[:, :lanes]
        target[j, owned:] = narrow(jnp.where(lane < owned, beside, 0.0))


def mix_forward(r, level, state, weights, squares, gain):
    normed, _ = norm_rows(state)
    u = narrow(normed * gain)
    rows, width = u.shape
    owned = width >> SEQ_BITS
    nothing = jnp.zeros((2, width), jnp.float32)
    r.ends[...] = jnp.zeros_like(r.ends)
    gate = None
    for branch in (1, 2, 0):
        block = narrow(dot(u, weights.wait(squares[branch])))
        r.next_projected[:, branch * width : (branch + 1) * width] = block
        block = wide(block)
        at = slice(2 * branch, 2 * branch + 2)
        r.next_head[at], r.next_tail[at] = block[:2], block[-2:]
        if branch > 0:
            spot = 4 * branch - 4
            r.ends[spot : spot + 2], r.ends[spot + 2 : spot + 4] = block[:2], block[-2:]
            items = (block, *shifted_down(block, nothing))
            part = tapped(taps_of(r, level, branch), items)
            gate = part if gate is None else gate * part
        if branch == 2:
            store_blocks(r.next_gated, flip(narrow(gate)), r.ends[...])
            r.flush(r.next_gated)
    r.next_head[6:] = jnp.zeros_like(r.next_head[6:])
    r.next_tail[6:] = jnp.zeros_like(r.next_tail[6:])
    r.flush(r.next_projected, r.next_head, r.next_tail)
    store_rows(r.next_rows, 0, 0, owned, flip(u))


def enter_kernel(r):
    weights = Weights(r.slots, r.sems)
    squares = weights.fetch_columns(r.in_proj.at[0], r.tokens.shape[1])
    r.begin()
    mix_forward(r, 0, wide(r.tokens[...]), weights, squares, r.mix_gain[0:1])


def after_conv(r, level, weights, squares, pieces):
    out_square, ups, downs = squares
    rows, width = r.state.shape
    owned = width >> SEQ_BITS
    conv = flip(r.conv[...].reshape(width, rows))
    r.conv_rows[...] = conv
    r.flush(r.conv_rows)
    mixed = narrow(wide(conv) * short_branch(r, level, 0))
    middle = wide(r.state[...]) + dot(mixed, weights.wait(out_square))
    r.middle[...] = middle
    r.flush(r.middle)
    normed, _ = norm_rows(middle)
    u = narrow(normed * r.mlp_gain[level : level + 1])
    hidden = dot(u, weights.wait(ups[0]))
    total = middle
    for j, down in enumerate(downs):
        following = weights.wait(ups[j + 1]) if j + 1 < len(ups) else None
        down = weights.wait(down)
        coming = None if following is None else dot(u, following)
        active, slope = gelu_and_slope(hidden)
        r.slope[:, j * width : (j + 1) * width] = narrow(slope)
        active = narrow(active)
        total = total + dot(active, down)
        store_rows(r.all_rows, 0, 4 * j, 4 * owned, flip(active))
        hidden = coming
    store_rows(r.all_rows, 4 * 4 * owned, 0, owned, flip(u))
    store_rows(r.all_rows, 5 * 4 * owned, 0, owned, flip(mixed))
    for core in range(2):
        for y in range(2):
            r.all_rows[core, y, 6 * 4 * owned :] = r.rows[core, y]
    core = r.place[1]
    for keep, send, start, count in pieces:
        r[send][...] = r.all_rows[1 - core, :, start : start + count]
        r[keep][...] = r.all_rows[core, :, start : start + count]
    return total


def before_conv_back(r, level, upstream, weights, squares):
    out_square, ups, downs = squares
    rows, width = upstream.shape
    half, wide_half = width // 2, 2 * width
    d_down = narrow(upstream)
    middle = r.middle[...]
    normed, scale = norm_rows(middle)
    d_u = jnp.zeros_like(middle)
    d_active = dot_rows(d_down, weights.wait(downs[0]))
    for j, up in enumerate(ups):
        following = weights.wait(downs[j + 1]) if j + 1 < len(downs) else None
        up = weights.wait(up)
        coming = None if following is None else dot_rows(d_down, following)
        d_hidden = narrow(d_active * wide(r.slope[:, j * width : (j + 1) * width]))
        side, at = divmod(j * width, wide_half)
        r.all_columns[side, :, at : at + width] = d_hidden
        d_u = d_u + dot_rows(d_hidden, up)
        d_active = coming
    r.g_mlp_gain[...] = jnp.broadcast_to(
        jnp.sum(d_u * normed, axis=0, keepdims=True), r.g_mlp_gain.shape
    )
    d_middle = upstream + norm_rows_back(d_u, normed, scale, r.mlp_gain[level : level + 1])
    d_branch = narrow(d_middle)
    d_mixed = wide(narrow(dot_rows(d_branch, weights.wait(out_square))))
    d_conv = narrow(d_mixed * short_branch(r, level, 0))
    d_x0 = d_mixed * wide(r.conv_rows[...])
    r.ends[...] = jnp.zeros_like(r.ends)
    r.ends[:2] = d_x0[:2]
    store_blocks(r.d_conv, flip(d_conv), r.ends[...])
    r.flush(r.d_conv)
    r.d_x0[...] = d_x0
    r.d_middle[...] = d_middle
    for side in range(2):
        at = slice(side * half, (side + 1) * half)
        r.all_columns[side, :, wide_half : wide_half + half] = d_branch[:, at]
        r.all_columns[side, :, wide_half + half : wide_half + width] = d_down[:, at]
    side = r.place[0]
    r.columns_send[...] = r.all_columns[1 - side]
    r.columns_keep[...] = r.all_columns[side]


def mlp_fetch(r, level, weights):
    width = r.out_proj.shape[2]
    out_square = weights.fetch(r.out_proj.at[level])
    ups, downs = [], []
    for j in range(r.up_proj.shape[2] // width):
        at = pl.ds(j * width, width)
        ups.append(weights.fetch(r.up_proj.at[level, :, at]))
        downs.append(weights.fetch(r.down_proj.at[level, at]))
    return out_square, ups, downs


def mlp_fetch_back(r, level, weights):
    width = r.out_proj.shape[2]
    ups, downs = [], []
    for j in range(r.up_proj.shape[2] // width):
        at = pl.ds(j * width, width)
        downs.append(weights.fetch(r.down_proj.at[level, at]))
        ups.append(weights.fetch(r.up_proj.at[level, :, at]))
    return weights.fetch(r.out_proj.at[level]), ups, downs


def middle_kernel(level, pieces):
    def body(r):
        weights = Weights(r.slots, r.sems)
        squares = mlp_fetch(r, level, weights)
        r.begin()
        mix_squares = weights.fetch_columns(r.in_proj.at[level + 1], r.state.shape[1])
        state = after_conv(r, level, weights, squares, pieces)
        r.next_state[...] = state
        gain = r.mix_gain[level + 1 : level + 2]
        mix_forward(r, level + 1, state, weights, mix_squares, gain)

    return body


def turn_kernel(level, pieces):
    def body(r):
        weights = Weights(r.slots, r.sems)
        squares = mlp_fetch(r, level, weights)
        r.begin()
        r.next_state[...] = after_conv(r, level, weights, squares, pieces)
        before_conv_back(r, level, wide(r.cotangent[...]), weights, squares)

    return body


def after_short_back(r, level, weights, squares):
    rows, width = r.d_x0.shape
    owned = width >> SEQ_BITS
    half, wide_half = width // 2, 3 * width // 2
    d_gated = wide(flip(r.d_gated[:, :owned].reshape(width, rows)))
    ahead = jnp.zeros((16, width), jnp.float32)
    for j in range(1 << SEQ_BITS):
        piece = wide(r.d_gated[j, owned:])
        filled = jnp.concatenate([piece, jnp.zeros((16, width - rows), jnp.float32)], axis=1)
        ahead = ahead + rotate(filled, j * owned)
    d_u = jnp.zeros_like(d_gated)
    shorted = {}
    for branch in (1, 2, 0):
        taps = taps_of(r, level, branch)
        items = lagged(r, branch)
        if branch == 0:
            d_block, d_ahead = r.d_x0[...], ahead[8:10]
        else:
            other = 3 - branch
            d_block = d_gated * short_branch(r, level, other)
            first, second = short_ahead(r, level, other)
            d_ahead = (ahead[0:1] * first, ahead[1:2] * second)
            d_ahead = jnp.concatenate(d_ahead, axis=0)
        d_projected = narrow(tapped(taps, (d_block, *shifted_up(d_block, d_ahead))))
        for piece in range(2):
            side, lane = divmod((branch * 2 + piece) * half, wide_half)
            lane += r.all_columns.shape[2] - wide_half
            r.all_columns[side, :, lane : lane + half] = d_projected[
                :, piece * half : (piece + 1) * half
            ]
        d_u = d_u + dot_rows(d_projected, weights.wait(squares[branch]))
        for lag, item in enumerate(items):
            store_line(r.small, 3 * lag + branch, jnp.sum(d_block * item, axis=0, keepdims=True))
    return d_u


def input_gradient(r, level, d_u):
    normed, scale = norm_rows(wide(r.state[...]))
    store_line(r.small, 9, jnp.sum(d_u * normed, axis=0, keepdims=True))
    store_line(r.small, 10, r.g_mlp_gain_in[0:1])
    lines = 11 * (r.state.shape[1] // 128)
    r.small[lines:] = jnp.zeros_like(r.small[lines:])
    return r.d_middle_in[...] + norm_rows_back(
        d_u, normed, scale, r.mix_gain[level : level + 1]
    )


def between_kernel(level):
    def body(r):
        weights = Weights(r.slots, r.sems)
        mix_squares = weights.fetch_columns(r.in_proj.at[level], r.d_x0_in.shape[1])
        r.begin()
        squares = mlp_fetch_back(r, level - 1, weights)
        upper = Renamed(
            r, d_x0="d_x0_in", projected="upper_projected", edge="upper_edge", ahead="upper_ahead"
        )
        d_u = after_short_back(upper, level, weights, mix_squares)
        upstream = input_gradient(upper, level, d_u)
        before_conv_back(r, level - 1, upstream, weights, squares)

    return body


def leave_kernel(r):
    weights = Weights(r.slots, r.sems)
    squares = weights.fetch_columns(r.in_proj.at[0], r.d_x0.shape[1])
    r.begin()
    d_u = after_short_back(r, 0, weights, squares)
    side = r.place[0]
    r.in_send[...] = r.all_columns[1 - side]
    r.in_keep[...] = r.all_columns[side]
    r.flush(r.in_send, r.in_keep)
    r.upstream[...] = input_gradient(r, 0, d_u)
    inner = r.packed_0.shape[0] // 2
    at = r.small_above.shape[0]
    for block in (r.packed_0[:inner], r.small_above[...], r.packed_1[:inner], r.packed_0[inner:], r.packed_1[inner:]):
        r.small[at : at + block.shape[0]] = block
        at += block.shape[0]


def filter_kernel(level):
    def body(r):
        shards, channels, rows = r.window.shape
        width = r.filter_last.shape[2]
        pick = (
            lax.broadcasted_iota(jnp.int32, (channels, width), 1)
            == lax.broadcasted_iota(jnp.int32, (channels, width), 0) + r.place[5]
        ).astype(jnp.float32)
        one, slope_one = sin_cos(across(r.filter_first[:, level], r.features[...], 0, 0))
        r.one[...] = one
        r.slope_one[...] = slope_one
        r.flush(r.one, r.slope_one)
        two, slope_two = sin_cos(across(r.filter_middle[level], one, 0, 0))
        r.two[...] = two
        r.slope_two[...] = slope_two
        r.flush(r.two, r.slope_two)
        last = across(pick, r.filter_last[level], 1, 1)
        r.last[...] = last
        r.raw[...] = across(last, two, 1, 0)

        def own(row):
            return jnp.sum(pick * row, axis=1, keepdims=True)

        rate = own(r.decay_rates[level : level + 1])
        lane = lax.broadcasted_iota(jnp.int32, r.near.shape, 1)
        near = jnp.broadcast_to(own(r.filter_skip[level : level + 1]), r.near.shape)
        for branch in (1, 2):
            for lag, row in enumerate(taps_of(r, level, branch)):
                near = jnp.where(lane == 3 * branch - 2 + lag, own(row), near)
        r.near[...] = near
        size = jnp.sqrt(rate + 1.0 / (shards * rows))
        step = lax.broadcasted_iota(jnp.int32, (channels, rows), 1)
        for j in range(shards):
            window = jnp.exp(-rate * (step + j * rows).astype(jnp.float32)) * size
            r.window[j] = window
            at = slice(j * rows, (j + 1) * rows)
            r.raw[:, at] = r.raw[:, at] * window
        r.flush(r.window)
        for chunk in chunks_of(channels):
            load_bins(
                [r.raw[chunk, j * rows : (j + 1) * rows] for j in range(shards)], r.bins, chunk
            )
        for k in range(shards + 1):
            r.filter_spec[k] = dot(r.bins[k], r.table[k]) * bin_scale(k, shards, rows)

    return body


def transformed(r, conjugate):
    shards, channels, rows = r.fixed.shape
    for chunk in chunks_of(channels):
        load_bins([r.fixed[j, chunk] for j in range(shards)], r.bins, chunk)
    for k in range(shards + 1):
        spec = dot(r.bins[k], r.table[k])
        r.spec[k] = narrow(spec)
        product = bin_product(spec, r.filter_spec[k], conjugate)
        r.back[k] = dot_rows(narrow(product), r.table[k])
    r.flush(r.spec)
    for chunk in chunks_of(channels):
        skip = r.near[chunk, 0:1]
        blocks = fold_bins(r.back, chunk, shards, rows)
        yield chunk, [block + skip * r.fixed[j, chunk] for j, block in enumerate(blocks)]


def conv_kernel(r):
    shards, channels, rows = r.fixed.shape
    ends = jnp.concatenate([wide(r.signal[j, channels:])[:8] for j in range(shards)], axis=0)
    ends = flip(ends)[:channels]
    lane = lax.broadcasted_iota(jnp.int32, ends.shape, 1)

    def first_two(block, taps):
        before_two = jnp.where(lane >= 8, rotate(block, 6), 0.0)
        before_one = jnp.where(lane >= 8, rotate(block, 5), 0.0)
        first = tapped(taps, (block, before_one, before_two))
        return first, tapped(taps, (rotate(block, -1), block, before_one))

    near = r.near[...]
    one = first_two(ends, [near[:, at : at + 1] for at in (1, 2, 3)])
    value = first_two(rotate(ends, -4), [near[:, at : at + 1] for at in (4, 5, 6)])
    first, second = (wide(narrow(a * b)) for a, b in zip(one, value, strict=True))
    both = jnp.where(lane % 8 == 0, first, rotate(second, 1))
    for j in range(shards):
        fixed = jnp.where(lane < 2, rotate(both, -8 * j), wide(r.signal[j, :channels]))
        r.fixed[j] = fixed
        r.gated[j] = narrow(fixed)
    r.flush(r.gated)
    for chunk, blocks in transformed(r, False):
        for j, block in enumerate(blocks):
            r.result[j, chunk] = narrow(block)


def conv_back_kernel(r):
    shards, channels, rows = r.fixed.shape
    for j in range(shards):
        r.fixed[j] = wide(r.signal[j, :channels])
    r.ends[...] = jnp.zeros_like(r.ends)
    for chunk, blocks in transformed(r, True):
        lane = lax.broadcasted_iota(jnp.int32, blocks[0].shape, 1)
        ends = jnp.zeros_like(blocks[0])
        for j, block in enumerate(blocks):
            block = narrow(block)
            r.result[j, chunk] = block
            inside = (lane >= 8 * j) & (lane < 8 * j + 2)
            ends = jnp.where(inside, rotate(wide(block), 8 * j), ends)
        r.ends[chunk] = ends
    ends = flip(r.ends[...])
    for j in range(shards - 1):
        beside = wide(r.signal[j + 1, channels:])[:8]
        ahead = jnp.concatenate([ends[8 * j + 8 : 8 * j + 16], beside], axis=0)
        r.result[j, channels:] = narrow(ahead)
    r.result[shards - 1, channels:] = jnp.zeros((16, rows), LOW)
    r.flush(r.result)
    if 0 in r.held:
        r[1][...] = r[0][...]


def filter_grads_kernel(level):
    def body(r):
        shards, channels, rows = r.gated.shape
        hidden = r.one.shape[0]
        feats = r.features.shape[0]
        for k in range(shards + 1):
            spec = bin_product(wide(r.d_spec[k]), wide(r.spec[k]), True)
            r.back[k] = dot_rows(narrow(spec * bin_scale(k, shards, rows)), r.table[k])
        r.packed[...] = jnp.zeros_like(r.packed)
        for chunk in chunks_of(channels):
            total = None
            for j, block in enumerate(fold_bins(r.back, chunk, shards, rows)):
                r.raw[chunk, j * rows : (j + 1) * rows] = block * r.window[j, chunk]
                term = wide(r.d_conv[j, chunk]) * wide(r.gated[j, chunk])
                total = term if total is None else total + term
            r.packed[hidden + chunk.start : hidden + chunk.stop, hidden : hidden + 1] = jnp.sum(
                total, axis=1, keepdims=True
            )
        d_raw = r.raw[...]
        r.packed[hidden:, :channels] = low_across(r.two[...], d_raw, 1, 1)
        d_two = low_across(r.last[...], d_raw, 0, 0) * r.slope_two[...]
        r.packed[:hidden, hidden:] = low_across(r.one[...], d_two, 1, 1)
        d_one = low_across(r.filter_middle[level], d_two, 1, 0) * r.slope_one[...]
        r.packed[:feats, :hidden] = low_across(r.features[...], d_one, 1, 1)

    return body


def fill_blocks(r, parts):
    tile = r.blocks.shape[3]
    for y in range(2):
        start = 0
        for rows_of, columns_of, row, count, column, columns in parts:
            at, lanes = slice(row, row + count), slice(column, column + columns)
            left = jnp.concatenate([r[0, rows_of, i][y, at] for i in range(4)], axis=1)
            right = jnp.concatenate([r[1, columns_of, i][:, lanes] for i in range(4)], axis=0)
            block = narrow(dot(left, right))
            owned = count // 4
            for z in range(4):
                for piece in range(columns // tile):
                    spot = start + piece * owned
                    r.blocks[y, z, spot : spot + owned] = block[
                        z * owned : (z + 1) * owned, piece * tile : (piece + 1) * tile
                    ]
            start += owned * (columns // tile)


def last_grad_kernel(parts):
    def body(r):
        y_own, low, high = r.place[2], r.place[3], r.place[4]
        fill_blocks(r, parts)
        tall = r.blocks.shape[2]
        for one in range(2):
            for two in range(2):
                z = (low ^ (1 - one)) + 2 * (high ^ (1 - two))
                at = 2 * one + two
                r.send[at * tall : (at + 1) * tall] = r.blocks[1 - y_own, z]
                r.keep[at] = r.blocks[y_own, z]
        height = r.small_keep.shape[0]
        for piece in range(3):
            lanes = slice(piece * 128, (piece + 1) * 128)
            block = narrow(r.small[piece * height : (piece + 1) * height])
            r.send[4 * tall :, lanes] = block
            r.small_keep[:, lanes] = block

    return body


def last_sum_kernel(r):
    count, tall = r.mine.shape[:2]
    for at in range(count):
        came = wide(r.came[at * tall : (at + 1) * tall])
        r.following[at * tall : (at + 1) * tall] = narrow(wide(r.keep[at]) + came)
    small = narrow(wide(r.small_keep[...]) + wide(r.came[2 * count * tall :]))
    r.following[count * tall :] = small
    r.flush(r.following)
    r.small_next[...] = small
    for at in range(count):
        came = wide(r.came[(count + at) * tall : (count + at + 1) * tall])
        r.mine[at] = wide(r.keep[count + at]) + came


def last_step(place, keep, small_keep, came, after):
    count, tall, tile = keep.shape
    height = small_keep.shape[0]
    return local_call(
        "last_sum",
        last_sum_kernel,
        place,
        dict(keep=keep, small_keep=small_keep, came=came),
        dict(
            following=((count // 2 * tall + height, tile), LOW),
            small_next=((height, tile), LOW),
            mine=((count // 2, tall, tile), FULL),
        ),
        after=after,
    )


def grad_kernel(parts, split):
    def body(r):
        y_own, low, high = r.place[2], r.place[3], r.place[4]
        fill_blocks(r, parts)
        for one in range(2):
            for two in range(2):
                z = (low ^ (1 - one)) + 2 * (high ^ (1 - two))
                r.p_send[one, two] = r.blocks[1 - y_own, z, :split]
                z, y = 2 * (high ^ (1 - two)), y_own ^ (1 - one)
                r.q_send[one, two] = r.blocks[y, z + 1 - low, split:]
        r.flush(r.p_send, r.q_send)
        for one in range(2):
            for two in range(2):
                z = (low ^ (1 - one)) + 2 * (high ^ (1 - two))
                r.p_keep[one, two] = r.blocks[y_own, z, :split]
                z, y = 2 * (high ^ (1 - two)), y_own ^ (1 - one)
                r.q_keep[one, two] = r.blocks[y, z + low, split:]

    return body


def crossed(block, bit):
    count = lax.axis_size("seq")
    return lax.ppermute(block, "seq", [(i, i ^ bit) for i in range(count)])


def other_sequence(block):
    return lax.ppermute(block, "dp", [(0, 1), (1, 0)])


def share_rows(keep, send):
    core = crossed(send, 1)
    return keep, other_sequence(keep), core, other_sequence(core)


def share_columns(keep, send):
    x = other_sequence(send)
    return keep, x, crossed(keep, 1), crossed(x, 1)


def partial_grads(name, place, rows, columns, parts, split, tile, cuts, after=()):
    tall = sum(count // 4 * (width // tile) for _, _, _, count, _, width in parts)
    near = {(0, key, i): item for key, items in rows.items() for i, item in enumerate(items)}
    near.update({(1, key, i): item for key, items in columns.items() for i, item in enumerate(items)})
    first, second = ((2, 2, split, tile), LOW), ((2, 2, tall - split, tile), LOW)
    return local_call(
        name,
        grad_kernel(parts, split),
        place,
        near,
        dict(p_send=first, q_send=second, p_keep=first, q_keep=second),
        dict(blocks=pltpu.VMEM((2, 4, tall, tile), LOW)),
        cuts={(0, key, i): cut for key, cut in cuts.items() for i in range(4)},
        after=after,
    )


def first_sum_kernel(r):
    for keep, one, following, mine in (
        (r.p_keep, r.p_one, r.p_next, r.p_mine),
        (r.q_keep, r.q_one, r.q_next, r.q_mine),
    ):
        following[...] = narrow(wide(keep[0]) + wide(one[0]))
        r.flush(following)
        mine[...] = wide(keep[1]) + wide(one[1])


def second_sum_kernel(r):
    split = r.p_two.shape[1]
    for mine, two, at in (
        (r.p_mine, r.p_two, slice(0, split)),
        (r.q_mine, r.q_two, slice(split, r.following.shape[0])),
    ):
        r.following[at] = narrow(mine[0] + wide(two[0]))
    r.flush(r.following)
    for mine, two, at in (
        (r.p_mine, r.p_two, slice(0, split)),
        (r.q_mine, r.q_two, slice(split, r.following.shape[0])),
    ):
        r.last[at] = mine[1] + wide(two[1])


class Reduction:
    def __init__(self, place, made):
        self.place, self.made = place, made
        self.p_one, self.q_one = crossed(made.p_send, 2), crossed(made.q_send, 4)
        self.p_shape, self.q_shape = made.p_send.shape[1:], made.q_send.shape[1:]

    def first(self, after=()):
        keep = dict(p_keep=self.made.p_keep, q_keep=self.made.q_keep)
        made = local_call(
            "first_sum",
            first_sum_kernel,
            self.place,
            dict(p_one=self.p_one, q_one=self.q_one, **keep),
            dict(
                p_next=(self.p_shape, LOW),
                q_next=(self.q_shape, LOW),
                p_mine=(self.p_shape, FULL),
                q_mine=(self.q_shape, FULL),
            ),
            after=after,
        )
        self.first_made = made
        self.p_two, self.q_two = crossed(made.p_next, 4), crossed(made.q_next, 2)
        return made.p_next

    def second(self, after=()):
        mine = dict(p_mine=self.first_made.p_mine, q_mine=self.first_made.q_mine)
        shape = (self.p_shape[1] + self.q_shape[1], self.p_shape[2])
        made = local_call(
            "second_sum",
            second_sum_kernel,
            self.place,
            dict(p_two=self.p_two, q_two=self.q_two, **mine),
            dict(following=(shape, LOW), last=(shape, FULL)),
            after=after,
        )
        self.three = crossed(made.following, 8)
        self.result = (made.last, self.three)
        return made.following


def collect_kernel(groups, owned):
    def body(r):
        for at, places in enumerate(groups):
            total = r[at, 0][...] + wide(r[at, 1][: r[at, 0].shape[0]])
            tile = total.shape[1]
            start = 0
            for output, level, count, pieces in places:
                for j in range(pieces):
                    r[output][level, :, j * tile : (j + 1) * tile] = total[start : start + count]
                    start += count
        width = r.g_mix_gain.shape[1]
        lines = width // 128
        hidden = r.g_middle.shape[1]
        packed = wide(r.small_last[...]) + wide(r[len(groups) - 1, 1][-r.small_last.shape[0] :])
        packed = jnp.concatenate([packed[:, j * 128 : (j + 1) * 128] for j in range(3)], axis=0)
        each = packed.shape[0] // 2
        for level in range(2):
            small = packed[level * each : (level + 1) * each]
            last = r.small_x[2 * each + level * hidden : 2 * each + (level + 1) * hidden]
            for j in range(lines):
                at = slice(j * 128, (j + 1) * 128)
                r.g_mix_gain[level : level + 1, at] = small[9 * lines + j : 9 * lines + j + 1]
                r.g_mlp_gain[level : level + 1, at] = small[10 * lines + j : 10 * lines + j + 1]
            for lag in range(3):
                for j in range(3 * lines):
                    line = 3 * lag * lines + j
                    r.g_taps[lag, level : level + 1, j * 128 : (j + 1) * 128] = small[
                        line : line + 1
                    ]
            start = each - hidden
            r.g_first[:, level] = small[start : start + r.g_first.shape[0], :hidden]
            r.g_middle[level] = small[start : start + hidden, hidden:]
            r.g_last[level] = last[:, :owned]
            r.g_skip[level : level + 1] = flip(last)[hidden : hidden + 1, :owned]

    return body


def fast_body(
    tokens,
    cotangent,
    mix_gain,
    in_proj,
    short_taps,
    filter_first,
    filter_middle,
    filter_last,
    filter_skip,
    decay_rates,
    out_proj,
    mlp_gain,
    up_proj,
    down_proj,
):
    tokens, cotangent = tokens[0], cotangent[0]
    rows, width = tokens.shape
    hidden = up_proj.shape[2]
    shards = lax.axis_size("seq")
    length = rows * shards
    owned = channels = width // shards
    inner, feats = filter_first.shape[2], filter_first.shape[1]
    seq = lax.axis_index("seq")
    place = jnp.stack(
        [lax.axis_index("dp"), seq & 1, (seq >> 1) & 1, (seq >> 2) & 1, (seq >> 3) & 1, seq * channels]
    ).astype(jnp.int32)
    features, table = position_table(length), turn_table(shards, rows)
    short_taps = short_taps.transpose(1, 0, 2)
    filter_first = filter_first.transpose(1, 0, 2)
    ups, tile, half = hidden // width, width // 2, hidden // 2
    bins, span = shards + 1, 2 * rows
    down_rows, rest_rows = 16 * owned, 12 * owned
    tall, mlp_rows = down_rows + rest_rows, 24 * owned

    def slots(count):
        return dict(
            slots=pltpu.VMEM((count, width, width), LOW), sems=pltpu.SemaphoreType.DMA((count,))
        )

    def exchange(block):
        return lax.all_to_all(block, "seq", split_axis=0, concat_axis=0, tiled=True)

    line, edges = ((rows, width), FULL), ((8, width), FULL)
    by_shard = ((shards, channels, rows), LOW)
    with_ends = ((shards, channels + 16, rows), LOW)
    spectrum = ((bins, channels, span), LOW)
    mix_outputs = dict(
        next_gated=with_ends,
        next_projected=((rows, 3 * width), LOW),
        next_tail=edges,
        next_head=edges,
        next_rows=((2, 2, 4 * owned, rows), LOW),
    )
    kept_outputs = dict(
        middle=line, slope=((rows, hidden), LOW), conv_rows=((rows, width), LOW)
    )
    rows_scratch = dict(all_rows=pltpu.VMEM((2, 2, tall, rows), LOW))

    def columns_outputs(count):
        return dict(columns_keep=((rows, count), LOW), columns_send=((rows, count), LOW))

    def columns_scratch(count):
        return dict(all_columns=pltpu.VMEM((2, rows, count), LOW), ends=ends_scratch)

    back_outputs = dict(
        d_conv=with_ends, d_x0=line, d_middle=line, g_mlp_gain=edges
    )
    small_output = ((80, 128), FULL)
    in_half = ((rows, 3 * tile), LOW)
    in_columns = ((2, *in_half[0]), LOW)
    bins_scratch = pltpu.VMEM((bins, channels, span), LOW)
    back_scratch = pltpu.VMEM((bins, channels, span), FULL)
    fixed_scratch = pltpu.VMEM((shards, channels, rows), FULL)
    ends_scratch = pltpu.VMEM((16, width), FULL)
    raw_scratch = pltpu.VMEM((channels, length), FULL)
    mlp_weights = dict(out_proj=out_proj, up_proj=up_proj, down_proj=down_proj)
    all_weights = dict(in_proj=in_proj, **mlp_weights)

    def filter_of(level):
        wave = ((inner, length), FULL)
        return local_call(
            "filter",
            filter_kernel(level),
            place,
            dict(
                features=features,
                filter_first=filter_first,
                filter_middle=filter_middle,
                filter_last=filter_last,
                decay_rates=decay_rates,
                filter_skip=filter_skip,
                short_taps=short_taps,
                table=table,
            ),
            dict(
                filter_spec=((bins, channels, span), FULL),
                near=((channels, rows), FULL),
                last=((channels, inner), FULL),
                one=wave,
                slope_one=wave,
                two=wave,
                slope_two=wave,
                window=((shards, channels, rows), FULL),
            ),
            dict(raw=raw_scratch, bins=bins_scratch),
        )

    def conv_inputs(signal, filters):
        return dict(
            signal=signal, near=filters.near, table=table, filter_spec=filters.filter_spec
        )

    conv_scratch = dict(bins=bins_scratch, back=back_scratch, fixed=fixed_scratch)

    def conv_of(signal, filters, after=()):
        return local_call(
            "conv",
            conv_kernel,
            place,
            conv_inputs(signal, filters),
            dict(spec=spectrum, gated=by_shard, result=by_shard),
            conv_scratch,
            after=after,
        )

    def conv_back_of(signal, filters, after=(), passing=None):
        near, made = conv_inputs(signal, filters), dict(spec=spectrum, result=with_ends)
        if passing is not None:
            near[0], made[1] = passing, (passing.shape, passing.dtype)
        return local_call(
            "conv_back",
            conv_back_kernel,
            place,
            near,
            made,
            dict(ends=pltpu.VMEM((rows, rows), FULL), **conv_scratch),
            after=after,
        )

    def filter_grads_of(level, filters, back, conv, d_conv, after=()):
        return local_call(
            "filter_grads",
            filter_grads_kernel(level),
            place,
            dict(
                d_spec=back.spec,
                spec=conv.spec,
                table=table,
                d_conv=d_conv,
                gated=conv.gated,
                window=filters.window,
                two=filters.two,
                last=filters.last,
                slope_two=filters.slope_two,
                one=filters.one,
                filter_middle=filter_middle,
                slope_one=filters.slope_one,
                features=features,
            ),
            dict(packed=((2 * inner, 128), FULL)),
            dict(back=back_scratch, raw=raw_scratch),
            after=after,
        )["packed"]

    def near_of(made):
        return dict(
            projected=made.next_projected,
            edge=from_behind(made.next_tail, "seq", 1),
            ahead=from_behind(made.next_head, "seq", -1),
        )

    def row_shape(count):
        return ((2, count, rows), LOW)

    entered = local_call(
        "enter",
        enter_kernel,
        place,
        dict(tokens=tokens, mix_gain=mix_gain, short_taps=short_taps),
        mix_outputs,
        dict(ends=ends_scratch, **slots(3)),
        far=dict(in_proj=in_proj),
    )
    filters_0 = filter_of(0)
    near_0 = near_of(entered)
    conv_0 = conv_of(exchange(entered.next_gated), filters_0)
    filters_1 = filter_of(1)
    lower = local_call(
        "middle",
        middle_kernel(0, ((0, 1, 0, mlp_rows), (2, 3, mlp_rows, tall - mlp_rows))),
        place,
        dict(
            conv=exchange(conv_0.result),
            projected=near_0["projected"],
            edge=near_0["edge"],
            short_taps=short_taps,
            state=tokens,
            mlp_gain=mlp_gain,
            mix_gain=mix_gain,
        ),
        {
            **mix_outputs,
            **kept_outputs,
            **dict(next_state=line),
            0: row_shape(mlp_rows),
            1: row_shape(mlp_rows),
            2: row_shape(tall - mlp_rows),
            3: row_shape(tall - mlp_rows),
        },
        dict(ends=ends_scratch, **rows_scratch, **slots(1 + 2 * ups + 3)),
        far=all_weights,
        after=[filters_1.near, near_0["ahead"]],
        later=dict(rows=entered.next_rows),
    )
    near_1 = near_of(lower)
    rows_0 = share_rows(lower[0], lower[1])
    conv_1 = conv_of(exchange(lower.next_gated), filters_1, after=[rows_0[2]])
    in_rows_0 = share_rows(lower[2], lower[3])
    upper = turn = local_call(
        "turn",
        turn_kernel(1, ((0, 1, 0, tall),)),
        place,
        dict(
            conv=exchange(conv_1.result),
            projected=near_1["projected"],
            edge=near_1["edge"],
            short_taps=short_taps,
            state=lower.next_state,
            mlp_gain=mlp_gain,
        ),
        {
            **dict(next_state=line),
            **back_outputs,
            **columns_outputs(half + width),
            0: row_shape(tall),
            1: row_shape(tall),
        },
        {
            **{key: pltpu.VMEM(*item) for key, item in kept_outputs.items()},
            **columns_scratch(half + width),
            **rows_scratch,
            **slots(1 + 2 * ups),
        },
        far=mlp_weights,
        after=[rows_0[1], rows_0[3], near_1["ahead"]],
        later=dict(cotangent=cotangent, rows=lower.next_rows),
    )
    rows_1 = share_rows(upper[0], upper[1])

    columns_1 = share_columns(turn.columns_keep, turn.columns_send)
    d_conv_1 = exchange(turn.d_conv)
    back_1 = conv_back_of(d_conv_1, filters_1, after=[rows_1[1], rows_1[2], columns_1[2]])
    packed_1 = filter_grads_of(1, filters_1, back_1, conv_1, d_conv_1)
    mlp_parts = (
        (0, 0, 0, 16 * owned, half + tile, tile),
        (0, 0, 16 * owned, 4 * owned, 0, half),
        (0, 0, 20 * owned, 4 * owned, half, tile),
    )
    between = local_call(
        "between",
        between_kernel(1),
        place,
        dict(
            d_gated=exchange(back_1.result),
            short_taps=short_taps,
            upper_projected=near_1["projected"],
            upper_edge=near_1["edge"],
            upper_ahead=near_1["ahead"],
            d_x0_in=turn.d_x0,
        ),
        dict(
            small=small_output, **back_outputs, **columns_outputs(half + width + 3 * tile)
        ),
        {**columns_scratch(half + width + 3 * tile), **slots(1 + 2 * ups + 3)},
        far=all_weights,
        after=[packed_1, rows_1[3]],
        later=dict(
            state=lower.next_state,
            d_middle_in=turn.d_middle,
            g_mlp_gain_in=turn.g_mlp_gain,
            mix_gain=mix_gain,
            middle=lower.middle,
            slope=lower.slope,
            mlp_gain=mlp_gain,
            projected=near_0["projected"],
            edge=near_0["edge"],
            conv_rows=lower.conv_rows,
        ),
    )

    keep, send = between.columns_keep, between.columns_send
    columns_0 = (keep, other_sequence(send), crossed(keep, 1))
    d_conv_0 = exchange(between.d_conv)
    mlp_sum = Reduction(
        place,
        partial_grads(
            "grad_mlp",
            place,
            {0: rows_1},
            {0: columns_1},
            mlp_parts,
            224,
            tile,
            {0: (0, 24 * owned)},
            after=[between.d_conv],
        ),
    )
    back_0 = conv_back_of(
        d_conv_0, filters_0, after=[mlp_sum.made.p_send], passing=columns_0[1]
    )
    columns_0 = (*columns_0, crossed(back_0[1], 1))
    packed_0 = filter_grads_of(0, filters_0, back_0, conv_0, d_conv_0)
    mark = mlp_sum.first(after=[packed_0, *in_rows_0[1:]])
    d_gated_0 = exchange(back_0.result)
    leave = local_call(
        "leave",
        leave_kernel,
        place,
        dict(
            d_gated=d_gated_0,
            short_taps=short_taps,
            **near_0,
            d_x0=between.d_x0,
        ),
        dict(in_send=in_half, in_keep=in_half, small=((160 + 4 * inner, 128), FULL), upstream=line),
        dict(all_columns=pltpu.VMEM(*in_columns), **slots(3)),
        far=dict(in_proj=in_proj),
        after=[mark],
        later=dict(
            state=tokens,
            d_middle_in=between.d_middle,
            g_mlp_gain_in=between.g_mlp_gain,
            mix_gain=mix_gain,
            packed_0=packed_0,
            small_above=between.small,
            packed_1=packed_1,
        ),
    )
    columns_in_0 = share_columns(leave.in_keep, leave.in_send)
    mark = mlp_sum.second(after=[leave.in_send])
    mid_sum = Reduction(
        place,
        partial_grads(
            "grad_mid",
            place,
            {0: rows_0, 1: rows_1},
            {0: columns_0},
            (*mlp_parts, (1, 0, 0, 4 * owned, half + width, 3 * tile)),
            288,
            tile,
            {1: (24 * owned, 4 * owned)},
            after=[mark],
        ),
    )
    small_x = leave.small + other_sequence(leave.small)
    small = small_x + crossed(small_x, 1)
    in_tall, height = 3 * owned, (small.shape[0] - 2 * inner) // 3
    near = {(0, 0, i): item for i, item in enumerate(in_rows_0)}
    near.update({(1, 0, i): item for i, item in enumerate(columns_in_0)})
    last = local_call(
        "grad_in",
        last_grad_kernel(((0, 0, 0, 4 * owned, 0, 3 * tile),)),
        place,
        {**near, **dict(small=small)},
        dict(
            send=((4 * in_tall + height, tile), LOW),
            keep=((4, in_tall, tile), LOW),
            small_keep=((height, tile), LOW),
        ),
        dict(blocks=pltpu.VMEM((2, 4, in_tall, tile), LOW)),
        after=[mid_sum.made.p_send],
    )
    mark = mid_sum.first(after=[last.send])
    step = last_step(place, last.keep, last.small_keep, crossed(last.send, 2), [mark, mlp_sum.three])
    mark = mid_sum.second(after=[step.following])
    step = last_step(place, step.mine, step.small_next, crossed(step.following, 4), [mark])
    sums = dict(small_last=step.small_next, small_x=small_x)
    in_result = (step.mine[0], crossed(step.following, 8))
    routes = [mlp_sum.result, mid_sum.result, in_result]

    made = dict(
        g_mix_gain=((2, width), FULL),
        g_in=((2, owned, 3 * tile), FULL),
        g_taps=((3, 2, 3 * width), FULL),
        g_first=((feats, 2, inner), FULL),
        g_middle=((2, inner, inner), FULL),
        g_last=((2, inner, owned), FULL),
        g_skip=((2, owned), FULL),
        g_out=((2, owned, tile), FULL),
        g_mlp_gain=((2, width), FULL),
        g_up=((2, owned, half), FULL),
        g_down=((2, 4 * owned, tile), FULL),
    )
    in_key, out_key, up_key, down_key = (list(made)[at] for at in (1, 7, 9, 10))
    groups = (
        ((down_key, 1, 4 * owned, 1), (up_key, 1, owned, 4), (out_key, 1, owned, 1)),
        (
            (down_key, 0, 4 * owned, 1),
            (up_key, 0, owned, 4),
            (out_key, 0, owned, 1),
            (in_key, 1, owned, 3),
        ),
        ((in_key, 0, owned, 3),),
    )
    sums.update({(at, i): item for at, route in enumerate(routes) for i, item in enumerate(route)})
    turned = [list(made)[at] for at in (2, 3)]
    made = local_call("collect", collect_kernel(groups, owned), place, sums, made).kept
    for key in turned:
        made[key] = made[key].transpose(1, 0, 2)
    return (upper.next_state[None], leave.upstream[None], *made.values())


def is_fast(mesh):
    return dict(mesh.shape) == dict(dp=2, seq=1 << SEQ_BITS)


def solution(mesh):
    in_specs = (
        P("dp", "seq", None),
        P("dp", "seq", None),
        P(),
        P(),
        P(),
        P(),
        P(),
        P(),
        P(),
        P(),
        P(),
        P(),
        P(),
        P(),
    )
    out_specs = (
        P("dp", "seq", None),
        P("dp", "seq", None),
        P(),
        P(None, "seq", "dp"),
        P(),
        P(),
        P(),
        P(None, None, "seq"),
        P(None, "seq"),
        P(None, "seq", "dp"),
        P(),
        P(None, "seq", "dp"),
        P(None, "seq", "dp"),
    )
    chosen = fast_body if is_fast(mesh) else body
    return jax.shard_map(chosen, mesh=mesh, in_specs=in_specs, out_specs=out_specs, check_vma=False)
```

```python
import functools
import math

import jax
import jax.numpy as jnp
import ml_dtypes
import numpy as np
from jax import lax
from jax.experimental import pallas as pl
from jax.experimental.pallas import tpu as pltpu
from jax.sharding import PartitionSpec as P

FEATS = 33
FFT_COLS = 512


HIGHEST = lax.Precision.HIGHEST
EPSILON = 1e-05


def from_behind(block, axis, distance):
    devices = range(lax.axis_size(axis))
    route = [(i - distance, i) for i in devices if i - distance in devices]
    return lax.ppermute(block, axis, route)


def high_einsum(form, left, right):
    return jnp.einsum(form, left, right, precision=HIGHEST)


def low_einsum(form, left, right):
    return jnp.einsum(form, left, right, preferred_element_type=jnp.float32)


def to_low(value):
    return lax.optimization_barrier(value.astype(jnp.bfloat16))


def angle_table(rows, columns, modulus):
    product = lax.broadcasted_iota(jnp.int32, (rows, columns), 0) * lax.broadcasted_iota(
        jnp.int32, (rows, columns), 1
    )
    angle = (product % modulus).astype(jnp.float32) * (2.0 * math.pi / modulus)
    return (jnp.cos(angle), jnp.sin(angle))


def transform_tables(length, columns):
    total = 2 * length
    rows = total // columns
    cos_rows, sin_rows = angle_table(rows, rows, rows)
    cos_columns, sin_columns = angle_table(columns, columns, columns)
    cos_turn, sin_turn = angle_table(rows, columns, total)
    return (cos_rows, sin_rows, cos_columns, sin_columns, cos_turn, sin_turn)


def forward_transform(signal, tables):
    cos_rows, sin_rows, cos_columns, sin_columns, cos_turn, sin_turn = tables
    channels, length = signal.shape
    rows, columns = cos_turn.shape
    padded = jnp.pad(signal, ((0, 0), (0, length))).reshape(channels, rows, columns)
    first_real = high_einsum("kq,cqp->ckp", cos_rows, padded)
    first_imag = -high_einsum("kq,cqp->ckp", sin_rows, padded)
    turned_real = first_real * cos_turn + first_imag * sin_turn
    turned_imag = first_imag * cos_turn - first_real * sin_turn
    spec_real = high_einsum("ckp,pj->ckj", turned_real, cos_columns) + high_einsum(
        "ckp,pj->ckj", turned_imag, sin_columns
    )
    spec_imag = high_einsum("ckp,pj->ckj", turned_imag, cos_columns) - high_einsum(
        "ckp,pj->ckj", turned_real, sin_columns
    )
    return (spec_real, spec_imag)


def inverse_transform(spec_real, spec_imag, tables):
    cos_rows, sin_rows, cos_columns, sin_columns, cos_turn, sin_turn = tables
    rows, columns = cos_turn.shape
    back_real = high_einsum("ckp,pj->ckj", spec_real, cos_columns) - high_einsum(
        "ckp,pj->ckj", spec_imag, sin_columns
    )
    back_imag = high_einsum("ckp,pj->ckj", spec_imag, cos_columns) + high_einsum(
        "ckp,pj->ckj", spec_real, sin_columns
    )
    turned_real = back_real * cos_turn - back_imag * sin_turn
    turned_imag = back_imag * cos_turn + back_real * sin_turn
    signal = high_einsum("qk,ckp->cqp", cos_rows, turned_real) - high_einsum(
        "qk,ckp->cqp", sin_rows, turned_imag
    )
    total = rows * columns
    return signal.reshape(signal.shape[0], total)[:, : total // 2] / total


def position_features(length):
    count = (FEATS - 1) // 2
    steps = lax.broadcasted_iota(jnp.int32, (count, length), 1)
    frequency = lax.broadcasted_iota(jnp.int32, (count, length), 0) + 1
    angle = (steps * frequency % length).astype(jnp.float32) * (2.0 * math.pi / length)
    ramp = lax.broadcasted_iota(jnp.int32, (1, length), 1).astype(jnp.float32) / length
    return jnp.concatenate([ramp, jnp.cos(angle), jnp.sin(angle)], axis=0)


def filter_forward(features, first, middle, last_columns, rate_columns, length):
    pre_one = high_einsum("fk,ft->kt", first, features)
    act_one = jnp.sin(pre_one)
    pre_two = high_einsum("kj,kt->jt", middle, act_one)
    act_two = jnp.sin(pre_two)
    raw = high_einsum("kc,kt->ct", last_columns, act_two)
    steps = lax.broadcasted_iota(jnp.int32, (1, length), 1).astype(jnp.float32)
    window = jnp.exp(-rate_columns[:, None] * steps) * jnp.sqrt(
        rate_columns[:, None] + 1.0 / length
    )
    return (raw * window, (pre_one, act_one, pre_two, act_two, window))


def filter_backward(d_response, features, middle, last_columns, kept):
    pre_one, act_one, pre_two, act_two, window = kept
    d_raw = d_response * window
    g_last = high_einsum("kt,ct->kc", act_two, d_raw)
    d_two = high_einsum("kc,ct->kt", last_columns, d_raw) * jnp.cos(pre_two)
    g_middle = high_einsum("kt,jt->kj", act_one, d_two)
    d_one = high_einsum("kj,jt->kt", middle, d_two) * jnp.cos(pre_one)
    g_first = high_einsum("ft,kt->fk", features, d_one)
    return (g_first, g_middle, g_last)


def normalize(state):
    centred = state - jnp.mean(state, axis=1, keepdims=True)
    scale = lax.rsqrt(jnp.mean(centred * centred, axis=1, keepdims=True) + EPSILON)
    return (centred * scale, scale)


def normalize_back(d_out, normed, scale, gain):
    d_normed = d_out * gain
    g_gain = jnp.sum(d_out * normed, axis=0)
    d_state = scale * (
        d_normed
        - jnp.mean(d_normed, axis=1, keepdims=True)
        - normed * jnp.mean(d_normed * normed, axis=1, keepdims=True)
    )
    return (d_state, g_gain)


def short_forward(extended, taps):
    length = extended.shape[-1] - 2
    return (
        taps[0] * extended[..., 2:]
        + taps[1] * extended[..., 1 : length + 1]
        + taps[2] * extended[..., :length]
    )


def short_backward(d_extended, taps):
    length = d_extended.shape[-1] - 2
    return (
        taps[0] * d_extended[..., :length]
        + taps[1] * d_extended[..., 1 : length + 1]
        + taps[2] * d_extended[..., 2:]
    )


def tap_grads(d_shorted, extended):
    length = d_shorted.shape[-1]
    return jnp.stack(
        [
            jnp.sum(d_shorted * extended[..., 2 - lag : 2 - lag + length], axis=-1)
            for lag in range(3)
        ]
    )


def long_forward(gated, filter_real, filter_imag, skip_columns, tables):
    signal = gated.astype(jnp.float32)
    sig_real, sig_imag = forward_transform(signal, tables)
    result = inverse_transform(
        sig_real * filter_real - sig_imag * filter_imag,
        sig_real * filter_imag + sig_imag * filter_real,
        tables,
    )
    return (result + skip_columns[:, None] * signal, (sig_real, sig_imag))


def long_backward(d_conv, gated, filter_real, filter_imag, skip_columns, signal_spec, tables):
    d_signal = d_conv.astype(jnp.float32)
    d_real, d_imag = forward_transform(d_signal, tables)
    sig_real, sig_imag = signal_spec
    d_gated = (
        inverse_transform(
            d_real * filter_real + d_imag * filter_imag,
            d_imag * filter_real - d_real * filter_imag,
            tables,
        )
        + skip_columns[:, None] * d_signal
    )
    d_response = inverse_transform(
        d_real * sig_real + d_imag * sig_imag, d_imag * sig_real - d_real * sig_imag, tables
    )
    g_skip = jnp.sum(d_signal * gated.astype(jnp.float32), axis=1)
    return (d_gated, d_response, g_skip)


def unit(k,n):
    k%=n
    if (4*k)%n==0:
        q=(4*k)//n
        return [(1.0,0.0),(0.0,-1.0),(-1.0,0.0),(0.0,1.0)][q]
    a=-2.0*math.pi*k/n
    return (math.cos(a),math.sin(a))
def times(z,w):
    re,im=z; c,s=w
    if s==0.0: return (re,im) if c==1.0 else (-re,-im)
    if c==0.0: return (-im,re) if s==1.0 else (im,-re)
    return (re*c-im*s, re*s+im*c)
def plus(a,b): return (a[0]+b[0],a[1]+b[1])
def minus(a,b): return (a[0]-b[0],a[1]-b[1])
def complex_dft(zs,sign):
    n=len(zs)
    if n==1: return zs
    ev=complex_dft(zs[0::2],sign); od=complex_dft(zs[1::2],sign)
    lo,hi=[],[]
    for k in range(n//2):
        v=times(od[k],unit(sign*k,n))
        lo.append(plus(ev[k],v)); hi.append(minus(ev[k],v))
    return lo+hi
def odd_bins(xs):
    n=len(xs); h=n//2; N=2*n
    zs=[times((xs[j],-xs[j+h]),unit(j,N)) for j in range(h)]
    bins={}
    for q,z in enumerate(complex_dft(zs,1)):
        k=4*q+1
        if k<=n: bins[k]=z
        else: bins[N-k]=(z[0],-z[1])
    return bins
def real_bins(xs):
    n=len(xs)
    if n==1: return {0:(xs[0],None)}
    if n==2: return {0:(xs[0]+xs[1],None),1:(xs[0]-xs[1],None)}
    h=n//2
    bins={2*k:z for k,z in real_bins([xs[j]+xs[j+h] for j in range(h)]).items()}
    bins.update(odd_bins([xs[j]-xs[j+h] for j in range(h)]))
    return bins
def padded_bins(xs):
    bins={2*k:z for k,z in real_bins(xs).items()}
    bins.update(odd_bins(xs))
    return bins
def odd_back(bins,n):
    h=n//2; N=2*n
    zs=[]
    for q in range(h):
        k=4*q+1
        if k<=n: zs.append(bins[k])
        else:
            re,im=bins[N-k]; zs.append((re,-im))
    vs=[times(z,unit(-j,N)) for j,z in enumerate(complex_dft(zs,-1))]
    return [v[0] for v in vs]+[-v[1] for v in vs]
def real_back(bins,n):
    if n==1: return [bins[0][0]]
    if n==2: return [bins[0][0]+bins[1][0],bins[0][0]-bins[1][0]]
    h=n//2
    ev=real_back({k//2:z for k,z in bins.items() if k%2==0},h)
    od=odd_back(bins,h)
    return [ev[j]+od[j] for j in range(h)]+[ev[j]-od[j] for j in range(h)]
def padded_back(bins,n):
    ev=real_back({k//2:z for k,z in bins.items() if k%2==0},n)
    od=odd_back(bins,n)
    return [a+b for a,b in zip(ev,od)]


def turn_table(shards, rows):
    total = 2 * shards * rows
    early = np.arange(rows)[None, :, None]
    late = np.arange(rows)[None, None, :]
    bins = np.arange(shards + 1)[:, None, None]
    angle = (early * (bins + 2 * shards * late) % total) * (2.0 * np.pi / total)
    cos, sin = np.cos(angle), np.sin(angle)
    top = np.concatenate([cos, -sin], axis=2)
    bottom = np.concatenate([sin, cos], axis=2)
    return jnp.asarray(np.concatenate([top, bottom], axis=1).astype(ml_dtypes.bfloat16))


def position_table(length):
    count = (FEATS - 1) // 2
    steps = np.arange(length)[None, :]
    angle = (steps * np.arange(1, count + 1)[:, None] % length) * (2.0 * np.pi / length)
    table = np.concatenate([steps / length, np.cos(angle), np.sin(angle)], axis=0)
    return jnp.asarray(table.astype(np.float32))


def chunks_of(channels):
    step = 16 if channels % 16 == 0 else channels
    return [slice(at, at + step) for at in range(0, channels, step)]


def load_bins(blocks, bins_ref, chunk):
    lanes = blocks[0].shape[-1]
    for k, (re, im) in padded_bins(blocks).items():
        im = jnp.zeros_like(re) if im is None else im
        bins_ref[k, chunk, :lanes] = re.astype(jnp.bfloat16)
        bins_ref[k, chunk, lanes:] = im.astype(jnp.bfloat16)


def fold_bins(back_ref, chunk, count, lanes):
    bins = {
        k: (back_ref[k, chunk, :lanes], back_ref[k, chunk, lanes:]) for k in range(count + 1)
    }
    return padded_back(bins, count)


def bin_scale(k, shards, rows):
    total = 2 * shards * rows
    return (1.0 if k in (0, shards) else 2.0) / total


def bin_product(left, right, conjugate):
    lanes = left.shape[1] // 2
    a, b = left[:, :lanes], left[:, lanes:]
    c, d = right[:, :lanes], right[:, lanes:]
    if conjugate:
        return jnp.concatenate([a * c + b * d, b * c - a * d], axis=1)
    return jnp.concatenate([a * c - b * d, a * d + b * c], axis=1)


def turn(left, table):
    return jnp.dot(left, table, preferred_element_type=jnp.float32)


def turn_back(left, table):
    return lax.dot_general(
        left.astype(jnp.bfloat16),
        table,
        (((1,), (1,)), ((), ())),
        preferred_element_type=jnp.float32,
    )


def sin_cos(angle):
    steps = jnp.floor(angle * (2.0 / math.pi) + 0.5)
    rest = angle - steps * 1.5703125
    rest = rest - steps * 4.837512969970703e-4
    rest = rest - steps * 7.549789954891882e-8
    square = rest * rest
    sin = rest + rest * square * (
        -1.6666654611e-1 + square * (8.3321608736e-3 + square * -1.9515295891e-4)
    )
    cos = (
        1.0
        - 0.5 * square
        + square
        * square
        * (4.166664568298827e-2 + square * (-1.388731625493765e-3 + square * 2.443315711809948e-5))
    )
    quarter = steps.astype(jnp.int32)
    odd = (quarter & 1) == 1
    sin_out = jnp.where(odd, cos, sin)
    cos_out = jnp.where(odd, sin, cos)
    sin_out = jnp.where((quarter & 2) == 2, -sin_out, sin_out)
    cos_out = jnp.where(((quarter + 1) & 2) == 2, -cos_out, cos_out)
    return sin_out, cos_out


def across(left, right, left_side, right_side):
    return lax.dot_general(
        left,
        right,
        (((left_side,), (right_side,)), ((), ())),
        precision=HIGHEST,
        preferred_element_type=jnp.float32,
    )


def filter_network_kernel(
    feature_ref,
    first_ref,
    middle_ref,
    last_ref,
    rate_ref,
    table_ref,
    spec_ref,
    one_ref,
    slope_one_ref,
    two_ref,
    slope_two_ref,
    window_ref,
    raw_ref,
    bins_ref,
):
    shards, channels, rows = window_ref.shape
    one, slope_one = sin_cos(across(first_ref[...], feature_ref[...], 0, 0))
    one_ref[...] = one
    slope_one_ref[...] = slope_one
    two, slope_two = sin_cos(across(middle_ref[...], one, 0, 0))
    two_ref[...] = two
    slope_two_ref[...] = slope_two
    raw_ref[...] = across(last_ref[...], two, 0, 0)
    rate = rate_ref[...]
    size = jnp.sqrt(rate + 1.0 / (shards * rows))
    step = lax.broadcasted_iota(jnp.int32, (channels, rows), 1)
    for j in range(shards):
        window = jnp.exp(-rate * (step + j * rows).astype(jnp.float32)) * size
        window_ref[j] = window
        at = slice(j * rows, (j + 1) * rows)
        raw_ref[:, at] = raw_ref[:, at] * window
    for chunk in chunks_of(channels):
        load_bins(
            [raw_ref[chunk, j * rows : (j + 1) * rows] for j in range(shards)], bins_ref, chunk
        )
    for k in range(shards + 1):
        spec_ref[k] = turn(bins_ref[k], table_ref[k]) * bin_scale(k, shards, rows)


def filter_network(features, first, middle, last, rates, table):
    hidden, channels = last.shape
    length = features.shape[1]
    bins, span, _ = table.shape
    rows = span // 2
    shards = length // rows
    wide = jax.ShapeDtypeStruct((hidden, length), jnp.float32)
    return pl.pallas_call(
        filter_network_kernel,
        out_shape=[
            jax.ShapeDtypeStruct((bins, channels, span), jnp.float32),
            wide,
            wide,
            wide,
            wide,
            jax.ShapeDtypeStruct((shards, channels, rows), jnp.float32),
        ],
        scratch_shapes=[
            pltpu.VMEM((channels, length), jnp.float32),
            pltpu.VMEM((bins, channels, span), jnp.bfloat16),
        ],
        compiler_params=pltpu.CompilerParams(vmem_limit_bytes=40 << 20),
        name="filter_network",
    )(features, first, middle, last, rates, table)


def conv_forward_kernel(
    gated_ref, filter_ref, skip_ref, table_ref, conv_ref, spec_ref, bins_ref, back_ref
):
    shards, channels, rows = gated_ref.shape
    for chunk in chunks_of(channels):
        load_bins(
            [gated_ref[j, chunk].astype(jnp.float32) for j in range(shards)], bins_ref, chunk
        )
    for k in range(shards + 1):
        spec = turn(bins_ref[k], table_ref[k])
        spec_ref[k] = spec.astype(jnp.bfloat16)
        back_ref[k] = turn_back(bin_product(spec, filter_ref[k], False), table_ref[k])
    for chunk in chunks_of(channels):
        skip = skip_ref[chunk]
        for j, block in enumerate(fold_bins(back_ref, chunk, shards, rows)):
            conv = block + skip * gated_ref[j, chunk].astype(jnp.float32)
            conv_ref[j, chunk] = conv.astype(jnp.bfloat16)


def conv_backward_kernel(
    gated_ref, filter_ref, skip_ref, table_ref, conv_ref, spec_ref, bins_ref, back_ref
):
    shards, channels, rows = gated_ref.shape
    for chunk in chunks_of(channels):
        load_bins(
            [gated_ref[j, chunk].astype(jnp.float32) for j in range(shards)], bins_ref, chunk
        )
    for k in range(shards + 1):
        spec = turn(bins_ref[k], table_ref[k])
        spec_ref[k] = spec.astype(jnp.bfloat16)
        back_ref[k] = turn_back(bin_product(spec, filter_ref[k], True), table_ref[k])
    for chunk in chunks_of(channels):
        skip = skip_ref[chunk]
        for j, block in enumerate(fold_bins(back_ref, chunk, shards, rows)):
            conv = block + skip * gated_ref[j, chunk].astype(jnp.float32)
            conv_ref[j, chunk] = conv.astype(jnp.bfloat16)


def conv_call(kernel, name, gated, filter_spec, skip, table):
    bins, channels, span = filter_spec.shape
    return pl.pallas_call(
        kernel,
        out_shape=[
            jax.ShapeDtypeStruct(gated.shape, jnp.bfloat16),
            jax.ShapeDtypeStruct((bins, channels, span), jnp.bfloat16),
        ],
        scratch_shapes=[
            pltpu.VMEM((bins, channels, span), jnp.bfloat16),
            pltpu.VMEM((bins, channels, span), jnp.float32),
        ],
        compiler_params=pltpu.CompilerParams(vmem_limit_bytes=40 << 20),
        name=name,
    )(gated, filter_spec, skip, table)


def conv_forward(gated, filter_spec, skip, table):
    return conv_call(conv_forward_kernel, "conv_forward", gated, filter_spec, skip, table)


def conv_backward(d_conv, filter_spec, skip, table):
    return conv_call(conv_backward_kernel, "conv_backward", d_conv, filter_spec, skip, table)


def filter_back_kernel(
    d_spec_ref,
    spec_ref,
    d_conv_ref,
    gated_ref,
    feature_ref,
    middle_ref,
    last_ref,
    one_ref,
    slope_one_ref,
    two_ref,
    slope_two_ref,
    window_ref,
    table_ref,
    g_first_ref,
    g_middle_ref,
    g_last_ref,
    g_skip_ref,
    back_ref,
    raw_ref,
):
    shards, channels, rows = d_conv_ref.shape
    for k in range(shards + 1):
        spec = bin_product(
            d_spec_ref[k].astype(jnp.float32), spec_ref[k].astype(jnp.float32), True
        )
        back_ref[k] = turn_back(spec * bin_scale(k, shards, rows), table_ref[k])
    for chunk in chunks_of(channels):
        total = None
        for j, block in enumerate(fold_bins(back_ref, chunk, shards, rows)):
            raw_ref[chunk, j * rows : (j + 1) * rows] = block * window_ref[j, chunk]
            term = d_conv_ref[j, chunk].astype(jnp.float32) * gated_ref[j, chunk].astype(
                jnp.float32
            )
            total = term if total is None else total + term
        g_skip_ref[chunk] = jnp.sum(total, axis=1, keepdims=True)
    d_raw = raw_ref[...]
    g_last_ref[...] = across(two_ref[...], d_raw, 1, 1)
    d_two = across(last_ref[...], d_raw, 1, 0) * slope_two_ref[...]
    g_middle_ref[...] = across(one_ref[...], d_two, 1, 1)
    d_one = across(middle_ref[...], d_two, 1, 0) * slope_one_ref[...]
    g_first_ref[...] = across(feature_ref[...], d_one, 1, 1)


def filter_network_back(
    d_spec, spec, d_conv, gated, features, middle, last, kept, table
):
    _, one, slope_one, two, slope_two, window = kept
    bins, channels, span = spec.shape
    hidden, length = one.shape
    feats = features.shape[0]
    return pl.pallas_call(
        filter_back_kernel,
        out_shape=[
            jax.ShapeDtypeStruct((feats, hidden), jnp.float32),
            jax.ShapeDtypeStruct((hidden, hidden), jnp.float32),
            jax.ShapeDtypeStruct((hidden, channels), jnp.float32),
            jax.ShapeDtypeStruct((channels, 1), jnp.float32),
        ],
        scratch_shapes=[
            pltpu.VMEM((bins, channels, span), jnp.float32),
            pltpu.VMEM((channels, length), jnp.float32),
        ],
        compiler_params=pltpu.CompilerParams(vmem_limit_bytes=40 << 20),
        name="filter_network_back",
    )(
        d_spec,
        spec,
        d_conv,
        gated,
        features,
        middle,
        last,
        one,
        slope_one,
        two,
        slope_two,
        window,
        table,
    )


def layer_forward(state, weights, setting):
    (
        mix_gain,
        in_proj,
        short_taps,
        first,
        middle,
        last,
        skip,
        rates,
        out_proj,
        mlp_gain,
        up_proj,
        down_proj,
    ) = weights
    features, tables, offset = setting
    rows, width = state.shape
    length = features.shape[1]
    channels = width // (length // rows)
    normed_mix, scale_mix = normalize(state)
    u_mix = to_low(normed_mix * mix_gain)
    projected = to_low(low_einsum("td,dc->ct", u_mix, in_proj)).reshape(3, width, rows)
    last_columns = lax.dynamic_slice_in_dim(last, offset, channels, 1)
    skip_columns = lax.dynamic_slice_in_dim(skip, offset, channels, 0)
    rate_columns = lax.dynamic_slice_in_dim(rates, offset, channels, 0)
    filter_kept = filter_network(
        features, first, middle, last_columns, rate_columns[:, None], tables
    )
    filter_spec = filter_kept[0]
    taps = short_taps.reshape(3, 3, width)
    edge = from_behind(projected[:, :, rows - 2 :], "seq", 1)
    extended = jnp.concatenate([edge, projected], axis=2).astype(jnp.float32)
    tap_use = taps[:, :, :, None]
    shorted = short_forward(extended, tap_use)
    gated_rows = to_low(shorted[2] * shorted[1])
    shards = length // rows
    gated = lax.all_to_all(
        gated_rows.reshape(shards, channels, rows), "seq", split_axis=0, concat_axis=0, tiled=True
    )
    conv_low, signal_spec = conv_forward(gated, filter_spec, skip_columns[:, None], tables)
    conv_here = lax.all_to_all(
        conv_low, "seq", split_axis=0, concat_axis=0, tiled=True
    ).reshape(width, rows)
    mixed = to_low(conv_here.astype(jnp.float32) * shorted[0])
    middle_state = state + low_einsum("ct,ce->te", mixed, out_proj)
    normed_mlp, scale_mlp = normalize(middle_state)
    u_mlp = to_low(normed_mlp * mlp_gain)
    hidden = low_einsum("td,df->tf", u_mlp, up_proj)
    active = to_low(jax.nn.gelu(hidden))
    result = middle_state + low_einsum("tf,fe->te", active, down_proj)
    kept = (
        normed_mix,
        scale_mix,
        u_mix,
        extended,
        shorted,
        gated,
        conv_here,
        mixed,
        filter_kept,
        filter_spec,
        signal_spec,
        normed_mlp,
        scale_mlp,
        u_mlp,
        hidden,
        active,
        last_columns,
        skip_columns,
        tap_use,
    )
    return (result, kept)


def layer_backward(upstream, kept, weights, setting):
    (
        mix_gain,
        in_proj,
        short_taps,
        first,
        middle,
        last,
        skip,
        rates,
        out_proj,
        mlp_gain,
        up_proj,
        down_proj,
    ) = weights
    features, tables, offset = setting
    (
        normed_mix,
        scale_mix,
        u_mix,
        extended,
        shorted,
        gated,
        conv_here,
        mixed,
        filter_kept,
        filter_spec,
        signal_spec,
        normed_mlp,
        scale_mlp,
        u_mlp,
        hidden,
        active,
        last_columns,
        skip_columns,
        tap_use,
    ) = kept
    rows, width = upstream.shape
    d_down = to_low(upstream)
    g_down = low_einsum("tf,te->fe", active, d_down)
    d_active = low_einsum("te,fe->tf", d_down, down_proj)
    d_hidden = to_low(jax.vjp(jax.nn.gelu, hidden)[1](d_active)[0])
    g_up = low_einsum("td,tf->df", u_mlp, d_hidden)
    d_u_mlp = low_einsum("tf,df->td", d_hidden, up_proj)
    d_middle, g_mlp_gain = normalize_back(d_u_mlp, normed_mlp, scale_mlp, mlp_gain)
    d_middle = d_middle + upstream
    d_branch = to_low(d_middle)
    g_out = low_einsum("ct,te->ce", mixed, d_branch)
    d_mixed = to_low(low_einsum("te,ce->ct", d_branch, out_proj))
    d_mixed_wide = d_mixed.astype(jnp.float32)
    d_conv_rows = to_low(d_mixed_wide * shorted[0])
    d_zero = d_mixed_wide * conv_here.astype(jnp.float32)
    shards, channels, _ = gated.shape
    d_conv = lax.all_to_all(
        d_conv_rows.reshape(gated.shape), "seq", split_axis=0, concat_axis=0, tiled=True
    )
    d_gated, d_spec = conv_backward(d_conv, filter_spec, skip_columns[:, None], tables)
    d_gated_rows = lax.all_to_all(
        d_gated, "seq", split_axis=0, concat_axis=0, tiled=True
    ).reshape(width, rows).astype(jnp.float32)
    d_shorted = jnp.stack([d_zero, d_gated_rows * shorted[2], d_gated_rows * shorted[1]])
    after = from_behind(d_shorted[:, :, :2], "seq", -1)
    d_extended = jnp.concatenate([d_shorted, after], axis=2)
    d_projected = to_low(short_backward(d_extended, tap_use))
    g_taps = tap_grads(d_shorted, extended)
    g_first, g_middle, g_last, g_skip = filter_network_back(
        d_spec, signal_spec, d_conv, gated, features, middle, last_columns, filter_kept, tables
    )
    g_skip = g_skip[:, 0]
    d_flat = d_projected.reshape(3 * width, rows)
    g_in = low_einsum("td,ct->dc", u_mix, d_flat)
    d_u_mix = low_einsum("ct,dc->td", d_flat, in_proj)
    d_state, g_mix_gain = normalize_back(d_u_mix, normed_mix, scale_mix, mix_gain)
    d_state = d_state + d_middle
    large = (g_in, g_out, g_up, g_down)
    small = (g_mix_gain, g_taps.reshape(3, 3 * width), g_first, g_middle, g_mlp_gain)
    column_part = (g_last, g_skip)
    return (d_state, large, small, column_part)


def body(
    tokens,
    cotangent,
    mix_gain,
    in_proj,
    short_taps,
    filter_first,
    filter_middle,
    filter_last,
    filter_skip,
    decay_rates,
    out_proj,
    mlp_gain,
    up_proj,
    down_proj,
):
    rows = tokens.shape[1]
    width = tokens.shape[2]
    layer_count = mix_gain.shape[0]
    shards = lax.axis_size("seq")
    length = rows * shards
    offset = lax.axis_index("seq") * (width // shards)
    setting = (position_table(length), turn_table(shards, rows), offset)
    stacks = (
        mix_gain,
        in_proj,
        short_taps,
        filter_first,
        filter_middle,
        filter_last,
        filter_skip,
        decay_rates,
        out_proj,
        mlp_gain,
        up_proj,
        down_proj,
    )
    state = tokens[0].astype(jnp.float32)
    kept_all = []
    for level in range(layer_count):
        weights = tuple((item[level] for item in stacks))
        state, kept = layer_forward(state, weights, setting)
        kept_all.append(kept)
    upstream = cotangent[0].astype(jnp.float32)
    large_all = [None] * layer_count
    small_all = [None] * layer_count
    column_all = [None] * layer_count
    for level in reversed(range(layer_count)):
        weights = tuple((item[level] for item in stacks))
        upstream, large, small, column_part = layer_backward(
            upstream, kept_all[level], weights, setting
        )
        large_all[level] = large
        small_all[level] = small
        column_all[level] = column_part
    stacked_large = [
        jnp.stack([large_all[level][member] for level in range(layer_count)]) for member in range(4)
    ]
    row_in, row_out, row_up, row_down = (
        lax.psum_scatter(stacked_large[0], "seq", scatter_dimension=1, tiled=True),
        lax.psum_scatter(stacked_large[1], "seq", scatter_dimension=1, tiled=True),
        lax.psum_scatter(stacked_large[2], "seq", scatter_dimension=1, tiled=True),
        lax.psum_scatter(stacked_large[3], "seq", scatter_dimension=1, tiled=True),
    )
    g_in, g_out, g_up, g_down = (
        lax.psum_scatter(row_in.astype(jnp.bfloat16), "dp", scatter_dimension=2, tiled=True).astype(
            jnp.float32
        ),
        lax.psum_scatter(
            row_out.astype(jnp.bfloat16), "dp", scatter_dimension=2, tiled=True
        ).astype(jnp.float32),
        lax.psum_scatter(row_up.astype(jnp.bfloat16), "dp", scatter_dimension=2, tiled=True).astype(
            jnp.float32
        ),
        lax.psum_scatter(
            row_down.astype(jnp.bfloat16), "dp", scatter_dimension=2, tiled=True
        ).astype(jnp.float32),
    )
    stacked_small = [
        jnp.stack([small_all[level][member] for level in range(layer_count)]) for member in range(5)
    ]
    g_mix_gain, g_taps, g_first, g_middle, g_mlp_gain = lax.psum(
        (stacked_small[0], stacked_small[1], stacked_small[2], stacked_small[3], stacked_small[4]),
        ("dp", "seq"),
    )
    stacked_last = jnp.stack([column_all[level][0] for level in range(layer_count)])
    stacked_skip = jnp.stack([column_all[level][1] for level in range(layer_count)])
    g_last, g_skip = lax.psum((stacked_last, stacked_skip), "dp")
    return (
        state[None],
        upstream[None],
        g_mix_gain,
        g_in,
        g_taps,
        g_first,
        g_middle,
        g_last,
        g_skip,
        g_out,
        g_mlp_gain,
        g_up,
        g_down,
    )


SEQ_BITS = 4
VMEM_BYTES = 64 << 20
COST = 3000
LOW, FULL = jnp.bfloat16, jnp.float32


class Board:
    def __init__(self, place, held, inputs, outputs, later):
        self.place = place
        self.held, self.arriving, self.outputs, self.leaving = held, {}, outputs, []
        self.later = {}
        for key, (source, target, sem) in inputs.items():
            copy = pltpu.make_async_copy(source, target, sem)
            if key in later:
                self.later[key] = copy
            else:
                copy.start()
                self.arriving[key] = copy
            held[key] = target
        for key, (source, _, _) in outputs.items():
            held[key] = source

    def begin(self):
        for key, copy in self.later.items():
            copy.start()
            self.arriving[key] = copy
        self.later = {}

    def __getattr__(self, key):
        return self[key]

    def __getitem__(self, key):
        if key in self.later:
            self.begin()
        if key in self.arriving:
            self.arriving.pop(key).wait()
        return self.held[key]

    def flush(self, *refs):
        for key in [key for key, item in self.outputs.items() if any(item[0] is ref for ref in refs)]:
            copy = pltpu.make_async_copy(*self.outputs.pop(key))
            copy.start()
            self.leaving.append(copy)

    def finish(self):
        self.begin()
        self.flush(*[item[0] for item in self.outputs.values()])
        for copy in [*self.arriving.values(), *self.leaving]:
            copy.wait()


class Made:
    def __init__(self, items):
        self.__dict__.update(kept=dict(items))

    def __getattr__(self, key):
        return self.kept[key]

    def __getitem__(self, key):
        return self.kept[key]


class Renamed:
    def __init__(self, board, **names):
        self.__dict__.update(board=board, names=names)

    def __getattr__(self, key):
        return getattr(self.__dict__["board"], self.__dict__["names"].get(key, key))


def local_call(
    name,
    body,
    place,
    near,
    outputs,
    scratch=None,
    far=None,
    cuts=None,
    after=(),
    later=None,
):
    scratch, far, cuts, later = scratch or {}, far or {}, cuts or {}, later or {}
    near = {**near, **later}
    arrays = [*near.values(), *far.values(), *after]

    def shape_of(key):
        shape = list(near[key].shape)
        if key in cuts:
            shape[1] = cuts[key][1]
        return tuple(shape)

    def cut(key, ref):
        return ref.at[:, pl.ds(*cuts[key])] if key in cuts else ref

    def kernel(*refs):
        refs = list(refs)
        place_ref = refs.pop(0)
        given = [refs.pop(0) for _ in arrays]
        made = [refs.pop(0) for _ in outputs]
        here = [refs.pop(0) for _ in near]
        staged = [refs.pop(0) for _ in outputs]
        spare = [refs.pop(0) for _ in scratch]
        sems_in, sems_out = refs
        held = dict(zip(far, given[len(near) :]))
        held.update(zip(scratch, spare))
        board = Board(
            place_ref,
            held,
            {key: (cut(key, given[at]), here[at], sems_in.at[at]) for at, key in enumerate(near)},
            {key: (staged[at], made[at], sems_out.at[at]) for at, key in enumerate(outputs)},
            later,
        )
        body(board)
        board.finish()

    made = pl.pallas_call(
        kernel,
        in_specs=[pl.BlockSpec(memory_space=pltpu.SMEM)]
        + [pl.BlockSpec(memory_space=pltpu.HBM)] * len(arrays),
        out_specs=[pl.BlockSpec(memory_space=pltpu.HBM)] * len(outputs),
        out_shape=[jax.ShapeDtypeStruct(*item) for item in outputs.values()],
        scratch_shapes=[pltpu.VMEM(shape_of(key), near[key].dtype) for key in near]
        + [pltpu.VMEM(*item) for item in outputs.values()]
        + list(scratch.values())
        + [
            pltpu.SemaphoreType.DMA((max(len(near), 1),)),
            pltpu.SemaphoreType.DMA((max(len(outputs), 1),)),
        ],
        compiler_params=pltpu.CompilerParams(vmem_limit_bytes=VMEM_BYTES),
        cost_estimate=pl.CostEstimate(flops=0, bytes_accessed=COST, transcendentals=0),
        name=name,
    )(place, *arrays)
    return Made(zip(outputs, made, strict=True))


class Weights:
    def __init__(self, slots, sems):
        self.slots, self.sems, self.copies = slots, sems, []

    def fetch(self, source):
        at = len(self.copies)
        copy = pltpu.make_async_copy(source, self.slots.at[at], self.sems.at[at])
        copy.start()
        self.copies.append(copy)
        return at

    def fetch_columns(self, source, width):
        count = source.shape[1] // width
        return [self.fetch(source.at[:, pl.ds(j * width, width)]) for j in range(count)]

    def fetch_rows(self, source, width):
        count = source.shape[0] // width
        return [self.fetch(source.at[pl.ds(j * width, width)]) for j in range(count)]

    def wait(self, at):
        if self.copies[at] is not None:
            self.copies[at].wait()
            self.copies[at] = None
        return self.slots[at]


def dot(left, right):
    return jnp.dot(left, right, preferred_element_type=jnp.float32)


def dot_rows(left, right):
    return lax.dot_general(
        left, right, (((1,), (1,)), ((), ())), preferred_element_type=jnp.float32
    )


def low_across(left, right, left_side, right_side):
    return lax.dot_general(
        narrow(left),
        narrow(right),
        (((left_side,), (right_side,)), ((), ())),
        preferred_element_type=jnp.float32,
    )


def flip(block):
    return block.T


def wide(value):
    return value.astype(jnp.float32)


def narrow(value):
    return value.astype(jnp.bfloat16)


def rotate(block, shift):
    return pltpu.roll(block, shift % block.shape[1], 1)


def shifted_down(block, edge):
    row = lax.broadcasted_iota(jnp.int32, block.shape, 0)
    one = jnp.where(row == 0, edge[1:2], pltpu.roll(block, 1, 0))
    two = jnp.where(row == 0, edge[0:1], jnp.where(row == 1, edge[1:2], pltpu.roll(block, 2, 0)))
    return one, two


def shifted_up(block, edge):
    rows = block.shape[0]
    row = lax.broadcasted_iota(jnp.int32, block.shape, 0)
    one = jnp.where(row == rows - 1, edge[0:1], pltpu.roll(block, rows - 1, 0))
    two = jnp.where(
        row == rows - 1,
        edge[1:2],
        jnp.where(row == rows - 2, edge[0:1], pltpu.roll(block, rows - 2, 0)),
    )
    return one, two


def branch_columns(r, branch):
    width = r.projected.shape[1] // 3
    return slice(branch * width, (branch + 1) * width)


def taps_of(r, level, branch):
    width = r.short_taps.shape[2] // 3
    at = slice(branch * width, (branch + 1) * width)
    return [r.short_taps[lag, level : level + 1, at] for lag in range(3)]


def lagged(r, branch):
    block = wide(r.projected[:, branch_columns(r, branch)])
    return (block, *shifted_down(block, r.edge[2 * branch : 2 * branch + 2]))


def tapped(taps, items):
    return taps[0] * items[0] + taps[1] * items[1] + taps[2] * items[2]


def short_branch(r, level, branch):
    return tapped(taps_of(r, level, branch), lagged(r, branch))


def short_ahead(r, level, branch):
    here = wide(r.projected[-16:, branch_columns(r, branch)])[-2:]
    ahead = r.ahead[2 * branch : 2 * branch + 2]
    taps = taps_of(r, level, branch)
    first = tapped(taps, (ahead[0:1], here[1:2], here[0:1]))
    return first, tapped(taps, (ahead[1:2], ahead[0:1], here[1:2]))


def norm_rows(state):
    centred = state - jnp.mean(state, axis=1, keepdims=True)
    scale = lax.rsqrt(jnp.mean(centred * centred, axis=1, keepdims=True) + EPSILON)
    return centred * scale, scale


def norm_rows_back(d_out, normed, scale, gain):
    q = d_out * gain
    return scale * (
        q
        - jnp.mean(q, axis=1, keepdims=True)
        - normed * jnp.mean(q * normed, axis=1, keepdims=True)
    )


def gelu_and_slope(x):
    square = x * x
    tanh = jnp.tanh(x * (0.7978845608028654 + 0.035677408136300125 * square))
    half = 0.5 + 0.5 * tanh
    inner = 0.7978845608028654 + 0.10703222440890037 * square
    return x * half, half + 0.5 * x * (1.0 - tanh * tanh) * inner


def store_rows(target, start, first_block, block_rows, flipped):
    for j in range(flipped.shape[0] // block_rows):
        owner = first_block + j
        z, y, core = owner >> 2, (owner >> 1) & 1, owner & 1
        at = start + z * block_rows
        target[core, y, at : at + block_rows] = flipped[j * block_rows : (j + 1) * block_rows]


def store_line(target, line, vector):
    lanes = target.shape[1]
    pieces = vector.shape[1] // lanes
    for j in range(pieces):
        target[line * pieces + j : line * pieces + j + 1] = vector[:, j * lanes : (j + 1) * lanes]


def store_blocks(target, flipped, ends):
    owned = flipped.shape[0] >> SEQ_BITS
    lanes = target.shape[2]
    lane = lax.broadcasted_iota(jnp.int32, (ends.shape[0], lanes), 1)
    for j in range(1 << SEQ_BITS):
        target[j, :owned] = flipped[j * owned : (j + 1) * owned]
        beside = rotate(ends, -j * owned)[:, :lanes]
        target[j, owned:] = narrow(jnp.where(lane < owned, beside, 0.0))


def mix_forward(r, level, state, weights, squares, gain):
    normed, _ = norm_rows(state)
    u = narrow(normed * gain)
    rows, width = u.shape
    owned = width >> SEQ_BITS
    nothing = jnp.zeros((2, width), jnp.float32)
    r.ends[...] = jnp.zeros_like(r.ends)
    gate = None
    for branch in (1, 2, 0):
        block = narrow(dot(u, weights.wait(squares[branch])))
        r.next_projected[:, branch * width : (branch + 1) * width] = block
        block = wide(block)
        at = slice(2 * branch, 2 * branch + 2)
        r.next_head[at], r.next_tail[at] = block[:2], block[-2:]
        if branch > 0:
            spot = 4 * branch - 4
            r.ends[spot : spot + 2], r.ends[spot + 2 : spot + 4] = block[:2], block[-2:]
            items = (block, *shifted_down(block, nothing))
            part = tapped(taps_of(r, level, branch), items)
            gate = part if gate is None else gate * part
        if branch == 2:
            store_blocks(r.next_gated, flip(narrow(gate)), r.ends[...])
            r.flush(r.next_gated)
    r.next_head[6:] = jnp.zeros_like(r.next_head[6:])
    r.next_tail[6:] = jnp.zeros_like(r.next_tail[6:])
    r.flush(r.next_projected, r.next_head, r.next_tail)
    store_rows(r.next_rows, 0, 0, owned, flip(u))


def enter_kernel(r):
    weights = Weights(r.slots, r.sems)
    squares = weights.fetch_columns(r.in_proj.at[0], r.tokens.shape[1])
    r.begin()
    mix_forward(r, 0, wide(r.tokens[...]), weights, squares, r.mix_gain[0:1])


def after_conv(r, level, weights, squares, pieces):
    out_square, ups, downs = squares
    rows, width = r.state.shape
    owned = width >> SEQ_BITS
    conv = flip(r.conv[...].reshape(width, rows))
    r.conv_rows[...] = conv
    r.flush(r.conv_rows)
    mixed = narrow(wide(conv) * short_branch(r, level, 0))
    middle = wide(r.state[...]) + dot(mixed, weights.wait(out_square))
    r.middle[...] = middle
    r.flush(r.middle)
    normed, _ = norm_rows(middle)
    u = narrow(normed * r.mlp_gain[level : level + 1])
    hidden = dot(u, weights.wait(ups[0]))
    total = middle
    for j, down in enumerate(downs):
        following = weights.wait(ups[j + 1]) if j + 1 < len(ups) else None
        down = weights.wait(down)
        coming = None if following is None else dot(u, following)
        active, slope = gelu_and_slope(hidden)
        r.slope[:, j * width : (j + 1) * width] = narrow(slope)
        active = narrow(active)
        total = total + dot(active, down)
        store_rows(r.all_rows, 0, 4 * j, 4 * owned, flip(active))
        hidden = coming
    store_rows(r.all_rows, 4 * 4 * owned, 0, owned, flip(u))
    store_rows(r.all_rows, 5 * 4 * owned, 0, owned, flip(mixed))
    for core in range(2):
        for y in range(2):
            r.all_rows[core, y, 6 * 4 * owned :] = r.rows[core, y]
    core = r.place[1]
    for keep, send, start, count in pieces:
        r[send][...] = r.all_rows[1 - core, :, start : start + count]
        r[keep][...] = r.all_rows[core, :, start : start + count]
    return total


def before_conv_back(r, level, upstream, weights, squares):
    out_square, ups, downs = squares
    rows, width = upstream.shape
    half, wide_half = width // 2, 2 * width
    d_down = narrow(upstream)
    middle = r.middle[...]
    normed, scale = norm_rows(middle)
    d_u = jnp.zeros_like(middle)
    d_active = dot_rows(d_down, weights.wait(downs[0]))
    for j, up in enumerate(ups):
        following = weights.wait(downs[j + 1]) if j + 1 < len(downs) else None
        up = weights.wait(up)
        coming = None if following is None else dot_rows(d_down, following)
        d_hidden = narrow(d_active * wide(r.slope[:, j * width : (j + 1) * width]))
        side, at = divmod(j * width, wide_half)
        r.all_columns[side, :, at : at + width] = d_hidden
        d_u = d_u + dot_rows(d_hidden, up)
        d_active = coming
    r.g_mlp_gain[...] = jnp.broadcast_to(
        jnp.sum(d_u * normed, axis=0, keepdims=True), r.g_mlp_gain.shape
    )
    d_middle = upstream + norm_rows_back(d_u, normed, scale, r.mlp_gain[level : level + 1])
    d_branch = narrow(d_middle)
    d_mixed = wide(narrow(dot_rows(d_branch, weights.wait(out_square))))
    d_conv = narrow(d_mixed * short_branch(r, level, 0))
    d_x0 = d_mixed * wide(r.conv_rows[...])
    r.ends[...] = jnp.zeros_like(r.ends)
    r.ends[:2] = d_x0[:2]
    store_blocks(r.d_conv, flip(d_conv), r.ends[...])
    r.flush(r.d_conv)
    r.d_x0[...] = d_x0
    r.d_middle[...] = d_middle
    for side in range(2):
        at = slice(side * half, (side + 1) * half)
        r.all_columns[side, :, wide_half : wide_half + half] = d_branch[:, at]
        r.all_columns[side, :, wide_half + half : wide_half + width] = d_down[:, at]
    side = r.place[0]
    r.columns_send[...] = r.all_columns[1 - side]
    r.columns_keep[...] = r.all_columns[side]


def mlp_fetch(r, level, weights):
    width = r.out_proj.shape[2]
    out_square = weights.fetch(r.out_proj.at[level])
    ups, downs = [], []
    for j in range(r.up_proj.shape[2] // width):
        at = pl.ds(j * width, width)
        ups.append(weights.fetch(r.up_proj.at[level, :, at]))
        downs.append(weights.fetch(r.down_proj.at[level, at]))
    return out_square, ups, downs


def mlp_fetch_back(r, level, weights):
    width = r.out_proj.shape[2]
    ups, downs = [], []
    for j in range(r.up_proj.shape[2] // width):
        at = pl.ds(j * width, width)
        downs.append(weights.fetch(r.down_proj.at[level, at]))
        ups.append(weights.fetch(r.up_proj.at[level, :, at]))
    return weights.fetch(r.out_proj.at[level]), ups, downs


def middle_kernel(level, pieces):
    def body(r):
        weights = Weights(r.slots, r.sems)
        squares = mlp_fetch(r, level, weights)
        r.begin()
        mix_squares = weights.fetch_columns(r.in_proj.at[level + 1], r.state.shape[1])
        state = after_conv(r, level, weights, squares, pieces)
        r.next_state[...] = state
        gain = r.mix_gain[level + 1 : level + 2]
        mix_forward(r, level + 1, state, weights, mix_squares, gain)

    return body


def turn_kernel(level, pieces):
    def body(r):
        weights = Weights(r.slots, r.sems)
        squares = mlp_fetch(r, level, weights)
        r.begin()
        r.next_state[...] = after_conv(r, level, weights, squares, pieces)
        before_conv_back(r, level, wide(r.cotangent[...]), weights, squares)

    return body


def after_short_back(r, level, weights, squares):
    rows, width = r.d_x0.shape
    owned = width >> SEQ_BITS
    half, wide_half = width // 2, 3 * width // 2
    d_gated = wide(flip(r.d_gated[:, :owned].reshape(width, rows)))
    ahead = jnp.zeros((16, width), jnp.float32)
    for j in range(1 << SEQ_BITS):
        piece = wide(r.d_gated[j, owned:])
        filled = jnp.concatenate([piece, jnp.zeros((16, width - rows), jnp.float32)], axis=1)
        ahead = ahead + rotate(filled, j * owned)
    d_u = jnp.zeros_like(d_gated)
    shorted = {}
    for branch in (1, 2, 0):
        taps = taps_of(r, level, branch)
        items = lagged(r, branch)
        if branch == 0:
            d_block, d_ahead = r.d_x0[...], ahead[8:10]
        else:
            other = 3 - branch
            d_block = d_gated * short_branch(r, level, other)
            first, second = short_ahead(r, level, other)
            d_ahead = (ahead[0:1] * first, ahead[1:2] * second)
            d_ahead = jnp.concatenate(d_ahead, axis=0)
        d_projected = narrow(tapped(taps, (d_block, *shifted_up(d_block, d_ahead))))
        for piece in range(2):
            side, lane = divmod((branch * 2 + piece) * half, wide_half)
            lane += r.all_columns.shape[2] - wide_half
            r.all_columns[side, :, lane : lane + half] = d_projected[
                :, piece * half : (piece + 1) * half
            ]
        d_u = d_u + dot_rows(d_projected, weights.wait(squares[branch]))
        for lag, item in enumerate(items):
            store_line(r.small, 3 * lag + branch, jnp.sum(d_block * item, axis=0, keepdims=True))
    return d_u


def input_gradient(r, level, d_u):
    normed, scale = norm_rows(wide(r.state[...]))
    store_line(r.small, 9, jnp.sum(d_u * normed, axis=0, keepdims=True))
    store_line(r.small, 10, r.g_mlp_gain_in[0:1])
    lines = 11 * (r.state.shape[1] // 128)
    r.small[lines:] = jnp.zeros_like(r.small[lines:])
    return r.d_middle_in[...] + norm_rows_back(
        d_u, normed, scale, r.mix_gain[level : level + 1]
    )


def between_kernel(level):
    def body(r):
        weights = Weights(r.slots, r.sems)
        mix_squares = weights.fetch_columns(r.in_proj.at[level], r.d_x0_in.shape[1])
        r.begin()
        squares = mlp_fetch_back(r, level - 1, weights)
        upper = Renamed(
            r, d_x0="d_x0_in", projected="upper_projected", edge="upper_edge", ahead="upper_ahead"
        )
        d_u = after_short_back(upper, level, weights, mix_squares)
        upstream = input_gradient(upper, level, d_u)
        before_conv_back(r, level - 1, upstream, weights, squares)

    return body


def leave_kernel(r):
    weights = Weights(r.slots, r.sems)
    squares = weights.fetch_columns(r.in_proj.at[0], r.d_x0.shape[1])
    r.begin()
    d_u = after_short_back(r, 0, weights, squares)
    side = r.place[0]
    r.in_send[...] = r.all_columns[1 - side]
    r.in_keep[...] = r.all_columns[side]
    r.flush(r.in_send, r.in_keep)
    r.upstream[...] = input_gradient(r, 0, d_u)
    r[2][...] = r[0][...]
    r[3][...] = r[1][...]


def filter_kernel(level):
    def body(r):
        shards, channels, rows = r.window.shape
        width = r.filter_last.shape[2]
        pick = (
            lax.broadcasted_iota(jnp.int32, (channels, width), 1)
            == lax.broadcasted_iota(jnp.int32, (channels, width), 0) + r.place[5]
        ).astype(jnp.float32)
        one, slope_one = sin_cos(across(r.filter_first[:, level], r.features[...], 0, 0))
        r.one[...] = one
        r.slope_one[...] = slope_one
        r.flush(r.one, r.slope_one)
        two, slope_two = sin_cos(across(r.filter_middle[level], one, 0, 0))
        r.two[...] = two
        r.slope_two[...] = slope_two
        r.flush(r.two, r.slope_two)
        last = across(pick, r.filter_last[level], 1, 1)
        r.last[...] = last
        r.raw[...] = across(last, two, 1, 0)

        def own(row):
            return jnp.sum(pick * row, axis=1, keepdims=True)

        rate = own(r.decay_rates[level : level + 1])
        lane = lax.broadcasted_iota(jnp.int32, r.near.shape, 1)
        near = jnp.broadcast_to(own(r.filter_skip[level : level + 1]), r.near.shape)
        for branch in (1, 2):
            for lag, row in enumerate(taps_of(r, level, branch)):
                near = jnp.where(lane == 3 * branch - 2 + lag, own(row), near)
        r.near[...] = near
        size = jnp.sqrt(rate + 1.0 / (shards * rows))
        step = lax.broadcasted_iota(jnp.int32, (channels, rows), 1)
        for j in range(shards):
            window = jnp.exp(-rate * (step + j * rows).astype(jnp.float32)) * size
            r.window[j] = window
            at = slice(j * rows, (j + 1) * rows)
            r.raw[:, at] = r.raw[:, at] * window
        r.flush(r.window)
        for chunk in chunks_of(channels):
            load_bins(
                [r.raw[chunk, j * rows : (j + 1) * rows] for j in range(shards)], r.bins, chunk
            )
        for k in range(shards + 1):
            r.filter_spec[k] = dot(r.bins[k], r.table[k]) * bin_scale(k, shards, rows)

    return body


def transformed(r, conjugate):
    shards, channels, rows = r.fixed.shape
    for chunk in chunks_of(channels):
        load_bins([r.fixed[j, chunk] for j in range(shards)], r.bins, chunk)
    for k in range(shards + 1):
        spec = dot(r.bins[k], r.table[k])
        r.spec[k] = narrow(spec)
        product = bin_product(spec, r.filter_spec[k], conjugate)
        r.back[k] = dot_rows(narrow(product), r.table[k])
    r.flush(r.spec)
    for chunk in chunks_of(channels):
        skip = r.near[chunk, 0:1]
        blocks = fold_bins(r.back, chunk, shards, rows)
        yield chunk, [block + skip * r.fixed[j, chunk] for j, block in enumerate(blocks)]


def conv_kernel(r):
    shards, channels, rows = r.fixed.shape
    ends = jnp.concatenate([wide(r.signal[j, channels:])[:8] for j in range(shards)], axis=0)
    ends = flip(ends)[:channels]
    lane = lax.broadcasted_iota(jnp.int32, ends.shape, 1)

    def first_two(block, taps):
        before_two = jnp.where(lane >= 8, rotate(block, 6), 0.0)
        before_one = jnp.where(lane >= 8, rotate(block, 5), 0.0)
        first = tapped(taps, (block, before_one, before_two))
        return first, tapped(taps, (rotate(block, -1), block, before_one))

    near = r.near[...]
    one = first_two(ends, [near[:, at : at + 1] for at in (1, 2, 3)])
    value = first_two(rotate(ends, -4), [near[:, at : at + 1] for at in (4, 5, 6)])
    first, second = (wide(narrow(a * b)) for a, b in zip(one, value, strict=True))
    both = jnp.where(lane % 8 == 0, first, rotate(second, 1))
    for j in range(shards):
        fixed = jnp.where(lane < 2, rotate(both, -8 * j), wide(r.signal[j, :channels]))
        r.fixed[j] = fixed
        r.gated[j] = narrow(fixed)
    r.flush(r.gated)
    for chunk, blocks in transformed(r, False):
        for j, block in enumerate(blocks):
            r.result[j, chunk] = narrow(block)


def conv_back_kernel(r):
    shards, channels, rows = r.fixed.shape
    for j in range(shards):
        r.fixed[j] = wide(r.signal[j, :channels])
    r.ends[...] = jnp.zeros_like(r.ends)
    for chunk, blocks in transformed(r, True):
        lane = lax.broadcasted_iota(jnp.int32, blocks[0].shape, 1)
        ends = jnp.zeros_like(blocks[0])
        for j, block in enumerate(blocks):
            block = narrow(block)
            r.result[j, chunk] = block
            inside = (lane >= 8 * j) & (lane < 8 * j + 2)
            ends = jnp.where(inside, rotate(wide(block), 8 * j), ends)
        r.ends[chunk] = ends
    ends = flip(r.ends[...])
    for j in range(shards - 1):
        beside = wide(r.signal[j + 1, channels:])[:8]
        ahead = jnp.concatenate([ends[8 * j + 8 : 8 * j + 16], beside], axis=0)
        r.result[j, channels:] = narrow(ahead)
    r.result[shards - 1, channels:] = jnp.zeros((16, rows), LOW)
    r.flush(r.result)
    if 0 in r.held:
        r[1][...] = r[0][...]


def filter_grads_kernel(level):
    def body(r):
        shards, channels, rows = r.gated.shape
        hidden = r.one.shape[0]
        feats = r.features.shape[0]
        for k in range(shards + 1):
            spec = bin_product(wide(r.d_spec[k]), wide(r.spec[k]), True)
            r.back[k] = dot_rows(narrow(spec * bin_scale(k, shards, rows)), r.table[k])
        r.packed[...] = jnp.zeros_like(r.packed)
        for chunk in chunks_of(channels):
            total = None
            for j, block in enumerate(fold_bins(r.back, chunk, shards, rows)):
                r.raw[chunk, j * rows : (j + 1) * rows] = block * r.window[j, chunk]
                term = wide(r.d_conv[j, chunk]) * wide(r.gated[j, chunk])
                total = term if total is None else total + term
            r.packed[hidden + chunk.start : hidden + chunk.stop, hidden : hidden + 1] = jnp.sum(
                total, axis=1, keepdims=True
            )
        d_raw = r.raw[...]
        r.packed[hidden:, :channels] = low_across(r.two[...], d_raw, 1, 1)
        d_two = low_across(r.last[...], d_raw, 0, 0) * r.slope_two[...]
        r.packed[:hidden, hidden:] = low_across(r.one[...], d_two, 1, 1)
        d_one = low_across(r.filter_middle[level], d_two, 1, 0) * r.slope_one[...]
        r.packed[:feats, :hidden] = low_across(r.features[...], d_one, 1, 1)
        if level == 0:
            at = 0
            for block in (
                r.small[...],
                r.packed[:hidden],
                r.small_above[...],
                r.packed_above[:hidden],
                r.packed[hidden:],
                r.packed_above[hidden:],
            ):
                r.joined[at : at + block.shape[0]] = block
                at += block.shape[0]

    return body


def fill_blocks(r, parts):
    tile = r.blocks.shape[3]
    for y in range(2):
        start = 0
        for rows_of, columns_of, row, count, column, columns in parts:
            at, lanes = slice(row, row + count), slice(column, column + columns)
            left = jnp.concatenate([r[0, rows_of, i][y, at] for i in range(4)], axis=1)
            right = jnp.concatenate([r[1, columns_of, i][:, lanes] for i in range(4)], axis=0)
            block = narrow(dot(left, right))
            owned = count // 4
            for z in range(4):
                for piece in range(columns // tile):
                    spot = start + piece * owned
                    r.blocks[y, z, spot : spot + owned] = block[
                        z * owned : (z + 1) * owned, piece * tile : (piece + 1) * tile
                    ]
            start += owned * (columns // tile)


def last_grad_kernel(parts):
    def body(r):
        y_own, low, high = r.place[2], r.place[3], r.place[4]
        fill_blocks(r, parts)
        tall = r.blocks.shape[2]
        for one in range(2):
            for two in range(2):
                z = (low ^ (1 - one)) + 2 * (high ^ (1 - two))
                at = 2 * one + two
                r.send[at * tall : (at + 1) * tall] = r.blocks[1 - y_own, z]
                r.keep[at] = r.blocks[y_own, z]
        height = r.small_keep.shape[0]
        for piece in range(3):
            lanes = slice(piece * 128, (piece + 1) * 128)
            block = narrow(r.small[piece * height : (piece + 1) * height])
            r.send[4 * tall :, lanes] = block
            r.small_keep[:, lanes] = block

    return body


def last_sum_kernel(r):
    count, tall = r.mine.shape[:2]
    for at in range(count):
        came = wide(r.came[at * tall : (at + 1) * tall])
        r.following[at * tall : (at + 1) * tall] = narrow(wide(r.keep[at]) + came)
    small = narrow(wide(r.small_keep[...]) + wide(r.came[2 * count * tall :]))
    r.following[count * tall :] = small
    r.flush(r.following)
    r.small_next[...] = small
    for at in range(count):
        came = wide(r.came[(count + at) * tall : (count + at + 1) * tall])
        r.mine[at] = wide(r.keep[count + at]) + came


def last_step(place, keep, small_keep, came, after):
    count, tall, tile = keep.shape
    height = small_keep.shape[0]
    return local_call(
        "last_sum",
        last_sum_kernel,
        place,
        dict(keep=keep, small_keep=small_keep, came=came),
        dict(
            following=((count // 2 * tall + height, tile), LOW),
            small_next=((height, tile), LOW),
            mine=((count // 2, tall, tile), FULL),
        ),
        after=after,
    )


def grad_kernel(parts, split):
    def body(r):
        y_own, low, high = r.place[2], r.place[3], r.place[4]
        fill_blocks(r, parts)
        for one in range(2):
            for two in range(2):
                z = (low ^ (1 - one)) + 2 * (high ^ (1 - two))
                r.p_send[one, two] = r.blocks[1 - y_own, z, :split]
                z, y = 2 * (high ^ (1 - two)), y_own ^ (1 - one)
                r.q_send[one, two] = r.blocks[y, z + 1 - low, split:]
        r.flush(r.p_send, r.q_send)
        for one in range(2):
            for two in range(2):
                z = (low ^ (1 - one)) + 2 * (high ^ (1 - two))
                r.p_keep[one, two] = r.blocks[y_own, z, :split]
                z, y = 2 * (high ^ (1 - two)), y_own ^ (1 - one)
                r.q_keep[one, two] = r.blocks[y, z + low, split:]

    return body


def crossed(block, bit):
    count = lax.axis_size("seq")
    return lax.ppermute(block, "seq", [(i, i ^ bit) for i in range(count)])


def other_sequence(block):
    return lax.ppermute(block, "dp", [(0, 1), (1, 0)])


def share_rows(keep, send):
    core = crossed(send, 1)
    return keep, other_sequence(keep), core, other_sequence(core)


def share_columns(keep, send):
    x = other_sequence(send)
    return keep, x, crossed(keep, 1), crossed(x, 1)


def partial_grads(name, place, rows, columns, parts, split, tile, cuts, after=()):
    tall = sum(count // 4 * (width // tile) for _, _, _, count, _, width in parts)
    near = {(0, key, i): item for key, items in rows.items() for i, item in enumerate(items)}
    near.update({(1, key, i): item for key, items in columns.items() for i, item in enumerate(items)})
    first, second = ((2, 2, split, tile), LOW), ((2, 2, tall - split, tile), LOW)
    return local_call(
        name,
        grad_kernel(parts, split),
        place,
        near,
        dict(p_send=first, q_send=second, p_keep=first, q_keep=second),
        dict(blocks=pltpu.VMEM((2, 4, tall, tile), LOW)),
        cuts={(0, key, i): cut for key, cut in cuts.items() for i in range(4)},
        after=after,
    )


def first_sum_kernel(r):
    for keep, one, following, mine in (
        (r.p_keep, r.p_one, r.p_next, r.p_mine),
        (r.q_keep, r.q_one, r.q_next, r.q_mine),
    ):
        following[...] = narrow(wide(keep[0]) + wide(one[0]))
        r.flush(following)
        mine[...] = wide(keep[1]) + wide(one[1])


def second_sum_kernel(r):
    split = r.p_two.shape[1]
    for mine, two, at in (
        (r.p_mine, r.p_two, slice(0, split)),
        (r.q_mine, r.q_two, slice(split, r.following.shape[0])),
    ):
        r.following[at] = narrow(mine[0] + wide(two[0]))
    r.flush(r.following)
    for mine, two, at in (
        (r.p_mine, r.p_two, slice(0, split)),
        (r.q_mine, r.q_two, slice(split, r.following.shape[0])),
    ):
        r.last[at] = mine[1] + wide(two[1])


class Reduction:
    def __init__(self, place, made, p_send=None, q_send=None):
        self.place, self.made = place, made
        p_send = made.p_send if p_send is None else p_send
        q_send = made.q_send if q_send is None else q_send
        self.p_one, self.q_one = crossed(p_send, 2), crossed(q_send, 4)
        self.p_shape, self.q_shape = made.p_send.shape[1:], made.q_send.shape[1:]

    def first(self, after=()):
        keep = dict(p_keep=self.made.p_keep, q_keep=self.made.q_keep)
        made = local_call(
            "first_sum",
            first_sum_kernel,
            self.place,
            dict(p_one=self.p_one, q_one=self.q_one, **keep),
            dict(
                p_next=(self.p_shape, LOW),
                q_next=(self.q_shape, LOW),
                p_mine=(self.p_shape, FULL),
                q_mine=(self.q_shape, FULL),
            ),
            after=after,
        )
        self.first_made = made
        self.p_two, self.q_two = crossed(made.p_next, 4), crossed(made.q_next, 2)
        return made.p_next

    def second(self, after=()):
        mine = dict(p_mine=self.first_made.p_mine, q_mine=self.first_made.q_mine)
        shape = (self.p_shape[1] + self.q_shape[1], self.p_shape[2])
        made = local_call(
            "second_sum",
            second_sum_kernel,
            self.place,
            dict(p_two=self.p_two, q_two=self.q_two, **mine),
            dict(following=(shape, LOW), last=(shape, FULL)),
            after=after,
        )
        self.three = crossed(made.following, 8)
        self.result = (made.last, self.three)
        return made.following


def collect_kernel(groups, owned):
    def body(r):
        for at, places in enumerate(groups):
            total = r[at, 0][...] + wide(r[at, 1][: r[at, 0].shape[0]])
            tile = total.shape[1]
            start = 0
            for output, level, count, pieces in places:
                for j in range(pieces):
                    r[output][level, :, j * tile : (j + 1) * tile] = total[start : start + count]
                    start += count
        width = r.g_mix_gain.shape[1]
        lines = width // 128
        hidden = r.g_middle.shape[1]
        packed = wide(r.small_last[...]) + wide(r[len(groups) - 1, 1][-r.small_last.shape[0] :])
        packed = jnp.concatenate([packed[:, j * 128 : (j + 1) * 128] for j in range(3)], axis=0)
        each = packed.shape[0] // 2
        for level in range(2):
            small = packed[level * each : (level + 1) * each]
            last = r.small_x[2 * each + level * hidden : 2 * each + (level + 1) * hidden]
            for j in range(lines):
                at = slice(j * 128, (j + 1) * 128)
                r.g_mix_gain[level : level + 1, at] = small[9 * lines + j : 9 * lines + j + 1]
                r.g_mlp_gain[level : level + 1, at] = small[10 * lines + j : 10 * lines + j + 1]
            for lag in range(3):
                for j in range(3 * lines):
                    line = 3 * lag * lines + j
                    r.g_taps[lag, level : level + 1, j * 128 : (j + 1) * 128] = small[
                        line : line + 1
                    ]
            start = each - hidden
            r.g_first[:, level] = small[start : start + r.g_first.shape[0], :hidden]
            r.g_middle[level] = small[start : start + hidden, hidden:]
            r.g_last[level] = last[:, :owned]
            r.g_skip[level : level + 1] = flip(last)[hidden : hidden + 1, :owned]

    return body


def fast_body(
    tokens,
    cotangent,
    mix_gain,
    in_proj,
    short_taps,
    filter_first,
    filter_middle,
    filter_last,
    filter_skip,
    decay_rates,
    out_proj,
    mlp_gain,
    up_proj,
    down_proj,
):
    tokens, cotangent = tokens[0], cotangent[0]
    rows, width = tokens.shape
    hidden = up_proj.shape[2]
    shards = lax.axis_size("seq")
    length = rows * shards
    owned = channels = width // shards
    inner, feats = filter_first.shape[2], filter_first.shape[1]
    seq = lax.axis_index("seq")
    place = jnp.stack(
        [lax.axis_index("dp"), seq & 1, (seq >> 1) & 1, (seq >> 2) & 1, (seq >> 3) & 1, seq * channels]
    ).astype(jnp.int32)
    features, table = position_table(length), turn_table(shards, rows)
    short_taps = short_taps.transpose(1, 0, 2)
    filter_first = filter_first.transpose(1, 0, 2)
    ups, tile, half = hidden // width, width // 2, hidden // 2
    bins, span = shards + 1, 2 * rows
    down_rows, rest_rows = 16 * owned, 12 * owned
    tall, mlp_rows = down_rows + rest_rows, 24 * owned

    def slots(count):
        return dict(
            slots=pltpu.VMEM((count, width, width), LOW), sems=pltpu.SemaphoreType.DMA((count,))
        )

    def exchange(block):
        return lax.all_to_all(block, "seq", split_axis=0, concat_axis=0, tiled=True)

    line, edges = ((rows, width), FULL), ((8, width), FULL)
    by_shard = ((shards, channels, rows), LOW)
    with_ends = ((shards, channels + 16, rows), LOW)
    spectrum = ((bins, channels, span), LOW)
    mix_outputs = dict(
        next_gated=with_ends,
        next_projected=((rows, 3 * width), LOW),
        next_tail=edges,
        next_head=edges,
        next_rows=((2, 2, 4 * owned, rows), LOW),
    )
    kept_outputs = dict(
        middle=line, slope=((rows, hidden), LOW), conv_rows=((rows, width), LOW)
    )
    rows_scratch = dict(all_rows=pltpu.VMEM((2, 2, tall, rows), LOW))

    def columns_outputs(count):
        return dict(columns_keep=((rows, count), LOW), columns_send=((rows, count), LOW))

    def columns_scratch(count):
        return dict(all_columns=pltpu.VMEM((2, rows, count), LOW), ends=ends_scratch)

    back_outputs = dict(
        d_conv=with_ends, d_x0=line, d_middle=line, g_mlp_gain=edges
    )
    small_output = ((80, 128), FULL)
    in_half = ((rows, 3 * tile), LOW)
    in_columns = ((2, *in_half[0]), LOW)
    bins_scratch = pltpu.VMEM((bins, channels, span), LOW)
    back_scratch = pltpu.VMEM((bins, channels, span), FULL)
    fixed_scratch = pltpu.VMEM((shards, channels, rows), FULL)
    ends_scratch = pltpu.VMEM((16, width), FULL)
    raw_scratch = pltpu.VMEM((channels, length), FULL)
    mlp_weights = dict(out_proj=out_proj, up_proj=up_proj, down_proj=down_proj)
    all_weights = dict(in_proj=in_proj, **mlp_weights)

    def filter_of(level):
        wave = ((inner, length), FULL)
        return local_call(
            "filter",
            filter_kernel(level),
            place,
            dict(
                features=features,
                filter_first=filter_first,
                filter_middle=filter_middle,
                filter_last=filter_last,
                decay_rates=decay_rates,
                filter_skip=filter_skip,
                short_taps=short_taps,
                table=table,
            ),
            dict(
                filter_spec=((bins, channels, span), FULL),
                near=((channels, rows), FULL),
                last=((channels, inner), FULL),
                one=wave,
                slope_one=wave,
                two=wave,
                slope_two=wave,
                window=((shards, channels, rows), FULL),
            ),
            dict(raw=raw_scratch, bins=bins_scratch),
        )

    def conv_inputs(signal, filters):
        return dict(
            signal=signal, near=filters.near, table=table, filter_spec=filters.filter_spec
        )

    conv_scratch = dict(bins=bins_scratch, back=back_scratch, fixed=fixed_scratch)

    def conv_of(signal, filters, after=()):
        return local_call(
            "conv",
            conv_kernel,
            place,
            conv_inputs(signal, filters),
            dict(spec=spectrum, gated=by_shard, result=by_shard),
            conv_scratch,
            after=after,
        )

    def conv_back_of(signal, filters, after=(), passing=None):
        near, made = conv_inputs(signal, filters), dict(spec=spectrum, result=with_ends)
        if passing is not None:
            near[0], made[1] = passing, (passing.shape, passing.dtype)
        return local_call(
            "conv_back",
            conv_back_kernel,
            place,
            near,
            made,
            dict(ends=pltpu.VMEM((rows, rows), FULL), **conv_scratch),
            after=after,
        )

    def filter_grads_of(level, filters, back, conv, d_conv, after=(), small=None):
        packed = dict(packed=((2 * inner, 128), FULL))
        scratch = dict(back=back_scratch, raw=raw_scratch)
        if small is not None:
            scratch.update({key: pltpu.VMEM(*item) for key, item in packed.items()})
            packed = dict(joined=((160 + 4 * inner, 128), FULL))
        return local_call(
            "filter_grads",
            filter_grads_kernel(level),
            place,
            dict(
                d_spec=back.spec,
                spec=conv.spec,
                table=table,
                d_conv=d_conv,
                gated=conv.gated,
                window=filters.window,
                two=filters.two,
                last=filters.last,
                slope_two=filters.slope_two,
                one=filters.one,
                filter_middle=filter_middle,
                slope_one=filters.slope_one,
                features=features,
            ),
            packed,
            scratch,
            after=after,
            later=small,
        )

    def near_of(made):
        return dict(
            projected=made.next_projected,
            edge=from_behind(made.next_tail, "seq", 1),
            ahead=from_behind(made.next_head, "seq", -1),
        )

    def row_shape(count):
        return ((2, count, rows), LOW)

    entered = local_call(
        "enter",
        enter_kernel,
        place,
        dict(tokens=tokens, mix_gain=mix_gain, short_taps=short_taps),
        mix_outputs,
        dict(ends=ends_scratch, **slots(3)),
        far=dict(in_proj=in_proj),
    )
    filters_0 = filter_of(0)
    near_0 = near_of(entered)
    conv_0 = conv_of(exchange(entered.next_gated), filters_0)
    filters_1 = filter_of(1)
    lower = local_call(
        "middle",
        middle_kernel(0, ((0, 1, 0, mlp_rows), (2, 3, mlp_rows, tall - mlp_rows))),
        place,
        dict(
            conv=exchange(conv_0.result),
            projected=near_0["projected"],
            edge=near_0["edge"],
            short_taps=short_taps,
            state=tokens,
            mlp_gain=mlp_gain,
            mix_gain=mix_gain,
        ),
        {
            **mix_outputs,
            **kept_outputs,
            **dict(next_state=line),
            0: row_shape(mlp_rows),
            1: row_shape(mlp_rows),
            2: row_shape(tall - mlp_rows),
            3: row_shape(tall - mlp_rows),
        },
        dict(ends=ends_scratch, **rows_scratch, **slots(1 + 2 * ups + 3)),
        far=all_weights,
        after=[filters_1.near, near_0["ahead"]],
        later=dict(rows=entered.next_rows),
    )
    near_1 = near_of(lower)
    rows_0 = share_rows(lower[0], lower[1])
    conv_1 = conv_of(exchange(lower.next_gated), filters_1, after=[rows_0[2]])
    in_rows_0 = share_rows(lower[2], lower[3])
    upper = turn = local_call(
        "turn",
        turn_kernel(1, ((0, 1, 0, tall),)),
        place,
        dict(
            conv=exchange(conv_1.result),
            projected=near_1["projected"],
            edge=near_1["edge"],
            short_taps=short_taps,
            state=lower.next_state,
            mlp_gain=mlp_gain,
        ),
        {
            **dict(next_state=line),
            **back_outputs,
            **columns_outputs(half + width),
            0: row_shape(tall),
            1: row_shape(tall),
        },
        {
            **{key: pltpu.VMEM(*item) for key, item in kept_outputs.items()},
            **columns_scratch(half + width),
            **rows_scratch,
            **slots(1 + 2 * ups),
        },
        far=mlp_weights,
        after=[rows_0[1], rows_0[3], near_1["ahead"]],
        later=dict(cotangent=cotangent, rows=lower.next_rows),
    )
    rows_1 = share_rows(upper[0], upper[1])

    columns_1 = share_columns(turn.columns_keep, turn.columns_send)
    d_conv_1 = exchange(turn.d_conv)
    back_1 = conv_back_of(d_conv_1, filters_1, after=[rows_1[1], rows_1[2], columns_1[2]])
    packed_1 = filter_grads_of(1, filters_1, back_1, conv_1, d_conv_1).packed
    mlp_parts = (
        (0, 0, 0, 16 * owned, half + tile, tile),
        (0, 0, 16 * owned, 4 * owned, 0, half),
        (0, 0, 20 * owned, 4 * owned, half, tile),
    )
    between = local_call(
        "between",
        between_kernel(1),
        place,
        dict(
            d_gated=exchange(back_1.result),
            short_taps=short_taps,
            upper_projected=near_1["projected"],
            upper_edge=near_1["edge"],
            upper_ahead=near_1["ahead"],
            d_x0_in=turn.d_x0,
        ),
        dict(
            small=small_output, **back_outputs, **columns_outputs(half + width + 3 * tile)
        ),
        {**columns_scratch(half + width + 3 * tile), **slots(1 + 2 * ups + 3)},
        far=all_weights,
        after=[packed_1, rows_1[3]],
        later=dict(
            state=lower.next_state,
            d_middle_in=turn.d_middle,
            g_mlp_gain_in=turn.g_mlp_gain,
            mix_gain=mix_gain,
            middle=lower.middle,
            slope=lower.slope,
            mlp_gain=mlp_gain,
            projected=near_0["projected"],
            edge=near_0["edge"],
            conv_rows=lower.conv_rows,
        ),
    )

    keep, send = between.columns_keep, between.columns_send
    columns_0 = (keep, other_sequence(send), crossed(keep, 1))
    d_conv_0 = exchange(between.d_conv)
    mlp_sum = Reduction(
        place,
        partial_grads(
            "grad_mlp",
            place,
            {0: rows_1},
            {0: columns_1},
            mlp_parts,
            224,
            tile,
            {0: (0, 24 * owned)},
            after=[between.d_conv],
        ),
    )
    back_0 = conv_back_of(
        d_conv_0, filters_0, after=[mlp_sum.made.p_send], passing=columns_0[1]
    )
    columns_0 = (*columns_0, crossed(back_0[1], 1))
    d_gated_0 = exchange(back_0.result)
    mark = mlp_sum.first(after=[back_0.spec])
    grad_mid = partial_grads(
            "grad_mid",
            place,
            {0: rows_0, 1: rows_1},
            {0: columns_0},
            (*mlp_parts, (1, 0, 0, 4 * owned, half + width, 3 * tile)),
            240,
            tile,
            {1: (24 * owned, 4 * owned)},
            after=[mark],
    )
    leave = local_call(
        "leave",
        leave_kernel,
        place,
        dict(
            d_gated=d_gated_0,
            short_taps=short_taps,
            **near_0,
            d_x0=between.d_x0,
        ),
        {2: (grad_mid.p_send.shape, LOW), 3: (grad_mid.q_send.shape, LOW)}
        | dict(in_send=in_half, in_keep=in_half, small=small_output, upstream=line),
        dict(all_columns=pltpu.VMEM(*in_columns), **slots(3)),
        far=dict(in_proj=in_proj),
        after=[mlp_sum.p_two, mlp_sum.q_two],
        later=dict(
            state=tokens,
            d_middle_in=between.d_middle,
            g_mlp_gain_in=between.g_mlp_gain,
            mix_gain=mix_gain,
        )
        | {0: grad_mid.p_send, 1: grad_mid.q_send},
    )
    mid_sum = Reduction(place, grad_mid, leave[2], leave[3])
    columns_in_0 = share_columns(leave.in_keep, leave.in_send)
    mark = mlp_sum.second(after=[leave.in_send])
    joined = filter_grads_of(
        0,
        filters_0,
        back_0,
        conv_0,
        d_conv_0,
        after=[mark],
        small=dict(small=leave.small, small_above=between.small, packed_above=packed_1),
    ).joined
    small_x = joined + other_sequence(joined)
    mark = mid_sum.first(after=[joined])
    small = small_x + crossed(small_x, 1)
    in_tall, height = 3 * owned, (small.shape[0] - 2 * inner) // 3
    near = {(0, 0, i): item for i, item in enumerate(in_rows_0)}
    near.update({(1, 0, i): item for i, item in enumerate(columns_in_0)})
    last = local_call(
        "grad_in",
        last_grad_kernel(((0, 0, 0, 4 * owned, 0, 3 * tile),)),
        place,
        {**near, **dict(small=small)},
        dict(
            send=((4 * in_tall + height, tile), LOW),
            keep=((4, in_tall, tile), LOW),
            small_keep=((height, tile), LOW),
        ),
        dict(blocks=pltpu.VMEM((2, 4, in_tall, tile), LOW)),
        after=[mark],
    )
    mark = mid_sum.second(after=[last.send, mlp_sum.three])
    step = last_step(place, last.keep, last.small_keep, crossed(last.send, 2), [mark])
    step = last_step(place, step.mine, step.small_next, crossed(step.following, 4), [])
    sums = dict(small_last=step.small_next, small_x=small_x)
    in_result = (step.mine[0], crossed(step.following, 8))
    routes = [mlp_sum.result, mid_sum.result, in_result]

    made = dict(
        g_mix_gain=((2, width), FULL),
        g_in=((2, owned, 3 * tile), FULL),
        g_taps=((3, 2, 3 * width), FULL),
        g_first=((feats, 2, inner), FULL),
        g_middle=((2, inner, inner), FULL),
        g_last=((2, inner, owned), FULL),
        g_skip=((2, owned), FULL),
        g_out=((2, owned, tile), FULL),
        g_mlp_gain=((2, width), FULL),
        g_up=((2, owned, half), FULL),
        g_down=((2, 4 * owned, tile), FULL),
    )
    in_key, out_key, up_key, down_key = (list(made)[at] for at in (1, 7, 9, 10))
    groups = (
        ((down_key, 1, 4 * owned, 1), (up_key, 1, owned, 4), (out_key, 1, owned, 1)),
        (
            (down_key, 0, 4 * owned, 1),
            (up_key, 0, owned, 4),
            (out_key, 0, owned, 1),
            (in_key, 1, owned, 3),
        ),
        ((in_key, 0, owned, 3),),
    )
    sums.update({(at, i): item for at, route in enumerate(routes) for i, item in enumerate(route)})
    turned = [list(made)[at] for at in (2, 3)]
    made = local_call("collect", collect_kernel(groups, owned), place, sums, made).kept
    for key in turned:
        made[key] = made[key].transpose(1, 0, 2)
    return (upper.next_state[None], leave.upstream[None], *made.values())


def is_fast(mesh):
    return dict(mesh.shape) == dict(dp=2, seq=1 << SEQ_BITS)


def solution(mesh):
    in_specs = (
        P("dp", "seq", None),
        P("dp", "seq", None),
        P(),
        P(),
        P(),
        P(),
        P(),
        P(),
        P(),
        P(),
        P(),
        P(),
        P(),
        P(),
    )
    out_specs = (
        P("dp", "seq", None),
        P("dp", "seq", None),
        P(),
        P(None, "seq", "dp"),
        P(),
        P(),
        P(),
        P(None, None, "seq"),
        P(None, "seq"),
        P(None, "seq", "dp"),
        P(),
        P(None, "seq", "dp"),
        P(None, "seq", "dp"),
    )
    chosen = fast_body if is_fast(mesh) else body
    return jax.shard_map(chosen, mesh=mesh, in_specs=in_specs, out_specs=out_specs, check_vma=False)
```

```python
import functools
import math

import jax
import jax.numpy as jnp
import ml_dtypes
import numpy as np
from jax import lax
from jax.experimental import pallas as pl
from jax.experimental.pallas import tpu as pltpu
from jax.sharding import PartitionSpec as P

FEATS = 33
FFT_COLS = 512


HIGHEST = lax.Precision.HIGHEST
EPSILON = 1e-05


def from_behind(block, axis, distance):
    devices = range(lax.axis_size(axis))
    route = [(i - distance, i) for i in devices if i - distance in devices]
    return lax.ppermute(block, axis, route)


def high_einsum(form, left, right):
    return jnp.einsum(form, left, right, precision=HIGHEST)


def low_einsum(form, left, right):
    return jnp.einsum(form, left, right, preferred_element_type=jnp.float32)


def to_low(value):
    return lax.optimization_barrier(value.astype(jnp.bfloat16))


def angle_table(rows, columns, modulus):
    product = lax.broadcasted_iota(jnp.int32, (rows, columns), 0) * lax.broadcasted_iota(
        jnp.int32, (rows, columns), 1
    )
    angle = (product % modulus).astype(jnp.float32) * (2.0 * math.pi / modulus)
    return (jnp.cos(angle), jnp.sin(angle))


def transform_tables(length, columns):
    total = 2 * length
    rows = total // columns
    cos_rows, sin_rows = angle_table(rows, rows, rows)
    cos_columns, sin_columns = angle_table(columns, columns, columns)
    cos_turn, sin_turn = angle_table(rows, columns, total)
    return (cos_rows, sin_rows, cos_columns, sin_columns, cos_turn, sin_turn)


def forward_transform(signal, tables):
    cos_rows, sin_rows, cos_columns, sin_columns, cos_turn, sin_turn = tables
    channels, length = signal.shape
    rows, columns = cos_turn.shape
    padded = jnp.pad(signal, ((0, 0), (0, length))).reshape(channels, rows, columns)
    first_real = high_einsum("kq,cqp->ckp", cos_rows, padded)
    first_imag = -high_einsum("kq,cqp->ckp", sin_rows, padded)
    turned_real = first_real * cos_turn + first_imag * sin_turn
    turned_imag = first_imag * cos_turn - first_real * sin_turn
    spec_real = high_einsum("ckp,pj->ckj", turned_real, cos_columns) + high_einsum(
        "ckp,pj->ckj", turned_imag, sin_columns
    )
    spec_imag = high_einsum("ckp,pj->ckj", turned_imag, cos_columns) - high_einsum(
        "ckp,pj->ckj", turned_real, sin_columns
    )
    return (spec_real, spec_imag)


def inverse_transform(spec_real, spec_imag, tables):
    cos_rows, sin_rows, cos_columns, sin_columns, cos_turn, sin_turn = tables
    rows, columns = cos_turn.shape
    back_real = high_einsum("ckp,pj->ckj", spec_real, cos_columns) - high_einsum(
        "ckp,pj->ckj", spec_imag, sin_columns
    )
    back_imag = high_einsum("ckp,pj->ckj", spec_imag, cos_columns) + high_einsum(
        "ckp,pj->ckj", spec_real, sin_columns
    )
    turned_real = back_real * cos_turn - back_imag * sin_turn
    turned_imag = back_imag * cos_turn + back_real * sin_turn
    signal = high_einsum("qk,ckp->cqp", cos_rows, turned_real) - high_einsum(
        "qk,ckp->cqp", sin_rows, turned_imag
    )
    total = rows * columns
    return signal.reshape(signal.shape[0], total)[:, : total // 2] / total


def position_features(length):
    count = (FEATS - 1) // 2
    steps = lax.broadcasted_iota(jnp.int32, (count, length), 1)
    frequency = lax.broadcasted_iota(jnp.int32, (count, length), 0) + 1
    angle = (steps * frequency % length).astype(jnp.float32) * (2.0 * math.pi / length)
    ramp = lax.broadcasted_iota(jnp.int32, (1, length), 1).astype(jnp.float32) / length
    return jnp.concatenate([ramp, jnp.cos(angle), jnp.sin(angle)], axis=0)


def filter_forward(features, first, middle, last_columns, rate_columns, length):
    pre_one = high_einsum("fk,ft->kt", first, features)
    act_one = jnp.sin(pre_one)
    pre_two = high_einsum("kj,kt->jt", middle, act_one)
    act_two = jnp.sin(pre_two)
    raw = high_einsum("kc,kt->ct", last_columns, act_two)
    steps = lax.broadcasted_iota(jnp.int32, (1, length), 1).astype(jnp.float32)
    window = jnp.exp(-rate_columns[:, None] * steps) * jnp.sqrt(
        rate_columns[:, None] + 1.0 / length
    )
    return (raw * window, (pre_one, act_one, pre_two, act_two, window))


def filter_backward(d_response, features, middle, last_columns, kept):
    pre_one, act_one, pre_two, act_two, window = kept
    d_raw = d_response * window
    g_last = high_einsum("kt,ct->kc", act_two, d_raw)
    d_two = high_einsum("kc,ct->kt", last_columns, d_raw) * jnp.cos(pre_two)
    g_middle = high_einsum("kt,jt->kj", act_one, d_two)
    d_one = high_einsum("kj,jt->kt", middle, d_two) * jnp.cos(pre_one)
    g_first = high_einsum("ft,kt->fk", features, d_one)
    return (g_first, g_middle, g_last)


def normalize(state):
    centred = state - jnp.mean(state, axis=1, keepdims=True)
    scale = lax.rsqrt(jnp.mean(centred * centred, axis=1, keepdims=True) + EPSILON)
    return (centred * scale, scale)


def normalize_back(d_out, normed, scale, gain):
    d_normed = d_out * gain
    g_gain = jnp.sum(d_out * normed, axis=0)
    d_state = scale * (
        d_normed
        - jnp.mean(d_normed, axis=1, keepdims=True)
        - normed * jnp.mean(d_normed * normed, axis=1, keepdims=True)
    )
    return (d_state, g_gain)


def short_forward(extended, taps):
    length = extended.shape[-1] - 2
    return (
        taps[0] * extended[..., 2:]
        + taps[1] * extended[..., 1 : length + 1]
        + taps[2] * extended[..., :length]
    )


def short_backward(d_extended, taps):
    length = d_extended.shape[-1] - 2
    return (
        taps[0] * d_extended[..., :length]
        + taps[1] * d_extended[..., 1 : length + 1]
        + taps[2] * d_extended[..., 2:]
    )


def tap_grads(d_shorted, extended):
    length = d_shorted.shape[-1]
    return jnp.stack(
        [
            jnp.sum(d_shorted * extended[..., 2 - lag : 2 - lag + length], axis=-1)
            for lag in range(3)
        ]
    )


def long_forward(gated, filter_real, filter_imag, skip_columns, tables):
    signal = gated.astype(jnp.float32)
    sig_real, sig_imag = forward_transform(signal, tables)
    result = inverse_transform(
        sig_real * filter_real - sig_imag * filter_imag,
        sig_real * filter_imag + sig_imag * filter_real,
        tables,
    )
    return (result + skip_columns[:, None] * signal, (sig_real, sig_imag))


def long_backward(d_conv, gated, filter_real, filter_imag, skip_columns, signal_spec, tables):
    d_signal = d_conv.astype(jnp.float32)
    d_real, d_imag = forward_transform(d_signal, tables)
    sig_real, sig_imag = signal_spec
    d_gated = (
        inverse_transform(
            d_real * filter_real + d_imag * filter_imag,
            d_imag * filter_real - d_real * filter_imag,
            tables,
        )
        + skip_columns[:, None] * d_signal
    )
    d_response = inverse_transform(
        d_real * sig_real + d_imag * sig_imag, d_imag * sig_real - d_real * sig_imag, tables
    )
    g_skip = jnp.sum(d_signal * gated.astype(jnp.float32), axis=1)
    return (d_gated, d_response, g_skip)


def unit(k,n):
    k%=n
    if (4*k)%n==0:
        q=(4*k)//n
        return [(1.0,0.0),(0.0,-1.0),(-1.0,0.0),(0.0,1.0)][q]
    a=-2.0*math.pi*k/n
    return (math.cos(a),math.sin(a))
def times(z,w):
    re,im=z; c,s=w
    if s==0.0: return (re,im) if c==1.0 else (-re,-im)
    if c==0.0: return (-im,re) if s==1.0 else (im,-re)
    return (re*c-im*s, re*s+im*c)
def plus(a,b): return (a[0]+b[0],a[1]+b[1])
def minus(a,b): return (a[0]-b[0],a[1]-b[1])
def complex_dft(zs,sign):
    n=len(zs)
    if n==1: return zs
    ev=complex_dft(zs[0::2],sign); od=complex_dft(zs[1::2],sign)
    lo,hi=[],[]
    for k in range(n//2):
        v=times(od[k],unit(sign*k,n))
        lo.append(plus(ev[k],v)); hi.append(minus(ev[k],v))
    return lo+hi
def odd_bins(xs):
    n=len(xs); h=n//2; N=2*n
    zs=[times((xs[j],-xs[j+h]),unit(j,N)) for j in range(h)]
    bins={}
    for q,z in enumerate(complex_dft(zs,1)):
        k=4*q+1
        if k<=n: bins[k]=z
        else: bins[N-k]=(z[0],-z[1])
    return bins
def real_bins(xs):
    n=len(xs)
    if n==1: return {0:(xs[0],None)}
    if n==2: return {0:(xs[0]+xs[1],None),1:(xs[0]-xs[1],None)}
    h=n//2
    bins={2*k:z for k,z in real_bins([xs[j]+xs[j+h] for j in range(h)]).items()}
    bins.update(odd_bins([xs[j]-xs[j+h] for j in range(h)]))
    return bins
def padded_bins(xs):
    bins={2*k:z for k,z in real_bins(xs).items()}
    bins.update(odd_bins(xs))
    return bins
def odd_back(bins,n):
    h=n//2; N=2*n
    zs=[]
    for q in range(h):
        k=4*q+1
        if k<=n: zs.append(bins[k])
        else:
            re,im=bins[N-k]; zs.append((re,-im))
    vs=[times(z,unit(-j,N)) for j,z in enumerate(complex_dft(zs,-1))]
    return [v[0] for v in vs]+[-v[1] for v in vs]
def real_back(bins,n):
    if n==1: return [bins[0][0]]
    if n==2: return [bins[0][0]+bins[1][0],bins[0][0]-bins[1][0]]
    h=n//2
    ev=real_back({k//2:z for k,z in bins.items() if k%2==0},h)
    od=odd_back(bins,h)
    return [ev[j]+od[j] for j in range(h)]+[ev[j]-od[j] for j in range(h)]
def padded_back(bins,n):
    ev=real_back({k//2:z for k,z in bins.items() if k%2==0},n)
    od=odd_back(bins,n)
    return [a+b for a,b in zip(ev,od)]


def turn_table(shards, rows):
    total = 2 * shards * rows
    early = np.arange(rows)[None, :, None]
    late = np.arange(rows)[None, None, :]
    bins = np.arange(shards + 1)[:, None, None]
    angle = (early * (bins + 2 * shards * late) % total) * (2.0 * np.pi / total)
    cos, sin = np.cos(angle), np.sin(angle)
    top = np.concatenate([cos, -sin], axis=2)
    bottom = np.concatenate([sin, cos], axis=2)
    return jnp.asarray(np.concatenate([top, bottom], axis=1).astype(ml_dtypes.bfloat16))


def position_table(length):
    count = (FEATS - 1) // 2
    steps = np.arange(length)[None, :]
    angle = (steps * np.arange(1, count + 1)[:, None] % length) * (2.0 * np.pi / length)
    table = np.concatenate([steps / length, np.cos(angle), np.sin(angle)], axis=0)
    return jnp.asarray(table.astype(np.float32))


def chunks_of(channels):
    step = 16 if channels % 16 == 0 else channels
    return [slice(at, at + step) for at in range(0, channels, step)]


def load_bins(blocks, bins_ref, chunk):
    lanes = blocks[0].shape[-1]
    for k, (re, im) in padded_bins(blocks).items():
        im = jnp.zeros_like(re) if im is None else im
        bins_ref[k, chunk, :lanes] = re.astype(jnp.bfloat16)
        bins_ref[k, chunk, lanes:] = im.astype(jnp.bfloat16)


def fold_bins(back_ref, chunk, count, lanes):
    bins = {
        k: (back_ref[k, chunk, :lanes], back_ref[k, chunk, lanes:]) for k in range(count + 1)
    }
    return padded_back(bins, count)


def bin_scale(k, shards, rows):
    total = 2 * shards * rows
    return (1.0 if k in (0, shards) else 2.0) / total


def bin_product(left, right, conjugate):
    lanes = left.shape[1] // 2
    a, b = left[:, :lanes], left[:, lanes:]
    c, d = right[:, :lanes], right[:, lanes:]
    if conjugate:
        return jnp.concatenate([a * c + b * d, b * c - a * d], axis=1)
    return jnp.concatenate([a * c - b * d, a * d + b * c], axis=1)


def turn(left, table):
    return jnp.dot(left, table, preferred_element_type=jnp.float32)


def turn_back(left, table):
    return lax.dot_general(
        left.astype(jnp.bfloat16),
        table,
        (((1,), (1,)), ((), ())),
        preferred_element_type=jnp.float32,
    )


def sin_cos(angle):
    steps = jnp.floor(angle * (2.0 / math.pi) + 0.5)
    rest = angle - steps * 1.5703125
    rest = rest - steps * 4.837512969970703e-4
    rest = rest - steps * 7.549789954891882e-8
    square = rest * rest
    sin = rest + rest * square * (
        -1.6666654611e-1 + square * (8.3321608736e-3 + square * -1.9515295891e-4)
    )
    cos = (
        1.0
        - 0.5 * square
        + square
        * square
        * (4.166664568298827e-2 + square * (-1.388731625493765e-3 + square * 2.443315711809948e-5))
    )
    quarter = steps.astype(jnp.int32)
    odd = (quarter & 1) == 1
    sin_out = jnp.where(odd, cos, sin)
    cos_out = jnp.where(odd, sin, cos)
    sin_out = jnp.where((quarter & 2) == 2, -sin_out, sin_out)
    cos_out = jnp.where(((quarter + 1) & 2) == 2, -cos_out, cos_out)
    return sin_out, cos_out


def across(left, right, left_side, right_side):
    return lax.dot_general(
        left,
        right,
        (((left_side,), (right_side,)), ((), ())),
        precision=HIGHEST,
        preferred_element_type=jnp.float32,
    )


def filter_network_kernel(
    feature_ref,
    first_ref,
    middle_ref,
    last_ref,
    rate_ref,
    table_ref,
    spec_ref,
    one_ref,
    slope_one_ref,
    two_ref,
    slope_two_ref,
    window_ref,
    raw_ref,
    bins_ref,
):
    shards, channels, rows = window_ref.shape
    one, slope_one = sin_cos(across(first_ref[...], feature_ref[...], 0, 0))
    one_ref[...] = one
    slope_one_ref[...] = slope_one
    two, slope_two = sin_cos(across(middle_ref[...], one, 0, 0))
    two_ref[...] = two
    slope_two_ref[...] = slope_two
    raw_ref[...] = across(last_ref[...], two, 0, 0)
    rate = rate_ref[...]
    size = jnp.sqrt(rate + 1.0 / (shards * rows))
    step = lax.broadcasted_iota(jnp.int32, (channels, rows), 1)
    for j in range(shards):
        window = jnp.exp(-rate * (step + j * rows).astype(jnp.float32)) * size
        window_ref[j] = window
        at = slice(j * rows, (j + 1) * rows)
        raw_ref[:, at] = raw_ref[:, at] * window
    for chunk in chunks_of(channels):
        load_bins(
            [raw_ref[chunk, j * rows : (j + 1) * rows] for j in range(shards)], bins_ref, chunk
        )
    for k in range(shards + 1):
        spec_ref[k] = turn(bins_ref[k], table_ref[k]) * bin_scale(k, shards, rows)


def filter_network(features, first, middle, last, rates, table):
    hidden, channels = last.shape
    length = features.shape[1]
    bins, span, _ = table.shape
    rows = span // 2
    shards = length // rows
    wide = jax.ShapeDtypeStruct((hidden, length), jnp.float32)
    return pl.pallas_call(
        filter_network_kernel,
        out_shape=[
            jax.ShapeDtypeStruct((bins, channels, span), jnp.float32),
            wide,
            wide,
            wide,
            wide,
            jax.ShapeDtypeStruct((shards, channels, rows), jnp.float32),
        ],
        scratch_shapes=[
            pltpu.VMEM((channels, length), jnp.float32),
            pltpu.VMEM((bins, channels, span), jnp.bfloat16),
        ],
        compiler_params=pltpu.CompilerParams(vmem_limit_bytes=40 << 20),
        name="filter_network",
    )(features, first, middle, last, rates, table)


def conv_forward_kernel(
    gated_ref, filter_ref, skip_ref, table_ref, conv_ref, spec_ref, bins_ref, back_ref
):
    shards, channels, rows = gated_ref.shape
    for chunk in chunks_of(channels):
        load_bins(
            [gated_ref[j, chunk].astype(jnp.float32) for j in range(shards)], bins_ref, chunk
        )
    for k in range(shards + 1):
        spec = turn(bins_ref[k], table_ref[k])
        spec_ref[k] = spec.astype(jnp.bfloat16)
        back_ref[k] = turn_back(bin_product(spec, filter_ref[k], False), table_ref[k])
    for chunk in chunks_of(channels):
        skip = skip_ref[chunk]
        for j, block in enumerate(fold_bins(back_ref, chunk, shards, rows)):
            conv = block + skip * gated_ref[j, chunk].astype(jnp.float32)
            conv_ref[j, chunk] = conv.astype(jnp.bfloat16)


def conv_backward_kernel(
    gated_ref, filter_ref, skip_ref, table_ref, conv_ref, spec_ref, bins_ref, back_ref
):
    shards, channels, rows = gated_ref.shape
    for chunk in chunks_of(channels):
        load_bins(
            [gated_ref[j, chunk].astype(jnp.float32) for j in range(shards)], bins_ref, chunk
        )
    for k in range(shards + 1):
        spec = turn(bins_ref[k], table_ref[k])
        spec_ref[k] = spec.astype(jnp.bfloat16)
        back_ref[k] = turn_back(bin_product(spec, filter_ref[k], True), table_ref[k])
    for chunk in chunks_of(channels):
        skip = skip_ref[chunk]
        for j, block in enumerate(fold_bins(back_ref, chunk, shards, rows)):
            conv = block + skip * gated_ref[j, chunk].astype(jnp.float32)
            conv_ref[j, chunk] = conv.astype(jnp.bfloat16)


def conv_call(kernel, name, gated, filter_spec, skip, table):
    bins, channels, span = filter_spec.shape
    return pl.pallas_call(
        kernel,
        out_shape=[
            jax.ShapeDtypeStruct(gated.shape, jnp.bfloat16),
            jax.ShapeDtypeStruct((bins, channels, span), jnp.bfloat16),
        ],
        scratch_shapes=[
            pltpu.VMEM((bins, channels, span), jnp.bfloat16),
            pltpu.VMEM((bins, channels, span), jnp.float32),
        ],
        compiler_params=pltpu.CompilerParams(vmem_limit_bytes=40 << 20),
        name=name,
    )(gated, filter_spec, skip, table)


def conv_forward(gated, filter_spec, skip, table):
    return conv_call(conv_forward_kernel, "conv_forward", gated, filter_spec, skip, table)


def conv_backward(d_conv, filter_spec, skip, table):
    return conv_call(conv_backward_kernel, "conv_backward", d_conv, filter_spec, skip, table)


def filter_back_kernel(
    d_spec_ref,
    spec_ref,
    d_conv_ref,
    gated_ref,
    feature_ref,
    middle_ref,
    last_ref,
    one_ref,
    slope_one_ref,
    two_ref,
    slope_two_ref,
    window_ref,
    table_ref,
    g_first_ref,
    g_middle_ref,
    g_last_ref,
    g_skip_ref,
    back_ref,
    raw_ref,
):
    shards, channels, rows = d_conv_ref.shape
    for k in range(shards + 1):
        spec = bin_product(
            d_spec_ref[k].astype(jnp.float32), spec_ref[k].astype(jnp.float32), True
        )
        back_ref[k] = turn_back(spec * bin_scale(k, shards, rows), table_ref[k])
    for chunk in chunks_of(channels):
        total = None
        for j, block in enumerate(fold_bins(back_ref, chunk, shards, rows)):
            raw_ref[chunk, j * rows : (j + 1) * rows] = block * window_ref[j, chunk]
            term = d_conv_ref[j, chunk].astype(jnp.float32) * gated_ref[j, chunk].astype(
                jnp.float32
            )
            total = term if total is None else total + term
        g_skip_ref[chunk] = jnp.sum(total, axis=1, keepdims=True)
    d_raw = raw_ref[...]
    g_last_ref[...] = across(two_ref[...], d_raw, 1, 1)
    d_two = across(last_ref[...], d_raw, 1, 0) * slope_two_ref[...]
    g_middle_ref[...] = across(one_ref[...], d_two, 1, 1)
    d_one = across(middle_ref[...], d_two, 1, 0) * slope_one_ref[...]
    g_first_ref[...] = across(feature_ref[...], d_one, 1, 1)


def filter_network_back(
    d_spec, spec, d_conv, gated, features, middle, last, kept, table
):
    _, one, slope_one, two, slope_two, window = kept
    bins, channels, span = spec.shape
    hidden, length = one.shape
    feats = features.shape[0]
    return pl.pallas_call(
        filter_back_kernel,
        out_shape=[
            jax.ShapeDtypeStruct((feats, hidden), jnp.float32),
            jax.ShapeDtypeStruct((hidden, hidden), jnp.float32),
            jax.ShapeDtypeStruct((hidden, channels), jnp.float32),
            jax.ShapeDtypeStruct((channels, 1), jnp.float32),
        ],
        scratch_shapes=[
            pltpu.VMEM((bins, channels, span), jnp.float32),
            pltpu.VMEM((channels, length), jnp.float32),
        ],
        compiler_params=pltpu.CompilerParams(vmem_limit_bytes=40 << 20),
        name="filter_network_back",
    )(
        d_spec,
        spec,
        d_conv,
        gated,
        features,
        middle,
        last,
        one,
        slope_one,
        two,
        slope_two,
        window,
        table,
    )


def layer_forward(state, weights, setting):
    (
        mix_gain,
        in_proj,
        short_taps,
        first,
        middle,
        last,
        skip,
        rates,
        out_proj,
        mlp_gain,
        up_proj,
        down_proj,
    ) = weights
    features, tables, offset = setting
    rows, width = state.shape
    length = features.shape[1]
    channels = width // (length // rows)
    normed_mix, scale_mix = normalize(state)
    u_mix = to_low(normed_mix * mix_gain)
    projected = to_low(low_einsum("td,dc->ct", u_mix, in_proj)).reshape(3, width, rows)
    last_columns = lax.dynamic_slice_in_dim(last, offset, channels, 1)
    skip_columns = lax.dynamic_slice_in_dim(skip, offset, channels, 0)
    rate_columns = lax.dynamic_slice_in_dim(rates, offset, channels, 0)
    filter_kept = filter_network(
        features, first, middle, last_columns, rate_columns[:, None], tables
    )
    filter_spec = filter_kept[0]
    taps = short_taps.reshape(3, 3, width)
    edge = from_behind(projected[:, :, rows - 2 :], "seq", 1)
    extended = jnp.concatenate([edge, projected], axis=2).astype(jnp.float32)
    tap_use = taps[:, :, :, None]
    shorted = short_forward(extended, tap_use)
    gated_rows = to_low(shorted[2] * shorted[1])
    shards = length // rows
    gated = lax.all_to_all(
        gated_rows.reshape(shards, channels, rows), "seq", split_axis=0, concat_axis=0, tiled=True
    )
    conv_low, signal_spec = conv_forward(gated, filter_spec, skip_columns[:, None], tables)
    conv_here = lax.all_to_all(
        conv_low, "seq", split_axis=0, concat_axis=0, tiled=True
    ).reshape(width, rows)
    mixed = to_low(conv_here.astype(jnp.float32) * shorted[0])
    middle_state = state + low_einsum("ct,ce->te", mixed, out_proj)
    normed_mlp, scale_mlp = normalize(middle_state)
    u_mlp = to_low(normed_mlp * mlp_gain)
    hidden = low_einsum("td,df->tf", u_mlp, up_proj)
    active = to_low(jax.nn.gelu(hidden))
    result = middle_state + low_einsum("tf,fe->te", active, down_proj)
    kept = (
        normed_mix,
        scale_mix,
        u_mix,
        extended,
        shorted,
        gated,
        conv_here,
        mixed,
        filter_kept,
        filter_spec,
        signal_spec,
        normed_mlp,
        scale_mlp,
        u_mlp,
        hidden,
        active,
        last_columns,
        skip_columns,
        tap_use,
    )
    return (result, kept)


def layer_backward(upstream, kept, weights, setting):
    (
        mix_gain,
        in_proj,
        short_taps,
        first,
        middle,
        last,
        skip,
        rates,
        out_proj,
        mlp_gain,
        up_proj,
        down_proj,
    ) = weights
    features, tables, offset = setting
    (
        normed_mix,
        scale_mix,
        u_mix,
        extended,
        shorted,
        gated,
        conv_here,
        mixed,
        filter_kept,
        filter_spec,
        signal_spec,
        normed_mlp,
        scale_mlp,
        u_mlp,
        hidden,
        active,
        last_columns,
        skip_columns,
        tap_use,
    ) = kept
    rows, width = upstream.shape
    d_down = to_low(upstream)
    g_down = low_einsum("tf,te->fe", active, d_down)
    d_active = low_einsum("te,fe->tf", d_down, down_proj)
    d_hidden = to_low(jax.vjp(jax.nn.gelu, hidden)[1](d_active)[0])
    g_up = low_einsum("td,tf->df", u_mlp, d_hidden)
    d_u_mlp = low_einsum("tf,df->td", d_hidden, up_proj)
    d_middle, g_mlp_gain = normalize_back(d_u_mlp, normed_mlp, scale_mlp, mlp_gain)
    d_middle = d_middle + upstream
    d_branch = to_low(d_middle)
    g_out = low_einsum("ct,te->ce", mixed, d_branch)
    d_mixed = to_low(low_einsum("te,ce->ct", d_branch, out_proj))
    d_mixed_wide = d_mixed.astype(jnp.float32)
    d_conv_rows = to_low(d_mixed_wide * shorted[0])
    d_zero = d_mixed_wide * conv_here.astype(jnp.float32)
    shards, channels, _ = gated.shape
    d_conv = lax.all_to_all(
        d_conv_rows.reshape(gated.shape), "seq", split_axis=0, concat_axis=0, tiled=True
    )
    d_gated, d_spec = conv_backward(d_conv, filter_spec, skip_columns[:, None], tables)
    d_gated_rows = lax.all_to_all(
        d_gated, "seq", split_axis=0, concat_axis=0, tiled=True
    ).reshape(width, rows).astype(jnp.float32)
    d_shorted = jnp.stack([d_zero, d_gated_rows * shorted[2], d_gated_rows * shorted[1]])
    after = from_behind(d_shorted[:, :, :2], "seq", -1)
    d_extended = jnp.concatenate([d_shorted, after], axis=2)
    d_projected = to_low(short_backward(d_extended, tap_use))
    g_taps = tap_grads(d_shorted, extended)
    g_first, g_middle, g_last, g_skip = filter_network_back(
        d_spec, signal_spec, d_conv, gated, features, middle, last_columns, filter_kept, tables
    )
    g_skip = g_skip[:, 0]
    d_flat = d_projected.reshape(3 * width, rows)
    g_in = low_einsum("td,ct->dc", u_mix, d_flat)
    d_u_mix = low_einsum("ct,dc->td", d_flat, in_proj)
    d_state, g_mix_gain = normalize_back(d_u_mix, normed_mix, scale_mix, mix_gain)
    d_state = d_state + d_middle
    large = (g_in, g_out, g_up, g_down)
    small = (g_mix_gain, g_taps.reshape(3, 3 * width), g_first, g_middle, g_mlp_gain)
    column_part = (g_last, g_skip)
    return (d_state, large, small, column_part)


def body(
    tokens,
    cotangent,
    mix_gain,
    in_proj,
    short_taps,
    filter_first,
    filter_middle,
    filter_last,
    filter_skip,
    decay_rates,
    out_proj,
    mlp_gain,
    up_proj,
    down_proj,
):
    rows = tokens.shape[1]
    width = tokens.shape[2]
    layer_count = mix_gain.shape[0]
    shards = lax.axis_size("seq")
    length = rows * shards
    offset = lax.axis_index("seq") * (width // shards)
    setting = (position_table(length), turn_table(shards, rows), offset)
    stacks = (
        mix_gain,
        in_proj,
        short_taps,
        filter_first,
        filter_middle,
        filter_last,
        filter_skip,
        decay_rates,
        out_proj,
        mlp_gain,
        up_proj,
        down_proj,
    )
    state = tokens[0].astype(jnp.float32)
    kept_all = []
    for level in range(layer_count):
        weights = tuple((item[level] for item in stacks))
        state, kept = layer_forward(state, weights, setting)
        kept_all.append(kept)
    upstream = cotangent[0].astype(jnp.float32)
    large_all = [None] * layer_count
    small_all = [None] * layer_count
    column_all = [None] * layer_count
    for level in reversed(range(layer_count)):
        weights = tuple((item[level] for item in stacks))
        upstream, large, small, column_part = layer_backward(
            upstream, kept_all[level], weights, setting
        )
        large_all[level] = large
        small_all[level] = small
        column_all[level] = column_part
    stacked_large = [
        jnp.stack([large_all[level][member] for level in range(layer_count)]) for member in range(4)
    ]
    row_in, row_out, row_up, row_down = (
        lax.psum_scatter(stacked_large[0], "seq", scatter_dimension=1, tiled=True),
        lax.psum_scatter(stacked_large[1], "seq", scatter_dimension=1, tiled=True),
        lax.psum_scatter(stacked_large[2], "seq", scatter_dimension=1, tiled=True),
        lax.psum_scatter(stacked_large[3], "seq", scatter_dimension=1, tiled=True),
    )
    g_in, g_out, g_up, g_down = (
        lax.psum_scatter(row_in.astype(jnp.bfloat16), "dp", scatter_dimension=2, tiled=True).astype(
            jnp.float32
        ),
        lax.psum_scatter(
            row_out.astype(jnp.bfloat16), "dp", scatter_dimension=2, tiled=True
        ).astype(jnp.float32),
        lax.psum_scatter(row_up.astype(jnp.bfloat16), "dp", scatter_dimension=2, tiled=True).astype(
            jnp.float32
        ),
        lax.psum_scatter(
            row_down.astype(jnp.bfloat16), "dp", scatter_dimension=2, tiled=True
        ).astype(jnp.float32),
    )
    stacked_small = [
        jnp.stack([small_all[level][member] for level in range(layer_count)]) for member in range(5)
    ]
    g_mix_gain, g_taps, g_first, g_middle, g_mlp_gain = lax.psum(
        (stacked_small[0], stacked_small[1], stacked_small[2], stacked_small[3], stacked_small[4]),
        ("dp", "seq"),
    )
    stacked_last = jnp.stack([column_all[level][0] for level in range(layer_count)])
    stacked_skip = jnp.stack([column_all[level][1] for level in range(layer_count)])
    g_last, g_skip = lax.psum((stacked_last, stacked_skip), "dp")
    return (
        state[None],
        upstream[None],
        g_mix_gain,
        g_in,
        g_taps,
        g_first,
        g_middle,
        g_last,
        g_skip,
        g_out,
        g_mlp_gain,
        g_up,
        g_down,
    )


SEQ_BITS = 4
VMEM_BYTES = 64 << 20
COST = 3000
LOW, FULL = jnp.bfloat16, jnp.float32


class Board:
    def __init__(self, place, held, inputs, outputs, later):
        self.place = place
        self.held, self.arriving, self.outputs, self.leaving = held, {}, outputs, []
        self.later = {}
        for key, (source, target, sem) in inputs.items():
            copy = pltpu.make_async_copy(source, target, sem)
            if key in later:
                self.later[key] = copy
            else:
                copy.start()
                self.arriving[key] = copy
            held[key] = target
        for key, (source, _, _) in outputs.items():
            held[key] = source

    def begin(self):
        for key, copy in self.later.items():
            copy.start()
            self.arriving[key] = copy
        self.later = {}

    def __getattr__(self, key):
        return self[key]

    def __getitem__(self, key):
        if key in self.later:
            self.begin()
        if key in self.arriving:
            self.arriving.pop(key).wait()
        return self.held[key]

    def flush(self, *refs):
        for key in [key for key, item in self.outputs.items() if any(item[0] is ref for ref in refs)]:
            copy = pltpu.make_async_copy(*self.outputs.pop(key))
            copy.start()
            self.leaving.append(copy)

    def finish(self):
        self.begin()
        self.flush(*[item[0] for item in self.outputs.values()])
        for copy in [*self.arriving.values(), *self.leaving]:
            copy.wait()


class Made:
    def __init__(self, items):
        self.__dict__.update(kept=dict(items))

    def __getattr__(self, key):
        return self.kept[key]

    def __getitem__(self, key):
        return self.kept[key]


class Renamed:
    def __init__(self, board, **names):
        self.__dict__.update(board=board, names=names)

    def __getattr__(self, key):
        return getattr(self.__dict__["board"], self.__dict__["names"].get(key, key))


def local_call(
    name,
    body,
    place,
    near,
    outputs,
    scratch=None,
    far=None,
    cuts=None,
    after=(),
    later=None,
):
    scratch, far, cuts, later = scratch or {}, far or {}, cuts or {}, later or {}
    near = {**near, **later}
    arrays = [*near.values(), *far.values(), *after]

    def shape_of(key):
        shape = list(near[key].shape)
        if key in cuts:
            shape[1] = cuts[key][1]
        return tuple(shape)

    def cut(key, ref):
        return ref.at[:, pl.ds(*cuts[key])] if key in cuts else ref

    def kernel(*refs):
        refs = list(refs)
        place_ref = refs.pop(0)
        given = [refs.pop(0) for _ in arrays]
        made = [refs.pop(0) for _ in outputs]
        here = [refs.pop(0) for _ in near]
        staged = [refs.pop(0) for _ in outputs]
        spare = [refs.pop(0) for _ in scratch]
        sems_in, sems_out = refs
        held = dict(zip(far, given[len(near) :]))
        held.update(zip(scratch, spare))
        board = Board(
            place_ref,
            held,
            {key: (cut(key, given[at]), here[at], sems_in.at[at]) for at, key in enumerate(near)},
            {key: (staged[at], made[at], sems_out.at[at]) for at, key in enumerate(outputs)},
            later,
        )
        body(board)
        board.finish()

    made = pl.pallas_call(
        kernel,
        in_specs=[pl.BlockSpec(memory_space=pltpu.SMEM)]
        + [pl.BlockSpec(memory_space=pltpu.HBM)] * len(arrays),
        out_specs=[pl.BlockSpec(memory_space=pltpu.HBM)] * len(outputs),
        out_shape=[jax.ShapeDtypeStruct(*item) for item in outputs.values()],
        scratch_shapes=[pltpu.VMEM(shape_of(key), near[key].dtype) for key in near]
        + [pltpu.VMEM(*item) for item in outputs.values()]
        + list(scratch.values())
        + [
            pltpu.SemaphoreType.DMA((max(len(near), 1),)),
            pltpu.SemaphoreType.DMA((max(len(outputs), 1),)),
        ],
        compiler_params=pltpu.CompilerParams(vmem_limit_bytes=VMEM_BYTES),
        cost_estimate=pl.CostEstimate(flops=0, bytes_accessed=COST, transcendentals=0),
        name=name,
    )(place, *arrays)
    return Made(zip(outputs, made, strict=True))


class Weights:
    def __init__(self, slots, sems):
        self.slots, self.sems, self.copies = slots, sems, []

    def fetch(self, source):
        at = len(self.copies)
        copy = pltpu.make_async_copy(source, self.slots.at[at], self.sems.at[at])
        copy.start()
        self.copies.append(copy)
        return at

    def fetch_columns(self, source, width):
        count = source.shape[1] // width
        return [self.fetch(source.at[:, pl.ds(j * width, width)]) for j in range(count)]

    def fetch_rows(self, source, width):
        count = source.shape[0] // width
        return [self.fetch(source.at[pl.ds(j * width, width)]) for j in range(count)]

    def wait(self, at):
        if self.copies[at] is not None:
            self.copies[at].wait()
            self.copies[at] = None
        return self.slots[at]


def dot(left, right):
    return jnp.dot(left, right, preferred_element_type=jnp.float32)


def dot_rows(left, right):
    return lax.dot_general(
        left, right, (((1,), (1,)), ((), ())), preferred_element_type=jnp.float32
    )


def low_across(left, right, left_side, right_side):
    return lax.dot_general(
        narrow(left),
        narrow(right),
        (((left_side,), (right_side,)), ((), ())),
        preferred_element_type=jnp.float32,
    )


def flip(block):
    return block.T


def wide(value):
    return value.astype(jnp.float32)


def narrow(value):
    return value.astype(jnp.bfloat16)


def rotate(block, shift):
    return pltpu.roll(block, shift % block.shape[1], 1)


def shifted_down(block, edge):
    row = lax.broadcasted_iota(jnp.int32, block.shape, 0)
    one = jnp.where(row == 0, edge[1:2], pltpu.roll(block, 1, 0))
    two = jnp.where(row == 0, edge[0:1], jnp.where(row == 1, edge[1:2], pltpu.roll(block, 2, 0)))
    return one, two


def shifted_up(block, edge):
    rows = block.shape[0]
    row = lax.broadcasted_iota(jnp.int32, block.shape, 0)
    one = jnp.where(row == rows - 1, edge[0:1], pltpu.roll(block, rows - 1, 0))
    two = jnp.where(
        row == rows - 1,
        edge[1:2],
        jnp.where(row == rows - 2, edge[0:1], pltpu.roll(block, rows - 2, 0)),
    )
    return one, two


def branch_columns(r, branch):
    width = r.projected.shape[1] // 3
    return slice(branch * width, (branch + 1) * width)


def taps_of(r, level, branch):
    width = r.short_taps.shape[2] // 3
    at = slice(branch * width, (branch + 1) * width)
    return [r.short_taps[lag, level : level + 1, at] for lag in range(3)]


def lagged(r, branch):
    block = wide(r.projected[:, branch_columns(r, branch)])
    return (block, *shifted_down(block, r.edge[2 * branch : 2 * branch + 2]))


def tapped(taps, items):
    return taps[0] * items[0] + taps[1] * items[1] + taps[2] * items[2]


def short_branch(r, level, branch):
    return tapped(taps_of(r, level, branch), lagged(r, branch))


def short_ahead(r, level, branch):
    here = wide(r.projected[-16:, branch_columns(r, branch)])[-2:]
    ahead = r.ahead[2 * branch : 2 * branch + 2]
    taps = taps_of(r, level, branch)
    first = tapped(taps, (ahead[0:1], here[1:2], here[0:1]))
    return first, tapped(taps, (ahead[1:2], ahead[0:1], here[1:2]))


def norm_rows(state):
    centred = state - jnp.mean(state, axis=1, keepdims=True)
    scale = lax.rsqrt(jnp.mean(centred * centred, axis=1, keepdims=True) + EPSILON)
    return centred * scale, scale


def norm_rows_back(d_out, normed, scale, gain):
    q = d_out * gain
    return scale * (
        q
        - jnp.mean(q, axis=1, keepdims=True)
        - normed * jnp.mean(q * normed, axis=1, keepdims=True)
    )


def gelu_and_slope(x):
    square = x * x
    tanh = jnp.tanh(x * (0.7978845608028654 + 0.035677408136300125 * square))
    half = 0.5 + 0.5 * tanh
    inner = 0.7978845608028654 + 0.10703222440890037 * square
    return x * half, half + 0.5 * x * (1.0 - tanh * tanh) * inner


def store_rows(target, start, first_block, block_rows, flipped):
    for j in range(flipped.shape[0] // block_rows):
        owner = first_block + j
        z, y, core = owner >> 2, (owner >> 1) & 1, owner & 1
        at = start + z * block_rows
        target[core, y, at : at + block_rows] = flipped[j * block_rows : (j + 1) * block_rows]


def store_line(target, line, vector):
    lanes = target.shape[1]
    pieces = vector.shape[1] // lanes
    for j in range(pieces):
        target[line * pieces + j : line * pieces + j + 1] = vector[:, j * lanes : (j + 1) * lanes]


def store_blocks(target, flipped, ends):
    owned = flipped.shape[0] >> SEQ_BITS
    lanes = target.shape[2]
    lane = lax.broadcasted_iota(jnp.int32, (ends.shape[0], lanes), 1)
    for j in range(1 << SEQ_BITS):
        target[j, :owned] = flipped[j * owned : (j + 1) * owned]
        beside = rotate(ends, -j * owned)[:, :lanes]
        target[j, owned:] = narrow(jnp.where(lane < owned, beside, 0.0))


def mix_forward(r, level, state, weights, squares, gain):
    normed, _ = norm_rows(state)
    u = narrow(normed * gain)
    rows, width = u.shape
    owned = width >> SEQ_BITS
    nothing = jnp.zeros((2, width), jnp.float32)
    r.ends[...] = jnp.zeros_like(r.ends)
    gate = None
    for branch in (1, 2, 0):
        block = narrow(dot(u, weights.wait(squares[branch])))
        r.next_projected[:, branch * width : (branch + 1) * width] = block
        block = wide(block)
        at = slice(2 * branch, 2 * branch + 2)
        r.next_head[at], r.next_tail[at] = block[:2], block[-2:]
        if branch > 0:
            spot = 4 * branch - 4
            r.ends[spot : spot + 2], r.ends[spot + 2 : spot + 4] = block[:2], block[-2:]
            items = (block, *shifted_down(block, nothing))
            part = tapped(taps_of(r, level, branch), items)
            gate = part if gate is None else gate * part
        if branch == 2:
            store_blocks(r.next_gated, flip(narrow(gate)), r.ends[...])
            r.flush(r.next_gated)
    r.next_head[6:] = jnp.zeros_like(r.next_head[6:])
    r.next_tail[6:] = jnp.zeros_like(r.next_tail[6:])
    r.flush(r.next_projected, r.next_head, r.next_tail)
    store_rows(r.next_rows, 0, 0, owned, flip(u))


def enter_kernel(r):
    weights = Weights(r.slots, r.sems)
    squares = weights.fetch_columns(r.in_proj.at[0], r.tokens.shape[1])
    r.begin()
    mix_forward(r, 0, wide(r.tokens[...]), weights, squares, r.mix_gain[0:1])


def after_conv(r, level, weights, squares, pieces):
    out_square, ups, downs = squares
    rows, width = r.state.shape
    owned = width >> SEQ_BITS
    conv = flip(r.conv[...].reshape(width, rows))
    r.conv_rows[...] = conv
    r.flush(r.conv_rows)
    mixed = narrow(wide(conv) * short_branch(r, level, 0))
    middle = wide(r.state[...]) + dot(mixed, weights.wait(out_square))
    r.middle[...] = middle
    r.flush(r.middle)
    normed, _ = norm_rows(middle)
    u = narrow(normed * r.mlp_gain[level : level + 1])
    hidden = dot(u, weights.wait(ups[0]))
    total = middle
    for j, down in enumerate(downs):
        following = weights.wait(ups[j + 1]) if j + 1 < len(ups) else None
        down = weights.wait(down)
        coming = None if following is None else dot(u, following)
        active, slope = gelu_and_slope(hidden)
        r.slope[:, j * width : (j + 1) * width] = narrow(slope)
        active = narrow(active)
        total = total + dot(active, down)
        store_rows(r.all_rows, 0, 4 * j, 4 * owned, flip(active))
        hidden = coming
    store_rows(r.all_rows, 4 * 4 * owned, 0, owned, flip(u))
    store_rows(r.all_rows, 5 * 4 * owned, 0, owned, flip(mixed))
    for core in range(2):
        for y in range(2):
            r.all_rows[core, y, 6 * 4 * owned :] = r.rows[core, y]
    core = r.place[1]
    for keep, send, start, count in pieces:
        r[send][...] = r.all_rows[1 - core, :, start : start + count]
        r[keep][...] = r.all_rows[core, :, start : start + count]
    return total


def before_conv_back(r, level, upstream, weights, squares):
    out_square, ups, downs = squares
    rows, width = upstream.shape
    half, wide_half = width // 2, 2 * width
    d_down = narrow(upstream)
    middle = r.middle[...]
    normed, scale = norm_rows(middle)
    d_u = jnp.zeros_like(middle)
    d_active = dot_rows(d_down, weights.wait(downs[0]))
    for j, up in enumerate(ups):
        following = weights.wait(downs[j + 1]) if j + 1 < len(downs) else None
        up = weights.wait(up)
        coming = None if following is None else dot_rows(d_down, following)
        d_hidden = narrow(d_active * wide(r.slope[:, j * width : (j + 1) * width]))
        side, at = divmod(j * width, wide_half)
        r.all_columns[side, :, at : at + width] = d_hidden
        d_u = d_u + dot_rows(d_hidden, up)
        d_active = coming
    r.g_mlp_gain[...] = jnp.broadcast_to(
        jnp.sum(d_u * normed, axis=0, keepdims=True), r.g_mlp_gain.shape
    )
    d_middle = upstream + norm_rows_back(d_u, normed, scale, r.mlp_gain[level : level + 1])
    d_branch = narrow(d_middle)
    d_mixed = wide(narrow(dot_rows(d_branch, weights.wait(out_square))))
    d_conv = narrow(d_mixed * short_branch(r, level, 0))
    d_x0 = d_mixed * wide(r.conv_rows[...])
    r.ends[...] = jnp.zeros_like(r.ends)
    r.ends[:2] = d_x0[:2]
    store_blocks(r.d_conv, flip(d_conv), r.ends[...])
    r.flush(r.d_conv)
    r.d_x0[...] = d_x0
    r.d_middle[...] = d_middle
    for side in range(2):
        at = slice(side * half, (side + 1) * half)
        r.all_columns[side, :, wide_half : wide_half + half] = d_branch[:, at]
        r.all_columns[side, :, wide_half + half : wide_half + width] = d_down[:, at]
    side = r.place[0]
    r.columns_send[...] = r.all_columns[1 - side]
    r.columns_keep[...] = r.all_columns[side]


def mlp_fetch(r, level, weights):
    width = r.out_proj.shape[2]
    out_square = weights.fetch(r.out_proj.at[level])
    ups, downs = [], []
    for j in range(r.up_proj.shape[2] // width):
        at = pl.ds(j * width, width)
        ups.append(weights.fetch(r.up_proj.at[level, :, at]))
        downs.append(weights.fetch(r.down_proj.at[level, at]))
    return out_square, ups, downs


def mlp_fetch_back(r, level, weights):
    width = r.out_proj.shape[2]
    ups, downs = [], []
    for j in range(r.up_proj.shape[2] // width):
        at = pl.ds(j * width, width)
        downs.append(weights.fetch(r.down_proj.at[level, at]))
        ups.append(weights.fetch(r.up_proj.at[level, :, at]))
    return weights.fetch(r.out_proj.at[level]), ups, downs


def middle_kernel(level, pieces):
    def body(r):
        weights = Weights(r.slots, r.sems)
        squares = mlp_fetch(r, level, weights)
        r.begin()
        mix_squares = weights.fetch_columns(r.in_proj.at[level + 1], r.state.shape[1])
        state = after_conv(r, level, weights, squares, pieces)
        r.next_state[...] = state
        gain = r.mix_gain[level + 1 : level + 2]
        mix_forward(r, level + 1, state, weights, mix_squares, gain)

    return body


def turn_kernel(level, pieces):
    def body(r):
        weights = Weights(r.slots, r.sems)
        squares = mlp_fetch(r, level, weights)
        r.begin()
        r.next_state[...] = after_conv(r, level, weights, squares, pieces)
        before_conv_back(r, level, wide(r.cotangent[...]), weights, squares)

    return body


def after_short_back(r, level, weights, squares):
    rows, width = r.d_x0.shape
    owned = width >> SEQ_BITS
    half, wide_half = width // 2, 3 * width // 2
    d_gated = wide(flip(r.d_gated[:, :owned].reshape(width, rows)))
    ahead = jnp.zeros((16, width), jnp.float32)
    for j in range(1 << SEQ_BITS):
        piece = wide(r.d_gated[j, owned:])
        filled = jnp.concatenate([piece, jnp.zeros((16, width - rows), jnp.float32)], axis=1)
        ahead = ahead + rotate(filled, j * owned)
    d_u = jnp.zeros_like(d_gated)
    shorted = {}
    for branch in (1, 2, 0):
        taps = taps_of(r, level, branch)
        items = lagged(r, branch)
        if branch == 0:
            d_block, d_ahead = r.d_x0[...], ahead[8:10]
        else:
            other = 3 - branch
            d_block = d_gated * short_branch(r, level, other)
            first, second = short_ahead(r, level, other)
            d_ahead = (ahead[0:1] * first, ahead[1:2] * second)
            d_ahead = jnp.concatenate(d_ahead, axis=0)
        d_projected = narrow(tapped(taps, (d_block, *shifted_up(d_block, d_ahead))))
        for piece in range(2):
            side, lane = divmod((branch * 2 + piece) * half, wide_half)
            lane += r.all_columns.shape[2] - wide_half
            r.all_columns[side, :, lane : lane + half] = d_projected[
                :, piece * half : (piece + 1) * half
            ]
        d_u = d_u + dot_rows(d_projected, weights.wait(squares[branch]))
        for lag, item in enumerate(items):
            store_line(r.small, 3 * lag + branch, jnp.sum(d_block * item, axis=0, keepdims=True))
    return d_u


def input_gradient(r, level, d_u):
    normed, scale = norm_rows(wide(r.state[...]))
    store_line(r.small, 9, jnp.sum(d_u * normed, axis=0, keepdims=True))
    store_line(r.small, 10, r.g_mlp_gain_in[0:1])
    lines = 11 * (r.state.shape[1] // 128)
    r.small[lines:] = jnp.zeros_like(r.small[lines:])
    return r.d_middle_in[...] + norm_rows_back(
        d_u, normed, scale, r.mix_gain[level : level + 1]
    )


def between_kernel(level):
    def body(r):
        weights = Weights(r.slots, r.sems)
        mix_squares = weights.fetch_columns(r.in_proj.at[level], r.d_x0_in.shape[1])
        r.begin()
        squares = mlp_fetch_back(r, level - 1, weights)
        upper = Renamed(
            r, d_x0="d_x0_in", projected="upper_projected", edge="upper_edge", ahead="upper_ahead"
        )
        d_u = after_short_back(upper, level, weights, mix_squares)
        upstream = input_gradient(upper, level, d_u)
        before_conv_back(r, level - 1, upstream, weights, squares)

    return body


def leave_kernel(r):
    weights = Weights(r.slots, r.sems)
    squares = weights.fetch_columns(r.in_proj.at[0], r.d_x0.shape[1])
    r.begin()
    d_u = after_short_back(r, 0, weights, squares)
    side = r.place[0]
    r.in_send[...] = r.all_columns[1 - side]
    r.in_keep[...] = r.all_columns[side]
    r.flush(r.in_send, r.in_keep)
    r.upstream[...] = input_gradient(r, 0, d_u)
    r[2][...] = r[0][...]
    r[3][...] = r[1][...]


def filter_kernel(level):
    def body(r):
        shards, channels, rows = r.window.shape
        width = r.filter_last.shape[2]
        pick = (
            lax.broadcasted_iota(jnp.int32, (channels, width), 1)
            == lax.broadcasted_iota(jnp.int32, (channels, width), 0) + r.place[5]
        ).astype(jnp.float32)
        one, slope_one = sin_cos(across(r.filter_first[:, level], r.features[...], 0, 0))
        r.one[...] = one
        r.slope_one[...] = slope_one
        r.flush(r.one, r.slope_one)
        two, slope_two = sin_cos(across(r.filter_middle[level], one, 0, 0))
        r.two[...] = two
        r.slope_two[...] = slope_two
        r.flush(r.two, r.slope_two)
        last = across(pick, r.filter_last[level], 1, 1)
        r.last[...] = last
        r.raw[...] = across(last, two, 1, 0)

        def own(row):
            return jnp.sum(pick * row, axis=1, keepdims=True)

        rate = own(r.decay_rates[level : level + 1])
        lane = lax.broadcasted_iota(jnp.int32, r.near.shape, 1)
        near = jnp.broadcast_to(own(r.filter_skip[level : level + 1]), r.near.shape)
        for branch in (1, 2):
            for lag, row in enumerate(taps_of(r, level, branch)):
                near = jnp.where(lane == 3 * branch - 2 + lag, own(row), near)
        r.near[...] = near
        size = jnp.sqrt(rate + 1.0 / (shards * rows))
        step = lax.broadcasted_iota(jnp.int32, (channels, rows), 1)
        for j in range(shards):
            window = jnp.exp(-rate * (step + j * rows).astype(jnp.float32)) * size
            r.window[j] = window
            at = slice(j * rows, (j + 1) * rows)
            r.raw[:, at] = r.raw[:, at] * window
        r.flush(r.window)
        for chunk in chunks_of(channels):
            load_bins(
                [r.raw[chunk, j * rows : (j + 1) * rows] for j in range(shards)], r.bins, chunk
            )
        for k in range(shards + 1):
            r.filter_spec[k] = dot(r.bins[k], r.table[k]) * bin_scale(k, shards, rows)

    return body


def transformed(r, conjugate):
    shards, channels, rows = r.fixed.shape
    for chunk in chunks_of(channels):
        load_bins([r.fixed[j, chunk] for j in range(shards)], r.bins, chunk)
    for k in range(shards + 1):
        spec = dot(r.bins[k], r.table[k])
        r.spec[k] = narrow(spec)
        product = bin_product(spec, r.filter_spec[k], conjugate)
        r.back[k] = dot_rows(narrow(product), r.table[k])
    r.flush(r.spec)
    for chunk in chunks_of(channels):
        skip = r.near[chunk, 0:1]
        blocks = fold_bins(r.back, chunk, shards, rows)
        yield chunk, [block + skip * r.fixed[j, chunk] for j, block in enumerate(blocks)]


def conv_kernel(r):
    shards, channels, rows = r.fixed.shape
    ends = jnp.concatenate([wide(r.signal[j, channels:])[:8] for j in range(shards)], axis=0)
    ends = flip(ends)[:channels]
    lane = lax.broadcasted_iota(jnp.int32, ends.shape, 1)

    def first_two(block, taps):
        before_two = jnp.where(lane >= 8, rotate(block, 6), 0.0)
        before_one = jnp.where(lane >= 8, rotate(block, 5), 0.0)
        first = tapped(taps, (block, before_one, before_two))
        return first, tapped(taps, (rotate(block, -1), block, before_one))

    near = r.near[...]
    one = first_two(ends, [near[:, at : at + 1] for at in (1, 2, 3)])
    value = first_two(rotate(ends, -4), [near[:, at : at + 1] for at in (4, 5, 6)])
    first, second = (wide(narrow(a * b)) for a, b in zip(one, value, strict=True))
    both = jnp.where(lane % 8 == 0, first, rotate(second, 1))
    for j in range(shards):
        fixed = jnp.where(lane < 2, rotate(both, -8 * j), wide(r.signal[j, :channels]))
        r.fixed[j] = fixed
        r.gated[j] = narrow(fixed)
    r.flush(r.gated)
    for chunk, blocks in transformed(r, False):
        for j, block in enumerate(blocks):
            r.result[j, chunk] = narrow(block)


def conv_back_kernel(r):
    shards, channels, rows = r.fixed.shape
    for j in range(shards):
        r.fixed[j] = wide(r.signal[j, :channels])
    r.ends[...] = jnp.zeros_like(r.ends)
    for chunk, blocks in transformed(r, True):
        lane = lax.broadcasted_iota(jnp.int32, blocks[0].shape, 1)
        ends = jnp.zeros_like(blocks[0])
        for j, block in enumerate(blocks):
            block = narrow(block)
            r.result[j, chunk] = block
            inside = (lane >= 8 * j) & (lane < 8 * j + 2)
            ends = jnp.where(inside, rotate(wide(block), 8 * j), ends)
        r.ends[chunk] = ends
    ends = flip(r.ends[...])
    for j in range(shards - 1):
        beside = wide(r.signal[j + 1, channels:])[:8]
        ahead = jnp.concatenate([ends[8 * j + 8 : 8 * j + 16], beside], axis=0)
        r.result[j, channels:] = narrow(ahead)
    r.result[shards - 1, channels:] = jnp.zeros((16, rows), LOW)
    r.flush(r.result)
    if 0 in r.held:
        r[1][...] = r[0][...]


def filter_grads_kernel(level):
    def body(r):
        shards, channels, rows = r.gated.shape
        hidden = r.one.shape[0]
        feats = r.features.shape[0]
        for k in range(shards + 1):
            spec = bin_product(wide(r.d_spec[k]), wide(r.spec[k]), True)
            r.back[k] = dot_rows(narrow(spec * bin_scale(k, shards, rows)), r.table[k])
        r.packed[...] = jnp.zeros_like(r.packed)
        for chunk in chunks_of(channels):
            total = None
            for j, block in enumerate(fold_bins(r.back, chunk, shards, rows)):
                r.raw[chunk, j * rows : (j + 1) * rows] = block * r.window[j, chunk]
                term = wide(r.d_conv[j, chunk]) * wide(r.gated[j, chunk])
                total = term if total is None else total + term
            r.packed[hidden + chunk.start : hidden + chunk.stop, hidden : hidden + 1] = jnp.sum(
                total, axis=1, keepdims=True
            )
        d_raw = r.raw[...]
        r.packed[hidden:, :channels] = low_across(r.two[...], d_raw, 1, 1)
        d_two = low_across(r.last[...], d_raw, 0, 0) * r.slope_two[...]
        r.packed[:hidden, hidden:] = low_across(r.one[...], d_two, 1, 1)
        d_one = low_across(r.filter_middle[level], d_two, 1, 0) * r.slope_one[...]
        r.packed[:feats, :hidden] = low_across(r.features[...], d_one, 1, 1)
        if level == 0:
            at = 0
            for block in (
                r.small[...],
                r.packed[:hidden],
                r.small_above[...],
                r.packed_above[:hidden],
                r.packed[hidden:],
                r.packed_above[hidden:],
            ):
                r.joined[at : at + block.shape[0]] = block
                at += block.shape[0]

    return body


def fill_blocks(r, parts):
    tile = r.blocks.shape[3]
    for y in range(2):
        start = 0
        for rows_of, columns_of, row, count, column, columns in parts:
            at, lanes = slice(row, row + count), slice(column, column + columns)
            left = jnp.concatenate([r[0, rows_of, i][y, at] for i in range(4)], axis=1)
            right = jnp.concatenate([r[1, columns_of, i][:, lanes] for i in range(4)], axis=0)
            block = narrow(dot(left, right))
            owned = count // 4
            for z in range(4):
                for piece in range(columns // tile):
                    spot = start + piece * owned
                    r.blocks[y, z, spot : spot + owned] = block[
                        z * owned : (z + 1) * owned, piece * tile : (piece + 1) * tile
                    ]
            start += owned * (columns // tile)


def last_grad_kernel(parts):
    def body(r):
        y_own, low, high = r.place[2], r.place[3], r.place[4]
        fill_blocks(r, parts)
        tall = r.blocks.shape[2]
        for one in range(2):
            for two in range(2):
                z = (low ^ (1 - one)) + 2 * (high ^ (1 - two))
                at = 2 * one + two
                r.send[at * tall : (at + 1) * tall] = r.blocks[1 - y_own, z]
                r.keep[at] = r.blocks[y_own, z]
        height = r.small_keep.shape[0]
        for piece in range(3):
            lanes = slice(piece * 128, (piece + 1) * 128)
            block = narrow(r.small[piece * height : (piece + 1) * height])
            r.send[4 * tall :, lanes] = block
            r.small_keep[:, lanes] = block

    return body


def last_sum_kernel(r):
    count, tall = r.mine.shape[:2]
    for at in range(count):
        came = wide(r.came[at * tall : (at + 1) * tall])
        r.following[at * tall : (at + 1) * tall] = narrow(wide(r.keep[at]) + came)
    small = narrow(wide(r.small_keep[...]) + wide(r.came[2 * count * tall :]))
    r.following[count * tall :] = small
    r.flush(r.following)
    r.small_next[...] = small
    for at in range(count):
        came = wide(r.came[(count + at) * tall : (count + at + 1) * tall])
        r.mine[at] = wide(r.keep[count + at]) + came


def last_step(place, keep, small_keep, came, after):
    count, tall, tile = keep.shape
    height = small_keep.shape[0]
    return local_call(
        "last_sum",
        last_sum_kernel,
        place,
        dict(keep=keep, small_keep=small_keep, came=came),
        dict(
            following=((count // 2 * tall + height, tile), LOW),
            small_next=((height, tile), LOW),
            mine=((count // 2, tall, tile), FULL),
        ),
        after=after,
    )


def grad_kernel(parts, split):
    def body(r):
        y_own, low, high = r.place[2], r.place[3], r.place[4]
        fill_blocks(r, parts)
        for one in range(2):
            for two in range(2):
                z = (low ^ (1 - one)) + 2 * (high ^ (1 - two))
                r.p_send[one, two] = r.blocks[1 - y_own, z, :split]
                z, y = 2 * (high ^ (1 - two)), y_own ^ (1 - one)
                r.q_send[one, two] = r.blocks[y, z + 1 - low, split:]
        r.flush(r.p_send, r.q_send)
        for one in range(2):
            for two in range(2):
                z = (low ^ (1 - one)) + 2 * (high ^ (1 - two))
                r.p_keep[one, two] = r.blocks[y_own, z, :split]
                z, y = 2 * (high ^ (1 - two)), y_own ^ (1 - one)
                r.q_keep[one, two] = r.blocks[y, z + low, split:]

    return body


def crossed(block, bit):
    count = lax.axis_size("seq")
    return lax.ppermute(block, "seq", [(i, i ^ bit) for i in range(count)])


def other_sequence(block):
    return lax.ppermute(block, "dp", [(0, 1), (1, 0)])


def share_rows(keep, send):
    core = crossed(send, 1)
    return keep, other_sequence(keep), core, other_sequence(core)


def share_columns(keep, send):
    x = other_sequence(send)
    return keep, x, crossed(keep, 1), crossed(x, 1)


def partial_grads(name, place, rows, columns, parts, split, tile, cuts, after=()):
    tall = sum(count // 4 * (width // tile) for _, _, _, count, _, width in parts)
    near = {(0, key, i): item for key, items in rows.items() for i, item in enumerate(items)}
    near.update({(1, key, i): item for key, items in columns.items() for i, item in enumerate(items)})
    first, second = ((2, 2, split, tile), LOW), ((2, 2, tall - split, tile), LOW)
    return local_call(
        name,
        grad_kernel(parts, split),
        place,
        near,
        dict(p_send=first, q_send=second, p_keep=first, q_keep=second),
        dict(blocks=pltpu.VMEM((2, 4, tall, tile), LOW)),
        cuts={(0, key, i): cut for key, cut in cuts.items() for i in range(4)},
        after=after,
    )


def first_sum_kernel(r):
    for keep, one, following, mine in (
        (r.p_keep, r.p_one, r.p_next, r.p_mine),
        (r.q_keep, r.q_one, r.q_next, r.q_mine),
    ):
        following[...] = narrow(wide(keep[0]) + wide(one[0]))
        r.flush(following)
        mine[...] = wide(keep[1]) + wide(one[1])


def second_sum_kernel(r):
    split = r.p_two.shape[1]
    for mine, two, at in (
        (r.p_mine, r.p_two, slice(0, split)),
        (r.q_mine, r.q_two, slice(split, r.following.shape[0])),
    ):
        r.following[at] = narrow(mine[0] + wide(two[0]))
    r.flush(r.following)
    for mine, two, at in (
        (r.p_mine, r.p_two, slice(0, split)),
        (r.q_mine, r.q_two, slice(split, r.following.shape[0])),
    ):
        r.last[at] = mine[1] + wide(two[1])


class Reduction:
    def __init__(self, place, made, p_send=None, q_send=None):
        self.place, self.made = place, made
        p_send = made.p_send if p_send is None else p_send
        q_send = made.q_send if q_send is None else q_send
        self.p_one, self.q_one = crossed(p_send, 2), crossed(q_send, 4)
        self.p_shape, self.q_shape = made.p_send.shape[1:], made.q_send.shape[1:]

    def first(self, after=()):
        keep = dict(p_keep=self.made.p_keep, q_keep=self.made.q_keep)
        made = local_call(
            "first_sum",
            first_sum_kernel,
            self.place,
            dict(p_one=self.p_one, q_one=self.q_one, **keep),
            dict(
                p_next=(self.p_shape, LOW),
                q_next=(self.q_shape, LOW),
                p_mine=(self.p_shape, FULL),
                q_mine=(self.q_shape, FULL),
            ),
            after=after,
        )
        self.first_made = made
        self.p_two, self.q_two = crossed(made.p_next, 4), crossed(made.q_next, 2)
        return made.p_next

    def second(self, after=()):
        mine = dict(p_mine=self.first_made.p_mine, q_mine=self.first_made.q_mine)
        shape = (self.p_shape[1] + self.q_shape[1], self.p_shape[2])
        made = local_call(
            "second_sum",
            second_sum_kernel,
            self.place,
            dict(p_two=self.p_two, q_two=self.q_two, **mine),
            dict(following=(shape, LOW), last=(shape, FULL)),
            after=after,
        )
        self.three = crossed(made.following, 8)
        self.result = (made.last, self.three)
        return made.following


def collect_kernel(groups, owned):
    def body(r):
        for at, places in enumerate(groups):
            total = r[at, 0][...] + wide(r[at, 1][: r[at, 0].shape[0]])
            tile = total.shape[1]
            start = 0
            for output, level, count, pieces in places:
                for j in range(pieces):
                    r[output][level, :, j * tile : (j + 1) * tile] = total[start : start + count]
                    start += count
        width = r.g_mix_gain.shape[1]
        lines = width // 128
        hidden = r.g_middle.shape[1]
        packed = wide(r.small_last[...]) + wide(r[len(groups) - 1, 1][-r.small_last.shape[0] :])
        packed = jnp.concatenate([packed[:, j * 128 : (j + 1) * 128] for j in range(3)], axis=0)
        each = packed.shape[0] // 2
        for level in range(2):
            small = packed[level * each : (level + 1) * each]
            last = r.small_x[2 * each + level * hidden : 2 * each + (level + 1) * hidden]
            for j in range(lines):
                at = slice(j * 128, (j + 1) * 128)
                r.g_mix_gain[level : level + 1, at] = small[9 * lines + j : 9 * lines + j + 1]
                r.g_mlp_gain[level : level + 1, at] = small[10 * lines + j : 10 * lines + j + 1]
            for lag in range(3):
                for j in range(3 * lines):
                    line = 3 * lag * lines + j
                    r.g_taps[lag, level : level + 1, j * 128 : (j + 1) * 128] = small[
                        line : line + 1
                    ]
            start = each - hidden
            r.g_first[:, level] = small[start : start + r.g_first.shape[0], :hidden]
            r.g_middle[level] = small[start : start + hidden, hidden:]
            last = flip(last)
            r.g_last[level] = last[:owned]
            r.g_skip[level : level + 1] = last[hidden : hidden + 1, :owned]

    return body


def fast_body(
    tokens,
    cotangent,
    mix_gain,
    in_proj,
    short_taps,
    filter_first,
    filter_middle,
    filter_last,
    filter_skip,
    decay_rates,
    out_proj,
    mlp_gain,
    up_proj,
    down_proj,
):
    tokens, cotangent = tokens[0], cotangent[0]
    rows, width = tokens.shape
    hidden = up_proj.shape[2]
    shards = lax.axis_size("seq")
    length = rows * shards
    owned = channels = width // shards
    inner, feats = filter_first.shape[2], filter_first.shape[1]
    seq = lax.axis_index("seq")
    place = jnp.stack(
        [lax.axis_index("dp"), seq & 1, (seq >> 1) & 1, (seq >> 2) & 1, (seq >> 3) & 1, seq * channels]
    ).astype(jnp.int32)
    features, table = position_table(length), turn_table(shards, rows)
    short_taps = short_taps.transpose(1, 0, 2)
    filter_first = filter_first.transpose(1, 0, 2)
    ups, tile, half = hidden // width, width // 2, hidden // 2
    bins, span = shards + 1, 2 * rows
    down_rows, rest_rows = 16 * owned, 12 * owned
    tall, mlp_rows = down_rows + rest_rows, 24 * owned

    def slots(count):
        return dict(
            slots=pltpu.VMEM((count, width, width), LOW), sems=pltpu.SemaphoreType.DMA((count,))
        )

    def exchange(block):
        return lax.all_to_all(block, "seq", split_axis=0, concat_axis=0, tiled=True)

    line, edges = ((rows, width), FULL), ((8, width), FULL)
    by_shard = ((shards, channels, rows), LOW)
    with_ends = ((shards, channels + 16, rows), LOW)
    spectrum = ((bins, channels, span), LOW)
    mix_outputs = dict(
        next_gated=with_ends,
        next_projected=((rows, 3 * width), LOW),
        next_tail=edges,
        next_head=edges,
        next_rows=((2, 2, 4 * owned, rows), LOW),
    )
    kept_outputs = dict(
        middle=line, slope=((rows, hidden), LOW), conv_rows=((rows, width), LOW)
    )
    rows_scratch = dict(all_rows=pltpu.VMEM((2, 2, tall, rows), LOW))

    def columns_outputs(count):
        return dict(columns_keep=((rows, count), LOW), columns_send=((rows, count), LOW))

    def columns_scratch(count):
        return dict(all_columns=pltpu.VMEM((2, rows, count), LOW), ends=ends_scratch)

    back_outputs = dict(
        d_conv=with_ends, d_x0=line, d_middle=line, g_mlp_gain=edges
    )
    small_output = ((80, 128), FULL)
    in_half = ((rows, 3 * tile), LOW)
    in_columns = ((2, *in_half[0]), LOW)
    bins_scratch = pltpu.VMEM((bins, channels, span), LOW)
    back_scratch = pltpu.VMEM((bins, channels, span), FULL)
    fixed_scratch = pltpu.VMEM((shards, channels, rows), FULL)
    ends_scratch = pltpu.VMEM((16, width), FULL)
    raw_scratch = pltpu.VMEM((channels, length), FULL)
    mlp_weights = dict(out_proj=out_proj, up_proj=up_proj, down_proj=down_proj)
    all_weights = dict(in_proj=in_proj, **mlp_weights)

    def filter_of(level):
        wave = ((inner, length), FULL)
        return local_call(
            "filter",
            filter_kernel(level),
            place,
            dict(
                features=features,
                filter_first=filter_first,
                filter_middle=filter_middle,
                filter_last=filter_last,
                decay_rates=decay_rates,
                filter_skip=filter_skip,
                short_taps=short_taps,
                table=table,
            ),
            dict(
                filter_spec=((bins, channels, span), FULL),
                near=((channels, rows), FULL),
                last=((channels, inner), FULL),
                one=wave,
                slope_one=wave,
                two=wave,
                slope_two=wave,
                window=((shards, channels, rows), FULL),
            ),
            dict(raw=raw_scratch, bins=bins_scratch),
        )

    def conv_inputs(signal, filters):
        return dict(
            signal=signal, near=filters.near, table=table, filter_spec=filters.filter_spec
        )

    conv_scratch = dict(bins=bins_scratch, back=back_scratch, fixed=fixed_scratch)

    def conv_of(signal, filters, after=()):
        return local_call(
            "conv",
            conv_kernel,
            place,
            conv_inputs(signal, filters),
            dict(spec=spectrum, gated=by_shard, result=by_shard),
            conv_scratch,
            after=after,
        )

    def conv_back_of(signal, filters, after=(), passing=None):
        near, made = conv_inputs(signal, filters), dict(spec=spectrum, result=with_ends)
        if passing is not None:
            near[0], made[1] = passing, (passing.shape, passing.dtype)
        return local_call(
            "conv_back",
            conv_back_kernel,
            place,
            near,
            made,
            dict(ends=pltpu.VMEM((rows, rows), FULL), **conv_scratch),
            after=after,
        )

    def filter_grads_of(level, filters, back, conv, d_conv, after=(), small=None):
        packed = dict(packed=((2 * inner, 128), FULL))
        scratch = dict(back=back_scratch, raw=raw_scratch)
        if small is not None:
            scratch.update({key: pltpu.VMEM(*item) for key, item in packed.items()})
            packed = dict(joined=((160 + 4 * inner, 128), FULL))
        return local_call(
            "filter_grads",
            filter_grads_kernel(level),
            place,
            dict(
                d_spec=back.spec,
                spec=conv.spec,
                table=table,
                d_conv=d_conv,
                gated=conv.gated,
                window=filters.window,
                two=filters.two,
                last=filters.last,
                slope_two=filters.slope_two,
                one=filters.one,
                filter_middle=filter_middle,
                slope_one=filters.slope_one,
                features=features,
            ),
            packed,
            scratch,
            after=after,
            later=small,
        )

    def near_of(made):
        return dict(
            projected=made.next_projected,
            edge=from_behind(made.next_tail, "seq", 1),
            ahead=from_behind(made.next_head, "seq", -1),
        )

    def row_shape(count):
        return ((2, count, rows), LOW)

    entered = local_call(
        "enter",
        enter_kernel,
        place,
        dict(tokens=tokens, mix_gain=mix_gain, short_taps=short_taps),
        mix_outputs,
        dict(ends=ends_scratch, **slots(3)),
        far=dict(in_proj=in_proj),
    )
    filters_0 = filter_of(0)
    near_0 = near_of(entered)
    conv_0 = conv_of(exchange(entered.next_gated), filters_0)
    filters_1 = filter_of(1)
    lower = local_call(
        "middle",
        middle_kernel(0, ((0, 1, 0, mlp_rows), (2, 3, mlp_rows, tall - mlp_rows))),
        place,
        dict(
            conv=exchange(conv_0.result),
            projected=near_0["projected"],
            edge=near_0["edge"],
            short_taps=short_taps,
            state=tokens,
            mlp_gain=mlp_gain,
            mix_gain=mix_gain,
        ),
        {
            **mix_outputs,
            **kept_outputs,
            **dict(next_state=line),
            0: row_shape(mlp_rows),
            1: row_shape(mlp_rows),
            2: row_shape(tall - mlp_rows),
            3: row_shape(tall - mlp_rows),
        },
        dict(ends=ends_scratch, **rows_scratch, **slots(1 + 2 * ups + 3)),
        far=all_weights,
        after=[filters_1.near, near_0["ahead"]],
        later=dict(rows=entered.next_rows),
    )
    near_1 = near_of(lower)
    rows_0 = share_rows(lower[0], lower[1])
    conv_1 = conv_of(exchange(lower.next_gated), filters_1, after=[rows_0[2]])
    in_rows_0 = share_rows(lower[2], lower[3])
    upper = turn = local_call(
        "turn",
        turn_kernel(1, ((0, 1, 0, tall),)),
        place,
        dict(
            conv=exchange(conv_1.result),
            projected=near_1["projected"],
            edge=near_1["edge"],
            short_taps=short_taps,
            state=lower.next_state,
            mlp_gain=mlp_gain,
        ),
        {
            **dict(next_state=line),
            **back_outputs,
            **columns_outputs(half + width),
            0: row_shape(tall),
            1: row_shape(tall),
        },
        {
            **{key: pltpu.VMEM(*item) for key, item in kept_outputs.items()},
            **columns_scratch(half + width),
            **rows_scratch,
            **slots(1 + 2 * ups),
        },
        far=mlp_weights,
        after=[rows_0[1], rows_0[3], near_1["ahead"]],
        later=dict(cotangent=cotangent, rows=lower.next_rows),
    )
    rows_1 = share_rows(upper[0], upper[1])

    columns_1 = share_columns(turn.columns_keep, turn.columns_send)
    d_conv_1 = exchange(turn.d_conv)
    back_1 = conv_back_of(d_conv_1, filters_1, after=[rows_1[1], rows_1[2], columns_1[2]])
    packed_1 = filter_grads_of(1, filters_1, back_1, conv_1, d_conv_1).packed
    mlp_parts = (
        (0, 0, 0, 16 * owned, half + tile, tile),
        (0, 0, 16 * owned, 4 * owned, 0, half),
        (0, 0, 20 * owned, 4 * owned, half, tile),
    )
    between = local_call(
        "between",
        between_kernel(1),
        place,
        dict(
            d_gated=exchange(back_1.result),
            short_taps=short_taps,
            upper_projected=near_1["projected"],
            upper_edge=near_1["edge"],
            upper_ahead=near_1["ahead"],
            d_x0_in=turn.d_x0,
        ),
        dict(
            small=small_output, **back_outputs, **columns_outputs(half + width + 3 * tile)
        ),
        {**columns_scratch(half + width + 3 * tile), **slots(1 + 2 * ups + 3)},
        far=all_weights,
        after=[packed_1, rows_1[3]],
        later=dict(
            state=lower.next_state,
            d_middle_in=turn.d_middle,
            g_mlp_gain_in=turn.g_mlp_gain,
            mix_gain=mix_gain,
            middle=lower.middle,
            slope=lower.slope,
            mlp_gain=mlp_gain,
            projected=near_0["projected"],
            edge=near_0["edge"],
            conv_rows=lower.conv_rows,
        ),
    )

    keep, send = between.columns_keep, between.columns_send
    columns_0 = (keep, other_sequence(send), crossed(keep, 1))
    d_conv_0 = exchange(between.d_conv)
    mlp_sum = Reduction(
        place,
        partial_grads(
            "grad_mlp",
            place,
            {0: rows_1},
            {0: columns_1},
            mlp_parts,
            224,
            tile,
            {0: (0, 24 * owned)},
            after=[between.d_conv],
        ),
    )
    back_0 = conv_back_of(
        d_conv_0, filters_0, after=[mlp_sum.made.p_send], passing=columns_0[1]
    )
    columns_0 = (*columns_0, crossed(back_0[1], 1))
    d_gated_0 = exchange(back_0.result)
    mark = mlp_sum.first(after=[back_0.spec])
    grad_mid = partial_grads(
            "grad_mid",
            place,
            {0: rows_0, 1: rows_1},
            {0: columns_0},
            (*mlp_parts, (1, 0, 0, 4 * owned, half + width, 3 * tile)),
            240,
            tile,
            {1: (24 * owned, 4 * owned)},
            after=[mark],
    )
    leave = local_call(
        "leave",
        leave_kernel,
        place,
        dict(
            d_gated=d_gated_0,
            short_taps=short_taps,
            **near_0,
            d_x0=between.d_x0,
        ),
        {2: (grad_mid.p_send.shape, LOW), 3: (grad_mid.q_send.shape, LOW)}
        | dict(in_send=in_half, in_keep=in_half, small=small_output, upstream=line),
        dict(all_columns=pltpu.VMEM(*in_columns), **slots(3)),
        far=dict(in_proj=in_proj),
        after=[mlp_sum.p_two, mlp_sum.q_two],
        later=dict(
            state=tokens,
            d_middle_in=between.d_middle,
            g_mlp_gain_in=between.g_mlp_gain,
            mix_gain=mix_gain,
        )
        | {0: grad_mid.p_send, 1: grad_mid.q_send},
    )
    mid_sum = Reduction(place, grad_mid, leave[2], leave[3])
    columns_in_0 = share_columns(leave.in_keep, leave.in_send)
    mark = mlp_sum.second(after=[leave.in_send])
    joined = filter_grads_of(
        0,
        filters_0,
        back_0,
        conv_0,
        d_conv_0,
        after=[mark],
        small=dict(small=leave.small, small_above=between.small, packed_above=packed_1),
    ).joined
    small_x = joined + other_sequence(joined)
    mark = mid_sum.first(after=[joined])
    small = small_x + crossed(small_x, 1)
    in_tall, height = 3 * owned, (small.shape[0] - 2 * inner) // 3
    near = {(0, 0, i): item for i, item in enumerate(in_rows_0)}
    near.update({(1, 0, i): item for i, item in enumerate(columns_in_0)})
    last = local_call(
        "grad_in",
        last_grad_kernel(((0, 0, 0, 4 * owned, 0, 3 * tile),)),
        place,
        {**near, **dict(small=small)},
        dict(
            send=((4 * in_tall + height, tile), LOW),
            keep=((4, in_tall, tile), LOW),
            small_keep=((height, tile), LOW),
        ),
        dict(blocks=pltpu.VMEM((2, 4, in_tall, tile), LOW)),
        after=[mark],
    )
    mark = mid_sum.second(after=[last.send, mlp_sum.three])
    step = last_step(place, last.keep, last.small_keep, crossed(last.send, 2), [mark])
    step = last_step(place, step.mine, step.small_next, crossed(step.following, 4), [])
    sums = dict(small_last=step.small_next, small_x=small_x)
    in_result = (step.mine[0], crossed(step.following, 8))
    routes = [mlp_sum.result, mid_sum.result, in_result]

    made = dict(
        g_mix_gain=((2, width), FULL),
        g_in=((2, owned, 3 * tile), FULL),
        g_taps=((3, 2, 3 * width), FULL),
        g_first=((feats, 2, inner), FULL),
        g_middle=((2, inner, inner), FULL),
        g_last=((2, owned, inner), FULL),
        g_skip=((2, owned), FULL),
        g_out=((2, owned, tile), FULL),
        g_mlp_gain=((2, width), FULL),
        g_up=((2, owned, half), FULL),
        g_down=((2, 4 * owned, tile), FULL),
    )
    in_key, out_key, up_key, down_key = (list(made)[at] for at in (1, 7, 9, 10))
    groups = (
        ((down_key, 1, 4 * owned, 1), (up_key, 1, owned, 4), (out_key, 1, owned, 1)),
        (
            (down_key, 0, 4 * owned, 1),
            (up_key, 0, owned, 4),
            (out_key, 0, owned, 1),
            (in_key, 1, owned, 3),
        ),
        ((in_key, 0, owned, 3),),
    )
    sums.update({(at, i): item for at, route in enumerate(routes) for i, item in enumerate(route)})
    orders = {list(made)[at]: order for at, order in ((2, (1, 0, 2)), (3, (1, 0, 2)), (5, (0, 2, 1)))}
    made = local_call("collect", collect_kernel(groups, owned), place, sums, made).kept
    for key, order in orders.items():
        made[key] = made[key].transpose(order)
    return (upper.next_state[None], leave.upstream[None], *made.values())


def is_fast(mesh):
    return dict(mesh.shape) == dict(dp=2, seq=1 << SEQ_BITS)


def solution(mesh):
    in_specs = (
        P("dp", "seq", None),
        P("dp", "seq", None),
        P(),
        P(),
        P(),
        P(),
        P(),
        P(),
        P(),
        P(),
        P(),
        P(),
        P(),
        P(),
    )
    out_specs = (
        P("dp", "seq", None),
        P("dp", "seq", None),
        P(),
        P(None, "seq", "dp"),
        P(),
        P(),
        P(),
        P(None, None, "seq"),
        P(None, "seq"),
        P(None, "seq", "dp"),
        P(),
        P(None, "seq", "dp"),
        P(None, "seq", "dp"),
    )
    chosen = fast_body if is_fast(mesh) else body
    return jax.shard_map(chosen, mesh=mesh, in_specs=in_specs, out_specs=out_specs, check_vma=False)
```
